32 devices in a mesh: blk: 16 (over z, y, core), inner: 2 (over x).
Axes of the slice: x: 2, y: 2, z: 4, core: 2. Of those that a mesh axis runs over, the one named last changes fastest.
Arguments:
- queries: bfloat16 [3072, 5120], P('blk', 'inner'), may hold values from -48 to 48
- keys: bfloat16 [3072, 1024], P('blk', 'inner'), may hold values from -48 to 48
- values: bfloat16 [3072, 1024], P('blk', 'inner'), may hold values from -6 to 6
- positions: int32 [3072], P('blk'), may hold values from 0 to 3071, as said below
- out_weight: bfloat16 [5120, 5120], P('inner'), may hold values from -0.078125 to 0.078125
Outputs:
- projected: bfloat16 [3072, 5120], P(('blk', 'inner'))
The draws below stay inside these ranges and needn't reach their ends.
Inputs may be any that keep to these rules, and one draw needn't show every extreme that they name: The rows of index b of blk (rows 192 b to 192 b + 191) hold the positions c * 96 to c * 96 + 95 followed by (31 - c) * 96 to (31 - c) * 96 + 95, in increasing order, with a different c from 0 to 15 for every b; every position appears once.
All inputs are finite; a program needn't handle non-finite values.
Results may differ from the reference program's by a relative error of at most 0.018.
Values may be sent and summed in bfloat16 or wider, within the bound.
No kernel may reach another device: no remote copies, remote signals or barrier semaphores. Data moves between devices by JAX's collectives and lax.ppermute only.
A program may use at most 128 MiB of HBM per device.

```python
import math
import jax
import jax.numpy as jnp
from jax import lax

D = 5120
HEAD_WIDTH = 128
KEY_VALUE_HEADS = 8
QUERY_PER_KEY = 5
HQ = 40
CH = 96
TOKEN_LENGTH = 3072
N_INNER = 2


def starting_field(key, shape):
    return jnp.clip(jax.random.normal(key, shape, jnp.float32), -6.0, 6.0)


def draw_queries(key, part):
    field_vector = starting_field(jax.random.fold_in(key, 1), (TOKEN_LENGTH, KEY_VALUE_HEADS, QUERY_PER_KEY, HEAD_WIDTH))
    return field_vector.reshape(TOKEN_LENGTH, KEY_VALUE_HEADS * QUERY_PER_KEY * HEAD_WIDTH).astype(jnp.bfloat16)


def draw_keys(key, part):
    field_vector = starting_field(jax.random.fold_in(key, 2), (TOKEN_LENGTH, KEY_VALUE_HEADS, HEAD_WIDTH))
    return field_vector.reshape(TOKEN_LENGTH, KEY_VALUE_HEADS * HEAD_WIDTH).astype(jnp.bfloat16)


def draw_positions(key, part):
    pair_count = TOKEN_LENGTH // (2 * CH)
    order = jax.random.permutation(key, pair_count)
    slot_ids = jnp.arange(2 * CH)
    early = order[:, None] * CH + slot_ids[None, :]
    late = (2 * pair_count - 1 - order[:, None]) * CH + slot_ids[None, :] - CH
    return jnp.where(slot_ids[None, :] < CH, early, late).reshape(TOKEN_LENGTH).astype(jnp.int32)


def shard_levels(key, shape, cuts, low, largest):
    gain, own = 1.0, jax.random.fold_in(key, 6)
    for dim, parts in cuts:
        heights = jnp.exp(jax.random.uniform(jax.random.fold_in(own, dim), (parts,), jnp.float32, low / len(cuts), largest / len(cuts)))
        gain = gain * jnp.repeat(heights, shape[dim] // parts).reshape([-1 if axis == dim else 1 for axis in range(len(shape))])
    return gain


def scatter_about(rng, dims, deviation, most, split=(), kind=jnp.bfloat16):
    result = deviation * jax.random.normal(rng, dims, jnp.float32)
    if split:
        result = result * shard_levels(rng, dims, split, -0.22, 0.18)
    return jnp.clip(result, -most, most).astype(kind)


def setup_inputs(seed: int = 0) -> dict:
    arg_keys = jax.random.split(jax.random.key(seed), 6)
    return {
        "queries": draw_queries(jax.random.fold_in(arg_keys[5], 71), 0),
        "keys": draw_keys(jax.random.fold_in(arg_keys[5], 71), 0),
        "values": scatter_about(arg_keys[2], (TOKEN_LENGTH, KEY_VALUE_HEADS * HEAD_WIDTH), 1.0, 6.0, ((0, 16), (1, 2))),
        "positions": draw_positions(jax.random.fold_in(arg_keys[5], 71), 0),
        "out_weight": scatter_about(arg_keys[4], (HQ * HEAD_WIDTH, D), (HQ * HEAD_WIDTH) ** -0.5, 0.078125, ((0, 2),)),
    }


def reference(queries, keys, values, positions, out_weight):
    row_total = queries.shape[0]
    per_head_queries = jnp.transpose(queries.reshape(row_total, KEY_VALUE_HEADS * QUERY_PER_KEY, HEAD_WIDTH), (1, 0, 2))
    per_head_keys = jnp.repeat(jnp.transpose(keys.reshape(row_total, KEY_VALUE_HEADS, HEAD_WIDTH), (1, 0, 2)), QUERY_PER_KEY, axis=0)
    per_head_values = jnp.repeat(jnp.transpose(values.reshape(row_total, KEY_VALUE_HEADS, HEAD_WIDTH), (1, 0, 2)), QUERY_PER_KEY, axis=0)
    visible = positions[None, :] <= positions[:, None]
    inverse_root = 1.0 / math.sqrt(HEAD_WIDTH)

    def one_head(operands):
        query_head, key_head, value_head = operands
        scores = jnp.dot(query_head, key_head.T, preferred_element_type=jnp.float32) * inverse_root
        scores = jnp.where(visible, scores, -1e+30)
        highest = lax.optimization_barrier(jnp.max(scores, axis=1, keepdims=True))
        weights = jnp.where(visible, jnp.exp(scores - highest), 0.0)
        totals = lax.optimization_barrier(jnp.sum(weights, axis=1, keepdims=True))
        mixed = jnp.dot(weights.astype(jnp.bfloat16), value_head, preferred_element_type=jnp.float32)
        return (mixed / totals).astype(jnp.bfloat16)
    head_outputs = lax.map(one_head, (per_head_queries, per_head_keys, per_head_values))
    attended_values = jnp.transpose(head_outputs, (1, 0, 2)).reshape(row_total, KEY_VALUE_HEADS * QUERY_PER_KEY * HEAD_WIDTH)
    group_columns = KEY_VALUE_HEADS * QUERY_PER_KEY * HEAD_WIDTH // N_INNER
    summed = jnp.zeros((row_total, out_weight.shape[1]), jnp.float32)
    for group_id in range(N_INNER):
        part_cols = attended_values[:, group_id * group_columns:(group_id + 1) * group_columns]
        part_rows = out_weight[group_id * group_columns:(group_id + 1) * group_columns]
        partial_term = jnp.dot(part_cols, part_rows, preferred_element_type=jnp.float32).astype(jnp.bfloat16)
        summed = summed + partial_term.astype(jnp.float32)
    return summed.astype(jnp.bfloat16)
```

```python
import functools
import math

import jax
import jax.numpy as jnp
from jax import lax
from jax.experimental import pallas as pl
from jax.experimental.pallas import tpu as pltpu
from jax.sharding import PartitionSpec as P

HEAD_WIDTH = 128
QUERY_PER_KEY = 5
EXP2_SCALE = math.log2(math.e) / math.sqrt(HEAD_WIDTH)
MASKED = -1e30
VMEM_LIMIT = 48 * 1024 * 1024
CONTRACT_LAST = (((1,), (1,)), ((), ()))


def ring_of_chips(chips):
    half = chips // 2
    if chips == 8:
        return [2 * z for z in range(half)] + [2 * z + 1 for z in reversed(range(half))]
    return list(range(half)) + list(reversed(range(half, chips)))


def ring_pairs(chips, step):
    ring = ring_of_chips(chips)
    return [
        (2 * ring[i] + core, 2 * ring[(i + step) % chips] + core)
        for i in range(chips)
        for core in range(2)
    ]


def slot_sources(chips):
    ring = ring_of_chips(chips)
    place = {chip: i for i, chip in enumerate(ring)}
    forward, backward = chips // 2, chips - 1 - chips // 2
    table = []
    for b in range(2 * chips):
        at, core = place[b // 2], b % 2
        hops = [0] + [-r for r in range(1, forward + 1)] + [r for r in range(1, backward + 1)]
        row = []
        for hop in hops:
            chip = ring[(at + hop) % chips]
            row += [2 * chip + core, 2 * chip + 1 - core]
        table.append(row)
    return table


def gather_packets(packet, chips, forward, backward):
    clock = ring_pairs(chips, 1)
    counter = ring_pairs(chips, -1)
    sibling = [(b, b ^ 1) for b in range(2 * chips)]
    swap = lambda x: lax.ppermute(x, "blk", sibling)
    ups, downs = [packet], [packet]
    for _ in range(forward):
        ups.append(lax.ppermute(ups[-1], "blk", clock))
    for _ in range(backward):
        downs.append(lax.ppermute(downs[-1], "blk", counter))
    arrived = {0: packet}
    for r in range(1, forward + 1):
        arrived[-r] = ups[r]
    for r in range(1, backward + 1):
        arrived[r] = downs[r]
    return arrived, {hop: swap(x) for hop, x in arrived.items()}, ups[-1], downs[-1]


def in_slot_order(arrived, swapped, chips):
    half = chips // 2
    hops = [0] + [-r for r in range(1, half + 1)] + [r for r in range(1, chips - half)]
    out = []
    for hop in hops:
        here = hop if hop in arrived else -hop
        out += [arrived[here], swapped[here]]
    return out


def fold(state, q, k, v, mask=None):
    s = lax.dot_general(q, k, CONTRACT_LAST, preferred_element_type=jnp.float32)
    if mask is not None:
        s = jnp.where(mask, s, MASKED)
    high = jnp.max(s, axis=1, keepdims=True)
    if state is not None:
        high = jnp.maximum(state[0], high)
    p = jnp.exp2((s - high) * EXP2_SCALE).astype(jnp.bfloat16)
    ones = jnp.ones(v.shape, v.dtype)
    sums = jnp.dot(p, jnp.concatenate([v, ones], axis=1), preferred_element_type=jnp.float32)
    if state is not None:
        sums = state[1] * jnp.exp2((state[0] - high) * EXP2_SCALE) + sums
    return high, sums


def stacked_queries(q_ref, first_row, rows, head):
    return jnp.concatenate(
        [
            q_ref[
                pl.ds(first_row, rows),
                pl.ds(pl.multiple_of((head * QUERY_PER_KEY + g) * HEAD_WIDTH, HEAD_WIDTH), HEAD_WIDTH),
            ]
            for g in range(QUERY_PER_KEY)
        ],
        axis=0,
    )


def store_attended(out_ref, sums, rows, head):
    mixed = (sums[:, :HEAD_WIDTH] / sums[:, HEAD_WIDTH:]).astype(out_ref.dtype)
    for g in range(QUERY_PER_KEY):
        out_ref[
            :, pl.ds(pl.multiple_of((head * QUERY_PER_KEY + g) * HEAD_WIDTH, HEAD_WIDTH), HEAD_WIDTH)
        ] = mixed[g * rows : (g + 1) * rows]


def start_packets(tab_ref, packets, kv_ref, sems, chunk, late):
    count = len(packets)
    copies = []
    for s, packet in enumerate(packets):
        c = tab_ref[1 + s]
        at = (count - 1 - c) if late else c
        copy = pltpu.make_async_copy(
            packet, kv_ref.at[pl.ds(pl.multiple_of(at * chunk, chunk), chunk)], sems.at[s]
        )
        copy.start()
        copies.append(copy)
    return copies


def key_value(kv_ref, heads, head, first, rows):
    k_at = pl.multiple_of(head * HEAD_WIDTH, HEAD_WIDTH)
    v_at = pl.multiple_of((heads + head) * HEAD_WIDTH, HEAD_WIDTH)
    return kv_ref[pl.ds(first, rows), pl.ds(k_at, HEAD_WIDTH)], kv_ref[
        pl.ds(first, rows), pl.ds(v_at, HEAD_WIDTH)
    ]


def causal_part(state, q, kv_ref, heads, head, chunk, visible_chunks):
    rows = q.shape[0]
    tile = 2 * chunk
    key_at = lax.broadcasted_iota(jnp.int32, (rows, tile), 1)
    query_at = lax.rem(lax.broadcasted_iota(jnp.int32, (rows, tile), 0), chunk)
    ahead = key_at - query_at

    def step(t, state):
        k, v = key_value(kv_ref, heads, head, pl.multiple_of(t * tile, tile), tile)
        return fold(state, q, k, v, ahead <= (visible_chunks - 1) * chunk - t * tile)

    return lax.fori_loop(0, (visible_chunks + 1) // 2, step, state)


def early_kernel(heads, chunk, tab_ref, q_ref, *rest):
    count = (len(rest) - 5)
    packets, (early_ref, high_ref, sums_ref, kv_ref, sems) = rest[:count], rest[count:]
    for copy in start_packets(tab_ref, packets, kv_ref, sems, chunk, False):
        copy.wait()
    c = tab_ref[0]
    keys = count * chunk
    tile = 512
    rows = QUERY_PER_KEY * chunk

    def one_head(head, carry):
        q = stacked_queries(q_ref, chunk, chunk, head)
        state = None
        for first in range(0, keys, tile):
            k, v = key_value(kv_ref, heads, head, first, min(tile, keys - first))
            state = fold(state, q, k, v)
        high_ref[head] = jnp.broadcast_to(state[0], (rows, HEAD_WIDTH))
        sums_ref[head] = state[1]
        q = stacked_queries(q_ref, 0, chunk, head)
        start = (
            jnp.full((rows, 1), MASKED, jnp.float32),
            jnp.zeros((rows, 2 * HEAD_WIDTH), jnp.float32),
        )
        state = causal_part(start, q, kv_ref, heads, head, chunk, c + 1)
        store_attended(early_ref, state[1], chunk, head)
        return carry

    lax.fori_loop(0, heads, one_head, 0)


def late_kernel(heads, chunk, tab_ref, q_ref, high_ref, sums_ref, *rest):
    count = len(rest) - 3
    packets, (late_ref, kv_ref, sems) = rest[:count], rest[count:]
    for copy in start_packets(tab_ref, packets, kv_ref, sems, chunk, True):
        copy.wait()
    c = tab_ref[0]

    def one_head(head, carry):
        q = stacked_queries(q_ref, chunk, chunk, head)
        state = (high_ref[head][:, :1], sums_ref[head])
        state = causal_part(state, q, kv_ref, heads, head, chunk, count - c)
        store_attended(late_ref, state[1], chunk, head)
        return carry

    lax.fori_loop(0, heads, one_head, 0)


def attend_early(table, queries, packets, heads, chunk):
    rows = QUERY_PER_KEY * chunk
    count = len(packets)
    flops = 4 * heads * rows * HEAD_WIDTH * (count * chunk * 3 // 2)
    vmem = pl.BlockSpec(memory_space=pltpu.VMEM)
    return pl.pallas_call(
        functools.partial(early_kernel, heads, chunk),
        out_shape=(
            jax.ShapeDtypeStruct((chunk, queries.shape[1]), jnp.bfloat16),
            jax.ShapeDtypeStruct((heads, rows, HEAD_WIDTH), jnp.float32),
            jax.ShapeDtypeStruct((heads, rows, 2 * HEAD_WIDTH), jnp.float32),
        ),
        in_specs=[pl.BlockSpec(memory_space=pltpu.SMEM), vmem]
        + [pl.BlockSpec(memory_space=pl.ANY)] * count,
        out_specs=(vmem, vmem, vmem),
        scratch_shapes=[
            pltpu.VMEM((count * chunk, 2 * heads * HEAD_WIDTH), jnp.bfloat16),
            pltpu.SemaphoreType.DMA((count,)),
        ],
        cost_estimate=pl.CostEstimate(
            flops=2 * flops, bytes_accessed=8 << 20, transcendentals=flops // 512
        ),
        compiler_params=pltpu.CompilerParams(vmem_limit_bytes=VMEM_LIMIT),
        name="attend_early",
    )(table, queries, *packets)


def attend_late(table, queries, high, sums, packets, heads, chunk):
    count = len(packets)
    rows = QUERY_PER_KEY * chunk
    flops = 4 * heads * rows * HEAD_WIDTH * (count * chunk // 2)
    vmem = pl.BlockSpec(memory_space=pltpu.VMEM)
    return pl.pallas_call(
        functools.partial(late_kernel, heads, chunk),
        out_shape=jax.ShapeDtypeStruct((chunk, queries.shape[1]), jnp.bfloat16),
        in_specs=[pl.BlockSpec(memory_space=pltpu.SMEM), vmem, vmem, vmem]
        + [pl.BlockSpec(memory_space=pl.ANY)] * count,
        out_specs=vmem,
        scratch_shapes=[
            pltpu.VMEM((count * chunk, 2 * heads * HEAD_WIDTH), jnp.bfloat16),
            pltpu.SemaphoreType.DMA((count,)),
        ],
        cost_estimate=pl.CostEstimate(
            flops=2 * flops, bytes_accessed=8 << 20, transcendentals=flops // 512
        ),
        compiler_params=pltpu.CompilerParams(vmem_limit_bytes=VMEM_LIMIT),
        name="attend_late",
    )(table, queries, high, sums, *packets)


def project_kernel(pick_ref, early_ref, late_ref, w_ref, out_ref):
    rows = jnp.where(pick_ref[0] == 1, late_ref[...], early_ref[...])
    out_ref[...] = jnp.dot(rows, w_ref[...], preferred_element_type=jnp.float32).astype(out_ref.dtype)


def project(pick, early, late, out_weight, first, width, tile):
    rows, depth = early.shape
    whole = lambda j: (0, 0)
    return pl.pallas_call(
        project_kernel,
        out_shape=jax.ShapeDtypeStruct((rows, width), jnp.bfloat16),
        grid=(width // tile,),
        in_specs=[
            pl.BlockSpec(memory_space=pltpu.SMEM),
            pl.BlockSpec((rows, depth), whole),
            pl.BlockSpec((rows, depth), whole),
            pl.BlockSpec((depth, tile), lambda j: (0, first // tile + j)),
        ],
        out_specs=pl.BlockSpec((rows, tile), lambda j: (0, j)),
        cost_estimate=pl.CostEstimate(
            flops=2 * rows * depth * width, bytes_accessed=2 * depth * width, transcendentals=0
        ),
        compiler_params=pltpu.CompilerParams(vmem_limit_bytes=VMEM_LIMIT),
        name="project",
    )(pick, early, late, out_weight)


def chunk_table(positions, chunk, count):
    known = positions[:1] // chunk
    bit = 1
    while bit < count:
        pairs = [(b, b ^ bit) for b in range(count)]
        known = jnp.concatenate([known, lax.ppermute(known, "blk", pairs)])
        bit *= 2
    return known


def shards(count, inner, queries, keys, values, positions, out_weight):
    chunk = queries.shape[0] // 2
    heads = keys.shape[1] // HEAD_WIDTH
    chips = count // 2
    half = chips // 2
    b = lax.axis_index("blk")

    packet = jnp.concatenate([keys, values], axis=1)
    early_packet, late_packet = packet[:chunk], packet[chunk:]
    arrived, swapped, up_end, down_end = gather_packets(early_packet, chips, half, chips - 1 - half)
    early_packets = in_slot_order(arrived, swapped, chips)
    late_packet, _, _ = lax.optimization_barrier((late_packet, arrived[-(half - 1)], down_end))
    arrived, swapped, _, _ = gather_packets(late_packet, chips, chips - 1 - half, half)
    late_packets = in_slot_order(arrived, swapped, chips)

    known = chunk_table(positions, chunk, count)
    sources = jnp.asarray(slot_sources(chips), jnp.int32)[b] ^ b
    table = jnp.concatenate([known[:1], known[sources]])

    early, high, sums = attend_early(table, queries, early_packets, heads, chunk)
    late = attend_late(table, queries, high, sums, late_packets, heads, chunk)

    width = out_weight.shape[1]
    if inner == 2:
        mine = lax.axis_index("inner").astype(jnp.int32).reshape(1)
        parts = 4
        step = width // parts
        swap = [(0, 1), (1, 0)]
        received = []
        for j in range(parts):
            sent = project(1 - mine, early, late, out_weight, j * step, step, step // 2)
            received.append(lax.ppermute(sent, "inner", swap))
        kept = project(mine, early, late, out_weight, 0, width, step // 2)
        other = jnp.concatenate(received, axis=1)
        return (kept.astype(jnp.float32) + other.astype(jnp.float32)).astype(jnp.bfloat16)
    partial = jnp.dot(
        jnp.concatenate([early, late], axis=0), out_weight, preferred_element_type=jnp.float32
    ).astype(jnp.bfloat16)
    return lax.psum_scatter(partial, "inner", scatter_dimension=0, tiled=True)


def solution(mesh):
    placed = (P("blk", "inner"), P("blk", "inner"), P("blk", "inner"), P("blk"), P("inner", None))
    return jax.shard_map(
        functools.partial(shards, mesh.shape["blk"], mesh.shape["inner"]),
        mesh=mesh,
        in_specs=placed,
        out_specs=P(("blk", "inner"), None),
        check_vma=False,
    )
```

```python
import functools
import math

import jax
import jax.numpy as jnp
from jax import lax
from jax.experimental import pallas as pl
from jax.experimental.pallas import tpu as pltpu
from jax.sharding import PartitionSpec as P

HEAD_WIDTH = 128
QUERY_PER_KEY = 5
GROUP = QUERY_PER_KEY * HEAD_WIDTH
EXP2_SCALE = math.log2(math.e) / math.sqrt(HEAD_WIDTH)
MASKED = -1e30
VMEM_LIMIT = 16 * 1024 * 1024
HEADER = 16
LAST_LAST = (((1,), (1,)), ((), ()))
FIRST_FIRST = (((0,), (0,)), ((), ()))


def ring_of_chips(chips):
    half = chips // 2
    if chips == 8:
        return [2 * z for z in range(half)] + [2 * z + 1 for z in reversed(range(half))]
    return list(range(half)) + list(reversed(range(half, chips)))


def ring_pairs(chips, step):
    ring = ring_of_chips(chips)
    return [
        (2 * ring[i] + core, 2 * ring[(i + step) % chips] + core)
        for i in range(chips)
        for core in range(2)
    ]


def fold(states, queries, keys, values, mask=None):
    out = []
    for state, q, k, v in zip(states, queries, keys, values):
        s = lax.dot_general(k, q, LAST_LAST, preferred_element_type=jnp.float32)
        if mask is not None:
            s = jnp.where(mask, s, MASKED)
        high = jnp.max(s, axis=0, keepdims=True)
        if state is not None:
            high = jnp.maximum(state[0], high)
        p = jnp.exp2((s - high) * EXP2_SCALE)
        totals = jnp.sum(p, axis=0, keepdims=True)
        sums = lax.dot_general(
            v, p.astype(jnp.bfloat16), FIRST_FIRST, preferred_element_type=jnp.float32
        )
        if state is not None:
            shrink = jnp.exp2((state[0] - high) * EXP2_SCALE)
            totals = state[1] * shrink + totals
            sums = state[2] * shrink + sums
        out.append((high, totals, sums))
    return out


def stacked_queries(q_ref, first_row, rows, first_column):
    return jnp.concatenate(
        [
            q_ref[
                pl.ds(first_row, rows),
                pl.ds(pl.multiple_of(first_column + g * HEAD_WIDTH, HEAD_WIDTH), HEAD_WIDTH),
            ]
            for g in range(QUERY_PER_KEY)
        ],
        axis=0,
    )


def attend_kernel(plan, *refs):
    heads, chunk = plan["heads"], plan["chunk"]
    owners, count = len(plan["owners"]), len(plan["members"])
    rows = QUERY_PER_KEY * chunk
    refs = list(refs)
    core_ref = refs.pop(0)
    q_refs = [refs.pop(0) for _ in range(owners)]
    mark_refs = [refs.pop(0) for _ in range(plan["marks"])]
    packets = [refs.pop(0) for _ in range(plan["packets"])]
    if plan["carried"]:
        in_ml, in_acc = refs.pop(0), refs.pop(0)
    if plan["last"]:
        out_refs = [refs.pop(0) for _ in range(owners)]
        ml_ref, acc_ref = refs.pop(0), refs.pop(0)
    else:
        ml_ref, acc_ref = refs.pop(0), refs.pop(0)
    early_ref, late_ref, head_ref, sems = refs

    places = plan["owner_headers"] + plan["headers"]
    sources = mark_refs + packets
    copies = []
    for i, (packet, row, column) in enumerate(places):
        copy = pltpu.make_async_copy(
            sources[packet].at[pl.ds(row, HEADER), pl.ds(column, HEAD_WIDTH)],
            head_ref.at[i],
            sems.at[2 * count + i],
        )
        copy.start()
        copies.append(copy)
    for copy in copies:
        copy.wait()
    numbers = [
        jnp.max(head_ref[i].astype(jnp.float32)).astype(jnp.int32) for i in range(len(places))
    ]
    owner_c, member_c = numbers[:owners], numbers[owners:]

    copies = []
    for j, (packet, row) in enumerate(plan["members"]):
        rank = sum((other < member_c[j]).astype(jnp.int32) for i, other in enumerate(member_c) if i != j)
        rank = jnp.clip(rank, 0, count - 1)
        for half, (ref, at) in enumerate(((early_ref, rank), (late_ref, count - 1 - rank))):
            copy = pltpu.make_async_copy(
                packets[packet].at[pl.ds(row + half * chunk, chunk)],
                ref.at[pl.ds(pl.multiple_of(at * chunk, chunk), chunk)],
                sems.at[2 * j + half],
            )
            copy.start()
            copies.append(copy)
    for copy in copies:
        copy.wait()

    def keys_of(ref, first, size):
        return (
            [ref[pl.ds(first, size), pl.ds(h * HEAD_WIDTH, HEAD_WIDTH)] for h in range(heads)],
            [ref[pl.ds(first, size), pl.ds((heads + h) * HEAD_WIDTH, HEAD_WIDTH)] for h in range(heads)],
        )

    def queries_of(i, half):
        base = core_ref[0] * (heads * GROUP) if plan["owners"][i] else 0
        return [stacked_queries(q_refs[i], half * chunk, chunk, base + h * GROUP) for h in range(heads)]

    def load(ml, acc, at):
        return [(ml[at + h][0:1], ml[at + h][1:2], acc[at + h]) for h in range(heads)]

    def store(states, at):
        for h, (high, totals, sums) in enumerate(states):
            ml_ref[at + h, 0:1] = high
            ml_ref[at + h, 1:2] = totals
            acc_ref[at + h] = sums

    tile = 2 * chunk

    def sweep(i, half, ref, at, full):
        def plain(t, carry):
            keys, values = keys_of(ref, pl.multiple_of(t * tile, tile), tile)
            store(fold(load(ml_ref, acc_ref, at), queries_of(i, half), keys, values), at)
            return carry

        lax.fori_loop(0, full // 2, plain, 0)
        if plan["own"]:
            first = (full // 2) * tile
            key_at = lax.broadcasted_iota(jnp.int32, (tile, rows), 0)
            query_at = lax.rem(lax.broadcasted_iota(jnp.int32, (tile, rows), 1), chunk)
            mask = key_at - query_at <= full * chunk - first
            keys, values = keys_of(ref, pl.multiple_of(first, tile), tile)
            store(fold(load(ml_ref, acc_ref, at), queries_of(i, half), keys, values, mask), at)
        else:

            @pl.when(full % 2 == 1)
            def _():
                keys, values = keys_of(ref, pl.multiple_of((full - 1) * chunk, chunk), chunk)
                store(fold(load(ml_ref, acc_ref, at), queries_of(i, half), keys, values), at)

    for i in range(owners):
        early_at, late_at = (2 * i) * heads, (2 * i + 1) * heads
        states = load(in_ml, in_acc, late_at) if plan["carried"] else [None] * heads
        keys_total = count * chunk
        cut = 480 if keys_total % 480 == 0 else 576 if keys_total % 576 == 0 else 512
        for first in range(0, keys_total, cut):
            keys, values = keys_of(early_ref, first, cut)
            states = fold(states, queries_of(i, 1), keys, values)
        store(states, late_at)
        if plan["carried"]:
            store(load(in_ml, in_acc, early_at), early_at)
        else:
            store(
                [
                    (
                        jnp.full((1, rows), MASKED, jnp.float32),
                        jnp.zeros((1, rows), jnp.float32),
                        jnp.zeros((HEAD_WIDTH, rows), jnp.float32),
                    )
                ]
                * heads,
                early_at,
            )
        below = sum((other < owner_c[i]).astype(jnp.int32) for other in member_c)
        above = sum((other > owner_c[i]).astype(jnp.int32) for other in member_c)
        most = count - 1 if plan["own"] else count
        sweep(i, 1, late_ref, late_at, jnp.clip(above, 0, most))
        sweep(i, 0, early_ref, early_at, jnp.clip(below, 0, most))
        if plan["last"]:
            for half, at in ((0, early_at), (1, late_at)):
                for h, (_, totals, sums) in enumerate(load(ml_ref, acc_ref, at)):
                    mixed = jnp.transpose(sums / totals).astype(out_refs[i].dtype)
                    for g in range(QUERY_PER_KEY):
                        out_refs[i][
                            half * chunk : (half + 1) * chunk,
                            h * GROUP + g * HEAD_WIDTH : h * GROUP + (g + 1) * HEAD_WIDTH,
                        ] = mixed[g * chunk : (g + 1) * chunk]


def attend(plan, core, queries, marks, packets, state):
    heads, chunk, count = plan["heads"], plan["chunk"], len(plan["members"])
    owners = len(plan["owners"])
    plan = dict(plan, marks=len(marks), packets=len(packets), carried=state is not None)
    rows = QUERY_PER_KEY * chunk
    slots = owners * 2 * heads
    vmem = pl.BlockSpec(memory_space=pltpu.VMEM)
    anywhere = pl.BlockSpec(memory_space=pl.ANY)
    ml_shape, acc_shape = (slots, 8, rows), (slots, HEAD_WIDTH, rows)
    scratch = [
        pltpu.VMEM((count * chunk, 2 * heads * HEAD_WIDTH), jnp.bfloat16),
        pltpu.VMEM((count * chunk, 2 * heads * HEAD_WIDTH), jnp.bfloat16),
        pltpu.VMEM((count + owners, HEADER, HEAD_WIDTH), jnp.bfloat16),
        pltpu.SemaphoreType.DMA((3 * count + owners,)),
    ]
    if plan["last"]:
        out_shape = [jax.ShapeDtypeStruct((2 * chunk, heads * GROUP), jnp.bfloat16)] * owners
        scratch = [pltpu.VMEM(ml_shape, jnp.float32), pltpu.VMEM(acc_shape, jnp.float32)] + scratch
    else:
        out_shape = [
            jax.ShapeDtypeStruct(ml_shape, jnp.float32),
            jax.ShapeDtypeStruct(acc_shape, jnp.float32),
        ]
    flops = 4 * owners * heads * rows * HEAD_WIDTH * count * chunk * 2
    return pl.pallas_call(
        functools.partial(attend_kernel, plan),
        out_shape=out_shape,
        in_specs=[pl.BlockSpec(memory_space=pltpu.SMEM)]
        + [vmem] * owners
        + [anywhere] * (len(marks) + len(packets))
        + [vmem] * (0 if state is None else 2),
        out_specs=[vmem] * len(out_shape),
        scratch_shapes=scratch,
        cost_estimate=pl.CostEstimate(
            flops=flops, bytes_accessed=4 << 20, transcendentals=flops // 512
        ),
        compiler_params=pltpu.CompilerParams(vmem_limit_bytes=VMEM_LIMIT),
        name="attend_last" if plan["last"] else "attend_first",
    )(core, *queries, *marks, *packets, *(state or ()))


def project_kernel(pick_ref, own_ref, other_ref, w_ref, out_ref, rows_ref):
    @pl.when(pl.program_id(0) == 0)
    def _():
        chunk, part = rows_ref.shape[0], own_ref.shape[1]
        at = pl.multiple_of(pick_ref[0] * chunk, chunk)
        own, other = own_ref[pl.ds(at, chunk)], other_ref[pl.ds(at, chunk)]
        first = pick_ref[1] == 0
        rows_ref[:, :part] = jnp.where(first, own, other)
        rows_ref[:, part:] = jnp.where(first, other, own)

    out_ref[...] = jnp.dot(
        rows_ref[...], w_ref[...], preferred_element_type=jnp.float32
    ).astype(out_ref.dtype)


def project(pick, own, other, out_weight, first, width, tile):
    chunk, depth = own.shape[0] // 2, out_weight.shape[0]
    whole = lambda j: (0, 0)
    return pl.pallas_call(
        project_kernel,
        out_shape=jax.ShapeDtypeStruct((chunk, width), jnp.bfloat16),
        grid=(width // tile,),
        in_specs=[
            pl.BlockSpec(memory_space=pltpu.SMEM),
            pl.BlockSpec(own.shape, whole),
            pl.BlockSpec(other.shape, whole),
            pl.BlockSpec((depth, tile), lambda j: (0, first // tile + j)),
        ],
        out_specs=pl.BlockSpec((chunk, tile), lambda j: (0, j)),
        scratch_shapes=[pltpu.VMEM((chunk, depth), jnp.bfloat16)],
        cost_estimate=pl.CostEstimate(
            flops=2 * chunk * depth * width, bytes_accessed=2 * depth * width, transcendentals=0
        ),
        compiler_params=pltpu.CompilerParams(vmem_limit_bytes=VMEM_LIMIT),
        name="project",
    )(pick, own, other, out_weight)


def after(value, *events):
    return lax.optimization_barrier((value, *events))[0]


def split_over_cores(count, queries, keys, values, c_rows):
    chips, half = count // 2, count // 4
    rows, chunk = queries.shape[0], queries.shape[0] // 2
    heads = keys.shape[1] // HEAD_WIDTH // 2
    core = lax.rem(lax.axis_index("blk"), 2).astype(jnp.int32)
    sibling = [(b, b ^ 1) for b in range(count)]
    clock, counter = ring_pairs(chips, 1), ring_pairs(chips, -1)
    width = heads * HEAD_WIDTH

    def of_core(k):
        return jnp.concatenate(
            [lax.dynamic_slice(x, (0, k * width), (rows, width)) for x in (keys, values)], axis=1
        )

    header = jnp.broadcast_to(c_rows, (HEADER, 2 * width))
    sent = jnp.concatenate([of_core(1 - core), header], axis=0)
    got = lax.ppermute(sent, "blk", sibling)
    packet = jnp.concatenate(
        [
            of_core(core),
            got[:rows],
            jnp.concatenate([header[:, :width], got[rows:, :width]], axis=1),
        ],
        axis=0,
    )
    q_sent = lax.dynamic_slice(queries, (0, (1 - core) * heads * GROUP), (rows, heads * GROUP))

    ups, downs = [packet], [packet]
    for r in range(half - 1):
        ups.append(lax.ppermute(ups[-1], "blk", clock))
        downs.append(lax.ppermute(downs[-1], "blk", counter))
        if r == 0:
            q_got = lax.ppermute(q_sent, "blk", sibling)
    far_up = lax.ppermute(ups[-1][:rows], "blk", clock)
    far_down = lax.ppermute(downs[-1][rows:], "blk", counter)

    def whole_packets(first, number):
        members = [(first + j, i * rows) for j in range(number) for i in range(2)]
        headers = [(1 + first + j, 2 * rows, i * width) for j in range(number) for i in range(2)]
        return members, headers

    shared = dict(heads=heads, chunk=chunk, owners=(True, False))
    owner_headers = [(0, 2 * rows, 0), (0, 2 * rows, width)]
    cores = core.reshape(1)
    near = [packet]
    for r in range(1, half - 1):
        near += [ups[r], downs[r]]
    members, headers = whole_packets(0, len(near))
    plan = dict(shared, own=True, last=False, members=members, headers=headers, owner_headers=owner_headers)
    state = attend(plan, cores, [queries, q_got], [packet], near, None)
    far = [ups[-1], downs[-1], far_up, far_down]
    members, headers = whole_packets(0, 2)
    members += [(2, 0), (3, 0)]
    headers += [(4, rows, 0), (4, rows, width)]
    plan = dict(shared, own=False, last=True, members=members, headers=headers, owner_headers=owner_headers)
    own, sibling_rows = attend(plan, cores, [queries, q_got], [packet], far, state)
    return own, lax.ppermute(sibling_rows, "blk", sibling), core


def one_head_a_device(count, queries, keys, values, c_rows):
    rows, chunk = queries.shape[0], queries.shape[0] // 2
    width = 2 * keys.shape[1]
    heads = keys.shape[1] // HEAD_WIDTH
    header = jnp.broadcast_to(c_rows, (HEADER, width))
    packet = jnp.concatenate([jnp.concatenate([keys, values], axis=1), header], axis=0)
    packets = lax.all_gather(packet, "blk", axis=0, tiled=True)
    size = rows + HEADER
    plan = dict(
        heads=heads,
        chunk=chunk,
        owners=(False,),
        own=True,
        last=True,
        members=[(0, j * size) for j in range(count)],
        headers=[(1, j * size + rows, 0) for j in range(count)],
        owner_headers=[(0, rows, 0)],
    )
    zero = jnp.zeros((1,), jnp.int32)
    return attend(plan, zero, [queries], [packet], [packets], None)[0]


def shards(count, inner, queries, keys, values, positions, out_weight):
    chunk = queries.shape[0] // 2
    heads = keys.shape[1] // HEAD_WIDTH
    c_rows = (positions[:1] // chunk).astype(jnp.bfloat16).reshape(1, 1)
    if heads % 2:
        attended = one_head_a_device(count, queries, keys, values, c_rows)
        partial = jnp.dot(attended, out_weight, preferred_element_type=jnp.float32)
        return lax.psum_scatter(
            partial.astype(jnp.bfloat16), "inner", scatter_dimension=0, tiled=True
        )
    own, other, core = split_over_cores(count, queries, keys, values, c_rows)
    mine = lax.axis_index("inner").astype(jnp.int32)
    sending, keeping = jnp.stack([1 - mine, core]), jnp.stack([mine, core])
    width = out_weight.shape[1]
    parts = 4
    step = width // parts
    received = []
    for j in range(parts):
        source = own if j < 2 else after(own, received[j - 2])
        sent = project(sending, source, other, out_weight, j * step, step, 256)
        received.append(lax.ppermute(sent, "inner", [(0, 1), (1, 0)]))
    kept = project(keeping, after(own, sent), other, out_weight, 0, width, 512)
    theirs = jnp.concatenate(received, axis=1)
    return (kept.astype(jnp.float32) + theirs.astype(jnp.float32)).astype(jnp.bfloat16)


def solution(mesh):
    placed = (P("blk", "inner"), P("blk", "inner"), P("blk", "inner"), P("blk"), P("inner", None))
    return jax.shard_map(
        functools.partial(shards, mesh.shape["blk"], mesh.shape["inner"]),
        mesh=mesh,
        in_specs=placed,
        out_specs=P(("blk", "inner"), None),
        check_vma=False,
    )
```

```python
import functools
import math

import jax
import jax.numpy as jnp
from jax import lax
from jax.experimental import pallas as pl
from jax.experimental.pallas import tpu as pltpu
from jax.sharding import PartitionSpec as P

HEAD_WIDTH = 128
QUERY_PER_KEY = 5
GROUP = QUERY_PER_KEY * HEAD_WIDTH
EXP2_SCALE = math.log2(math.e) / math.sqrt(HEAD_WIDTH)
MASKED = -1e30
VMEM_LIMIT = 16 * 1024 * 1024
HEADER = 16
LAST_LAST = (((1,), (1,)), ((), ()))


def ring_of_chips(chips):
    half = chips // 2
    if chips == 8:
        return [2 * z for z in range(half)] + [2 * z + 1 for z in reversed(range(half))]
    return list(range(half)) + list(reversed(range(half, chips)))


def ring_pairs(chips, step):
    ring = ring_of_chips(chips)
    return [
        (2 * ring[i] + core, 2 * ring[(i + step) % chips] + core)
        for i in range(chips)
        for core in range(2)
    ]


def fold(carried, q, keys, values, mask=None):
    scores = [lax.dot_general(k, q, LAST_LAST, preferred_element_type=jnp.float32) for k in keys]
    if mask is not None:
        scores = [jnp.where(mask, s, MASKED) for s in scores]
    high = functools.reduce(jnp.maximum, [jnp.max(s, axis=0, keepdims=True) for s in scores])
    if carried is not None:
        high = jnp.maximum(carried[0], high)
    sums = None
    for s, v in zip(scores, values):
        p = jnp.exp2((s - high) * EXP2_SCALE).astype(jnp.bfloat16)
        part = jnp.dot(v, p, preferred_element_type=jnp.float32)
        sums = part if sums is None else sums + part
    if carried is not None:
        sums = carried[1] * jnp.exp2((carried[0] - high) * EXP2_SCALE) + sums
    return high, sums


def stacked_queries(q_ref, first_row, rows, first_column):
    return jnp.concatenate(
        [
            q_ref[
                pl.ds(first_row, rows),
                pl.ds(pl.multiple_of(first_column + g * HEAD_WIDTH, HEAD_WIDTH), HEAD_WIDTH),
            ]
            for g in range(QUERY_PER_KEY)
        ],
        axis=0,
    )


def my_core():
    return lax.rem(lax.axis_index("blk"), 2).astype(jnp.int32)


def attend_kernel(plan, *refs):
    heads, chunk = plan["heads"], plan["chunk"]
    owners, count = len(plan["owners"]), len(plan["members"])
    rows, tile = QUERY_PER_KEY * chunk, 2 * chunk
    tiles = count // 2
    refs = list(refs)
    q_refs = [refs.pop(0) for _ in range(owners)]
    mark_refs = [refs.pop(0) for _ in range(plan["marks"])]
    packets = [refs.pop(0) for _ in range(plan["packets"])]
    if plan["carried"]:
        in_high, in_sums = refs.pop(0), refs.pop(0)
    high_ref, sums_ref = refs.pop(0), refs.pop(0)
    if plan["last"]:
        out_refs = [refs.pop(0) for _ in range(owners)]
    early_ref, late_ref, turned_ref, head_ref, sems = refs

    places = plan["owner_headers"] + plan["headers"]
    sources = mark_refs + packets
    copies = []
    for i, (packet, row, column) in enumerate(places):
        copy = pltpu.make_async_copy(
            sources[packet].at[pl.ds(row, HEADER), pl.ds(column, HEAD_WIDTH)],
            head_ref.at[i],
            sems.at[2 * count + i],
        )
        copy.start()
        copies.append(copy)
    for copy in copies:
        copy.wait()
    numbers = [
        jnp.max(head_ref[i].astype(jnp.float32)).astype(jnp.int32) for i in range(len(places))
    ]
    owner_c, member_c = numbers[:owners], numbers[owners:]

    copies = []
    for j, (packet, row) in enumerate(plan["members"]):
        rank = sum((other < member_c[j]).astype(jnp.int32) for i, other in enumerate(member_c) if i != j)
        rank = jnp.clip(rank, 0, count - 1)
        for half, (ref, at) in enumerate(((early_ref, rank), (late_ref, count - 1 - rank))):
            copy = pltpu.make_async_copy(
                packets[packet].at[pl.ds(row + half * chunk, chunk)],
                ref.at[pl.ds(pl.multiple_of(at * chunk, chunk), chunk)],
                sems.at[2 * j + half],
            )
            copy.start()
            copies.append(copy)
    for copy in copies:
        copy.wait()

    turned_ref[:, HEAD_WIDTH:] = jnp.ones((turned_ref.shape[0], HEADER, tile), jnp.bfloat16)
    key_refs = (early_ref, late_ref)

    def slot(half, h, t):
        return (half * heads + h) * tiles + t

    for half in range(2):
        for h in range(heads):
            for t in range(tiles):
                v = key_refs[half][
                    t * tile : (t + 1) * tile, (heads + h) * HEAD_WIDTH : (heads + h + 1) * HEAD_WIDTH
                ]
                turned_ref[slot(half, h, t), :HEAD_WIDTH] = jnp.transpose(v)

    def keys_of(half, h, t):
        first = t * tile if isinstance(t, int) else pl.multiple_of(t * tile, tile)
        k = key_refs[half][pl.ds(first, tile), h * HEAD_WIDTH : (h + 1) * HEAD_WIDTH]
        return k, turned_ref[slot(half, h, t)]

    def queries_of(i, half, h):
        base = my_core() * (heads * GROUP) if plan["owners"][i] else 0
        return stacked_queries(q_refs[i], half * chunk, chunk, base + h * GROUP)

    def state_at(i, half, h):
        return (2 * i + half) * heads + h

    def store(at, state):
        high_ref[at], sums_ref[at] = state

    for h in range(heads):
        for i in range(owners):
            at = state_at(i, 1, h)
            state = (in_high[at], in_sums[at]) if plan["carried"] else None
            for first in range(0, tiles, 5):
                blocks = [keys_of(0, h, t) for t in range(first, min(first + 5, tiles))]
                state = fold(state, queries_of(i, 1, h), [k for k, _ in blocks], [v for _, v in blocks])
            store(at, state)
            at = state_at(i, 0, h)
            if plan["carried"]:
                store(at, (in_high[at], in_sums[at]))
            else:
                high_ref[at] = jnp.full(high_ref.shape[1:], MASKED, jnp.float32)
                sums_ref[at] = jnp.zeros(sums_ref.shape[1:], jnp.float32)

    def sweep(i, half, full):
        def block(t, mask):
            for h in range(heads):
                at = state_at(i, half, h)
                k, v = keys_of(half, h, t)
                store(at, fold((high_ref[at], sums_ref[at]), queries_of(i, half, h), [k], [v], mask))

        def plain(t, carry):
            block(t, None)
            return carry

        lax.fori_loop(0, full // 2, plain, 0)
        key_at = lax.broadcasted_iota(jnp.int32, (tile, rows), 0)
        if plan["own"]:
            query_at = lax.rem(lax.broadcasted_iota(jnp.int32, (tile, rows), 1), chunk)
            block(full // 2, key_at - query_at <= lax.rem(full, 2) * chunk)
        else:

            @pl.when(lax.rem(full, 2) == 1)
            def _():
                block(full // 2, key_at < chunk)

    for i in range(owners):
        below = sum((other < owner_c[i]).astype(jnp.int32) for other in member_c)
        above = sum((other > owner_c[i]).astype(jnp.int32) for other in member_c)
        most = count - 1 if plan["own"] else count
        sweep(i, 1, jnp.clip(above, 0, most))
        sweep(i, 0, jnp.clip(below, 0, most))
        if plan["last"]:
            for half in range(2):
                for h in range(heads):
                    sums = sums_ref[state_at(i, half, h)]
                    mixed = sums[:HEAD_WIDTH] / sums[HEAD_WIDTH : HEAD_WIDTH + 1]
                    mixed = jnp.transpose(mixed).astype(out_refs[i].dtype)
                    for g in range(QUERY_PER_KEY):
                        out_refs[i][
                            half * chunk : (half + 1) * chunk,
                            h * GROUP + g * HEAD_WIDTH : h * GROUP + (g + 1) * HEAD_WIDTH,
                        ] = mixed[g * chunk : (g + 1) * chunk]


def attend(plan, queries, marks, packets, state):
    heads, chunk, count = plan["heads"], plan["chunk"], len(plan["members"])
    owners = len(plan["owners"])
    plan = dict(plan, marks=len(marks), packets=len(packets), carried=state is not None)
    rows = QUERY_PER_KEY * chunk
    slots = owners * 2 * heads
    vmem = pl.BlockSpec(memory_space=pltpu.VMEM)
    anywhere = pl.BlockSpec(memory_space=pl.ANY)
    out_shape = [
        jax.ShapeDtypeStruct((slots, 1, rows), jnp.float32),
        jax.ShapeDtypeStruct((slots, HEAD_WIDTH + HEADER, rows), jnp.float32),
    ]
    if plan["last"]:
        out_shape += [jax.ShapeDtypeStruct((2 * chunk, heads * GROUP), jnp.bfloat16)] * owners
    operands = owners + len(marks) + len(packets)
    flops = 4 * owners * heads * rows * HEAD_WIDTH * count * chunk * 2
    return pl.pallas_call(
        functools.partial(attend_kernel, plan),
        out_shape=out_shape,
        in_specs=[vmem] * owners
        + [anywhere] * (len(marks) + len(packets))
        + [vmem] * (0 if state is None else 2),
        out_specs=[vmem] * len(out_shape),
        input_output_aliases={} if state is None else {operands: 0, operands + 1: 1},
        scratch_shapes=[
            pltpu.VMEM((count * chunk, 2 * heads * HEAD_WIDTH), jnp.bfloat16),
            pltpu.VMEM((count * chunk, 2 * heads * HEAD_WIDTH), jnp.bfloat16),
            pltpu.VMEM((count * heads, HEAD_WIDTH + HEADER, 2 * chunk), jnp.bfloat16),
            pltpu.VMEM((count + owners, HEADER, HEAD_WIDTH), jnp.bfloat16),
            pltpu.SemaphoreType.DMA((3 * count + owners,)),
        ],
        cost_estimate=pl.CostEstimate(
            flops=flops, bytes_accessed=4 << 20, transcendentals=flops // 512
        ),
        compiler_params=pltpu.CompilerParams(vmem_limit_bytes=VMEM_LIMIT),
        name="attend",
    )(*queries, *marks, *packets, *(state or ()))


def project_kernel(own_ref, other_ref, w_ref, sent_ref, kept_ref, rows_ref):
    chunk, part = sent_ref.shape[0], own_ref.shape[1]

    @pl.when(pl.program_id(0) == 0)
    def _():
        mine = lax.axis_index("inner").astype(jnp.int32)
        first = my_core() == 0
        for place, half in enumerate((1 - mine, mine)):
            at = pl.multiple_of(half * chunk, chunk)
            own, other = own_ref[pl.ds(at, chunk)], other_ref[pl.ds(at, chunk)]
            to = pl.ds(place * chunk, chunk)
            rows_ref[to, :part] = jnp.where(first, own, other)
            rows_ref[to, part:] = jnp.where(first, other, own)

    product = jnp.dot(rows_ref[...], w_ref[...], preferred_element_type=jnp.float32)
    product = product.astype(sent_ref.dtype)
    sent_ref[...] = product[:chunk]
    kept_ref[...] = product[chunk:]


def project(own, other, out_weight, first, width, tile):
    rows, depth = own.shape[0], out_weight.shape[0]
    whole = lambda j: (0, 0)
    return pl.pallas_call(
        project_kernel,
        out_shape=[jax.ShapeDtypeStruct((rows // 2, width), jnp.bfloat16)] * 2,
        grid=(width // tile,),
        in_specs=[
            pl.BlockSpec(own.shape, whole),
            pl.BlockSpec(other.shape, whole),
            pl.BlockSpec((depth, tile), lambda j: (0, first // tile + j)),
        ],
        out_specs=[pl.BlockSpec((rows // 2, tile), lambda j: (0, j))] * 2,
        scratch_shapes=[pltpu.VMEM((rows, depth), jnp.bfloat16)],
        cost_estimate=pl.CostEstimate(
            flops=2 * rows * depth * width, bytes_accessed=2 * depth * width, transcendentals=0
        ),
        compiler_params=pltpu.CompilerParams(vmem_limit_bytes=VMEM_LIMIT),
        name="project",
    )(own, other, out_weight)


def prepare_kernel(chunk, k_ref, v_ref, position_ref, sent_ref, kept_ref):
    rows, width = k_ref.shape[0], k_ref.shape[1] // 2
    c = lax.div(position_ref[0], jnp.int32(chunk)).astype(jnp.float32)
    header = jnp.full((HEADER, 2 * width), c, jnp.float32).astype(jnp.bfloat16)
    for ref, core in ((kept_ref, my_core()), (sent_ref, 1 - my_core())):
        at = pl.ds(pl.multiple_of(core * width, width), width)
        ref[:rows, :width] = k_ref[:, at]
        ref[:rows, width:] = v_ref[:, at]
        ref[rows:] = header


def prepare(keys, values, positions):
    vmem = pl.BlockSpec(memory_space=pltpu.VMEM)
    rows = keys.shape[0]
    return pl.pallas_call(
        functools.partial(prepare_kernel, rows // 2),
        out_shape=[jax.ShapeDtypeStruct((rows + HEADER, keys.shape[1]), jnp.bfloat16)] * 2,
        in_specs=[vmem, vmem, pl.BlockSpec(memory_space=pltpu.SMEM)],
        out_specs=[vmem, vmem],
        compiler_params=pltpu.CompilerParams(vmem_limit_bytes=VMEM_LIMIT),
        name="prepare",
    )(keys, values, positions)


def after(value, *events):
    return lax.optimization_barrier((value, *events))[0]


def split_over_cores(count, queries, keys, values, positions):
    chips, half = count // 2, count // 4
    rows, chunk = queries.shape[0], queries.shape[0] // 2
    heads = keys.shape[1] // HEAD_WIDTH // 2
    sibling = [(b, b ^ 1) for b in range(count)]
    clock, counter = ring_pairs(chips, 1), ring_pairs(chips, -1)
    width = heads * HEAD_WIDTH

    sent, kept = prepare(keys, values, positions)
    got = lax.ppermute(sent, "blk", sibling)
    packet = jnp.concatenate(
        [kept[:rows], got[:rows], jnp.concatenate([kept[rows:, :width], got[rows:, :width]], axis=1)],
        axis=0,
    )
    q_sent = lax.dynamic_slice(
        queries, (0, (1 - my_core()) * heads * GROUP), (rows, heads * GROUP)
    )
    q_got = lax.ppermute(q_sent, "blk", sibling)

    shared = dict(heads=heads, chunk=chunk, owners=(True, False))
    shared["owner_headers"] = [(0, 2 * rows, 0), (0, 2 * rows, width)]

    def call(packets, state, own):
        each = range(len(packets))
        members = [(j, i * rows) for j in each for i in range(2)]
        headers = [(1 + j, 2 * rows, i * width) for j in each for i in range(2)]
        plan = dict(shared, own=own, last=False, members=members, headers=headers)
        return attend(plan, [queries, q_got], [packet], packets, state)

    ups, downs, state = [packet], [packet], None
    for r in range(1, half):
        up, down = ups[-1], downs[-1]
        if state is not None:
            up, down, *state = lax.optimization_barrier((up, down, *state))
        ups.append(lax.ppermute(up, "blk", clock))
        downs.append(lax.ppermute(down, "blk", counter))
        if r >= 2:
            here = [ups[r - 1], downs[r - 1]]
            state = call([packet] + here if r == 2 else here, state, r == 2)
    up, down, *state = lax.optimization_barrier((ups[-1], downs[-1], *state))
    far_up = lax.ppermute(up[:rows], "blk", clock)
    far_down = lax.ppermute(down[rows:], "blk", counter)
    state = call([up, down], state, False)
    plan = dict(
        shared,
        own=False,
        last=True,
        members=[(0, 0), (1, 0)],
        headers=[(2, rows, 0), (2, rows, width)],
    )
    _, _, own, theirs = attend(plan, [queries, q_got], [packet], [far_up, far_down], state)
    return own, lax.ppermute(theirs, "blk", sibling)


def one_head_a_device(count, queries, keys, values, positions):
    rows, chunk = queries.shape[0], queries.shape[0] // 2
    heads = keys.shape[1] // HEAD_WIDTH
    c = (positions[:1] // chunk).astype(jnp.bfloat16).reshape(1, 1)
    header = jnp.broadcast_to(c, (HEADER, 2 * keys.shape[1]))
    packet = jnp.concatenate([jnp.concatenate([keys, values], axis=1), header], axis=0)
    packets = lax.all_gather(packet, "blk", axis=0, tiled=True)
    size = rows + HEADER
    plan = dict(
        heads=heads,
        chunk=chunk,
        owners=(False,),
        own=True,
        last=True,
        members=[(0, j * size) for j in range(count)],
        headers=[(1, j * size + rows, 0) for j in range(count)],
        owner_headers=[(0, rows, 0)],
    )
    return attend(plan, [queries], [packet], [packets], None)[2]


def shards(count, inner, queries, keys, values, positions, out_weight):
    heads = keys.shape[1] // HEAD_WIDTH
    if heads % 2:
        attended = one_head_a_device(count, queries, keys, values, positions)
        partial = jnp.dot(attended, out_weight, preferred_element_type=jnp.float32)
        return lax.psum_scatter(
            partial.astype(jnp.bfloat16), "inner", scatter_dimension=0, tiled=True
        )
    own, other = split_over_cores(count, queries, keys, values, positions)
    out_weight = pltpu.with_memory_space_constraint(out_weight, pltpu.HBM)
    width, tile = out_weight.shape[1], 256
    shares = (3, 4, 6, 7)
    received, kept, first = [], [], 0
    for j, share in enumerate(shares):
        columns = width * share // sum(shares)
        source = own if j < 2 else after(own, received[j - 2])
        sent, keep = project(source, other, out_weight, first, columns, tile)
        received.append(lax.ppermute(sent, "inner", [(0, 1), (1, 0)]))
        kept.append(keep)
        first += columns
    mine, theirs = jnp.concatenate(kept, axis=1), jnp.concatenate(received, axis=1)
    return (mine.astype(jnp.float32) + theirs.astype(jnp.float32)).astype(jnp.bfloat16)


def solution(mesh):
    placed = (P("blk", "inner"), P("blk", "inner"), P("blk", "inner"), P("blk"), P("inner", None))
    return jax.shard_map(
        functools.partial(shards, mesh.shape["blk"], mesh.shape["inner"]),
        mesh=mesh,
        in_specs=placed,
        out_specs=P(("blk", "inner"), None),
        check_vma=False,
    )
```

```python
import functools
import math

import jax
import jax.numpy as jnp
from jax import lax
from jax.experimental import pallas as pl
from jax.experimental.pallas import tpu as pltpu
from jax.sharding import PartitionSpec as P

HEAD_WIDTH = 128
QUERY_PER_KEY = 5
GROUP = QUERY_PER_KEY * HEAD_WIDTH
EXP2_SCALE = math.log2(math.e) / math.sqrt(HEAD_WIDTH)
MASKED = -1e30
VMEM_LIMIT = 16 * 1024 * 1024
HEADER = 16


def ring_of_chips(chips):
    half = chips // 2
    if chips == 8:
        return [2 * z for z in range(half)] + [2 * z + 1 for z in reversed(range(half))]
    return list(range(half)) + list(reversed(range(half, chips)))


def ring_pairs(chips, step):
    ring = ring_of_chips(chips)
    return [
        (2 * ring[i] + core, 2 * ring[(i + step) % chips] + core)
        for i in range(chips)
        for core in range(2)
    ]


def my_core():
    return lax.rem(lax.axis_index("blk"), 2).astype(jnp.int32)


def product(a, b):
    return jnp.dot(a, b, preferred_element_type=jnp.float32)


def weigh(scores, high):
    return jnp.exp2((scores - high) * EXP2_SCALE).astype(jnp.bfloat16)


def turned_values(blocks):
    v = jnp.concatenate(blocks, axis=0)
    return jnp.concatenate([jnp.transpose(v), jnp.ones((HEADER, v.shape[0]), v.dtype)], axis=0)


def attend_kernel(plan, *refs):
    heads, chunk, owners = plan["heads"], plan["chunk"], plan["owners"]
    refs = list(refs)
    q_ref = refs.pop(0)
    mark_refs = [refs.pop(0) for _ in range(plan["marks"])]
    packets = [refs.pop(0) for _ in range(plan["packets"])]
    if plan["carried"]:
        in_high, in_sums = refs.pop(0), refs.pop(0)
    high_ref, sums_ref = refs.pop(0), refs.pop(0)
    out_refs = refs

    sources = mark_refs + packets
    numbers = [
        jnp.max(
            sources[packet][row : row + HEADER, column : column + HEAD_WIDTH].astype(jnp.float32)
        ).astype(jnp.int32)
        for packet, row, column in plan["owner_headers"] + plan["headers"]
    ]
    owner_c, member_c = numbers[:owners], numbers[owners:]

    def rows_of(j, half, column):
        packet, row = plan["members"][j]
        at = row + half * chunk
        at = at if isinstance(half, int) else pl.multiple_of(at, HEADER)
        return packets[packet][pl.ds(at, chunk), column : column + HEAD_WIDTH]

    def state_at(i, half, h):
        return (2 * i + half) * heads + h

    rows = QUERY_PER_KEY * chunk
    causal = lax.broadcasted_iota(jnp.int32, (chunk, rows), 0) <= lax.rem(
        lax.broadcasted_iota(jnp.int32, (chunk, rows), 1), chunk
    )
    count = len(plan["members"])
    for first in range(0, count, 6):
        group = range(first, min(first + 6, count))
        for h in range(heads):
            k_at, v_at = h * HEAD_WIDTH, (heads + h) * HEAD_WIDTH
            early_keys = jnp.concatenate([rows_of(j, 0, k_at) for j in group], axis=0)
            early_values = turned_values([rows_of(j, 0, v_at) for j in group])
            for i in range(owners):
                late_at, early_at = state_at(i, 1, h), state_at(i, 0, h)
                carried = None
                if first > 0:
                    carried = [(ref[early_at], ref[late_at]) for ref in (high_ref, sums_ref)]
                elif plan["carried"]:
                    carried = [(ref[early_at], ref[late_at]) for ref in (in_high, in_sums)]

                pairs = []
                for j in group:
                    if plan["own"] and j == plan["own_at"](i):
                        pairs += [(j, 0, causal), (j, 1, causal)]
                    else:
                        pairs.append((j, (member_c[j] > owner_c[i]).astype(jnp.int32), None))
                base = product(early_keys, q_ref[late_at])
                scores = []
                for j, half, mask in pairs:
                    s = product(rows_of(j, half, k_at), q_ref[state_at(i, half, h)])
                    scores.append(s if mask is None else jnp.where(mask, s, MASKED))
                tops = [jnp.max(s, axis=0, keepdims=True) for s in scores]
                highs = []
                for side in range(2):
                    some = [jnp.where(half == side, top, MASKED) for (_, half, _), top in zip(pairs, tops)]
                    if side == 1:
                        some.append(jnp.max(base, axis=0, keepdims=True))
                    if carried is not None:
                        some.append(carried[0][side])
                    highs.append(functools.reduce(jnp.maximum, some))
                weights = [
                    weigh(s, jnp.where(half == 1, highs[1], highs[0]))
                    for (_, half, _), s in zip(pairs, scores)
                ]
                values = turned_values([rows_of(j, half, v_at) for j, half, _ in pairs])
                zero = jnp.zeros_like(weights[0])
                for side, at in ((0, early_at), (1, late_at)):
                    chosen = [
                        jnp.where(half == side, w, zero) for (_, half, _), w in zip(pairs, weights)
                    ]
                    sums = product(values, jnp.concatenate(chosen, axis=0))
                    if side == 1:
                        sums = sums + product(early_values, weigh(base, highs[1]))
                    if carried is not None:
                        shrink = jnp.exp2((carried[0][side] - highs[side]) * EXP2_SCALE)
                        sums = sums + carried[1][side] * shrink
                    high_ref[at] = highs[side]
                    sums_ref[at] = sums
                    if plan["last"] and first + 6 >= count:
                        mixed = sums[:HEAD_WIDTH] / sums[HEAD_WIDTH : HEAD_WIDTH + 1]
                        mixed = jnp.transpose(mixed).astype(out_refs[i].dtype)
                        for g in range(QUERY_PER_KEY):
                            out_refs[i][
                                side * chunk : (side + 1) * chunk,
                                h * GROUP + g * HEAD_WIDTH : h * GROUP + (g + 1) * HEAD_WIDTH,
                            ] = mixed[g * chunk : (g + 1) * chunk]


def attend(plan, turned, marks, packets, state):
    heads, chunk, owners = plan["heads"], plan["chunk"], plan["owners"]
    count = len(plan["members"])
    plan = dict(plan, marks=len(marks), packets=len(packets), carried=state is not None)
    rows = QUERY_PER_KEY * chunk
    slots = owners * 2 * heads
    vmem = pl.BlockSpec(memory_space=pltpu.VMEM)
    out_shape = [
        jax.ShapeDtypeStruct((slots, 1, rows), jnp.float32),
        jax.ShapeDtypeStruct((slots, HEAD_WIDTH + HEADER, rows), jnp.float32),
    ]
    if plan["last"]:
        out_shape += [jax.ShapeDtypeStruct((2 * chunk, heads * GROUP), jnp.bfloat16)] * owners
    operands = 1 + len(marks) + len(packets)
    flops = 4 * owners * heads * rows * HEAD_WIDTH * count * chunk * 2
    return pl.pallas_call(
        functools.partial(attend_kernel, plan),
        out_shape=out_shape,
        in_specs=[vmem] * (operands + (0 if state is None else 2)),
        out_specs=[vmem] * len(out_shape),
        input_output_aliases={} if state is None else {operands: 0, operands + 1: 1},
        cost_estimate=pl.CostEstimate(
            flops=flops, bytes_accessed=4 << 20, transcendentals=flops // 512
        ),
        compiler_params=pltpu.CompilerParams(vmem_limit_bytes=VMEM_LIMIT),
        name="attend",
    )(turned, *marks, *packets, *(state or ()))


def turn_kernel(heads, chunk, whole_rows, *refs):
    q_refs, turned_ref = refs[:-1], refs[-1]
    for i, q_ref in enumerate(q_refs):
        base = my_core() * (heads * GROUP) if whole_rows[i] else 0
        for half in range(2):
            for h in range(heads):
                columns = [
                    pl.ds(pl.multiple_of(base + h * GROUP + g * HEAD_WIDTH, HEAD_WIDTH), HEAD_WIDTH)
                    for g in range(QUERY_PER_KEY)
                ]
                q = jnp.concatenate(
                    [q_ref[half * chunk : (half + 1) * chunk, at] for at in columns], axis=0
                )
                turned_ref[(2 * i + half) * heads + h] = jnp.transpose(q)


def turn(heads, chunk, whole_rows, queries):
    vmem = pl.BlockSpec(memory_space=pltpu.VMEM)
    owners = len(queries)
    shape = (2 * owners * heads, HEAD_WIDTH, QUERY_PER_KEY * chunk)
    return pl.pallas_call(
        functools.partial(turn_kernel, heads, chunk, whole_rows),
        out_shape=jax.ShapeDtypeStruct(shape, jnp.bfloat16),
        in_specs=[vmem] * owners,
        out_specs=vmem,
        cost_estimate=pl.CostEstimate(flops=1 << 20, bytes_accessed=4 << 20, transcendentals=0),
        compiler_params=pltpu.CompilerParams(vmem_limit_bytes=VMEM_LIMIT),
        name="turn",
    )(*queries)


def project_kernel(own_ref, other_ref, w_ref, sent_ref, kept_ref, rows_ref):
    chunk, part = sent_ref.shape[0], own_ref.shape[1]

    @pl.when(pl.program_id(0) == 0)
    def _():
        mine = lax.axis_index("inner").astype(jnp.int32)
        first = my_core() == 0
        for place, half in enumerate((1 - mine, mine)):
            at = pl.multiple_of(half * chunk, chunk)
            own, other = own_ref[pl.ds(at, chunk)], other_ref[pl.ds(at, chunk)]
            to = pl.ds(place * chunk, chunk)
            rows_ref[to, :part] = jnp.where(first, own, other)
            rows_ref[to, part:] = jnp.where(first, other, own)

    both = product(rows_ref[...], w_ref[...]).astype(sent_ref.dtype)
    sent_ref[...] = both[:chunk]
    kept_ref[...] = both[chunk:]


def project(own, other, out_weight, first, width, tile):
    rows, depth = own.shape[0], out_weight.shape[0]
    whole = lambda j: (0, 0)
    return pl.pallas_call(
        project_kernel,
        out_shape=[jax.ShapeDtypeStruct((rows // 2, width), jnp.bfloat16)] * 2,
        grid=(width // tile,),
        in_specs=[
            pl.BlockSpec(own.shape, whole),
            pl.BlockSpec(other.shape, whole),
            pl.BlockSpec((depth, tile), lambda j: (0, first // tile + j)),
        ],
        out_specs=[pl.BlockSpec((rows // 2, tile), lambda j: (0, j))] * 2,
        scratch_shapes=[pltpu.VMEM((rows, depth), jnp.bfloat16)],
        cost_estimate=pl.CostEstimate(
            flops=2 * rows * depth * width, bytes_accessed=2 * depth * width, transcendentals=0
        ),
        compiler_params=pltpu.CompilerParams(vmem_limit_bytes=VMEM_LIMIT),
        name="project",
    )(own, other, out_weight)


def prepare_kernel(chunk, k_ref, v_ref, position_ref, sent_ref, kept_ref, first_ref, sems):
    rows, width = k_ref.shape[0], k_ref.shape[1] // 2
    copies = [pltpu.make_async_copy(position_ref, first_ref, sems.at[4])]
    for n, (ref, core) in enumerate(((sent_ref, 1 - my_core()), (kept_ref, my_core()))):
        at = pl.ds(pl.multiple_of(core * width, width), width)
        for m, source in enumerate((k_ref, v_ref)):
            to = ref.at[pl.ds(0, rows), pl.ds(m * width, width)]
            copies.append(pltpu.make_async_copy(source.at[:, at], to, sems.at[2 * n + m]))
    for copy in copies:
        copy.start()
    copies[0].wait()
    c = lax.div(first_ref[0], jnp.int32(chunk)).astype(jnp.float32)
    header = jnp.full((HEADER, 2 * width), c, jnp.float32).astype(jnp.bfloat16)
    sent_ref[rows:] = header
    kept_ref[rows:] = header
    for copy in copies[1:]:
        copy.wait()


def prepare(keys, values, positions):
    vmem = pl.BlockSpec(memory_space=pltpu.VMEM)
    hbm = pl.BlockSpec(memory_space=pltpu.HBM)
    rows = keys.shape[0]
    return pl.pallas_call(
        functools.partial(prepare_kernel, rows // 2),
        out_shape=[jax.ShapeDtypeStruct((rows + HEADER, keys.shape[1]), jnp.bfloat16)] * 2,
        in_specs=[hbm, hbm, hbm],
        out_specs=[vmem, vmem],
        scratch_shapes=[
            pltpu.SMEM(positions.shape, jnp.int32),
            pltpu.SemaphoreType.DMA((5,)),
        ],
        compiler_params=pltpu.CompilerParams(vmem_limit_bytes=VMEM_LIMIT),
        name="prepare",
    )(keys, values, positions)


def after(value, *events):
    return lax.optimization_barrier((value, *events))[0]


def split_over_cores(count, queries, keys, values, positions):
    chips, half = count // 2, count // 4
    rows, chunk = queries.shape[0], queries.shape[0] // 2
    heads = keys.shape[1] // HEAD_WIDTH // 2
    sibling = [(b, b ^ 1) for b in range(count)]
    clock, counter = ring_pairs(chips, 1), ring_pairs(chips, -1)
    width = heads * HEAD_WIDTH

    sent, kept = prepare(keys, values, positions)
    got = lax.ppermute(sent, "blk", sibling)
    packet = jnp.concatenate(
        [kept[:rows], got[:rows], jnp.concatenate([kept[rows:, :width], got[rows:, :width]], axis=1)],
        axis=0,
    )
    q_sent = lax.dynamic_slice(
        queries, (0, (1 - my_core()) * heads * GROUP), (rows, heads * GROUP)
    )
    q_got = lax.ppermute(q_sent, "blk", sibling)

    shared = dict(heads=heads, chunk=chunk, owners=2, own_at=lambda i: i)
    shared["owner_headers"] = [(0, 2 * rows, 0), (0, 2 * rows, width)]

    def call(packets, state, own):
        each = range(len(packets))
        members = [(j, i * rows) for j in each for i in range(2)]
        headers = [(1 + j, 2 * rows, i * width) for j in each for i in range(2)]
        plan = dict(shared, own=own, last=False, members=members, headers=headers)
        return attend(plan, turned, [packet], packets, state)

    turned = turn(heads, chunk, (True, False), [queries, q_got])
    ups, downs, state = [packet], [packet], None
    for r in range(1, half):
        up, down = ups[-1], downs[-1]
        if r == 2:
            up, down, turned = lax.optimization_barrier((up, down, turned))
        elif r > 2:
            up, down, *state = lax.optimization_barrier((up, down, *state))
        ups.append(lax.ppermute(up, "blk", clock))
        downs.append(lax.ppermute(down, "blk", counter))
        if r >= 2:
            here = [ups[r - 1], downs[r - 1]]
            state = call([packet] + here if r == 2 else here, state, r == 2)
    up, down, *state = lax.optimization_barrier((ups[-1], downs[-1], *state))
    far_up = lax.ppermute(up[:rows], "blk", clock)
    far_down = lax.ppermute(down[rows:], "blk", counter)
    state = call([up, down], state, False)
    plan = dict(
        shared,
        own=False,
        last=True,
        members=[(0, 0), (1, 0)],
        headers=[(2, rows, 0), (2, rows, width)],
    )
    _, _, own, theirs = attend(plan, turned, [packet], [far_up, far_down], state)
    return own, lax.ppermute(theirs, "blk", sibling)


def one_head_a_device(count, queries, keys, values, positions):
    rows, chunk = queries.shape[0], queries.shape[0] // 2
    heads = keys.shape[1] // HEAD_WIDTH
    c = (positions[:1] // chunk).astype(jnp.bfloat16).reshape(1, 1)
    header = jnp.broadcast_to(c, (HEADER, 2 * keys.shape[1]))
    packet = jnp.concatenate([jnp.concatenate([keys, values], axis=1), header], axis=0)
    packets = lax.all_gather(packet, "blk", axis=0, tiled=True)
    size = rows + HEADER
    here = lax.axis_index("blk")
    order = lax.rem(here + jnp.arange(count), count)
    packets = packets.reshape(count, size, -1)[order].reshape(count * size, -1)
    plan = dict(
        heads=heads,
        chunk=chunk,
        owners=1,
        own=True,
        own_at=lambda i: 0,
        last=True,
        members=[(0, j * size) for j in range(count)],
        headers=[(0, j * size + rows, 0) for j in range(count)],
        owner_headers=[(0, rows, 0)],
    )
    turned = turn(heads, chunk, (False,), [queries])
    return attend(plan, turned, [], [packets], None)[2]


def shards(count, inner, queries, keys, values, positions, out_weight):
    heads = keys.shape[1] // HEAD_WIDTH
    if heads % 2:
        attended = one_head_a_device(count, queries, keys, values, positions)
        partial = jnp.dot(attended, out_weight, preferred_element_type=jnp.float32)
        return lax.psum_scatter(
            partial.astype(jnp.bfloat16), "inner", scatter_dimension=0, tiled=True
        )
    own, other = split_over_cores(count, queries, keys, values, positions)
    out_weight = pltpu.with_memory_space_constraint(out_weight, pltpu.HBM)
    width, tile = out_weight.shape[1], 512
    shares = (2, 2, 3, 3)
    received, kept, first, source = [], [], 0, own
    for j, share in enumerate(shares):
        columns = width * share // sum(shares)
        if j > 0:
            source = after(own, sent, *received[: j - 1][-1:])
        sent, keep = project(source, other, out_weight, first, columns, tile)
        received.append(lax.ppermute(sent, "inner", [(0, 1), (1, 0)]))
        kept.append(keep)
        first += columns
    mine, theirs = jnp.concatenate(kept, axis=1), jnp.concatenate(received, axis=1)
    return (mine.astype(jnp.float32) + theirs.astype(jnp.float32)).astype(jnp.bfloat16)


def solution(mesh):
    placed = (P("blk", "inner"), P("blk", "inner"), P("blk", "inner"), P("blk"), P("inner", None))
    return jax.shard_map(
        functools.partial(shards, mesh.shape["blk"], mesh.shape["inner"]),
        mesh=mesh,
        in_specs=placed,
        out_specs=P(("blk", "inner"), None),
        check_vma=False,
    )
```

```python
import functools
import math

import jax
import jax.numpy as jnp
from jax import lax
from jax.experimental import pallas as pl
from jax.experimental.pallas import tpu as pltpu
from jax.sharding import PartitionSpec as P

HEAD_WIDTH = 128
QUERY_PER_KEY = 5
GROUP = QUERY_PER_KEY * HEAD_WIDTH
EXP2_SCALE = math.log2(math.e) / math.sqrt(HEAD_WIDTH)
MASKED = -1e30
VMEM_LIMIT = 16 * 1024 * 1024
HEADER = 16


def ring_of_chips(chips):
    half = chips // 2
    if chips == 8:
        return [2 * z for z in range(half)] + [2 * z + 1 for z in reversed(range(half))]
    return list(range(half)) + list(reversed(range(half, chips)))


def ring_pairs(chips, step):
    ring = ring_of_chips(chips)
    return [
        (2 * ring[i] + core, 2 * ring[(i + step) % chips] + core)
        for i in range(chips)
        for core in range(2)
    ]


def my_core():
    return lax.rem(lax.axis_index("blk"), 2).astype(jnp.int32)


def product(a, b):
    return jnp.dot(a, b, preferred_element_type=jnp.float32)


def weigh(scores, high):
    return jnp.exp2((scores - high) * EXP2_SCALE).astype(jnp.bfloat16)


def turned_values(blocks):
    v = jnp.concatenate(blocks, axis=0)
    return jnp.concatenate([jnp.transpose(v), jnp.ones((HEADER, v.shape[0]), v.dtype)], axis=0)


def attend_kernel(plan, *refs):
    heads, chunk, owners = plan["heads"], plan["chunk"], plan["owners"]
    refs = list(refs)
    q_ref = refs.pop(0)
    mark_refs = [refs.pop(0) for _ in range(plan["marks"])]
    packets = [refs.pop(0) for _ in range(plan["packets"])]
    if plan["carried"]:
        in_high, in_sums = refs.pop(0), refs.pop(0)
    high_ref, sums_ref = refs.pop(0), refs.pop(0)
    out_refs = refs

    sources = mark_refs + packets
    numbers = [
        jnp.max(
            sources[packet][row : row + HEADER, column : column + HEAD_WIDTH].astype(jnp.float32)
        ).astype(jnp.int32)
        for packet, row, column in plan["owner_headers"] + plan["headers"]
    ]
    owner_c, member_c = numbers[:owners], numbers[owners:]

    def rows_of(j, half, column):
        packet, row = plan["members"][j]
        at = row + half * chunk
        at = at if isinstance(half, int) else pl.multiple_of(at, HEADER)
        return packets[packet][pl.ds(at, chunk), column : column + HEAD_WIDTH]

    def state_at(i, half, h):
        return (2 * i + half) * heads + h

    rows = QUERY_PER_KEY * chunk
    causal = lax.broadcasted_iota(jnp.int32, (chunk, rows), 0) <= lax.rem(
        lax.broadcasted_iota(jnp.int32, (chunk, rows), 1), chunk
    )
    count = len(plan["members"])
    for first in range(0, count, 6):
        group = range(first, min(first + 6, count))
        for h in range(heads):
            k_at, v_at = h * HEAD_WIDTH, (heads + h) * HEAD_WIDTH
            early_keys = jnp.concatenate([rows_of(j, 0, k_at) for j in group], axis=0)
            early_values = turned_values([rows_of(j, 0, v_at) for j in group])
            for i in range(owners):
                late_at, early_at = state_at(i, 1, h), state_at(i, 0, h)
                carried = None
                if first > 0:
                    carried = [(ref[early_at], ref[late_at]) for ref in (high_ref, sums_ref)]
                elif plan["carried"]:
                    carried = [(ref[early_at], ref[late_at]) for ref in (in_high, in_sums)]

                pairs = []
                for j in group:
                    if plan["own"] and j == plan["own_at"](i):
                        pairs += [(j, 0, causal), (j, 1, causal)]
                    else:
                        pairs.append((j, (member_c[j] > owner_c[i]).astype(jnp.int32), None))
                base = product(early_keys, q_ref[late_at])
                scores = []
                for j, half, mask in pairs:
                    s = product(rows_of(j, half, k_at), q_ref[state_at(i, half, h)])
                    scores.append(s if mask is None else jnp.where(mask, s, MASKED))
                tops = [jnp.max(s, axis=0, keepdims=True) for s in scores]
                highs = []
                for side in range(2):
                    some = [jnp.where(half == side, top, MASKED) for (_, half, _), top in zip(pairs, tops)]
                    if side == 1:
                        some.append(jnp.max(base, axis=0, keepdims=True))
                    if carried is not None:
                        some.append(carried[0][side])
                    highs.append(functools.reduce(jnp.maximum, some))
                weights = [
                    weigh(s, jnp.where(half == 1, highs[1], highs[0]))
                    for (_, half, _), s in zip(pairs, scores)
                ]
                values = turned_values([rows_of(j, half, v_at) for j, half, _ in pairs])
                zero = jnp.zeros_like(weights[0])
                for side, at in ((0, early_at), (1, late_at)):
                    chosen = [
                        jnp.where(half == side, w, zero) for (_, half, _), w in zip(pairs, weights)
                    ]
                    sums = product(values, jnp.concatenate(chosen, axis=0))
                    if side == 1:
                        sums = sums + product(early_values, weigh(base, highs[1]))
                    if carried is not None:
                        shrink = jnp.exp2((carried[0][side] - highs[side]) * EXP2_SCALE)
                        sums = sums + carried[1][side] * shrink
                    high_ref[at] = highs[side]
                    sums_ref[at] = sums
                    if plan["last"] and first + 6 >= count:
                        mixed = sums[:HEAD_WIDTH] / sums[HEAD_WIDTH : HEAD_WIDTH + 1]
                        mixed = jnp.transpose(mixed).astype(out_refs[i].dtype)
                        for g in range(QUERY_PER_KEY):
                            out_refs[i][
                                side * chunk : (side + 1) * chunk,
                                h * GROUP + g * HEAD_WIDTH : h * GROUP + (g + 1) * HEAD_WIDTH,
                            ] = mixed[g * chunk : (g + 1) * chunk]


def attend(plan, turned, marks, packets, state):
    heads, chunk, owners = plan["heads"], plan["chunk"], plan["owners"]
    count = len(plan["members"])
    plan = dict(plan, marks=len(marks), packets=len(packets), carried=state is not None)
    rows = QUERY_PER_KEY * chunk
    slots = owners * 2 * heads
    vmem = pl.BlockSpec(memory_space=pltpu.VMEM)
    out_shape = [
        jax.ShapeDtypeStruct((slots, 1, rows), jnp.float32),
        jax.ShapeDtypeStruct((slots, HEAD_WIDTH + HEADER, rows), jnp.float32),
    ]
    if plan["last"]:
        out_shape += [jax.ShapeDtypeStruct((2 * chunk, heads * GROUP), jnp.bfloat16)] * owners
    operands = 1 + len(marks) + len(packets)
    flops = 4 * owners * heads * rows * HEAD_WIDTH * count * chunk * 2
    return pl.pallas_call(
        functools.partial(attend_kernel, plan),
        out_shape=out_shape,
        in_specs=[vmem] * (operands + (0 if state is None else 2)),
        out_specs=[vmem] * len(out_shape),
        input_output_aliases={} if state is None else {operands: 0, operands + 1: 1},
        cost_estimate=pl.CostEstimate(
            flops=flops, bytes_accessed=4 << 20, transcendentals=flops // 512
        ),
        compiler_params=pltpu.CompilerParams(vmem_limit_bytes=VMEM_LIMIT),
        name="attend",
    )(turned, *marks, *packets, *(state or ()))


def turn_kernel(heads, chunk, whole_rows, *refs):
    q_refs, turned_ref = refs[:-1], refs[-1]
    for i, q_ref in enumerate(q_refs):
        base = my_core() * (heads * GROUP) if whole_rows[i] else 0
        for half in range(2):
            for h in range(heads):
                columns = [
                    pl.ds(pl.multiple_of(base + h * GROUP + g * HEAD_WIDTH, HEAD_WIDTH), HEAD_WIDTH)
                    for g in range(QUERY_PER_KEY)
                ]
                q = jnp.concatenate(
                    [q_ref[half * chunk : (half + 1) * chunk, at] for at in columns], axis=0
                )
                turned_ref[(2 * i + half) * heads + h] = jnp.transpose(q)


def turn(heads, chunk, whole_rows, queries):
    vmem = pl.BlockSpec(memory_space=pltpu.VMEM)
    owners = len(queries)
    shape = (2 * owners * heads, HEAD_WIDTH, QUERY_PER_KEY * chunk)
    return pl.pallas_call(
        functools.partial(turn_kernel, heads, chunk, whole_rows),
        out_shape=jax.ShapeDtypeStruct(shape, jnp.bfloat16),
        in_specs=[vmem] * owners,
        out_specs=vmem,
        cost_estimate=pl.CostEstimate(flops=1 << 20, bytes_accessed=4 << 20, transcendentals=0),
        compiler_params=pltpu.CompilerParams(vmem_limit_bytes=VMEM_LIMIT),
        name="turn",
    )(*queries)


def project_kernel(keep, own_ref, other_ref, w_ref, out_ref, rows_ref, total_ref):
    step = pl.program_id(0)
    chunk, part = rows_ref.shape[0], own_ref.shape[1]
    depth = w_ref.shape[0]

    @pl.when(step == 0)
    def _():
        mine = lax.axis_index("inner").astype(jnp.int32)
        half = mine if keep else 1 - mine
        at = pl.ds(pl.multiple_of(half * chunk, chunk), chunk)
        own, other = own_ref[at], other_ref[at]
        left = my_core() == 0
        rows_ref[:, :part] = jnp.where(left, own, other)
        rows_ref[:, part:] = jnp.where(left, other, own)
        total_ref[...] = jnp.zeros_like(total_ref)

    at = pl.multiple_of(step * depth, depth)
    total_ref[...] += product(rows_ref[:, pl.ds(at, depth)], w_ref[...])

    @pl.when(step == pl.num_programs(0) - 1)
    def _():
        out_ref[...] = total_ref[...].astype(out_ref.dtype)


def project(own, other, out_weight, first, width, depth, keep):
    chunk = own.shape[0] // 2
    whole = lambda j: (0, 0)
    return pl.pallas_call(
        functools.partial(project_kernel, keep),
        out_shape=jax.ShapeDtypeStruct((chunk, width), jnp.bfloat16),
        grid=(out_weight.shape[0] // depth,),
        in_specs=[
            pl.BlockSpec(own.shape, whole),
            pl.BlockSpec(other.shape, whole),
            pl.BlockSpec((pl.Element(depth), pl.Element(width)), lambda j: (j * depth, first)),
        ],
        out_specs=pl.BlockSpec((chunk, width), whole),
        scratch_shapes=[
            pltpu.VMEM((chunk, out_weight.shape[0]), jnp.bfloat16),
            pltpu.VMEM((chunk, width), jnp.float32),
        ],
        cost_estimate=pl.CostEstimate(
            flops=2 * chunk * out_weight.shape[0] * width,
            bytes_accessed=2 * out_weight.shape[0] * width,
            transcendentals=0,
        ),
        compiler_params=pltpu.CompilerParams(vmem_limit_bytes=VMEM_LIMIT),
        name="project",
    )(own, other, out_weight)


def prepare_kernel(chunk, k_ref, v_ref, position_ref, sent_ref, kept_ref, mark_ref, first_ref, sems):
    rows, width = k_ref.shape[0], k_ref.shape[1] // 2
    copies = [pltpu.make_async_copy(position_ref, first_ref, sems.at[4])]
    for n, (ref, core) in enumerate(((sent_ref, 1 - my_core()), (kept_ref, my_core()))):
        at = pl.ds(pl.multiple_of(core * width, width), width)
        for m, source in enumerate((k_ref, v_ref)):
            to = ref.at[pl.ds(0, rows), pl.ds(m * width, width)]
            copies.append(pltpu.make_async_copy(source.at[:, at], to, sems.at[2 * n + m]))
    for copy in copies:
        copy.start()
    copies[0].wait()
    c = lax.div(first_ref[0], jnp.int32(chunk)).astype(jnp.float32)
    mark_ref[...] = jnp.full(mark_ref.shape, c, jnp.float32).astype(jnp.bfloat16)
    sent_ref[rows:] = jnp.full((HEADER, 2 * width), c, jnp.float32).astype(jnp.bfloat16)
    for copy in copies[1:]:
        copy.wait()


def prepare(keys, values, positions):
    vmem = pl.BlockSpec(memory_space=pltpu.VMEM)
    hbm = pl.BlockSpec(memory_space=pltpu.HBM)
    rows, width = keys.shape
    operands = [pltpu.with_memory_space_constraint(x, pltpu.HBM) for x in (keys, values, positions)]
    return pl.pallas_call(
        functools.partial(prepare_kernel, rows // 2),
        out_shape=[
            jax.ShapeDtypeStruct((rows + HEADER, width), jnp.bfloat16),
            jax.ShapeDtypeStruct((rows, width), jnp.bfloat16),
            jax.ShapeDtypeStruct((HEADER, width // 2), jnp.bfloat16),
        ],
        in_specs=[hbm, hbm, hbm],
        out_specs=[vmem, vmem, vmem],
        scratch_shapes=[
            pltpu.SMEM(positions.shape, jnp.int32),
            pltpu.SemaphoreType.DMA((5,)),
        ],
        compiler_params=pltpu.CompilerParams(vmem_limit_bytes=VMEM_LIMIT),
        name="prepare",
    )(*operands)


def after(value, *events):
    return lax.optimization_barrier((value, *events))[0]


def split_over_cores(count, queries, keys, values, positions):
    chips, half = count // 2, count // 4
    rows, chunk = queries.shape[0], queries.shape[0] // 2
    heads = keys.shape[1] // HEAD_WIDTH // 2
    sibling = [(b, b ^ 1) for b in range(count)]
    clock, counter = ring_pairs(chips, 1), ring_pairs(chips, -1)
    width = heads * HEAD_WIDTH
    up = lambda x: lax.ppermute(x, "blk", clock)
    down = lambda x: lax.ppermute(x, "blk", counter)

    sent, x, mark = prepare(keys, values, positions)
    got = lax.ppermute(sent, "blk", sibling)
    y = jnp.concatenate(
        [got[:rows], jnp.concatenate([mark, got[rows:, :width]], axis=1)], axis=0
    )
    q_sent = lax.dynamic_slice(
        queries, (0, (1 - my_core()) * heads * GROUP), (rows, heads * GROUP)
    )
    q_got = lax.ppermute(q_sent, "blk", sibling)
    turned = turn(heads, chunk, (True, False), [queries, q_got])

    def call(pairs, state, own, last=False):
        each = range(len(pairs))
        plan = dict(
            heads=heads,
            chunk=chunk,
            owners=2,
            own=own,
            own_at=lambda i: i,
            last=last,
            members=[(2 * j + i, 0) for j in each for i in range(2)],
            headers=[(2 + 2 * j, rows, i * width) for j in each for i in range(2)],
            owner_headers=[(0, rows, 0), (0, rows, width)],
        )
        return attend(plan, turned, [y], [packet for pair in pairs for packet in pair], state)

    state = None
    ups = downs = (x, y)
    arrived = [(x, y)]
    for r in range(1, half):
        (x_up, y_up), (x_down, y_down) = ups, downs
        if r == 2:
            x_up, x_down, turned = lax.optimization_barrier((x_up, x_down, turned))
        elif r > 2:
            x_up, x_down, *state = lax.optimization_barrier((x_up, x_down, *state))
        ups, downs = (up(x_up), up(y_up)), (down(x_down), down(y_down))
        if r >= 2:
            state = call(arrived, state, r == 2)
            arrived = []
        arrived += [ups, downs]
    x_up, y_down, *state = lax.optimization_barrier((ups[0], downs[1], *state))
    far = (up(x_up), down(y_down))
    state = call(arrived, state, False)
    _, _, own, theirs = call([far], state, False, True)
    return own, lax.ppermute(theirs, "blk", sibling)


def one_head_a_device(count, queries, keys, values, positions):
    rows, chunk = queries.shape[0], queries.shape[0] // 2
    heads = keys.shape[1] // HEAD_WIDTH
    c = (positions[:1] // chunk).astype(jnp.bfloat16).reshape(1, 1)
    header = jnp.broadcast_to(c, (HEADER, 2 * keys.shape[1]))
    packet = jnp.concatenate([jnp.concatenate([keys, values], axis=1), header], axis=0)
    packets = lax.all_gather(packet, "blk", axis=0, tiled=True)
    size = rows + HEADER
    here = lax.axis_index("blk")
    order = lax.rem(here + jnp.arange(count), count)
    packets = packets.reshape(count, size, -1)[order].reshape(count * size, -1)
    plan = dict(
        heads=heads,
        chunk=chunk,
        owners=1,
        own=True,
        own_at=lambda i: 0,
        last=True,
        members=[(0, j * size) for j in range(count)],
        headers=[(0, j * size + rows, 0) for j in range(count)],
        owner_headers=[(0, rows, 0)],
    )
    turned = turn(heads, chunk, (False,), [queries])
    return attend(plan, turned, [], [packets], None)[2]


def shards(count, inner, queries, keys, values, positions, out_weight):
    heads = keys.shape[1] // HEAD_WIDTH
    if heads % 2:
        attended = one_head_a_device(count, queries, keys, values, positions)
        partial = jnp.dot(attended, out_weight, preferred_element_type=jnp.float32)
        return lax.psum_scatter(
            partial.astype(jnp.bfloat16), "inner", scatter_dimension=0, tiled=True
        )
    own, other = split_over_cores(count, queries, keys, values, positions)
    out_weight = pltpu.with_memory_space_constraint(out_weight, pltpu.HBM)
    width = out_weight.shape[1]
    shares = (5, 5, 6, 4)
    received, first, source = [], 0, own
    for j, share in enumerate(shares):
        columns = width * share // sum(shares)
        if j > 0:
            source = after(own, sent, *received[: j - 1][-1:])
        sent = project(source, other, out_weight, first, columns, 512, False)
        received.append(lax.ppermute(sent, "inner", [(0, 1), (1, 0)]))
        first += columns
    kept = project(after(own, sent), other, out_weight, 0, width, 256, True)
    theirs = jnp.concatenate(received, axis=1)
    return (kept.astype(jnp.float32) + theirs.astype(jnp.float32)).astype(jnp.bfloat16)


def solution(mesh):
    placed = (P("blk", "inner"), P("blk", "inner"), P("blk", "inner"), P("blk"), P("inner", None))
    return jax.shard_map(
        functools.partial(shards, mesh.shape["blk"], mesh.shape["inner"]),
        mesh=mesh,
        in_specs=placed,
        out_specs=P(("blk", "inner"), None),
        check_vma=False,
    )
```

```python
import functools
import math

import jax
import jax.numpy as jnp
from jax import lax
from jax.experimental import pallas as pl
from jax.experimental.pallas import tpu as pltpu
from jax.sharding import PartitionSpec as P

HEAD_WIDTH = 128
QUERY_PER_KEY = 5
GROUP = QUERY_PER_KEY * HEAD_WIDTH
EXP2_SCALE = math.log2(math.e) / math.sqrt(HEAD_WIDTH)
MASKED = -1e30
VMEM_LIMIT = 16 * 1024 * 1024
HEADER = 16


def ring_of_chips(chips):
    half = chips // 2
    if chips == 8:
        return [2 * z for z in range(half)] + [2 * z + 1 for z in reversed(range(half))]
    return list(range(half)) + list(reversed(range(half, chips)))


def ring_pairs(chips, step):
    ring = ring_of_chips(chips)
    return [
        (2 * ring[i] + core, 2 * ring[(i + step) % chips] + core)
        for i in range(chips)
        for core in range(2)
    ]


def my_core():
    return lax.rem(lax.axis_index("blk"), 2).astype(jnp.int32)


def product(a, b):
    return jnp.dot(a, b, preferred_element_type=jnp.float32)


def weigh(scores, high):
    return jnp.exp2((scores - high) * EXP2_SCALE).astype(jnp.bfloat16)


def turned_values(blocks):
    v = jnp.concatenate(blocks, axis=0)
    return jnp.concatenate([jnp.transpose(v), jnp.ones((HEADER, v.shape[0]), v.dtype)], axis=0)


def attend_kernel(plan, *refs):
    heads, chunk, owners = plan["heads"], plan["chunk"], plan["owners"]
    refs = list(refs)
    q_ref = refs.pop(0)
    mark_refs = [refs.pop(0) for _ in range(plan["marks"])]
    packets = [refs.pop(0) for _ in range(plan["packets"])]
    if plan["carried"]:
        in_high, in_sums = refs.pop(0), refs.pop(0)
    high_ref, sums_ref = refs.pop(0), refs.pop(0)
    out_refs = refs

    sources = mark_refs + packets
    numbers = [
        jnp.max(
            sources[packet][row : row + HEADER, column : column + HEAD_WIDTH].astype(jnp.float32)
        ).astype(jnp.int32)
        for packet, row, column in plan["owner_headers"] + plan["headers"]
    ]
    owner_c, member_c = numbers[:owners], numbers[owners:]

    def rows_of(j, half, column):
        packet, row = plan["members"][j]
        at = row + half * chunk
        at = at if isinstance(half, int) else pl.multiple_of(at, HEADER)
        return packets[packet][pl.ds(at, chunk), column : column + HEAD_WIDTH]

    def state_at(i, half, h):
        return (2 * i + half) * heads + h

    rows = QUERY_PER_KEY * chunk
    causal = lax.broadcasted_iota(jnp.int32, (chunk, rows), 0) <= lax.rem(
        lax.broadcasted_iota(jnp.int32, (chunk, rows), 1), chunk
    )
    count = len(plan["members"])
    for first in range(0, count, 6):
        group = range(first, min(first + 6, count))
        for h in range(heads):
            k_at, v_at = h * HEAD_WIDTH, (heads + h) * HEAD_WIDTH
            early_keys = jnp.concatenate([rows_of(j, 0, k_at) for j in group], axis=0)
            early_values = turned_values([rows_of(j, 0, v_at) for j in group])
            for i in range(owners):
                late_at, early_at = state_at(i, 1, h), state_at(i, 0, h)
                carried = None
                if first > 0:
                    carried = [(ref[early_at], ref[late_at]) for ref in (high_ref, sums_ref)]
                elif plan["carried"]:
                    carried = [(ref[early_at], ref[late_at]) for ref in (in_high, in_sums)]

                pairs = []
                for j in group:
                    if plan["own"] and j == plan["own_at"](i):
                        pairs += [(j, 0, causal), (j, 1, causal)]
                    else:
                        pairs.append((j, (member_c[j] > owner_c[i]).astype(jnp.int32), None))
                base = product(early_keys, q_ref[late_at])
                scores = []
                for j, half, mask in pairs:
                    s = product(rows_of(j, half, k_at), q_ref[state_at(i, half, h)])
                    scores.append(s if mask is None else jnp.where(mask, s, MASKED))
                tops = [jnp.max(s, axis=0, keepdims=True) for s in scores]
                highs = []
                for side in range(2):
                    some = [jnp.where(half == side, top, MASKED) for (_, half, _), top in zip(pairs, tops)]
                    if side == 1:
                        some.append(jnp.max(base, axis=0, keepdims=True))
                    if carried is not None:
                        some.append(carried[0][side])
                    highs.append(functools.reduce(jnp.maximum, some))
                weights = [
                    weigh(s, jnp.where(half == 1, highs[1], highs[0]))
                    for (_, half, _), s in zip(pairs, scores)
                ]
                values = turned_values([rows_of(j, half, v_at) for j, half, _ in pairs])
                zero = jnp.zeros_like(weights[0])
                for side, at in ((0, early_at), (1, late_at)):
                    chosen = [
                        jnp.where(half == side, w, zero) for (_, half, _), w in zip(pairs, weights)
                    ]
                    sums = product(values, jnp.concatenate(chosen, axis=0))
                    if side == 1:
                        sums = sums + product(early_values, weigh(base, highs[1]))
                    if carried is not None:
                        shrink = jnp.exp2((carried[0][side] - highs[side]) * EXP2_SCALE)
                        sums = sums + carried[1][side] * shrink
                    high_ref[at] = highs[side]
                    sums_ref[at] = sums
                    if plan["last"] and first + 6 >= count:
                        mixed = sums[:HEAD_WIDTH] * (1.0 / sums[HEAD_WIDTH : HEAD_WIDTH + 1])
                        mixed = jnp.transpose(mixed.astype(out_refs[i].dtype))
                        for g in range(QUERY_PER_KEY):
                            out_refs[i][
                                side * chunk : (side + 1) * chunk,
                                h * GROUP + g * HEAD_WIDTH : h * GROUP + (g + 1) * HEAD_WIDTH,
                            ] = mixed[g * chunk : (g + 1) * chunk]


def attend(plan, turned, marks, packets, state):
    heads, chunk, owners = plan["heads"], plan["chunk"], plan["owners"]
    count = len(plan["members"])
    plan = dict(plan, marks=len(marks), packets=len(packets), carried=state is not None)
    rows = QUERY_PER_KEY * chunk
    slots = owners * 2 * heads
    vmem = pl.BlockSpec(memory_space=pltpu.VMEM)
    out_shape = [
        jax.ShapeDtypeStruct((slots, 1, rows), jnp.float32),
        jax.ShapeDtypeStruct((slots, HEAD_WIDTH + HEADER, rows), jnp.float32),
    ]
    if plan["last"]:
        out_shape += [jax.ShapeDtypeStruct((2 * chunk, heads * GROUP), jnp.bfloat16)] * owners
    operands = 1 + len(marks) + len(packets)
    flops = 4 * owners * heads * rows * HEAD_WIDTH * count * chunk * 2
    return pl.pallas_call(
        functools.partial(attend_kernel, plan),
        out_shape=out_shape,
        in_specs=[vmem] * (operands + (0 if state is None else 2)),
        out_specs=[vmem] * len(out_shape),
        input_output_aliases={} if state is None else {operands: 0, operands + 1: 1},
        cost_estimate=pl.CostEstimate(
            flops=flops, bytes_accessed=4 << 20, transcendentals=flops // 512
        ),
        compiler_params=pltpu.CompilerParams(vmem_limit_bytes=VMEM_LIMIT),
        name="attend",
    )(turned, *marks, *packets, *(state or ()))


def turn_kernel(heads, chunk, whole_rows, *refs):
    q_refs, turned_ref = refs[:-1], refs[-1]
    for i, q_ref in enumerate(q_refs):
        base = my_core() * (heads * GROUP) if whole_rows[i] else 0
        for half in range(2):
            for h in range(heads):
                columns = [
                    pl.ds(pl.multiple_of(base + h * GROUP + g * HEAD_WIDTH, HEAD_WIDTH), HEAD_WIDTH)
                    for g in range(QUERY_PER_KEY)
                ]
                q = jnp.concatenate(
                    [q_ref[half * chunk : (half + 1) * chunk, at] for at in columns], axis=0
                )
                turned_ref[(2 * i + half) * heads + h] = jnp.transpose(q)


def turn(heads, chunk, whole_rows, queries):
    vmem = pl.BlockSpec(memory_space=pltpu.VMEM)
    owners = len(queries)
    shape = (2 * owners * heads, HEAD_WIDTH, QUERY_PER_KEY * chunk)
    return pl.pallas_call(
        functools.partial(turn_kernel, heads, chunk, whole_rows),
        out_shape=jax.ShapeDtypeStruct(shape, jnp.bfloat16),
        in_specs=[vmem] * owners,
        out_specs=vmem,
        cost_estimate=pl.CostEstimate(flops=1 << 20, bytes_accessed=4 << 20, transcendentals=0),
        compiler_params=pltpu.CompilerParams(vmem_limit_bytes=VMEM_LIMIT),
        name="turn",
    )(*queries)


def project_kernel(first, own_ref, other_ref, w_ref, sent_ref, kept_ref, rows_ref, held_ref, sems):
    chunk, width = sent_ref.shape
    pieces = sems.shape[0]
    depth = held_ref.shape[0] // pieces
    copies = []
    for p in range(pieces):
        at = pl.ds(p * depth, depth)
        copies.append(
            pltpu.make_async_copy(w_ref.at[at, pl.ds(first, width)], held_ref.at[at], sems.at[p])
        )
        copies[-1].start()
    part = own_ref.shape[1]
    mine = lax.axis_index("inner").astype(jnp.int32)
    left = my_core() == 0
    for place, half in enumerate((1 - mine, mine)):
        at = pl.ds(pl.multiple_of(half * chunk, chunk), chunk)
        own, other = own_ref[at], other_ref[at]
        to = slice(place * chunk, (place + 1) * chunk)
        rows_ref[to, :part] = jnp.where(left, own, other)
        rows_ref[to, part:] = jnp.where(left, other, own)
    total = None
    for p in range(pieces):
        copies[p].wait()
        at = slice(p * depth, (p + 1) * depth)
        term = product(rows_ref[:, at], held_ref[at])
        total = term if total is None else total + term
    total = total.astype(sent_ref.dtype)
    sent_ref[...] = total[:chunk]
    kept_ref[...] = total[chunk:]


def project(own, other, out_weight, first, width, pieces):
    rows, depth = own.shape[0], out_weight.shape[0]
    vmem = pl.BlockSpec(memory_space=pltpu.VMEM)
    return pl.pallas_call(
        functools.partial(project_kernel, first),
        out_shape=[jax.ShapeDtypeStruct((rows // 2, width), jnp.bfloat16)] * 2,
        in_specs=[vmem, vmem, pl.BlockSpec(memory_space=pltpu.HBM)],
        out_specs=[vmem, vmem],
        scratch_shapes=[
            pltpu.VMEM((rows, depth), jnp.bfloat16),
            pltpu.VMEM((depth, width), jnp.bfloat16),
            pltpu.SemaphoreType.DMA((pieces,)),
        ],
        cost_estimate=pl.CostEstimate(
            flops=2 * rows * depth * width, bytes_accessed=2 * depth * width, transcendentals=0
        ),
        compiler_params=pltpu.CompilerParams(vmem_limit_bytes=VMEM_LIMIT),
        name="project",
    )(own, other, out_weight)


def prepare_kernel(chunk, k_ref, v_ref, position_ref, sent_ref, kept_ref, mark_ref, first_ref, sems):
    rows, width = k_ref.shape[0], k_ref.shape[1] // 2
    copies = [pltpu.make_async_copy(position_ref, first_ref, sems.at[4])]
    for n, (ref, core) in enumerate(((sent_ref, 1 - my_core()), (kept_ref, my_core()))):
        at = pl.ds(pl.multiple_of(core * width, width), width)
        for m, source in enumerate((k_ref, v_ref)):
            to = ref.at[pl.ds(0, rows), pl.ds(m * width, width)]
            copies.append(pltpu.make_async_copy(source.at[:, at], to, sems.at[2 * n + m]))
    for copy in copies:
        copy.start()
    copies[0].wait()
    c = lax.div(first_ref[0], jnp.int32(chunk)).astype(jnp.float32)
    mark_ref[...] = jnp.full(mark_ref.shape, c, jnp.float32).astype(jnp.bfloat16)
    sent_ref[rows:] = jnp.full((HEADER, 2 * width), c, jnp.float32).astype(jnp.bfloat16)
    for copy in copies[1:]:
        copy.wait()


def prepare(keys, values, positions):
    vmem = pl.BlockSpec(memory_space=pltpu.VMEM)
    hbm = pl.BlockSpec(memory_space=pltpu.HBM)
    rows, width = keys.shape
    operands = [pltpu.with_memory_space_constraint(x, pltpu.HBM) for x in (keys, values, positions)]
    return pl.pallas_call(
        functools.partial(prepare_kernel, rows // 2),
        out_shape=[
            jax.ShapeDtypeStruct((rows + HEADER, width), jnp.bfloat16),
            jax.ShapeDtypeStruct((rows, width), jnp.bfloat16),
            jax.ShapeDtypeStruct((HEADER, width // 2), jnp.bfloat16),
        ],
        in_specs=[hbm, hbm, hbm],
        out_specs=[vmem, vmem, vmem],
        scratch_shapes=[
            pltpu.SMEM(positions.shape, jnp.int32),
            pltpu.SemaphoreType.DMA((5,)),
        ],
        compiler_params=pltpu.CompilerParams(vmem_limit_bytes=VMEM_LIMIT),
        name="prepare",
    )(*operands)


def after(value, *events):
    return lax.optimization_barrier((value, *events))[0]


def split_over_cores(count, queries, keys, values, positions):
    chips, half = count // 2, count // 4
    rows, chunk = queries.shape[0], queries.shape[0] // 2
    heads = keys.shape[1] // HEAD_WIDTH // 2
    sibling = [(b, b ^ 1) for b in range(count)]
    clock, counter = ring_pairs(chips, 1), ring_pairs(chips, -1)
    width = heads * HEAD_WIDTH
    up = lambda x: lax.ppermute(x, "blk", clock)
    down = lambda x: lax.ppermute(x, "blk", counter)

    sent, x, mark = prepare(keys, values, positions)
    got = lax.ppermute(sent, "blk", sibling)
    y = jnp.concatenate(
        [got[:rows], jnp.concatenate([mark, got[rows:, :width]], axis=1)], axis=0
    )
    q_sent = lax.dynamic_slice(
        queries, (0, (1 - my_core()) * heads * GROUP), (rows, heads * GROUP)
    )
    q_got = lax.ppermute(q_sent, "blk", sibling)
    turned = turn(heads, chunk, (True, False), [queries, q_got])

    def call(pairs, state, own, last=False):
        each = range(len(pairs))
        plan = dict(
            heads=heads,
            chunk=chunk,
            owners=2,
            own=own,
            own_at=lambda i: i,
            last=last,
            members=[(2 * j + i, 0) for j in each for i in range(2)],
            headers=[(2 + 2 * j, rows, i * width) for j in each for i in range(2)],
            owner_headers=[(0, rows, 0), (0, rows, width)],
        )
        return attend(plan, turned, [y], [packet for pair in pairs for packet in pair], state)

    state = None
    ups = downs = (x, y)
    arrived = [(x, y)]
    for r in range(1, half):
        (x_up, y_up), (x_down, y_down) = ups, downs
        if r == 2:
            x_up, x_down, turned = lax.optimization_barrier((x_up, x_down, turned))
        elif r > 2:
            x_up, x_down, *state = lax.optimization_barrier((x_up, x_down, *state))
        ups, downs = (up(x_up), up(y_up)), (down(x_down), down(y_down))
        if r >= 2:
            state = call(arrived, state, r == 2)
            arrived = []
        arrived += [ups, downs]
    x_up, y_down, *state = lax.optimization_barrier((ups[0], downs[1], *state))
    far = (up(x_up), down(y_down))
    state = call(arrived, state, False)
    _, _, own, theirs = call([far], state, False, True)
    return own, lax.ppermute(theirs, "blk", sibling)


def one_head_a_device(count, queries, keys, values, positions):
    rows, chunk = queries.shape[0], queries.shape[0] // 2
    heads = keys.shape[1] // HEAD_WIDTH
    c = (positions[:1] // chunk).astype(jnp.bfloat16).reshape(1, 1)
    header = jnp.broadcast_to(c, (HEADER, 2 * keys.shape[1]))
    packet = jnp.concatenate([jnp.concatenate([keys, values], axis=1), header], axis=0)
    packets = lax.all_gather(packet, "blk", axis=0, tiled=True)
    size = rows + HEADER
    here = lax.axis_index("blk")
    order = lax.rem(here + jnp.arange(count), count)
    packets = packets.reshape(count, size, -1)[order].reshape(count * size, -1)
    plan = dict(
        heads=heads,
        chunk=chunk,
        owners=1,
        own=True,
        own_at=lambda i: 0,
        last=True,
        members=[(0, j * size) for j in range(count)],
        headers=[(0, j * size + rows, 0) for j in range(count)],
        owner_headers=[(0, rows, 0)],
    )
    turned = turn(heads, chunk, (False,), [queries])
    return attend(plan, turned, [], [packets], None)[2]


def shards(count, inner, queries, keys, values, positions, out_weight):
    heads = keys.shape[1] // HEAD_WIDTH
    if heads % 2:
        attended = one_head_a_device(count, queries, keys, values, positions)
        partial = jnp.dot(attended, out_weight, preferred_element_type=jnp.float32)
        return lax.psum_scatter(
            partial.astype(jnp.bfloat16), "inner", scatter_dimension=0, tiled=True
        )
    own, other = split_over_cores(count, queries, keys, values, positions)
    out_weight = pltpu.with_memory_space_constraint(out_weight, pltpu.HBM)
    width = out_weight.shape[1]
    shares = (4, 4, 7, 5)
    received, kept, first, source = [], [], 0, own
    for j, share in enumerate(shares):
        columns = width * share // sum(shares)
        if j > 0:
            source = after(own, sent, *received[: j - 1][-1:])
        sent, keep = project(source, other, out_weight, first, columns, 5)
        received.append(lax.ppermute(sent, "inner", [(0, 1), (1, 0)]))
        kept.append(keep)
        first += columns
    mine, theirs = jnp.concatenate(kept, axis=1), jnp.concatenate(received, axis=1)
    return (mine.astype(jnp.float32) + theirs.astype(jnp.float32)).astype(jnp.bfloat16)


def solution(mesh):
    placed = (P("blk", "inner"), P("blk", "inner"), P("blk", "inner"), P("blk"), P("inner", None))
    return jax.shard_map(
        functools.partial(shards, mesh.shape["blk"], mesh.shape["inner"]),
        mesh=mesh,
        in_specs=placed,
        out_specs=P(("blk", "inner"), None),
        check_vma=False,
    )
```

```python
import functools
import math

import jax
import jax.numpy as jnp
from jax import lax
from jax.experimental import pallas as pl
from jax.experimental.pallas import tpu as pltpu
from jax.sharding import PartitionSpec as P

HEAD_WIDTH = 128
QUERY_PER_KEY = 5
GROUP = QUERY_PER_KEY * HEAD_WIDTH
EXP2_SCALE = math.log2(math.e) / math.sqrt(HEAD_WIDTH)
MASKED = -1e30
VMEM_LIMIT = 16 * 1024 * 1024
HEADER = 16
PIECES = 5


def ring_of_chips(chips):
    half = chips // 2
    if chips == 8:
        return [2 * z for z in range(half)] + [2 * z + 1 for z in reversed(range(half))]
    return list(range(half)) + list(reversed(range(half, chips)))


def ring_pairs(chips, step):
    ring = ring_of_chips(chips)
    return [
        (2 * ring[i] + core, 2 * ring[(i + step) % chips] + core)
        for i in range(chips)
        for core in range(2)
    ]


def my_core():
    return lax.rem(lax.axis_index("blk"), 2).astype(jnp.int32)


def product(a, b):
    return jnp.dot(a, b, preferred_element_type=jnp.float32)


def weigh(scores, high):
    return jnp.exp2((scores - high) * EXP2_SCALE).astype(jnp.bfloat16)


def turned_values(blocks):
    v = jnp.concatenate(blocks, axis=0)
    return jnp.concatenate([jnp.transpose(v), jnp.ones((HEADER, v.shape[0]), v.dtype)], axis=0)


def fetch_columns(w_ref, first, held_ref, sems):
    pieces = sems.shape[0]
    depth, width = held_ref.shape[0] // pieces, held_ref.shape[1]
    copies = []
    for p in range(pieces):
        at = pl.ds(p * depth, depth)
        copies.append(
            pltpu.make_async_copy(w_ref.at[at, pl.ds(first, width)], held_ref.at[at], sems.at[p])
        )
        copies[-1].start()
    return copies


def attend_kernel(plan, *refs):
    heads, chunk, owners = plan["heads"], plan["chunk"], plan["owners"]
    refs = list(refs)
    q_ref = refs.pop(0)
    mark_refs = [refs.pop(0) for _ in range(plan["marks"])]
    packets = [refs.pop(0) for _ in range(plan["packets"])]
    if plan["carried"]:
        in_high, in_sums = refs.pop(0), refs.pop(0)
    fetch = plan["fetch"]
    if fetch:
        w_ref = refs.pop(0)
    if plan["last"]:
        out_refs = [refs.pop(0) for _ in range(owners)]
    if fetch:
        held_ref, sems = (refs.pop(0) if plan["last"] else refs.pop(2)), refs.pop()
        copies = fetch_columns(w_ref, fetch[0], held_ref, sems)
    high_ref, sums_ref = refs

    sources = mark_refs + packets
    numbers = [
        jnp.max(
            sources[packet][row : row + HEADER, column : column + HEAD_WIDTH].astype(jnp.float32)
        ).astype(jnp.int32)
        for packet, row, column in plan["owner_headers"] + plan["headers"]
    ]
    owner_c, member_c = numbers[:owners], numbers[owners:]

    def rows_of(j, half, column):
        packet, row = plan["members"][j]
        at = row + half * chunk
        at = at if isinstance(half, int) else pl.multiple_of(at, HEADER)
        return packets[packet][pl.ds(at, chunk), column : column + HEAD_WIDTH]

    def state_at(i, half, h):
        return (2 * i + half) * heads + h

    rows = QUERY_PER_KEY * chunk
    causal = lax.broadcasted_iota(jnp.int32, (chunk, rows), 0) <= lax.rem(
        lax.broadcasted_iota(jnp.int32, (chunk, rows), 1), chunk
    )
    count = len(plan["members"])
    for first in range(0, count, 6):
        group = range(first, min(first + 6, count))
        for h in range(heads):
            k_at, v_at = h * HEAD_WIDTH, (heads + h) * HEAD_WIDTH
            early_keys = jnp.concatenate([rows_of(j, 0, k_at) for j in group], axis=0)
            early_values = turned_values([rows_of(j, 0, v_at) for j in group])
            for i in range(owners):
                late_at, early_at = state_at(i, 1, h), state_at(i, 0, h)
                carried = None
                if first > 0:
                    carried = [(ref[early_at], ref[late_at]) for ref in (high_ref, sums_ref)]
                elif plan["carried"]:
                    carried = [(ref[early_at], ref[late_at]) for ref in (in_high, in_sums)]

                pairs = []
                for j in group:
                    if plan["own"] and j == plan["own_at"](i):
                        pairs += [(j, 0, causal), (j, 1, causal)]
                    else:
                        pairs.append((j, (member_c[j] > owner_c[i]).astype(jnp.int32), None))
                base = product(early_keys, q_ref[late_at])
                scores = []
                for j, half, mask in pairs:
                    s = product(rows_of(j, half, k_at), q_ref[state_at(i, half, h)])
                    scores.append(s if mask is None else jnp.where(mask, s, MASKED))
                tops = [jnp.max(s, axis=0, keepdims=True) for s in scores]
                highs = []
                for side in range(2):
                    some = [jnp.where(half == side, top, MASKED) for (_, half, _), top in zip(pairs, tops)]
                    if side == 1:
                        some.append(jnp.max(base, axis=0, keepdims=True))
                    if carried is not None:
                        some.append(carried[0][side])
                    highs.append(functools.reduce(jnp.maximum, some))
                weights = [
                    weigh(s, jnp.where(half == 1, highs[1], highs[0]))
                    for (_, half, _), s in zip(pairs, scores)
                ]
                values = turned_values([rows_of(j, half, v_at) for j, half, _ in pairs])
                zero = jnp.zeros_like(weights[0])
                for side, at in ((0, early_at), (1, late_at)):
                    chosen = [
                        jnp.where(half == side, w, zero) for (_, half, _), w in zip(pairs, weights)
                    ]
                    sums = product(values, jnp.concatenate(chosen, axis=0))
                    if side == 1:
                        sums = sums + product(early_values, weigh(base, highs[1]))
                    if carried is not None:
                        shrink = jnp.exp2((carried[0][side] - highs[side]) * EXP2_SCALE)
                        sums = sums + carried[1][side] * shrink
                    high_ref[at] = highs[side]
                    sums_ref[at] = sums
                    if plan["last"] and first + 6 >= count:
                        mixed = sums[:HEAD_WIDTH] * (1.0 / sums[HEAD_WIDTH : HEAD_WIDTH + 1])
                        mixed = jnp.transpose(mixed.astype(out_refs[i].dtype))
                        for g in range(QUERY_PER_KEY):
                            out_refs[i][
                                side * chunk : (side + 1) * chunk,
                                h * GROUP + g * HEAD_WIDTH : h * GROUP + (g + 1) * HEAD_WIDTH,
                            ] = mixed[g * chunk : (g + 1) * chunk]
    if fetch:
        for copy in copies:
            copy.wait()


def attend(plan, turned, marks, packets, state, out_weight=None):
    heads, chunk, owners = plan["heads"], plan["chunk"], plan["owners"]
    count = len(plan["members"])
    plan = dict(plan, marks=len(marks), packets=len(packets), carried=state is not None)
    fetch = plan.setdefault("fetch", None)
    rows = QUERY_PER_KEY * chunk
    slots = owners * 2 * heads
    vmem = pl.BlockSpec(memory_space=pltpu.VMEM)
    kept = [(slots, 1, rows), (slots, HEAD_WIDTH + HEADER, rows)]
    if plan["last"]:
        out_shape = [jax.ShapeDtypeStruct((2 * chunk, heads * GROUP), jnp.bfloat16)] * owners
    else:
        out_shape = [jax.ShapeDtypeStruct(shape, jnp.float32) for shape in kept]
    operands = 1 + len(marks) + len(packets) + (0 if state is None else 2)
    in_specs = [vmem] * operands
    scratch = [pltpu.VMEM(shape, jnp.float32) for shape in kept] if plan["last"] else []
    if fetch:
        in_specs.append(pl.BlockSpec(memory_space=pltpu.HBM))
        out_shape.append(jax.ShapeDtypeStruct((out_weight.shape[0], fetch[1]), out_weight.dtype))
        scratch.append(pltpu.SemaphoreType.DMA((PIECES,)))
    flops = 4 * owners * heads * rows * HEAD_WIDTH * count * chunk * 2
    return pl.pallas_call(
        functools.partial(attend_kernel, plan),
        out_shape=out_shape,
        in_specs=in_specs,
        out_specs=[vmem] * len(out_shape),
        scratch_shapes=scratch,
        cost_estimate=pl.CostEstimate(
            flops=flops, bytes_accessed=4 << 20, transcendentals=flops // 512
        ),
        compiler_params=pltpu.CompilerParams(vmem_limit_bytes=VMEM_LIMIT),
        name="attend",
    )(turned, *marks, *packets, *(state or ()), *([out_weight] if fetch else []))


def turn_kernel(heads, chunk, whole_rows, *refs):
    q_refs, turned_ref = refs[:-1], refs[-1]
    for i, q_ref in enumerate(q_refs):
        base = my_core() * (heads * GROUP) if whole_rows[i] else 0
        for half in range(2):
            for h in range(heads):
                columns = [
                    pl.ds(pl.multiple_of(base + h * GROUP + g * HEAD_WIDTH, HEAD_WIDTH), HEAD_WIDTH)
                    for g in range(QUERY_PER_KEY)
                ]
                q = jnp.concatenate(
                    [q_ref[half * chunk : (half + 1) * chunk, at] for at in columns], axis=0
                )
                turned_ref[(2 * i + half) * heads + h] = jnp.transpose(q)


def turn(heads, chunk, whole_rows, queries):
    vmem = pl.BlockSpec(memory_space=pltpu.VMEM)
    owners = len(queries)
    shape = (2 * owners * heads, HEAD_WIDTH, QUERY_PER_KEY * chunk)
    return pl.pallas_call(
        functools.partial(turn_kernel, heads, chunk, whole_rows),
        out_shape=jax.ShapeDtypeStruct(shape, jnp.bfloat16),
        in_specs=[vmem] * owners,
        out_specs=vmem,
        cost_estimate=pl.CostEstimate(flops=1 << 20, bytes_accessed=4 << 20, transcendentals=0),
        compiler_params=pltpu.CompilerParams(vmem_limit_bytes=VMEM_LIMIT),
        name="turn",
    )(*queries)


def project_kernel(following, own_ref, other_ref, held_ref, *refs):
    if following:
        w_ref, sent_ref, kept_ref, next_ref, rows_ref, sems = refs
        copies = fetch_columns(w_ref, following[0], next_ref, sems)
    else:
        sent_ref, kept_ref, rows_ref = refs
    chunk, part = sent_ref.shape[0], own_ref.shape[1]
    mine = lax.axis_index("inner").astype(jnp.int32)
    left = my_core() == 0
    for place, half in enumerate((1 - mine, mine)):
        at = pl.ds(pl.multiple_of(half * chunk, chunk), chunk)
        own, other = own_ref[at], other_ref[at]
        to = slice(place * chunk, (place + 1) * chunk)
        rows_ref[to, :part] = jnp.where(left, own, other)
        rows_ref[to, part:] = jnp.where(left, other, own)
    both = product(rows_ref[...], held_ref[...]).astype(sent_ref.dtype)
    sent_ref[...] = both[:chunk]
    kept_ref[...] = both[chunk:]
    if following:
        for copy in copies:
            copy.wait()


def project(own, other, held, out_weight, following):
    rows, (depth, width) = own.shape[0], held.shape
    vmem = pl.BlockSpec(memory_space=pltpu.VMEM)
    out_shape = [jax.ShapeDtypeStruct((rows // 2, width), jnp.bfloat16)] * 2
    in_specs, operands = [vmem] * 3, [own, other, held]
    scratch = [pltpu.VMEM((rows, depth), jnp.bfloat16)]
    if following:
        out_shape.append(jax.ShapeDtypeStruct((depth, following[1]), held.dtype))
        in_specs.append(pl.BlockSpec(memory_space=pltpu.HBM))
        operands.append(out_weight)
        scratch.append(pltpu.SemaphoreType.DMA((PIECES,)))
    return pl.pallas_call(
        functools.partial(project_kernel, following),
        out_shape=out_shape,
        in_specs=in_specs,
        out_specs=[vmem] * len(out_shape),
        scratch_shapes=scratch,
        cost_estimate=pl.CostEstimate(
            flops=2 * rows * depth * width, bytes_accessed=2 * depth * width, transcendentals=0
        ),
        compiler_params=pltpu.CompilerParams(vmem_limit_bytes=VMEM_LIMIT),
        name="project",
    )(*operands)


def prepare_kernel(chunk, k_ref, v_ref, position_ref, sent_ref, kept_ref, mark_ref, first_ref, sems):
    rows, width = k_ref.shape[0], k_ref.shape[1] // 2
    copies = [pltpu.make_async_copy(position_ref, first_ref, sems.at[4])]
    for n, (ref, core) in enumerate(((sent_ref, 1 - my_core()), (kept_ref, my_core()))):
        at = pl.ds(pl.multiple_of(core * width, width), width)
        for m, source in enumerate((k_ref, v_ref)):
            to = ref.at[pl.ds(0, rows), pl.ds(m * width, width)]
            copies.append(pltpu.make_async_copy(source.at[:, at], to, sems.at[2 * n + m]))
    for copy in copies:
        copy.start()
    copies[0].wait()
    c = lax.div(first_ref[0], jnp.int32(chunk)).astype(jnp.float32)
    mark_ref[...] = jnp.full(mark_ref.shape, c, jnp.float32).astype(jnp.bfloat16)
    sent_ref[rows:] = jnp.full((HEADER, 2 * width), c, jnp.float32).astype(jnp.bfloat16)
    for copy in copies[1:]:
        copy.wait()


def prepare(keys, values, positions):
    vmem = pl.BlockSpec(memory_space=pltpu.VMEM)
    hbm = pl.BlockSpec(memory_space=pltpu.HBM)
    rows, width = keys.shape
    operands = [pltpu.with_memory_space_constraint(x, pltpu.HBM) for x in (keys, values, positions)]
    return pl.pallas_call(
        functools.partial(prepare_kernel, rows // 2),
        out_shape=[
            jax.ShapeDtypeStruct((rows + HEADER, width), jnp.bfloat16),
            jax.ShapeDtypeStruct((rows, width), jnp.bfloat16),
            jax.ShapeDtypeStruct((HEADER, width // 2), jnp.bfloat16),
        ],
        in_specs=[hbm, hbm, hbm],
        out_specs=[vmem, vmem, vmem],
        scratch_shapes=[
            pltpu.SMEM(positions.shape, jnp.int32),
            pltpu.SemaphoreType.DMA((5,)),
        ],
        compiler_params=pltpu.CompilerParams(vmem_limit_bytes=VMEM_LIMIT),
        name="prepare",
    )(*operands)


def after(value, *events):
    return lax.optimization_barrier((value, *events))[0]


def split_over_cores(count, queries, keys, values, positions, out_weight, fetch):
    chips, half = count // 2, count // 4
    rows, chunk = queries.shape[0], queries.shape[0] // 2
    heads = keys.shape[1] // HEAD_WIDTH // 2
    sibling = [(b, b ^ 1) for b in range(count)]
    clock, counter = ring_pairs(chips, 1), ring_pairs(chips, -1)
    width = heads * HEAD_WIDTH
    up = lambda x: lax.ppermute(x, "blk", clock)
    down = lambda x: lax.ppermute(x, "blk", counter)

    sent, x, mark = prepare(keys, values, positions)
    got = lax.ppermute(sent, "blk", sibling)
    y = jnp.concatenate(
        [got[:rows], jnp.concatenate([mark, got[rows:, :width]], axis=1)], axis=0
    )
    q_sent = lax.dynamic_slice(
        queries, (0, (1 - my_core()) * heads * GROUP), (rows, heads * GROUP)
    )
    q_got = lax.ppermute(q_sent, "blk", sibling)
    turned = turn(heads, chunk, (True, False), [queries, q_got])

    def call(pairs, state, own, last=False):
        each = range(len(pairs))
        plan = dict(
            heads=heads,
            chunk=chunk,
            owners=2,
            own=own,
            own_at=lambda i: i,
            last=last,
            members=[(2 * j + i, 0) for j in each for i in range(2)],
            headers=[(2 + 2 * j, rows, i * width) for j in each for i in range(2)],
            owner_headers=[(0, rows, 0), (0, rows, width)],
            fetch=fetch if last else None,
        )
        packets = [packet for pair in pairs for packet in pair]
        return attend(plan, turned, [y], packets, state, out_weight)

    state = None
    ups = downs = (x, y)
    arrived = [(x, y)]
    for r in range(1, half):
        (x_up, y_up), (x_down, y_down) = ups, downs
        if r == 2:
            x_up, x_down, turned = lax.optimization_barrier((x_up, x_down, turned))
        elif r > 2:
            x_up, x_down, *state = lax.optimization_barrier((x_up, x_down, *state))
        ups, downs = (up(x_up), up(y_up)), (down(x_down), down(y_down))
        if r >= 2:
            state = call(arrived, state, r == 2)
            arrived = []
        arrived += [ups, downs]
    x_up, y_down, *state = lax.optimization_barrier((ups[0], downs[1], *state))
    far = (up(x_up), down(y_down))
    state = call(arrived, state, False)
    own, theirs, held = call([far], state, False, True)
    return own, lax.ppermute(theirs, "blk", sibling), held


def one_head_a_device(count, queries, keys, values, positions):
    rows, chunk = queries.shape[0], queries.shape[0] // 2
    heads = keys.shape[1] // HEAD_WIDTH
    c = (positions[:1] // chunk).astype(jnp.bfloat16).reshape(1, 1)
    header = jnp.broadcast_to(c, (HEADER, 2 * keys.shape[1]))
    packet = jnp.concatenate([jnp.concatenate([keys, values], axis=1), header], axis=0)
    packets = lax.all_gather(packet, "blk", axis=0, tiled=True)
    size = rows + HEADER
    here = lax.axis_index("blk")
    order = lax.rem(here + jnp.arange(count), count)
    packets = packets.reshape(count, size, -1)[order].reshape(count * size, -1)
    plan = dict(
        heads=heads,
        chunk=chunk,
        owners=1,
        own=True,
        own_at=lambda i: 0,
        last=True,
        members=[(0, j * size) for j in range(count)],
        headers=[(0, j * size + rows, 0) for j in range(count)],
        owner_headers=[(0, rows, 0)],
    )
    turned = turn(heads, chunk, (False,), [queries])
    return attend(plan, turned, [], [packets], None)[0]


def shards(count, inner, queries, keys, values, positions, out_weight):
    heads = keys.shape[1] // HEAD_WIDTH
    if heads % 2:
        attended = one_head_a_device(count, queries, keys, values, positions)
        partial = jnp.dot(attended, out_weight, preferred_element_type=jnp.float32)
        return lax.psum_scatter(
            partial.astype(jnp.bfloat16), "inner", scatter_dimension=0, tiled=True
        )
    out_weight = pltpu.with_memory_space_constraint(out_weight, pltpu.HBM)
    shares = (5, 5, 6, 4)
    widths = [out_weight.shape[1] * share // sum(shares) for share in shares]
    cuts = [(sum(widths[:j]), columns) for j, columns in enumerate(widths)]
    own, other, held = split_over_cores(
        count, queries, keys, values, positions, out_weight, cuts[0]
    )
    received, kept, source = [], [], own
    for j in range(len(cuts)):
        if j > 0:
            source = after(own, sent, *received[: j - 1][-1:])
        following = cuts[j + 1] if j + 1 < len(cuts) else None
        sent, keep, *rest = project(source, other, held, out_weight, following)
        if rest:
            held = rest[0]
        received.append(lax.ppermute(sent, "inner", [(0, 1), (1, 0)]))
        kept.append(keep)
    mine, theirs = jnp.concatenate(kept, axis=1), jnp.concatenate(received, axis=1)
    return (mine.astype(jnp.float32) + theirs.astype(jnp.float32)).astype(jnp.bfloat16)


def solution(mesh):
    placed = (P("blk", "inner"), P("blk", "inner"), P("blk", "inner"), P("blk"), P("inner", None))
    return jax.shard_map(
        functools.partial(shards, mesh.shape["blk"], mesh.shape["inner"]),
        mesh=mesh,
        in_specs=placed,
        out_specs=P(("blk", "inner"), None),
        check_vma=False,
    )
```

```python
import functools
import math

import jax
import jax.numpy as jnp
from jax import lax
from jax.experimental import pallas as pl
from jax.experimental.pallas import tpu as pltpu
from jax.sharding import PartitionSpec as P

HEAD_WIDTH = 128
QUERY_PER_KEY = 5
GROUP = QUERY_PER_KEY * HEAD_WIDTH
EXP2_SCALE = math.log2(math.e) / math.sqrt(HEAD_WIDTH)
MASKED = -1e30
VMEM_LIMIT = 16 * 1024 * 1024
HEADER = 16
PIECES = 5


def ring_of_chips(chips):
    half = chips // 2
    if chips == 8:
        return [2 * z for z in range(half)] + [2 * z + 1 for z in reversed(range(half))]
    return list(range(half)) + list(reversed(range(half, chips)))


def ring_pairs(chips, step):
    ring = ring_of_chips(chips)
    return [
        (2 * ring[i] + core, 2 * ring[(i + step) % chips] + core)
        for i in range(chips)
        for core in range(2)
    ]


def my_core():
    return lax.rem(lax.axis_index("blk"), 2).astype(jnp.int32)


def product(a, b):
    return jnp.dot(a, b, preferred_element_type=jnp.float32)


def weigh(scores, high):
    return jnp.exp2((scores - high) * EXP2_SCALE).astype(jnp.bfloat16)


def turned_values(blocks):
    v = jnp.concatenate(blocks, axis=0)
    return jnp.concatenate([jnp.transpose(v), jnp.ones((HEADER, v.shape[0]), v.dtype)], axis=0)


def fetch_columns(w_ref, first, held_ref, sems, sem):
    depth, width = held_ref.shape[0] // PIECES, held_ref.shape[1]
    copies = []
    for p in range(PIECES):
        at = pl.ds(p * depth, depth)
        copies.append(
            pltpu.make_async_copy(
                w_ref.at[at, pl.ds(first, width)], held_ref.at[at], sems.at[sem + p]
            )
        )
        copies[-1].start()
    return copies


def attend_kernel(plan, *refs):
    heads, chunk, owners = plan["heads"], plan["chunk"], plan["owners"]
    refs = list(refs)
    q_ref = refs.pop(0)
    mark_refs = [refs.pop(0) for _ in range(plan["marks"])]
    packets = [refs.pop(0) for _ in range(plan["packets"])]
    if plan["carried"]:
        in_high, in_sums = refs.pop(0), refs.pop(0)
    fetch = plan["fetch"]
    if fetch:
        w_ref = refs.pop(0)
    if plan["last"]:
        out_refs = [refs.pop(0) for _ in range(owners)]
    copies = []
    if fetch:
        sems = refs.pop()
        for n, (first, _) in enumerate(fetch):
            held_ref = refs.pop(0 if plan["last"] else 2)
            copies += fetch_columns(w_ref, first, held_ref, sems, n * PIECES)
    high_ref, sums_ref = refs

    sources = mark_refs + packets
    numbers = [
        jnp.max(
            sources[packet][row : row + HEADER, column : column + HEAD_WIDTH].astype(jnp.float32)
        ).astype(jnp.int32)
        for packet, row, column in plan["owner_headers"] + plan["headers"]
    ]
    owner_c, member_c = numbers[:owners], numbers[owners:]

    def rows_of(j, half, column):
        packet, row = plan["members"][j]
        at = row + half * chunk
        at = at if isinstance(half, int) else pl.multiple_of(at, HEADER)
        return packets[packet][pl.ds(at, chunk), column : column + HEAD_WIDTH]

    def state_at(i, half, h):
        return (2 * i + half) * heads + h

    rows = QUERY_PER_KEY * chunk
    causal = lax.broadcasted_iota(jnp.int32, (chunk, rows), 0) <= lax.rem(
        lax.broadcasted_iota(jnp.int32, (chunk, rows), 1), chunk
    )
    count = len(plan["members"])
    for first in range(0, count, 6):
        group = range(first, min(first + 6, count))
        for h in range(heads):
            k_at, v_at = h * HEAD_WIDTH, (heads + h) * HEAD_WIDTH
            early_keys = jnp.concatenate([rows_of(j, 0, k_at) for j in group], axis=0)
            early_values = turned_values([rows_of(j, 0, v_at) for j in group])
            for i in range(owners):
                late_at, early_at = state_at(i, 1, h), state_at(i, 0, h)
                carried = None
                if first > 0:
                    carried = [(ref[early_at], ref[late_at]) for ref in (high_ref, sums_ref)]
                elif plan["carried"]:
                    carried = [(ref[early_at], ref[late_at]) for ref in (in_high, in_sums)]

                pairs = []
                for j in group:
                    if plan["own"] and j == plan["own_at"](i):
                        pairs += [(j, 0, causal), (j, 1, causal)]
                    else:
                        pairs.append((j, (member_c[j] > owner_c[i]).astype(jnp.int32), None))
                base = product(early_keys, q_ref[late_at])
                scores = []
                for j, half, mask in pairs:
                    s = product(rows_of(j, half, k_at), q_ref[state_at(i, half, h)])
                    scores.append(s if mask is None else jnp.where(mask, s, MASKED))
                tops = [jnp.max(s, axis=0, keepdims=True) for s in scores]
                highs = []
                for side in range(2):
                    some = [jnp.where(half == side, top, MASKED) for (_, half, _), top in zip(pairs, tops)]
                    if side == 1:
                        some.append(jnp.max(base, axis=0, keepdims=True))
                    if carried is not None:
                        some.append(carried[0][side])
                    highs.append(functools.reduce(jnp.maximum, some))
                weights = [
                    weigh(s, jnp.where(half == 1, highs[1], highs[0]))
                    for (_, half, _), s in zip(pairs, scores)
                ]
                values = turned_values([rows_of(j, half, v_at) for j, half, _ in pairs])
                zero = jnp.zeros_like(weights[0])
                for side, at in ((0, early_at), (1, late_at)):
                    chosen = [
                        jnp.where(half == side, w, zero) for (_, half, _), w in zip(pairs, weights)
                    ]
                    sums = product(values, jnp.concatenate(chosen, axis=0))
                    if side == 1:
                        sums = sums + product(early_values, weigh(base, highs[1]))
                    if carried is not None:
                        shrink = jnp.exp2((carried[0][side] - highs[side]) * EXP2_SCALE)
                        sums = sums + carried[1][side] * shrink
                    high_ref[at] = highs[side]
                    sums_ref[at] = sums
                    if plan["last"] and first + 6 >= count:
                        mixed = sums[:HEAD_WIDTH] * (1.0 / sums[HEAD_WIDTH : HEAD_WIDTH + 1])
                        mixed = jnp.transpose(mixed.astype(out_refs[i].dtype))
                        for g in range(QUERY_PER_KEY):
                            out_refs[i][
                                side * chunk : (side + 1) * chunk,
                                h * GROUP + g * HEAD_WIDTH : h * GROUP + (g + 1) * HEAD_WIDTH,
                            ] = mixed[g * chunk : (g + 1) * chunk]
    for copy in copies:
        copy.wait()


def attend(plan, turned, marks, packets, state, out_weight=None):
    heads, chunk, owners = plan["heads"], plan["chunk"], plan["owners"]
    count = len(plan["members"])
    plan = dict(plan, marks=len(marks), packets=len(packets), carried=state is not None)
    fetch = plan.setdefault("fetch", None)
    rows = QUERY_PER_KEY * chunk
    slots = owners * 2 * heads
    vmem = pl.BlockSpec(memory_space=pltpu.VMEM)
    kept = [(slots, 1, rows), (slots, HEAD_WIDTH + HEADER, rows)]
    if plan["last"]:
        out_shape = [jax.ShapeDtypeStruct((2 * chunk, heads * GROUP), jnp.bfloat16)] * owners
    else:
        out_shape = [jax.ShapeDtypeStruct(shape, jnp.float32) for shape in kept]
    operands = 1 + len(marks) + len(packets) + (0 if state is None else 2)
    in_specs = [vmem] * operands
    scratch = [pltpu.VMEM(shape, jnp.float32) for shape in kept] if plan["last"] else []
    if fetch:
        in_specs.append(pl.BlockSpec(memory_space=pltpu.HBM))
        for _, columns in fetch:
            out_shape.append(jax.ShapeDtypeStruct((out_weight.shape[0], columns), out_weight.dtype))
        scratch.append(pltpu.SemaphoreType.DMA((PIECES * len(fetch),)))
    flops = 4 * owners * heads * rows * HEAD_WIDTH * count * chunk * 2
    return pl.pallas_call(
        functools.partial(attend_kernel, plan),
        out_shape=out_shape,
        in_specs=in_specs,
        out_specs=[vmem] * len(out_shape),
        scratch_shapes=scratch,
        cost_estimate=pl.CostEstimate(
            flops=flops, bytes_accessed=4 << 20, transcendentals=flops // 512
        ),
        compiler_params=pltpu.CompilerParams(vmem_limit_bytes=VMEM_LIMIT),
        name="attend",
    )(turned, *marks, *packets, *(state or ()), *([out_weight] if fetch else []))


def turn_kernel(heads, chunk, whole_rows, *refs):
    q_refs, turned_ref = refs[:-1], refs[-1]
    for i, q_ref in enumerate(q_refs):
        base = my_core() * (heads * GROUP) if whole_rows[i] else 0
        for half in range(2):
            for h in range(heads):
                columns = [
                    pl.ds(pl.multiple_of(base + h * GROUP + g * HEAD_WIDTH, HEAD_WIDTH), HEAD_WIDTH)
                    for g in range(QUERY_PER_KEY)
                ]
                q = jnp.concatenate(
                    [q_ref[half * chunk : (half + 1) * chunk, at] for at in columns], axis=0
                )
                turned_ref[(2 * i + half) * heads + h] = jnp.transpose(q)


def turn(heads, chunk, whole_rows, queries):
    vmem = pl.BlockSpec(memory_space=pltpu.VMEM)
    owners = len(queries)
    shape = (2 * owners * heads, HEAD_WIDTH, QUERY_PER_KEY * chunk)
    return pl.pallas_call(
        functools.partial(turn_kernel, heads, chunk, whole_rows),
        out_shape=jax.ShapeDtypeStruct(shape, jnp.bfloat16),
        in_specs=[vmem] * owners,
        out_specs=vmem,
        cost_estimate=pl.CostEstimate(flops=1 << 20, bytes_accessed=4 << 20, transcendentals=0),
        compiler_params=pltpu.CompilerParams(vmem_limit_bytes=VMEM_LIMIT),
        name="turn",
    )(*queries)


def project_kernel(following, own_ref, other_ref, held_ref, *refs):
    if following:
        w_ref, sent_ref, kept_ref, next_ref, rows_ref, sems = refs
        copies = fetch_columns(w_ref, following[0], next_ref, sems, 0)
    else:
        sent_ref, kept_ref, rows_ref = refs
    chunk, part = sent_ref.shape[0], own_ref.shape[1]
    mine = lax.axis_index("inner").astype(jnp.int32)
    left = my_core() == 0
    for place, half in enumerate((1 - mine, mine)):
        at = pl.ds(pl.multiple_of(half * chunk, chunk), chunk)
        own, other = own_ref[at], other_ref[at]
        to = slice(place * chunk, (place + 1) * chunk)
        rows_ref[to, :part] = jnp.where(left, own, other)
        rows_ref[to, part:] = jnp.where(left, other, own)
    both = product(rows_ref[...], held_ref[...]).astype(sent_ref.dtype)
    sent_ref[...] = both[:chunk]
    kept_ref[...] = both[chunk:]
    if following:
        for copy in copies:
            copy.wait()


def project(own, other, held, out_weight, following):
    rows, (depth, width) = own.shape[0], held.shape
    vmem = pl.BlockSpec(memory_space=pltpu.VMEM)
    out_shape = [jax.ShapeDtypeStruct((rows // 2, width), jnp.bfloat16)] * 2
    in_specs, operands = [vmem] * 3, [own, other, held]
    scratch = [pltpu.VMEM((rows, depth), jnp.bfloat16)]
    if following:
        out_shape.append(jax.ShapeDtypeStruct((depth, following[1]), held.dtype))
        in_specs.append(pl.BlockSpec(memory_space=pltpu.HBM))
        operands.append(out_weight)
        scratch.append(pltpu.SemaphoreType.DMA((PIECES,)))
    return pl.pallas_call(
        functools.partial(project_kernel, following),
        out_shape=out_shape,
        in_specs=in_specs,
        out_specs=[vmem] * len(out_shape),
        scratch_shapes=scratch,
        cost_estimate=pl.CostEstimate(
            flops=2 * rows * depth * width, bytes_accessed=2 * depth * width, transcendentals=0
        ),
        compiler_params=pltpu.CompilerParams(vmem_limit_bytes=VMEM_LIMIT),
        name="project",
    )(*operands)


def prepare_kernel(chunk, k_ref, v_ref, position_ref, sent_ref, kept_ref, mark_ref, first_ref, sems):
    rows, width = k_ref.shape[0], k_ref.shape[1] // 2
    copies = [pltpu.make_async_copy(position_ref, first_ref, sems.at[4])]
    for n, (ref, core) in enumerate(((sent_ref, 1 - my_core()), (kept_ref, my_core()))):
        at = pl.ds(pl.multiple_of(core * width, width), width)
        for m, source in enumerate((k_ref, v_ref)):
            to = ref.at[pl.ds(0, rows), pl.ds(m * width, width)]
            copies.append(pltpu.make_async_copy(source.at[:, at], to, sems.at[2 * n + m]))
    for copy in copies:
        copy.start()
    copies[0].wait()
    c = lax.div(first_ref[0], jnp.int32(chunk)).astype(jnp.float32)
    mark_ref[...] = jnp.full(mark_ref.shape, c, jnp.float32).astype(jnp.bfloat16)
    sent_ref[rows:] = jnp.full((HEADER, 2 * width), c, jnp.float32).astype(jnp.bfloat16)
    for copy in copies[1:]:
        copy.wait()


def prepare(keys, values, positions):
    vmem = pl.BlockSpec(memory_space=pltpu.VMEM)
    hbm = pl.BlockSpec(memory_space=pltpu.HBM)
    rows, width = keys.shape
    operands = [pltpu.with_memory_space_constraint(x, pltpu.HBM) for x in (keys, values, positions)]
    return pl.pallas_call(
        functools.partial(prepare_kernel, rows // 2),
        out_shape=[
            jax.ShapeDtypeStruct((rows + HEADER, width), jnp.bfloat16),
            jax.ShapeDtypeStruct((rows, width), jnp.bfloat16),
            jax.ShapeDtypeStruct((HEADER, width // 2), jnp.bfloat16),
        ],
        in_specs=[hbm, hbm, hbm],
        out_specs=[vmem, vmem, vmem],
        scratch_shapes=[
            pltpu.SMEM(positions.shape, jnp.int32),
            pltpu.SemaphoreType.DMA((5,)),
        ],
        compiler_params=pltpu.CompilerParams(vmem_limit_bytes=VMEM_LIMIT),
        name="prepare",
    )(*operands)


def after(value, *events):
    return lax.optimization_barrier((value, *events))[0]


def split_over_cores(count, queries, keys, values, positions, out_weight, fetch):
    chips, half = count // 2, count // 4
    rows, chunk = queries.shape[0], queries.shape[0] // 2
    heads = keys.shape[1] // HEAD_WIDTH // 2
    sibling = [(b, b ^ 1) for b in range(count)]
    clock, counter = ring_pairs(chips, 1), ring_pairs(chips, -1)
    width = heads * HEAD_WIDTH
    up = lambda x: lax.ppermute(x, "blk", clock)
    down = lambda x: lax.ppermute(x, "blk", counter)

    sent, x, mark = prepare(keys, values, positions)
    got = lax.ppermute(sent, "blk", sibling)
    y = jnp.concatenate(
        [got[:rows], jnp.concatenate([mark, got[rows:, :width]], axis=1)], axis=0
    )
    q_sent = lax.dynamic_slice(
        queries, (0, (1 - my_core()) * heads * GROUP), (rows, heads * GROUP)
    )
    q_got = lax.ppermute(q_sent, "blk", sibling)
    turned = turn(heads, chunk, (True, False), [queries, q_got])

    def call(pairs, state, own=False, last=False, fetch=None):
        each = range(len(pairs))
        plan = dict(
            heads=heads,
            chunk=chunk,
            owners=2,
            own=own,
            own_at=lambda i: i,
            last=last,
            members=[(2 * j + i, 0) for j in each for i in range(2)],
            headers=[(2 + 2 * j, rows, i * width) for j in each for i in range(2)],
            owner_headers=[(0, rows, 0), (0, rows, width)],
            fetch=fetch,
        )
        packets = [packet for pair in pairs for packet in pair]
        return attend(plan, turned, [y], packets, state, out_weight)

    ups = downs = (x, y)
    for r in range(1, half):
        (x_up, y_up), (x_down, y_down) = ups, downs
        if r > 1:
            y_up, y_down, *state = lax.optimization_barrier((y_up, y_down, *state))
        ups, downs = (up(x_up), up(y_up)), (down(x_down), down(y_down))
        if r == 1:
            *state, first, second = call([(x, y)], None, own=True, fetch=fetch)
        else:
            state = call(arrived, state)
        arrived = [ups, downs]
    x_up, y_down, *state = lax.optimization_barrier((ups[0], downs[1], *state))
    far = (up(x_up), down(y_down))
    state = call(arrived, state)
    own, theirs = call([far], state, last=True)
    return own, lax.ppermute(theirs, "blk", sibling), [first, second]


def one_head_a_device(count, queries, keys, values, positions):
    rows, chunk = queries.shape[0], queries.shape[0] // 2
    heads = keys.shape[1] // HEAD_WIDTH
    c = (positions[:1] // chunk).astype(jnp.bfloat16).reshape(1, 1)
    header = jnp.broadcast_to(c, (HEADER, 2 * keys.shape[1]))
    packet = jnp.concatenate([jnp.concatenate([keys, values], axis=1), header], axis=0)
    packets = lax.all_gather(packet, "blk", axis=0, tiled=True)
    size = rows + HEADER
    here = lax.axis_index("blk")
    order = lax.rem(here + jnp.arange(count), count)
    packets = packets.reshape(count, size, -1)[order].reshape(count * size, -1)
    plan = dict(
        heads=heads,
        chunk=chunk,
        owners=1,
        own=True,
        own_at=lambda i: 0,
        last=True,
        members=[(0, j * size) for j in range(count)],
        headers=[(0, j * size + rows, 0) for j in range(count)],
        owner_headers=[(0, rows, 0)],
    )
    turned = turn(heads, chunk, (False,), [queries])
    return attend(plan, turned, [], [packets], None)[0]


def shards(count, inner, queries, keys, values, positions, out_weight):
    heads = keys.shape[1] // HEAD_WIDTH
    if heads % 2:
        attended = one_head_a_device(count, queries, keys, values, positions)
        partial = jnp.dot(attended, out_weight, preferred_element_type=jnp.float32)
        return lax.psum_scatter(
            partial.astype(jnp.bfloat16), "inner", scatter_dimension=0, tiled=True
        )
    out_weight = pltpu.with_memory_space_constraint(out_weight, pltpu.HBM)
    shares = (5, 5, 6, 4)
    widths = [out_weight.shape[1] * share // sum(shares) for share in shares]
    cuts = [(sum(widths[:j]), columns) for j, columns in enumerate(widths)]
    own, other, held = split_over_cores(
        count, queries, keys, values, positions, out_weight, cuts[:2]
    )
    received, kept, source = [], [], own
    for j in range(len(cuts)):
        if j > 0:
            source = after(own, sent, *received[: j - 1][-1:])
        following = cuts[j + 1] if 0 < j < len(cuts) - 1 else None
        sent, keep, *rest = project(source, other, held[j], out_weight, following)
        held += rest
        received.append(lax.ppermute(sent, "inner", [(0, 1), (1, 0)]))
        kept.append(keep)
    mine, theirs = jnp.concatenate(kept, axis=1), jnp.concatenate(received, axis=1)
    return (mine.astype(jnp.float32) + theirs.astype(jnp.float32)).astype(jnp.bfloat16)


def solution(mesh):
    placed = (P("blk", "inner"), P("blk", "inner"), P("blk", "inner"), P("blk"), P("inner", None))
    return jax.shard_map(
        functools.partial(shards, mesh.shape["blk"], mesh.shape["inner"]),
        mesh=mesh,
        in_specs=placed,
        out_specs=P(("blk", "inner"), None),
        check_vma=False,
    )
```

```python
import functools
import math

import jax
import jax.numpy as jnp
from jax import lax
from jax.experimental import pallas as pl
from jax.experimental.pallas import tpu as pltpu
from jax.sharding import PartitionSpec as P

HEAD_WIDTH = 128
QUERY_PER_KEY = 5
GROUP = QUERY_PER_KEY * HEAD_WIDTH
EXP2_SCALE = math.log2(math.e) / math.sqrt(HEAD_WIDTH)
MASKED = -1e30
VMEM_LIMIT = 16 * 1024 * 1024
HEADER = 16
PIECES = 5


def ring_of_chips(chips):
    half = chips // 2
    if chips == 8:
        return [2 * z for z in range(half)] + [2 * z + 1 for z in reversed(range(half))]
    return list(range(half)) + list(reversed(range(half, chips)))


def ring_pairs(chips, step):
    ring = ring_of_chips(chips)
    return [
        (2 * ring[i] + core, 2 * ring[(i + step) % chips] + core)
        for i in range(chips)
        for core in range(2)
    ]


def my_core():
    return lax.rem(lax.axis_index("blk"), 2).astype(jnp.int32)


def product(a, b):
    return jnp.dot(a, b, preferred_element_type=jnp.float32)


def weigh(scores, high):
    return jnp.exp2((scores - high) * EXP2_SCALE).astype(jnp.bfloat16)


def turned_values(blocks):
    v = jnp.concatenate(blocks, axis=0)
    return jnp.concatenate([jnp.transpose(v), jnp.ones((HEADER, v.shape[0]), v.dtype)], axis=0)


def fetch_columns(w_ref, first, held_ref, sems, sem):
    depth, width = held_ref.shape[0] // PIECES, held_ref.shape[1]
    copies = []
    for p in range(PIECES):
        at = pl.ds(p * depth, depth)
        copies.append(
            pltpu.make_async_copy(
                w_ref.at[at, pl.ds(first, width)], held_ref.at[at], sems.at[sem + p]
            )
        )
        copies[-1].start()
    return copies


def attend_kernel(plan, *refs):
    heads, chunk, owners = plan["heads"], plan["chunk"], plan["owners"]
    refs = list(refs)
    q_ref = refs.pop(0)
    mark_refs = [refs.pop(0) for _ in range(plan["marks"])]
    packets = [refs.pop(0) for _ in range(plan["packets"])]
    if plan["carried"]:
        in_high, in_sums = refs.pop(0), refs.pop(0)
    fetch = plan["fetch"]
    if fetch:
        w_ref = refs.pop(0)
    if plan["last"]:
        out_refs = [refs.pop(0) for _ in range(owners)]
    copies = []
    if fetch:
        sems = refs.pop()
        for n, (first, _) in enumerate(fetch):
            held_ref = refs.pop(0 if plan["last"] else 2)
            copies += fetch_columns(w_ref, first, held_ref, sems, n * PIECES)
    high_ref, sums_ref = refs

    sources = mark_refs + packets
    numbers = [
        jnp.max(
            sources[packet][row : row + HEADER, column : column + HEAD_WIDTH].astype(jnp.float32)
        ).astype(jnp.int32)
        for packet, row, column in plan["owner_headers"] + plan["headers"]
    ]
    owner_c, member_c = numbers[:owners], numbers[owners:]

    def rows_of(j, half, column):
        packet, row = plan["members"][j]
        at = row + half * chunk
        at = at if isinstance(half, int) else pl.multiple_of(at, HEADER)
        return packets[packet][pl.ds(at, chunk), pl.ds(column, HEAD_WIDTH)]

    def state_at(i, half, h):
        return (2 * i + half) * heads + h

    rows = QUERY_PER_KEY * chunk
    causal = lax.broadcasted_iota(jnp.int32, (chunk, rows), 0) <= lax.rem(
        lax.broadcasted_iota(jnp.int32, (chunk, rows), 1), chunk
    )
    count = len(plan["members"])
    for first in range(0, count, 6):
        group = range(first, min(first + 6, count))

        def one_head(h, carry, first=first, group=group):
            k_at = pl.multiple_of(h * HEAD_WIDTH, HEAD_WIDTH)
            v_at = pl.multiple_of((heads + h) * HEAD_WIDTH, HEAD_WIDTH)
            early_keys = jnp.concatenate([rows_of(j, 0, k_at) for j in group], axis=0)
            early_values = turned_values([rows_of(j, 0, v_at) for j in group])
            for i in range(owners):
                late_at, early_at = state_at(i, 1, h), state_at(i, 0, h)
                carried = None
                if first > 0:
                    carried = [(ref[early_at], ref[late_at]) for ref in (high_ref, sums_ref)]
                elif plan["carried"]:
                    carried = [(ref[early_at], ref[late_at]) for ref in (in_high, in_sums)]

                pairs = []
                for j in group:
                    if plan["own"] and j == plan["own_at"](i):
                        pairs += [(j, 0, causal), (j, 1, causal)]
                    else:
                        pairs.append((j, (member_c[j] > owner_c[i]).astype(jnp.int32), None))
                base = product(early_keys, q_ref[late_at])
                scores = []
                for j, half, mask in pairs:
                    s = product(rows_of(j, half, k_at), q_ref[state_at(i, half, h)])
                    scores.append(s if mask is None else jnp.where(mask, s, MASKED))
                tops = [jnp.max(s, axis=0, keepdims=True) for s in scores]
                highs = []
                for side in range(2):
                    some = [jnp.where(half == side, top, MASKED) for (_, half, _), top in zip(pairs, tops)]
                    if side == 1:
                        some.append(jnp.max(base, axis=0, keepdims=True))
                    if carried is not None:
                        some.append(carried[0][side])
                    highs.append(functools.reduce(jnp.maximum, some))
                weights = [
                    weigh(s, jnp.where(half == 1, highs[1], highs[0]))
                    for (_, half, _), s in zip(pairs, scores)
                ]
                values = turned_values([rows_of(j, half, v_at) for j, half, _ in pairs])
                zero = jnp.zeros_like(weights[0])
                for side, at in ((0, early_at), (1, late_at)):
                    chosen = [
                        jnp.where(half == side, w, zero) for (_, half, _), w in zip(pairs, weights)
                    ]
                    sums = product(values, jnp.concatenate(chosen, axis=0))
                    if side == 1:
                        sums = sums + product(early_values, weigh(base, highs[1]))
                    if carried is not None:
                        shrink = jnp.exp2((carried[0][side] - highs[side]) * EXP2_SCALE)
                        sums = sums + carried[1][side] * shrink
                    high_ref[at] = highs[side]
                    sums_ref[at] = sums
                    if plan["last"] and first + 6 >= count:
                        mixed = sums[:HEAD_WIDTH] * (1.0 / sums[HEAD_WIDTH : HEAD_WIDTH + 1])
                        mixed = jnp.transpose(mixed.astype(out_refs[i].dtype))
                        for g in range(QUERY_PER_KEY):
                            to = pl.multiple_of(h * GROUP + g * HEAD_WIDTH, HEAD_WIDTH)
                            out_refs[i][
                                side * chunk : (side + 1) * chunk, pl.ds(to, HEAD_WIDTH)
                            ] = mixed[g * chunk : (g + 1) * chunk]
            return carry

        lax.fori_loop(0, heads, one_head, 0)
    for copy in copies:
        copy.wait()


def attend(plan, turned, marks, packets, state, out_weight=None):
    heads, chunk, owners = plan["heads"], plan["chunk"], plan["owners"]
    count = len(plan["members"])
    plan = dict(plan, marks=len(marks), packets=len(packets), carried=state is not None)
    fetch = plan.setdefault("fetch", None)
    rows = QUERY_PER_KEY * chunk
    slots = owners * 2 * heads
    vmem = pl.BlockSpec(memory_space=pltpu.VMEM)
    kept = [(slots, 1, rows), (slots, HEAD_WIDTH + HEADER, rows)]
    if plan["last"]:
        out_shape = [jax.ShapeDtypeStruct((2 * chunk, heads * GROUP), jnp.bfloat16)] * owners
    else:
        out_shape = [jax.ShapeDtypeStruct(shape, jnp.float32) for shape in kept]
    operands = 1 + len(marks) + len(packets) + (0 if state is None else 2)
    in_specs = [vmem] * operands
    scratch = [pltpu.VMEM(shape, jnp.float32) for shape in kept] if plan["last"] else []
    if fetch:
        in_specs.append(pl.BlockSpec(memory_space=pltpu.HBM))
        for _, columns in fetch:
            out_shape.append(jax.ShapeDtypeStruct((out_weight.shape[0], columns), out_weight.dtype))
        scratch.append(pltpu.SemaphoreType.DMA((PIECES * len(fetch),)))
    flops = 4 * owners * heads * rows * HEAD_WIDTH * count * chunk * 2
    return pl.pallas_call(
        functools.partial(attend_kernel, plan),
        out_shape=out_shape,
        in_specs=in_specs,
        out_specs=[vmem] * len(out_shape),
        scratch_shapes=scratch,
        cost_estimate=pl.CostEstimate(
            flops=flops, bytes_accessed=4 << 20, transcendentals=flops // 512
        ),
        compiler_params=pltpu.CompilerParams(vmem_limit_bytes=VMEM_LIMIT),
        name="attend",
    )(turned, *marks, *packets, *(state or ()), *([out_weight] if fetch else []))


def turn_kernel(heads, chunk, whole_rows, *refs):
    q_refs, turned_ref = refs[:-1], refs[-1]
    for i, q_ref in enumerate(q_refs):
        base = my_core() * (heads * GROUP) if whole_rows[i] else 0
        for half in range(2):
            for h in range(heads):
                columns = [
                    pl.ds(pl.multiple_of(base + h * GROUP + g * HEAD_WIDTH, HEAD_WIDTH), HEAD_WIDTH)
                    for g in range(QUERY_PER_KEY)
                ]
                q = jnp.concatenate(
                    [q_ref[half * chunk : (half + 1) * chunk, at] for at in columns], axis=0
                )
                turned_ref[(2 * i + half) * heads + h] = jnp.transpose(q)


def turn(heads, chunk, whole_rows, queries):
    vmem = pl.BlockSpec(memory_space=pltpu.VMEM)
    owners = len(queries)
    shape = (2 * owners * heads, HEAD_WIDTH, QUERY_PER_KEY * chunk)
    return pl.pallas_call(
        functools.partial(turn_kernel, heads, chunk, whole_rows),
        out_shape=jax.ShapeDtypeStruct(shape, jnp.bfloat16),
        in_specs=[vmem] * owners,
        out_specs=vmem,
        cost_estimate=pl.CostEstimate(flops=1 << 20, bytes_accessed=4 << 20, transcendentals=0),
        compiler_params=pltpu.CompilerParams(vmem_limit_bytes=VMEM_LIMIT),
        name="turn",
    )(*queries)


def project_kernel(columns, bring, own_ref, other_ref, *refs):
    refs = list(refs)
    held_ref = None if bring and bring[0] == columns else refs.pop(0)
    if bring:
        w_ref = refs.pop(0)
    sent_ref, kept_ref = refs.pop(0), refs.pop(0)
    copies = []
    if bring:
        sems = refs.pop()
        rows_ref = refs.pop()
        for n, (first, _) in enumerate(bring):
            if n == 0 and held_ref is None:
                here_ref = refs.pop()
            else:
                here_ref = refs.pop(0)
            copies.append(fetch_columns(w_ref, first, here_ref, sems, n * PIECES))
            if n == 0 and held_ref is None:
                held_ref = here_ref
    else:
        rows_ref = refs.pop()
    chunk, part = sent_ref.shape[0], own_ref.shape[1]
    mine = lax.axis_index("inner").astype(jnp.int32)
    left = my_core() == 0
    for place, half in enumerate((1 - mine, mine)):
        at = pl.ds(pl.multiple_of(half * chunk, chunk), chunk)
        own, other = own_ref[at], other_ref[at]
        to = slice(place * chunk, (place + 1) * chunk)
        rows_ref[to, :part] = jnp.where(left, own, other)
        rows_ref[to, part:] = jnp.where(left, other, own)
    if bring and bring[0] == columns:
        depth = held_ref.shape[0] // PIECES
        total = None
        for p, copy in enumerate(copies.pop(0)):
            copy.wait()
            at = slice(p * depth, (p + 1) * depth)
            term = product(rows_ref[:, at], held_ref[at])
            total = term if total is None else total + term
    else:
        total = product(rows_ref[...], held_ref[...])
    both = total.astype(sent_ref.dtype)
    sent_ref[...] = both[:chunk]
    kept_ref[...] = both[chunk:]
    for group in copies:
        for copy in group:
            copy.wait()


def project(own, other, held, out_weight, columns, bring):
    rows, depth = own.shape[0], out_weight.shape[0]
    width = columns[1]
    vmem = pl.BlockSpec(memory_space=pltpu.VMEM)
    out_shape = [jax.ShapeDtypeStruct((rows // 2, width), jnp.bfloat16)] * 2
    operands, in_specs, scratch = [own, other], [vmem] * 2, []
    for there in bring:
        shape = (depth, there[1])
        if there == columns:
            scratch.append(pltpu.VMEM(shape, out_weight.dtype))
        else:
            out_shape.append(jax.ShapeDtypeStruct(shape, out_weight.dtype))
    if not scratch:
        operands.append(held)
        in_specs.append(vmem)
    scratch.append(pltpu.VMEM((rows, depth), jnp.bfloat16))
    if bring:
        operands.append(out_weight)
        in_specs.append(pl.BlockSpec(memory_space=pltpu.HBM))
        scratch.append(pltpu.SemaphoreType.DMA((PIECES * len(bring),)))
    return pl.pallas_call(
        functools.partial(project_kernel, columns, bring),
        out_shape=out_shape,
        in_specs=in_specs,
        out_specs=[vmem] * len(out_shape),
        scratch_shapes=scratch,
        cost_estimate=pl.CostEstimate(flops=1 << 10, bytes_accessed=1 << 10, transcendentals=0),
        compiler_params=pltpu.CompilerParams(vmem_limit_bytes=VMEM_LIMIT),
        name="project",
    )(*operands)


def prepare_kernel(chunk, k_ref, v_ref, position_ref, sent_ref, kept_ref, mark_ref, first_ref, sems):
    rows, width = k_ref.shape[0], k_ref.shape[1] // 2
    copies = [pltpu.make_async_copy(position_ref, first_ref, sems.at[4])]
    for n, (ref, core) in enumerate(((sent_ref, 1 - my_core()), (kept_ref, my_core()))):
        at = pl.ds(pl.multiple_of(core * width, width), width)
        for m, source in enumerate((k_ref, v_ref)):
            to = ref.at[pl.ds(0, rows), pl.ds(m * width, width)]
            copies.append(pltpu.make_async_copy(source.at[:, at], to, sems.at[2 * n + m]))
    for copy in copies:
        copy.start()
    copies[0].wait()
    c = lax.div(first_ref[0], jnp.int32(chunk)).astype(jnp.float32)
    mark_ref[...] = jnp.full(mark_ref.shape, c, jnp.float32).astype(jnp.bfloat16)
    sent_ref[rows:] = jnp.full((HEADER, 2 * width), c, jnp.float32).astype(jnp.bfloat16)
    for copy in copies[1:]:
        copy.wait()


def prepare(keys, values, positions):
    vmem = pl.BlockSpec(memory_space=pltpu.VMEM)
    hbm = pl.BlockSpec(memory_space=pltpu.HBM)
    rows, width = keys.shape
    operands = [pltpu.with_memory_space_constraint(x, pltpu.HBM) for x in (keys, values, positions)]
    return pl.pallas_call(
        functools.partial(prepare_kernel, rows // 2),
        out_shape=[
            jax.ShapeDtypeStruct((rows + HEADER, width), jnp.bfloat16),
            jax.ShapeDtypeStruct((rows, width), jnp.bfloat16),
            jax.ShapeDtypeStruct((HEADER, width // 2), jnp.bfloat16),
        ],
        in_specs=[hbm, hbm, hbm],
        out_specs=[vmem, vmem, vmem],
        scratch_shapes=[
            pltpu.SMEM(positions.shape, jnp.int32),
            pltpu.SemaphoreType.DMA((5,)),
        ],
        compiler_params=pltpu.CompilerParams(vmem_limit_bytes=VMEM_LIMIT),
        name="prepare",
    )(*operands)


def after(value, *events):
    return lax.optimization_barrier((value, *events))[0]


def split_over_cores(count, queries, keys, values, positions, out_weight, fetch):
    chips, half = count // 2, count // 4
    rows, chunk = queries.shape[0], queries.shape[0] // 2
    heads = keys.shape[1] // HEAD_WIDTH // 2
    sibling = [(b, b ^ 1) for b in range(count)]
    clock, counter = ring_pairs(chips, 1), ring_pairs(chips, -1)
    width = heads * HEAD_WIDTH
    up = lambda x: lax.ppermute(x, "blk", clock)
    down = lambda x: lax.ppermute(x, "blk", counter)

    sent, x, mark = prepare(keys, values, positions)
    got = lax.ppermute(sent, "blk", sibling)
    y = jnp.concatenate(
        [got[:rows], jnp.concatenate([mark, got[rows:, :width]], axis=1)], axis=0
    )
    q_sent = lax.dynamic_slice(
        queries, (0, (1 - my_core()) * heads * GROUP), (rows, heads * GROUP)
    )
    q_got = lax.ppermute(q_sent, "blk", sibling)
    turned = turn(heads, chunk, (True, False), [queries, q_got])

    def call(pairs, state, own=False, last=False, fetch=None):
        each = range(len(pairs))
        plan = dict(
            heads=heads,
            chunk=chunk,
            owners=2,
            own=own,
            own_at=lambda i: i,
            last=last,
            members=[(2 * j + i, 0) for j in each for i in range(2)],
            headers=[(2 + 2 * j, rows, i * width) for j in each for i in range(2)],
            owner_headers=[(0, rows, 0), (0, rows, width)],
            fetch=fetch,
        )
        packets = [packet for pair in pairs for packet in pair]
        return attend(plan, turned, [y], packets, state, out_weight)

    ups = downs = (x, y)
    for r in range(1, half):
        (x_up, y_up), (x_down, y_down) = ups, downs
        if r > 1:
            y_up, y_down, *state = lax.optimization_barrier((y_up, y_down, *state))
        ups, downs = (up(x_up), up(y_up)), (down(x_down), down(y_down))
        if r == 1:
            *state, held = call([(x, y)], None, own=True, fetch=fetch)
        else:
            state = call(arrived, state)
        arrived = [ups, downs]
    x_up, y_down, *state = lax.optimization_barrier((ups[0], downs[1], *state))
    far = (up(x_up), down(y_down))
    state = call(arrived, state)
    own, theirs = call([far], state, last=True)
    return own, lax.ppermute(theirs, "blk", sibling), held


def one_head_a_device(count, queries, keys, values, positions):
    rows, chunk = queries.shape[0], queries.shape[0] // 2
    heads = keys.shape[1] // HEAD_WIDTH
    c = (positions[:1] // chunk).astype(jnp.bfloat16).reshape(1, 1)
    header = jnp.broadcast_to(c, (HEADER, 2 * keys.shape[1]))
    packet = jnp.concatenate([jnp.concatenate([keys, values], axis=1), header], axis=0)
    packets = lax.all_gather(packet, "blk", axis=0, tiled=True)
    size = rows + HEADER
    here = lax.axis_index("blk")
    order = lax.rem(here + jnp.arange(count), count)
    packets = packets.reshape(count, size, -1)[order].reshape(count * size, -1)
    plan = dict(
        heads=heads,
        chunk=chunk,
        owners=1,
        own=True,
        own_at=lambda i: 0,
        last=True,
        members=[(0, j * size) for j in range(count)],
        headers=[(0, j * size + rows, 0) for j in range(count)],
        owner_headers=[(0, rows, 0)],
    )
    turned = turn(heads, chunk, (False,), [queries])
    return attend(plan, turned, [], [packets], None)[0]


def shards(count, inner, queries, keys, values, positions, out_weight):
    heads = keys.shape[1] // HEAD_WIDTH
    if heads % 2:
        attended = one_head_a_device(count, queries, keys, values, positions)
        partial = jnp.dot(attended, out_weight, preferred_element_type=jnp.float32)
        return lax.psum_scatter(
            partial.astype(jnp.bfloat16), "inner", scatter_dimension=0, tiled=True
        )
    out_weight = pltpu.with_memory_space_constraint(out_weight, pltpu.HBM)
    shares = (12, 11, 9, 8)
    widths = [out_weight.shape[1] * share // sum(shares) for share in shares]
    cuts = [(sum(widths[:j]), columns) for j, columns in enumerate(widths)]
    own, other, held = split_over_cores(
        count, queries, keys, values, positions, out_weight, cuts[:1]
    )
    bring = ((), (cuts[1], cuts[2]), (cuts[3],), ())
    received, kept = [], []
    for j in range(len(cuts)):
        source = own if j == 0 else after(own, sent)
        sent, keep, *rest = project(source, other, held, out_weight, cuts[j], bring[j])
        if rest:
            held = rest[0]
        received.append(lax.ppermute(sent, "inner", [(0, 1), (1, 0)]))
        kept.append(keep)
    mine, theirs = jnp.concatenate(kept, axis=1), jnp.concatenate(received, axis=1)
    return (mine.astype(jnp.float32) + theirs.astype(jnp.float32)).astype(jnp.bfloat16)


def solution(mesh):
    placed = (P("blk", "inner"), P("blk", "inner"), P("blk", "inner"), P("blk"), P("inner", None))
    return jax.shard_map(
        functools.partial(shards, mesh.shape["blk"], mesh.shape["inner"]),
        mesh=mesh,
        in_specs=placed,
        out_specs=P(("blk", "inner"), None),
        check_vma=False,
    )
```

```python
import functools
import math

import jax
import jax.numpy as jnp
from jax import lax
from jax.experimental import pallas as pl
from jax.experimental.pallas import tpu as pltpu
from jax.sharding import PartitionSpec as P

HEAD_WIDTH = 128
QUERY_PER_KEY = 5
GROUP = QUERY_PER_KEY * HEAD_WIDTH
EXP2_SCALE = math.log2(math.e) / math.sqrt(HEAD_WIDTH)
MASKED = -1e30
VMEM_LIMIT = 16 * 1024 * 1024
HEADER = 16
PIECES = 5


def ring_of_chips(chips):
    half = chips // 2
    if chips == 8:
        return [2 * z for z in range(half)] + [2 * z + 1 for z in reversed(range(half))]
    return list(range(half)) + list(reversed(range(half, chips)))


def ring_pairs(chips, step):
    ring = ring_of_chips(chips)
    return [
        (2 * ring[i] + core, 2 * ring[(i + step) % chips] + core)
        for i in range(chips)
        for core in range(2)
    ]


def my_core():
    return lax.rem(lax.axis_index("blk"), 2).astype(jnp.int32)


def product(a, b):
    return jnp.dot(a, b, preferred_element_type=jnp.float32)


def weigh(scores, high):
    return jnp.exp2((scores - high) * EXP2_SCALE).astype(jnp.bfloat16)


def turned_values(blocks):
    v = jnp.concatenate(blocks, axis=0)
    return jnp.concatenate([jnp.transpose(v), jnp.ones((HEADER, v.shape[0]), v.dtype)], axis=0)


def fetch_columns(w_ref, first, held_ref, sems, sem):
    depth, width = held_ref.shape[0] // PIECES, held_ref.shape[1]
    copies = []
    for p in range(PIECES):
        at = pl.ds(p * depth, depth)
        copies.append(
            pltpu.make_async_copy(
                w_ref.at[at, pl.ds(first, width)], held_ref.at[at], sems.at[sem + p]
            )
        )
        copies[-1].start()
    return copies


def attend_kernel(plan, *refs):
    heads, chunk, owners = plan["heads"], plan["chunk"], plan["owners"]
    refs = list(refs)
    q_ref = refs.pop(0)
    mark_refs = [refs.pop(0) for _ in range(plan["marks"])]
    packets = [refs.pop(0) for _ in range(plan["packets"])]
    if plan["carried"]:
        in_high, in_sums = refs.pop(0), refs.pop(0)
    fetch = plan["fetch"]
    if fetch:
        w_ref = refs.pop(0)
    if plan["last"]:
        out_refs = [refs.pop(0) for _ in range(owners)]
    copies = []
    if fetch:
        sems = refs.pop()
        for n, (first, _) in enumerate(fetch):
            held_ref = refs.pop(0 if plan["last"] else 2)
            copies += fetch_columns(w_ref, first, held_ref, sems, n * PIECES)
    high_ref, sums_ref = refs

    sources = mark_refs + packets
    numbers = [
        jnp.max(
            sources[packet][row : row + HEADER, column : column + HEAD_WIDTH].astype(jnp.float32)
        ).astype(jnp.int32)
        for packet, row, column in plan["owner_headers"] + plan["headers"]
    ]
    owner_c, member_c = numbers[:owners], numbers[owners:]

    def rows_of(j, half, column):
        packet, row = plan["members"][j]
        at = row + half * chunk
        at = at if isinstance(half, int) else pl.multiple_of(at, HEADER)
        return packets[packet][pl.ds(at, chunk), pl.ds(column, HEAD_WIDTH)]

    def state_at(i, half, h):
        return (2 * i + half) * heads + h

    rows = QUERY_PER_KEY * chunk
    causal = lax.broadcasted_iota(jnp.int32, (chunk, rows), 0) <= lax.rem(
        lax.broadcasted_iota(jnp.int32, (chunk, rows), 1), chunk
    )
    count = len(plan["members"])

    def one_chain(group, h, i, shared):
        first, done = group[0], group[-1] == count - 1
        k_at = pl.multiple_of(h * HEAD_WIDTH, HEAD_WIDTH)
        v_at = pl.multiple_of((heads + h) * HEAD_WIDTH, HEAD_WIDTH)
        late_at, early_at = state_at(i, 1, h), state_at(i, 0, h)
        if i == 0:
            shared["keys"] = jnp.concatenate([rows_of(j, 0, k_at) for j in group], axis=0)
            shared["values"] = turned_values([rows_of(j, 0, v_at) for j in group])
        carried = None
        if first > 0:
            carried = [(ref[early_at], ref[late_at]) for ref in (high_ref, sums_ref)]
        elif plan["carried"]:
            carried = [(ref[early_at], ref[late_at]) for ref in (in_high, in_sums)]
        pairs = []
        for j in group:
            if plan["own"] and j == plan["own_at"](i):
                pairs += [(j, 0, causal), (j, 1, causal)]
            else:
                pairs.append((j, (member_c[j] > owner_c[i]).astype(jnp.int32), None))
        base = product(shared["keys"], q_ref[late_at])
        scores = []
        for j, half, mask in pairs:
            s = product(rows_of(j, half, k_at), q_ref[state_at(i, half, h)])
            scores.append(s if mask is None else jnp.where(mask, s, MASKED))
        values = turned_values([rows_of(j, half, v_at) for j, half, _ in pairs])
        tops = [jnp.max(s, axis=0, keepdims=True) for s in scores]
        highs = []
        for side in range(2):
            some = [jnp.where(half == side, top, MASKED) for (_, half, _), top in zip(pairs, tops)]
            if side == 1:
                some.append(jnp.max(base, axis=0, keepdims=True))
            if carried is not None:
                some.append(carried[0][side])
            highs.append(functools.reduce(jnp.maximum, some))
        yield
        base_weights = weigh(base, highs[1])
        weights = [
            weigh(s, jnp.where(half == 1, highs[1], highs[0])) for (_, half, _), s in zip(pairs, scores)
        ]
        zero = jnp.zeros_like(weights[0])
        chosen = [
            jnp.concatenate(
                [jnp.where(half == side, w, zero) for (_, half, _), w in zip(pairs, weights)], axis=0
            )
            for side in range(2)
        ]
        yield
        for side, at in ((0, early_at), (1, late_at)):
            sums = product(values, chosen[side])
            if side == 1:
                sums = sums + product(shared["values"], base_weights)
            if carried is not None:
                shrink = jnp.exp2((carried[0][side] - highs[side]) * EXP2_SCALE)
                sums = sums + carried[1][side] * shrink
            if plan["last"] and done:
                mixed = sums[:HEAD_WIDTH] * (1.0 / sums[HEAD_WIDTH : HEAD_WIDTH + 1])
                mixed = jnp.transpose(mixed.astype(out_refs[i].dtype))
                for g in range(QUERY_PER_KEY):
                    to = pl.multiple_of(h * GROUP + g * HEAD_WIDTH, HEAD_WIDTH)
                    out_refs[i][side * chunk : (side + 1) * chunk, pl.ds(to, HEAD_WIDTH)] = mixed[
                        g * chunk : (g + 1) * chunk
                    ]
            else:
                high_ref[at] = highs[side]
                sums_ref[at] = sums
        yield

    def staggered(chains):
        for t in range(len(chains) + 2):
            for stage in (2, 1, 0):
                if 0 <= t - stage < len(chains):
                    next(chains[t - stage])

    for first in range(0, count, 6):
        group = range(first, min(first + 6, count))

        def run(heads_at_once, group=group):
            chains = []
            for h in heads_at_once:
                shared = {}
                chains += [one_chain(group, h, i, shared) for i in range(owners)]
            staggered(chains)

        if fetch:

            def one_head(h, carry):
                run([h])
                return carry

            lax.fori_loop(0, heads, one_head, 0)
        else:
            run(range(heads))
    for copy in copies:
        copy.wait()


def attend(plan, turned, marks, packets, state, out_weight=None):
    heads, chunk, owners = plan["heads"], plan["chunk"], plan["owners"]
    count = len(plan["members"])
    plan = dict(plan, marks=len(marks), packets=len(packets), carried=state is not None)
    fetch = plan.setdefault("fetch", None)
    rows = QUERY_PER_KEY * chunk
    slots = owners * 2 * heads
    vmem = pl.BlockSpec(memory_space=pltpu.VMEM)
    kept = [(slots, 1, rows), (slots, HEAD_WIDTH + HEADER, rows)]
    if plan["last"]:
        out_shape = [jax.ShapeDtypeStruct((2 * chunk, heads * GROUP), jnp.bfloat16)] * owners
    else:
        out_shape = [jax.ShapeDtypeStruct(shape, jnp.float32) for shape in kept]
    operands = 1 + len(marks) + len(packets) + (0 if state is None else 2)
    in_specs = [vmem] * operands
    scratch = [pltpu.VMEM(shape, jnp.float32) for shape in kept] if plan["last"] else []
    if fetch:
        in_specs.append(pl.BlockSpec(memory_space=pltpu.HBM))
        for _, columns in fetch:
            out_shape.append(jax.ShapeDtypeStruct((out_weight.shape[0], columns), out_weight.dtype))
        scratch.append(pltpu.SemaphoreType.DMA((PIECES * len(fetch),)))
    flops = 4 * owners * heads * rows * HEAD_WIDTH * count * chunk * 2
    return pl.pallas_call(
        functools.partial(attend_kernel, plan),
        out_shape=out_shape,
        in_specs=in_specs,
        out_specs=[vmem] * len(out_shape),
        scratch_shapes=scratch,
        cost_estimate=pl.CostEstimate(
            flops=flops, bytes_accessed=4 << 20, transcendentals=flops // 512
        ),
        compiler_params=pltpu.CompilerParams(vmem_limit_bytes=VMEM_LIMIT),
        name="attend",
    )(turned, *marks, *packets, *(state or ()), *([out_weight] if fetch else []))


def turn_kernel(heads, chunk, whole_rows, *refs):
    q_refs, turned_ref = refs[:-1], refs[-1]
    for i, q_ref in enumerate(q_refs):
        base = my_core() * (heads * GROUP) if whole_rows[i] else 0
        for half in range(2):
            for h in range(heads):
                columns = [
                    pl.ds(pl.multiple_of(base + h * GROUP + g * HEAD_WIDTH, HEAD_WIDTH), HEAD_WIDTH)
                    for g in range(QUERY_PER_KEY)
                ]
                q = jnp.concatenate(
                    [q_ref[half * chunk : (half + 1) * chunk, at] for at in columns], axis=0
                )
                turned_ref[(2 * i + half) * heads + h] = jnp.transpose(q)


def turn(heads, chunk, whole_rows, queries):
    vmem = pl.BlockSpec(memory_space=pltpu.VMEM)
    owners = len(queries)
    shape = (2 * owners * heads, HEAD_WIDTH, QUERY_PER_KEY * chunk)
    return pl.pallas_call(
        functools.partial(turn_kernel, heads, chunk, whole_rows),
        out_shape=jax.ShapeDtypeStruct(shape, jnp.bfloat16),
        in_specs=[vmem] * owners,
        out_specs=vmem,
        cost_estimate=pl.CostEstimate(flops=1 << 20, bytes_accessed=4 << 20, transcendentals=0),
        compiler_params=pltpu.CompilerParams(vmem_limit_bytes=VMEM_LIMIT),
        name="turn",
    )(*queries)


def project_kernel(bring, own_ref, other_ref, held_ref, *refs):
    copies = []
    if bring:
        w_ref, sent_ref, kept_ref, *next_refs, rows_ref, sems = refs
        for n, ((first, _), next_ref) in enumerate(zip(bring, next_refs)):
            copies += fetch_columns(w_ref, first, next_ref, sems, n * PIECES)
    else:
        sent_ref, kept_ref, rows_ref = refs
    chunk, part = sent_ref.shape[0], own_ref.shape[1]
    mine = lax.axis_index("inner").astype(jnp.int32)
    left = my_core() == 0
    for place, half in enumerate((1 - mine, mine)):
        at = pl.ds(pl.multiple_of(half * chunk, chunk), chunk)
        own, other = own_ref[at], other_ref[at]
        to = slice(place * chunk, (place + 1) * chunk)
        rows_ref[to, :part] = jnp.where(left, own, other)
        rows_ref[to, part:] = jnp.where(left, other, own)
    both = product(rows_ref[...], held_ref[...]).astype(sent_ref.dtype)
    sent_ref[...] = both[:chunk]
    kept_ref[...] = both[chunk:]
    for copy in copies:
        copy.wait()


def project(own, other, held, out_weight, bring):
    rows, (depth, width) = own.shape[0], held.shape
    vmem = pl.BlockSpec(memory_space=pltpu.VMEM)
    out_shape = [jax.ShapeDtypeStruct((rows // 2, width), jnp.bfloat16)] * 2
    out_shape += [jax.ShapeDtypeStruct((depth, columns), held.dtype) for _, columns in bring]
    in_specs, operands = [vmem] * 3, [own, other, held]
    scratch = [pltpu.VMEM((rows, depth), jnp.bfloat16)]
    if bring:
        in_specs.append(pl.BlockSpec(memory_space=pltpu.HBM))
        operands.append(out_weight)
        scratch.append(pltpu.SemaphoreType.DMA((PIECES * len(bring),)))
    return pl.pallas_call(
        functools.partial(project_kernel, bring),
        out_shape=out_shape,
        in_specs=in_specs,
        out_specs=[vmem] * len(out_shape),
        scratch_shapes=scratch,
        cost_estimate=pl.CostEstimate(flops=1 << 10, bytes_accessed=1 << 10, transcendentals=0),
        compiler_params=pltpu.CompilerParams(vmem_limit_bytes=VMEM_LIMIT),
        name="project",
    )(*operands)


def prepare_kernel(
    chunk, q_ref, k_ref, v_ref, position_ref, sent_ref, kept_ref, mark_ref, query_ref, first_ref, sems
):
    rows, width = k_ref.shape[0], k_ref.shape[1] // 2
    columns = query_ref.shape[1]
    copies = [pltpu.make_async_copy(position_ref, first_ref, sems.at[4])]
    for n, (ref, core) in enumerate(((sent_ref, 1 - my_core()), (kept_ref, my_core()))):
        at = pl.ds(pl.multiple_of(core * width, width), width)
        for m, source in enumerate((k_ref, v_ref)):
            to = ref.at[pl.ds(0, rows), pl.ds(m * width, width)]
            copies.append(pltpu.make_async_copy(source.at[:, at], to, sems.at[2 * n + m]))
    at = pl.ds(pl.multiple_of((1 - my_core()) * columns, columns), columns)
    copies.append(pltpu.make_async_copy(q_ref.at[:, at], query_ref, sems.at[5]))
    for copy in copies:
        copy.start()
    copies[0].wait()
    c = lax.div(first_ref[0], jnp.int32(chunk)).astype(jnp.float32)
    mark_ref[...] = jnp.full(mark_ref.shape, c, jnp.float32).astype(jnp.bfloat16)
    sent_ref[rows:] = jnp.full((HEADER, 2 * width), c, jnp.float32).astype(jnp.bfloat16)
    for copy in copies[1:]:
        copy.wait()


def prepare(queries, keys, values, positions):
    vmem = pl.BlockSpec(memory_space=pltpu.VMEM)
    hbm = pl.BlockSpec(memory_space=pltpu.HBM)
    rows, width = keys.shape
    operands = [pltpu.with_memory_space_constraint(x, pltpu.HBM) for x in (queries, keys, values, positions)]
    return pl.pallas_call(
        functools.partial(prepare_kernel, rows // 2),
        out_shape=[
            jax.ShapeDtypeStruct((rows + HEADER, width), jnp.bfloat16),
            jax.ShapeDtypeStruct((rows, width), jnp.bfloat16),
            jax.ShapeDtypeStruct((HEADER, width // 2), jnp.bfloat16),
            jax.ShapeDtypeStruct((rows, queries.shape[1] // 2), jnp.bfloat16),
        ],
        in_specs=[hbm] * 4,
        out_specs=[vmem] * 4,
        scratch_shapes=[
            pltpu.SMEM(positions.shape, jnp.int32),
            pltpu.SemaphoreType.DMA((6,)),
        ],
        compiler_params=pltpu.CompilerParams(vmem_limit_bytes=VMEM_LIMIT),
        name="prepare",
    )(*operands)


def finish_kernel(first, pairs, *refs):
    out_ref, total_ref, sem = refs[-3:]
    at = 0
    for mine, theirs in zip(refs[:pairs], refs[pairs : 2 * pairs]):
        width = mine.shape[1]
        total = mine[...].astype(jnp.float32) + theirs[...].astype(jnp.float32)
        total_ref[:, at : at + width] = total.astype(total_ref.dtype)
        at += width
    copy = pltpu.make_async_copy(total_ref, out_ref.at[:, pl.ds(first, at)], sem)
    copy.start()
    copy.wait()


def finish(kept, received, first, columns, written=None):
    vmem, hbm = pl.BlockSpec(memory_space=pltpu.VMEM), pl.BlockSpec(memory_space=pltpu.HBM)
    rows, width = kept[0].shape[0], sum(part.shape[1] for part in kept)
    pairs = len(kept)
    return pl.pallas_call(
        functools.partial(finish_kernel, first, pairs),
        out_shape=jax.ShapeDtypeStruct((rows, columns), kept[0].dtype),
        in_specs=[vmem] * (2 * pairs) + ([] if written is None else [hbm]),
        out_specs=hbm,
        input_output_aliases={} if written is None else {2 * pairs: 0},
        scratch_shapes=[pltpu.VMEM((rows, width), kept[0].dtype), pltpu.SemaphoreType.DMA],
        cost_estimate=pl.CostEstimate(flops=1 << 10, bytes_accessed=1 << 10, transcendentals=0),
        compiler_params=pltpu.CompilerParams(vmem_limit_bytes=VMEM_LIMIT),
        name="finish",
    )(*kept, *received, *([] if written is None else [written]))


def after(value, *events):
    return lax.optimization_barrier((value, *events))[0]


def split_over_cores(count, queries, keys, values, positions, out_weight, fetch):
    chips, half = count // 2, count // 4
    rows, chunk = queries.shape[0], queries.shape[0] // 2
    heads = keys.shape[1] // HEAD_WIDTH // 2
    sibling = [(b, b ^ 1) for b in range(count)]
    clock, counter = ring_pairs(chips, 1), ring_pairs(chips, -1)
    width = heads * HEAD_WIDTH
    up = lambda x: lax.ppermute(x, "blk", clock)
    down = lambda x: lax.ppermute(x, "blk", counter)

    sent, x, mark, q_sent = prepare(queries, keys, values, positions)
    got = lax.ppermute(sent, "blk", sibling)
    y = jnp.concatenate(
        [got[:rows], jnp.concatenate([mark, got[rows:, :width]], axis=1)], axis=0
    )
    q_got = lax.ppermute(q_sent, "blk", sibling)
    turned = turn(heads, chunk, (True, False), [queries, q_got])

    def call(pairs, state, own=False, last=False, fetch=None):
        each = range(len(pairs))
        plan = dict(
            heads=heads,
            chunk=chunk,
            owners=2,
            own=own,
            own_at=lambda i: i,
            last=last,
            members=[(2 * j + i, 0) for j in each for i in range(2)],
            headers=[(2 + 2 * j, rows, i * width) for j in each for i in range(2)],
            owner_headers=[(0, rows, 0), (0, rows, width)],
            fetch=fetch,
        )
        packets = [packet for pair in pairs for packet in pair]
        return attend(plan, turned, [y], packets, state, out_weight)

    ups = downs = (x, y)
    for r in range(1, half):
        (x_up, y_up), (x_down, y_down) = ups, downs
        if r > 1:
            y_up, y_down, *state = lax.optimization_barrier((y_up, y_down, *state))
        ups, downs = (up(x_up), up(y_up)), (down(x_down), down(y_down))
        if r == 1:
            *state, held = call([(x, y)], None, own=True, fetch=fetch[:1])
        elif r == 2:
            *state, more = call(arrived, state, fetch=fetch[1:])
        else:
            state = call(arrived, state)
        arrived = [ups, downs]
    x_up, y_down, *state = lax.optimization_barrier((ups[0], downs[1], *state))
    far = (up(x_up), down(y_down))
    state = call(arrived, state)
    own, theirs = call([far], state, last=True)
    return own, lax.ppermute(theirs, "blk", sibling), [held, more]


def one_head_a_device(count, queries, keys, values, positions):
    rows, chunk = queries.shape[0], queries.shape[0] // 2
    heads = keys.shape[1] // HEAD_WIDTH
    c = (positions[:1] // chunk).astype(jnp.bfloat16).reshape(1, 1)
    header = jnp.broadcast_to(c, (HEADER, 2 * keys.shape[1]))
    packet = jnp.concatenate([jnp.concatenate([keys, values], axis=1), header], axis=0)
    packets = lax.all_gather(packet, "blk", axis=0, tiled=True)
    size = rows + HEADER
    here = lax.axis_index("blk")
    order = lax.rem(here + jnp.arange(count), count)
    packets = packets.reshape(count, size, -1)[order].reshape(count * size, -1)
    plan = dict(
        heads=heads,
        chunk=chunk,
        owners=1,
        own=True,
        own_at=lambda i: 0,
        last=True,
        members=[(0, j * size) for j in range(count)],
        headers=[(0, j * size + rows, 0) for j in range(count)],
        owner_headers=[(0, rows, 0)],
    )
    turned = turn(heads, chunk, (False,), [queries])
    return attend(plan, turned, [], [packets], None)[0]


def shards(count, inner, queries, keys, values, positions, out_weight):
    heads = keys.shape[1] // HEAD_WIDTH
    if heads % 2:
        attended = one_head_a_device(count, queries, keys, values, positions)
        partial = jnp.dot(attended, out_weight, preferred_element_type=jnp.float32)
        return lax.psum_scatter(
            partial.astype(jnp.bfloat16), "inner", scatter_dimension=0, tiled=True
        )
    out_weight = pltpu.with_memory_space_constraint(out_weight, pltpu.HBM)
    shares = (10, 9, 8, 7, 6)
    widths = [out_weight.shape[1] * share // sum(shares) for share in shares]
    cuts = [(sum(widths[:j]), columns) for j, columns in enumerate(widths)]
    own, other, held = split_over_cores(
        count, queries, keys, values, positions, out_weight, cuts[:2]
    )
    bring = [cuts[j + 1 : j + 2] if j > 0 else [] for j in range(len(cuts))]
    received, kept = [], []
    for j in range(len(cuts)):
        source = own if j == 0 else after(own, sent)
        sent, keep, *rest = project(source, other, held[j], out_weight, bring[j])
        held += rest
        received.append(lax.ppermute(sent, "inner", [(0, 1), (1, 0)]))
        kept.append(keep)
    columns = out_weight.shape[1]
    result = finish(kept[:-1], received[:-1], 0, columns)
    return finish(kept[-1:], received[-1:], cuts[-1][0], columns, result)


def solution(mesh):
    placed = (P("blk", "inner"), P("blk", "inner"), P("blk", "inner"), P("blk"), P("inner", None))
    return jax.shard_map(
        functools.partial(shards, mesh.shape["blk"], mesh.shape["inner"]),
        mesh=mesh,
        in_specs=placed,
        out_specs=P(("blk", "inner"), None),
        check_vma=False,
    )
```

```python
import functools
import math

import jax
import jax.numpy as jnp
from jax import lax
from jax.experimental import pallas as pl
from jax.experimental.pallas import tpu as pltpu
from jax.sharding import PartitionSpec as P

HEAD_WIDTH = 128
QUERY_PER_KEY = 5
GROUP = QUERY_PER_KEY * HEAD_WIDTH
EXP2_SCALE = math.log2(math.e) / math.sqrt(HEAD_WIDTH)
MASKED = -1e30
VMEM_LIMIT = 16 * 1024 * 1024
TILE = 16
HEADER = 8
PIECES = 5


def ring_of_chips(chips):
    half = chips // 2
    if chips == 8:
        return [2 * z for z in range(half)] + [2 * z + 1 for z in reversed(range(half))]
    return list(range(half)) + list(reversed(range(half, chips)))


def ring_pairs(chips, step):
    ring = ring_of_chips(chips)
    return [
        (2 * ring[i] + core, 2 * ring[(i + step) % chips] + core)
        for i in range(chips)
        for core in range(2)
    ]


def my_core():
    return lax.rem(lax.axis_index("blk"), 2).astype(jnp.int32)


def product(a, b):
    return jnp.dot(a, b, preferred_element_type=jnp.float32)


def weigh(scores, high):
    return jnp.exp2((scores - high) * EXP2_SCALE).astype(jnp.bfloat16)


def turned_values(blocks):
    v = jnp.concatenate(blocks, axis=0)
    return jnp.concatenate([jnp.transpose(v), jnp.ones((TILE, v.shape[0]), v.dtype)], axis=0)


def fetch_columns(w_ref, first, held_ref, sems, sem):
    depth, width = held_ref.shape[0] // PIECES, held_ref.shape[1]
    copies = []
    for p in range(PIECES):
        at = pl.ds(p * depth, depth)
        copies.append(
            pltpu.make_async_copy(
                w_ref.at[at, pl.ds(first, width)], held_ref.at[at], sems.at[sem + p]
            )
        )
        copies[-1].start()
    return copies


def attend_kernel(plan, *refs):
    heads, chunk, owners = plan["heads"], plan["chunk"], plan["owners"]
    refs = list(refs)
    q_ref = refs.pop(0)
    mark_refs = [refs.pop(0) for _ in range(plan["marks"])]
    packets = [refs.pop(0) for _ in range(plan["packets"])]
    if plan["carried"]:
        in_high, in_sums = refs.pop(0), refs.pop(0)
    fetch = plan["fetch"]
    if fetch:
        w_ref = refs.pop(0)
    if plan["last"]:
        out_refs = {i: refs.pop(0) for i in plan["which"]}
    copies = []
    if fetch:
        sems = refs.pop()
        for n, (first, _) in enumerate(fetch):
            held_ref = refs.pop(0 if plan["last"] else 2)
            copies += fetch_columns(w_ref, first, held_ref, sems, n * PIECES)
    high_ref, sums_ref = refs

    sources = mark_refs + packets
    numbers = [
        jnp.max(
            sources[packet][row : row + HEADER, column : column + HEAD_WIDTH].astype(jnp.float32)
        ).astype(jnp.int32)
        for packet, row, column in plan["owner_headers"] + plan["headers"]
    ]
    owner_c, member_c = numbers[:owners], numbers[owners:]

    def rows_of(j, half, column):
        packet, row = plan["members"][j]
        at = row + half * chunk
        at = at if isinstance(half, int) else pl.multiple_of(at, TILE)
        return packets[packet][pl.ds(at, chunk), pl.ds(column, HEAD_WIDTH)]

    def state_at(i, half, h):
        return (2 * i + half) * heads + h

    rows = QUERY_PER_KEY * chunk
    causal = lax.broadcasted_iota(jnp.int32, (chunk, rows), 0) <= lax.rem(
        lax.broadcasted_iota(jnp.int32, (chunk, rows), 1), chunk
    )
    count = len(plan["members"])

    def one_chain(group, h, i, shared):
        first, done = group[0], group[-1] == count - 1
        k_at = pl.multiple_of(h * HEAD_WIDTH, HEAD_WIDTH)
        v_at = pl.multiple_of((heads + h) * HEAD_WIDTH, HEAD_WIDTH)
        late_at, early_at = state_at(i, 1, h), state_at(i, 0, h)
        if "keys" not in shared:
            shared["keys"] = jnp.concatenate([rows_of(j, 0, k_at) for j in group], axis=0)
            shared["values"] = turned_values([rows_of(j, 0, v_at) for j in group])
        carried = None
        if first > 0:
            carried = [(ref[early_at], ref[late_at]) for ref in (high_ref, sums_ref)]
        elif plan["carried"]:
            carried = [(ref[early_at], ref[late_at]) for ref in (in_high, in_sums)]
        pairs = []
        for j in group:
            if plan["own"] and j == plan["own_at"](i):
                pairs += [(j, 0, causal), (j, 1, causal)]
            else:
                pairs.append((j, (member_c[j] > owner_c[i]).astype(jnp.int32), None))
        base = product(shared["keys"], q_ref[late_at])
        scores = []
        for j, half, mask in pairs:
            s = product(rows_of(j, half, k_at), q_ref[state_at(i, half, h)])
            scores.append(s if mask is None else jnp.where(mask, s, MASKED))
        values = turned_values([rows_of(j, half, v_at) for j, half, _ in pairs])
        tops = [jnp.max(s, axis=0, keepdims=True) for s in scores]
        highs = []
        for side in range(2):
            some = [jnp.where(half == side, top, MASKED) for (_, half, _), top in zip(pairs, tops)]
            if side == 1:
                some.append(jnp.max(base, axis=0, keepdims=True))
            if carried is not None:
                some.append(carried[0][side])
            highs.append(functools.reduce(jnp.maximum, some))
        yield
        base_weights = weigh(base, highs[1])
        weights = [
            weigh(s, jnp.where(half == 1, highs[1], highs[0])) for (_, half, _), s in zip(pairs, scores)
        ]
        zero = jnp.zeros_like(weights[0])
        chosen = [
            jnp.concatenate(
                [jnp.where(half == side, w, zero) for (_, half, _), w in zip(pairs, weights)], axis=0
            )
            for side in range(2)
        ]
        yield
        for side, at in ((0, early_at), (1, late_at)):
            sums = product(values, chosen[side])
            if side == 1:
                sums = sums + product(shared["values"], base_weights)
            if carried is not None:
                shrink = jnp.exp2((carried[0][side] - highs[side]) * EXP2_SCALE)
                sums = sums + carried[1][side] * shrink
            if plan["last"] and done:
                mixed = sums[:HEAD_WIDTH] * (1.0 / sums[HEAD_WIDTH : HEAD_WIDTH + 1])
                mixed = jnp.transpose(mixed.astype(out_refs[i].dtype))
                for g in range(QUERY_PER_KEY):
                    to = pl.multiple_of(h * GROUP + g * HEAD_WIDTH, HEAD_WIDTH)
                    out_refs[i][side * chunk : (side + 1) * chunk, pl.ds(to, HEAD_WIDTH)] = mixed[
                        g * chunk : (g + 1) * chunk
                    ]
            else:
                high_ref[at] = highs[side]
                sums_ref[at] = sums
        yield

    def staggered(chains):
        for t in range(len(chains) + 2):
            for stage in (2, 1, 0):
                if 0 <= t - stage < len(chains):
                    next(chains[t - stage])

    for first in range(0, count, 6):
        group = range(first, min(first + 6, count))

        def run(heads_at_once, group=group):
            chains = []
            for h in heads_at_once:
                shared = {}
                chains += [one_chain(group, h, i, shared) for i in plan["which"]]
            staggered(chains)

        if fetch:

            def one_head(h, carry):
                run([h])
                return carry

            lax.fori_loop(0, heads, one_head, 0)
        else:
            run(range(heads))
    for copy in copies:
        copy.wait()


def attend(plan, turned, marks, packets, state, out_weight=None):
    heads, chunk, owners = plan["heads"], plan["chunk"], plan["owners"]
    count = len(plan["members"])
    plan = dict(plan, marks=len(marks), packets=len(packets), carried=state is not None)
    fetch = plan.setdefault("fetch", None)
    which = plan.setdefault("which", range(owners))
    rows = QUERY_PER_KEY * chunk
    slots = owners * 2 * heads
    vmem = pl.BlockSpec(memory_space=pltpu.VMEM)
    kept = [(slots, 1, rows), (slots, HEAD_WIDTH + TILE, rows)]
    if plan["last"]:
        out_shape = [jax.ShapeDtypeStruct((2 * chunk, heads * GROUP), jnp.bfloat16)] * len(which)
    else:
        out_shape = [jax.ShapeDtypeStruct(shape, jnp.float32) for shape in kept]
    operands = 1 + len(marks) + len(packets) + (0 if state is None else 2)
    in_specs = [vmem] * operands
    scratch = [pltpu.VMEM(shape, jnp.float32) for shape in kept] if plan["last"] else []
    if fetch:
        in_specs.append(pl.BlockSpec(memory_space=pltpu.HBM))
        for _, columns in fetch:
            out_shape.append(jax.ShapeDtypeStruct((out_weight.shape[0], columns), out_weight.dtype))
        scratch.append(pltpu.SemaphoreType.DMA((PIECES * len(fetch),)))
    flops = 4 * owners * heads * rows * HEAD_WIDTH * count * chunk * 2
    return pl.pallas_call(
        functools.partial(attend_kernel, plan),
        out_shape=out_shape,
        in_specs=in_specs,
        out_specs=[vmem] * len(out_shape),
        scratch_shapes=scratch,
        cost_estimate=pl.CostEstimate(
            flops=flops, bytes_accessed=4 << 20, transcendentals=flops // 512
        ),
        compiler_params=pltpu.CompilerParams(vmem_limit_bytes=VMEM_LIMIT),
        name="attend",
    )(turned, *marks, *packets, *(state or ()), *([out_weight] if fetch else []))


def turn_kernel(heads, chunk, whole_rows, *refs):
    q_refs, turned_ref = refs[:-1], refs[-1]
    for i, q_ref in enumerate(q_refs):
        base = my_core() * (heads * GROUP) if whole_rows[i] else 0
        for half in range(2):
            for h in range(heads):
                columns = [
                    pl.ds(pl.multiple_of(base + h * GROUP + g * HEAD_WIDTH, HEAD_WIDTH), HEAD_WIDTH)
                    for g in range(QUERY_PER_KEY)
                ]
                q = jnp.concatenate(
                    [q_ref[half * chunk : (half + 1) * chunk, at] for at in columns], axis=0
                )
                turned_ref[(2 * i + half) * heads + h] = jnp.transpose(q)


def turn(heads, chunk, whole_rows, queries):
    vmem = pl.BlockSpec(memory_space=pltpu.VMEM)
    owners = len(queries)
    shape = (2 * owners * heads, HEAD_WIDTH, QUERY_PER_KEY * chunk)
    return pl.pallas_call(
        functools.partial(turn_kernel, heads, chunk, whole_rows),
        out_shape=jax.ShapeDtypeStruct(shape, jnp.bfloat16),
        in_specs=[vmem] * owners,
        out_specs=vmem,
        cost_estimate=pl.CostEstimate(flops=1 << 20, bytes_accessed=4 << 20, transcendentals=0),
        compiler_params=pltpu.CompilerParams(vmem_limit_bytes=VMEM_LIMIT),
        name="turn",
    )(*queries)


def leaving_first(ref):
    chunk = ref.shape[0] // 2
    mine = lax.axis_index("inner").astype(jnp.int32)
    halves = [ref[pl.ds(pl.multiple_of(half * chunk, chunk), chunk)] for half in (1 - mine, mine)]
    return jnp.concatenate(halves, axis=0)


def rows_of_core(held_ref, core):
    depth = held_ref.shape[0] // 2
    return held_ref[pl.ds(pl.multiple_of(core * depth, depth), depth)]


def begin_kernel(own_ref, held_ref, begun_ref):
    begun_ref[...] = product(leaving_first(own_ref), rows_of_core(held_ref, my_core()))


def begin(own, held):
    vmem = pl.BlockSpec(memory_space=pltpu.VMEM)
    return pl.pallas_call(
        begin_kernel,
        out_shape=jax.ShapeDtypeStruct((own.shape[0], held.shape[1]), jnp.float32),
        in_specs=[vmem, vmem],
        out_specs=vmem,
        cost_estimate=pl.CostEstimate(flops=1 << 10, bytes_accessed=1 << 10, transcendentals=0),
        compiler_params=pltpu.CompilerParams(vmem_limit_bytes=VMEM_LIMIT),
        name="begin",
    )(own, held)


def project_kernel(bring, begun, own_ref, other_ref, held_ref, *refs):
    refs, copies = list(refs), []
    if bring:
        w_ref, sems = refs.pop(0), refs.pop()
    if begun:
        begun_ref = refs.pop(0)
    sent_ref, kept_ref = refs.pop(0), refs.pop(0)
    for n, (first, _) in enumerate(bring):
        copies += fetch_columns(w_ref, first, refs.pop(0), sems, n * PIECES)
    chunk, core = sent_ref.shape[0], my_core()
    total = product(leaving_first(other_ref), rows_of_core(held_ref, 1 - core))
    if begun:
        total = total + begun_ref[...]
    else:
        total = total + product(leaving_first(own_ref), rows_of_core(held_ref, core))
    both = total.astype(sent_ref.dtype)
    sent_ref[...] = both[:chunk]
    kept_ref[...] = both[chunk:]
    for copy in copies:
        copy.wait()


def project(own, other, held, out_weight, bring, begun=None):
    rows, (depth, width) = own.shape[0], held.shape
    vmem = pl.BlockSpec(memory_space=pltpu.VMEM)
    out_shape = [jax.ShapeDtypeStruct((rows // 2, width), jnp.bfloat16)] * 2
    out_shape += [jax.ShapeDtypeStruct((depth, columns), held.dtype) for _, columns in bring]
    in_specs, operands, scratch = [vmem] * 3, [own, other, held], []
    if bring:
        in_specs.append(pl.BlockSpec(memory_space=pltpu.HBM))
        operands.append(out_weight)
        scratch.append(pltpu.SemaphoreType.DMA((PIECES * len(bring),)))
    if begun is not None:
        in_specs.append(vmem)
        operands.append(begun)
    return pl.pallas_call(
        functools.partial(project_kernel, bring, begun is not None),
        out_shape=out_shape,
        in_specs=in_specs,
        out_specs=[vmem] * len(out_shape),
        scratch_shapes=scratch,
        cost_estimate=pl.CostEstimate(flops=1 << 10, bytes_accessed=1 << 10, transcendentals=0),
        compiler_params=pltpu.CompilerParams(vmem_limit_bytes=VMEM_LIMIT),
        name="project",
    )(*operands)


def prepare_kernel(
    chunk, q_ref, k_ref, v_ref, position_ref, sent_ref, kept_ref, mark_ref, query_ref, first_ref, sems
):
    rows, width = k_ref.shape[0], k_ref.shape[1] // 2
    columns = query_ref.shape[1]
    copies = [pltpu.make_async_copy(position_ref, first_ref, sems.at[4])]
    for n, (ref, core) in enumerate(((sent_ref, 1 - my_core()), (kept_ref, my_core()))):
        at = pl.ds(pl.multiple_of(core * width, width), width)
        for m, source in enumerate((k_ref, v_ref)):
            to = ref.at[pl.ds(0, rows), pl.ds(m * width, width)]
            copies.append(pltpu.make_async_copy(source.at[:, at], to, sems.at[2 * n + m]))
    at = pl.ds(pl.multiple_of((1 - my_core()) * columns, columns), columns)
    copies.append(pltpu.make_async_copy(q_ref.at[:, at], query_ref, sems.at[5]))
    for copy in copies:
        copy.start()
    copies[0].wait()
    c = lax.div(first_ref[0], jnp.int32(chunk)).astype(jnp.float32)
    mark_ref[...] = jnp.full(mark_ref.shape, c, jnp.float32).astype(jnp.bfloat16)
    sent_ref[rows:] = jnp.full((TILE, 2 * width), c, jnp.float32).astype(jnp.bfloat16)
    for copy in copies[1:]:
        copy.wait()


def prepare(queries, keys, values, positions):
    vmem = pl.BlockSpec(memory_space=pltpu.VMEM)
    hbm = pl.BlockSpec(memory_space=pltpu.HBM)
    rows, width = keys.shape
    operands = [pltpu.with_memory_space_constraint(x, pltpu.HBM) for x in (queries, keys, values, positions)]
    return pl.pallas_call(
        functools.partial(prepare_kernel, rows // 2),
        out_shape=[
            jax.ShapeDtypeStruct((rows + TILE, width), jnp.bfloat16),
            jax.ShapeDtypeStruct((rows, width), jnp.bfloat16),
            jax.ShapeDtypeStruct((HEADER, width // 2), jnp.bfloat16),
            jax.ShapeDtypeStruct((rows, queries.shape[1] // 2), jnp.bfloat16),
        ],
        in_specs=[hbm] * 4,
        out_specs=[vmem] * 4,
        scratch_shapes=[
            pltpu.SMEM(positions.shape, jnp.int32),
            pltpu.SemaphoreType.DMA((6,)),
        ],
        compiler_params=pltpu.CompilerParams(vmem_limit_bytes=VMEM_LIMIT),
        name="prepare",
    )(*operands)


def finish_kernel(first, pairs, *refs):
    out_ref, total_ref, sem = refs[-3:]
    at = 0
    for mine, theirs in zip(refs[:pairs], refs[pairs : 2 * pairs]):
        width = mine.shape[1]
        total = mine[...].astype(jnp.float32) + theirs[...].astype(jnp.float32)
        total_ref[:, at : at + width] = total.astype(total_ref.dtype)
        at += width
    copy = pltpu.make_async_copy(total_ref, out_ref.at[:, pl.ds(first, at)], sem)
    copy.start()
    copy.wait()


def finish(kept, received, first, columns, written=None):
    vmem, hbm = pl.BlockSpec(memory_space=pltpu.VMEM), pl.BlockSpec(memory_space=pltpu.HBM)
    rows, width = kept[0].shape[0], sum(part.shape[1] for part in kept)
    pairs = len(kept)
    return pl.pallas_call(
        functools.partial(finish_kernel, first, pairs),
        out_shape=jax.ShapeDtypeStruct((rows, columns), kept[0].dtype),
        in_specs=[vmem] * (2 * pairs) + ([] if written is None else [hbm]),
        out_specs=hbm,
        input_output_aliases={} if written is None else {2 * pairs: 0},
        scratch_shapes=[pltpu.VMEM((rows, width), kept[0].dtype), pltpu.SemaphoreType.DMA],
        cost_estimate=pl.CostEstimate(flops=1 << 10, bytes_accessed=1 << 10, transcendentals=0),
        compiler_params=pltpu.CompilerParams(vmem_limit_bytes=VMEM_LIMIT),
        name="finish",
    )(*kept, *received, *([] if written is None else [written]))


def after(value, *events):
    return lax.optimization_barrier((value, *events))[0]


def split_over_cores(count, queries, keys, values, positions, out_weight, fetch):
    chips, half = count // 2, count // 4
    rows, chunk = queries.shape[0], queries.shape[0] // 2
    heads = keys.shape[1] // HEAD_WIDTH // 2
    sibling = [(b, b ^ 1) for b in range(count)]
    clock, counter = ring_pairs(chips, 1), ring_pairs(chips, -1)
    width = heads * HEAD_WIDTH
    up = lambda x: lax.ppermute(x, "blk", clock)
    down = lambda x: lax.ppermute(x, "blk", counter)

    sent, x, mark, q_sent = prepare(queries, keys, values, positions)
    got = lax.ppermute(sent, "blk", sibling)
    y = jnp.concatenate(
        [got[:rows], jnp.concatenate([mark, got[rows : rows + HEADER, :width]], axis=1)], axis=0
    )
    q_got = lax.ppermute(q_sent, "blk", sibling)
    turned = turn(heads, chunk, (True, False), [queries, q_got])

    def call(pairs, state, own=False, last=False, fetch=None, which=(0, 1)):
        each = range(len(pairs))
        plan = dict(
            heads=heads,
            chunk=chunk,
            owners=2,
            own=own,
            own_at=lambda i: i,
            last=last,
            members=[(2 * j + i, 0) for j in each for i in range(2)],
            headers=[(2 + 2 * j, rows, i * width) for j in each for i in range(2)],
            owner_headers=[(0, rows, 0), (0, rows, width)],
            fetch=fetch,
            which=which,
        )
        packets = [packet for pair in pairs for packet in pair]
        return attend(plan, turned, [y], packets, state, out_weight)

    ups = downs = (x, y)
    for r in range(1, half):
        (x_up, y_up), (x_down, y_down) = ups, downs
        if r > 1:
            y_up, y_down, *state = lax.optimization_barrier((y_up, y_down, *state))
        ups, downs = (up(x_up), up(y_up)), (down(x_down), down(y_down))
        if r == 1:
            *state, held = call([(x, y)], None, own=True, fetch=fetch[:1])
        elif r == 2:
            *state, more = call(arrived, state, fetch=fetch[1:])
        else:
            state = call(arrived, state)
        arrived = [ups, downs]
    x_up, y_down, y_up, *state = lax.optimization_barrier((ups[0], downs[1], ups[1], *state))
    arrived = [(x_up, y_up), downs]
    far = (up(x_up), down(y_down))
    state = call(arrived, state)
    (theirs,) = call([far], state, last=True, which=(1,))
    other = lax.ppermute(theirs, "blk", sibling)
    (own,) = call([far], state, last=True, which=(0,))
    return own, other, [held, more]


def one_head_a_device(count, queries, keys, values, positions):
    rows, chunk = queries.shape[0], queries.shape[0] // 2
    heads = keys.shape[1] // HEAD_WIDTH
    c = (positions[:1] // chunk).astype(jnp.bfloat16).reshape(1, 1)
    header = jnp.broadcast_to(c, (TILE, 2 * keys.shape[1]))
    packet = jnp.concatenate([jnp.concatenate([keys, values], axis=1), header], axis=0)
    packets = lax.all_gather(packet, "blk", axis=0, tiled=True)
    size = rows + TILE
    here = lax.axis_index("blk")
    order = lax.rem(here + jnp.arange(count), count)
    packets = packets.reshape(count, size, -1)[order].reshape(count * size, -1)
    plan = dict(
        heads=heads,
        chunk=chunk,
        owners=1,
        own=True,
        own_at=lambda i: 0,
        last=True,
        members=[(0, j * size) for j in range(count)],
        headers=[(0, j * size + rows, 0) for j in range(count)],
        owner_headers=[(0, rows, 0)],
    )
    turned = turn(heads, chunk, (False,), [queries])
    return attend(plan, turned, [], [packets], None)[0]


def shards(count, inner, queries, keys, values, positions, out_weight):
    heads = keys.shape[1] // HEAD_WIDTH
    if heads % 2:
        attended = one_head_a_device(count, queries, keys, values, positions)
        partial = jnp.dot(attended, out_weight, preferred_element_type=jnp.float32)
        return lax.psum_scatter(
            partial.astype(jnp.bfloat16), "inner", scatter_dimension=0, tiled=True
        )
    out_weight = pltpu.with_memory_space_constraint(out_weight, pltpu.HBM)
    shares = (10, 9, 8, 7, 6)
    widths = [out_weight.shape[1] * share // sum(shares) for share in shares]
    cuts = [(sum(widths[:j]), columns) for j, columns in enumerate(widths)]
    own, other, held = split_over_cores(
        count, queries, keys, values, positions, out_weight, cuts[:2]
    )
    bring = [cuts[j + 1 : j + 2] if j > 0 else [] for j in range(len(cuts))]
    received, kept = [], []
    for j in range(len(cuts)):
        source = own if j == 0 else after(own, sent)
        begun = begin(own, held[0]) if j == 0 else None
        sent, keep, *rest = project(source, other, held[j], out_weight, bring[j], begun)
        held += rest
        received.append(lax.ppermute(sent, "inner", [(0, 1), (1, 0)]))
        kept.append(keep)
    columns = out_weight.shape[1]
    result = finish(kept[:-1], received[:-1], 0, columns)
    return finish(kept[-1:], received[-1:], cuts[-1][0], columns, result)


def solution(mesh):
    placed = (P("blk", "inner"), P("blk", "inner"), P("blk", "inner"), P("blk"), P("inner", None))
    return jax.shard_map(
        functools.partial(shards, mesh.shape["blk"], mesh.shape["inner"]),
        mesh=mesh,
        in_specs=placed,
        out_specs=P(("blk", "inner"), None),
        check_vma=False,
    )
```

```python
import functools
import math

import jax
import jax.numpy as jnp
from jax import lax
from jax.experimental import pallas as pl
from jax.experimental.pallas import tpu as pltpu
from jax.sharding import PartitionSpec as P

HEAD_WIDTH = 128
QUERY_PER_KEY = 5
GROUP = QUERY_PER_KEY * HEAD_WIDTH
EXP2_SCALE = math.log2(math.e) / math.sqrt(HEAD_WIDTH)
MASKED = -1e30
VMEM_LIMIT = 16 * 1024 * 1024
TILE = 16
HEADER = 8
PIECES = 5


def ring_of_chips(chips):
    half = chips // 2
    if chips == 8:
        return [2 * z for z in range(half)] + [2 * z + 1 for z in reversed(range(half))]
    return list(range(half)) + list(reversed(range(half, chips)))


def ring_pairs(chips, step):
    ring = ring_of_chips(chips)
    return [
        (2 * ring[i] + core, 2 * ring[(i + step) % chips] + core)
        for i in range(chips)
        for core in range(2)
    ]


def my_core():
    return lax.rem(lax.axis_index("blk"), 2).astype(jnp.int32)


def product(a, b):
    return jnp.dot(a, b, preferred_element_type=jnp.float32)


def weigh(scores, high):
    return jnp.exp2((scores - high) * EXP2_SCALE).astype(jnp.bfloat16)


def turned_values(blocks):
    v = jnp.concatenate(blocks, axis=0)
    return jnp.concatenate([jnp.transpose(v), jnp.ones((TILE, v.shape[0]), v.dtype)], axis=0)


def fetch_columns(w_ref, first, held_ref, sems, sem):
    depth, width = held_ref.shape[0] // PIECES, held_ref.shape[1]
    copies = []
    for p in range(PIECES):
        at = pl.ds(p * depth, depth)
        copies.append(
            pltpu.make_async_copy(
                w_ref.at[at, pl.ds(first, width)], held_ref.at[at], sems.at[sem + p]
            )
        )
        copies[-1].start()
    return copies


def attend_kernel(plan, *refs):
    heads, chunk, owners = plan["heads"], plan["chunk"], plan["owners"]
    refs = list(refs)
    q_ref = refs.pop(0)
    mark_refs = [refs.pop(0) for _ in range(plan["marks"])]
    packets = [refs.pop(0) for _ in range(plan["packets"])]
    if plan["carried"]:
        in_high, in_sums = refs.pop(0), refs.pop(0)
    fetch = plan["fetch"]
    if fetch:
        w_ref = refs.pop(0)
    if plan["last"]:
        out_refs = {i: refs.pop(0) for i in plan["which"]}
    copies = []
    if fetch:
        sems = refs.pop()
        for n, (first, _) in enumerate(fetch):
            held_ref = refs.pop(0 if plan["last"] else 2)
            copies += fetch_columns(w_ref, first, held_ref, sems, n * PIECES)
    high_ref, sums_ref = refs

    sources = mark_refs + packets
    numbers = [
        jnp.max(
            sources[packet][row : row + HEADER, column : column + HEAD_WIDTH].astype(jnp.float32)
        ).astype(jnp.int32)
        for packet, row, column in plan["owner_headers"] + plan["headers"]
    ]
    owner_c, member_c = numbers[:owners], numbers[owners:]

    def rows_of(j, half, column):
        packet, row = plan["members"][j]
        at = row + half * chunk
        at = at if isinstance(half, int) else pl.multiple_of(at, TILE)
        return packets[packet][pl.ds(at, chunk), pl.ds(column, HEAD_WIDTH)]

    def state_at(i, half, h):
        return (2 * i + half) * heads + h

    rows = QUERY_PER_KEY * chunk
    causal = lax.broadcasted_iota(jnp.int32, (chunk, rows), 0) <= lax.rem(
        lax.broadcasted_iota(jnp.int32, (chunk, rows), 1), chunk
    )
    count = len(plan["members"])

    def one_chain(group, h, i, shared):
        first, done = group[0], group[-1] == count - 1
        k_at = pl.multiple_of(h * HEAD_WIDTH, HEAD_WIDTH)
        v_at = pl.multiple_of((heads + h) * HEAD_WIDTH, HEAD_WIDTH)
        late_at, early_at = state_at(i, 1, h), state_at(i, 0, h)
        if "keys" not in shared:
            shared["keys"] = jnp.concatenate([rows_of(j, 0, k_at) for j in group], axis=0)
            shared["values"] = turned_values([rows_of(j, 0, v_at) for j in group])
        carried = None
        if first > 0:
            carried = [(ref[early_at], ref[late_at]) for ref in (high_ref, sums_ref)]
        elif plan["carried"]:
            carried = [(ref[early_at], ref[late_at]) for ref in (in_high, in_sums)]
        pairs = []
        for j in group:
            if plan["own"] and j == plan["own_at"](i):
                pairs += [(j, 0, causal), (j, 1, causal)]
            else:
                pairs.append((j, (member_c[j] > owner_c[i]).astype(jnp.int32), None))
        base = product(shared["keys"], q_ref[late_at])
        scores = []
        for j, half, mask in pairs:
            s = product(rows_of(j, half, k_at), q_ref[state_at(i, half, h)])
            scores.append(s if mask is None else jnp.where(mask, s, MASKED))
        values = turned_values([rows_of(j, half, v_at) for j, half, _ in pairs])
        tops = [jnp.max(s, axis=0, keepdims=True) for s in scores]
        highs = []
        for side in range(2):
            some = [jnp.where(half == side, top, MASKED) for (_, half, _), top in zip(pairs, tops)]
            if side == 1:
                some.append(jnp.max(base, axis=0, keepdims=True))
            if carried is not None:
                some.append(carried[0][side])
            highs.append(functools.reduce(jnp.maximum, some))
        yield
        base_weights = weigh(base, highs[1])
        weights = [
            weigh(s, jnp.where(half == 1, highs[1], highs[0])) for (_, half, _), s in zip(pairs, scores)
        ]
        zero = jnp.zeros_like(weights[0])
        chosen = [
            jnp.concatenate(
                [jnp.where(half == side, w, zero) for (_, half, _), w in zip(pairs, weights)], axis=0
            )
            for side in range(2)
        ]
        yield
        for side, at in ((0, early_at), (1, late_at)):
            sums = product(values, chosen[side])
            if side == 1:
                sums = sums + product(shared["values"], base_weights)
            if carried is not None:
                shrink = jnp.exp2((carried[0][side] - highs[side]) * EXP2_SCALE)
                sums = sums + carried[1][side] * shrink
            if plan["last"] and done:
                mixed = sums[:HEAD_WIDTH] * (1.0 / sums[HEAD_WIDTH : HEAD_WIDTH + 1])
                mixed = jnp.transpose(mixed.astype(out_refs[i].dtype))
                for g in range(QUERY_PER_KEY):
                    to = pl.multiple_of(h * GROUP + g * HEAD_WIDTH, HEAD_WIDTH)
                    out_refs[i][side * chunk : (side + 1) * chunk, pl.ds(to, HEAD_WIDTH)] = mixed[
                        g * chunk : (g + 1) * chunk
                    ]
            else:
                high_ref[at] = highs[side]
                sums_ref[at] = sums
        yield

    def staggered(chains):
        for t in range(len(chains) + 2):
            for stage in (2, 1, 0):
                if 0 <= t - stage < len(chains):
                    next(chains[t - stage])

    for first in range(0, count, 6):
        group = range(first, min(first + 6, count))

        def run(heads_at_once, group=group):
            chains = []
            for h in heads_at_once:
                shared = {}
                chains += [one_chain(group, h, i, shared) for i in plan["which"]]
            staggered(chains)

        if fetch:

            def one_head(h, carry):
                run([h])
                return carry

            lax.fori_loop(0, heads, one_head, 0)
        else:
            run(range(heads))
    for copy in copies:
        copy.wait()


def attend(plan, turned, marks, packets, state, out_weight=None):
    heads, chunk, owners = plan["heads"], plan["chunk"], plan["owners"]
    count = len(plan["members"])
    plan = dict(plan, marks=len(marks), packets=len(packets), carried=state is not None)
    fetch = plan.setdefault("fetch", None)
    which = plan.setdefault("which", range(owners))
    rows = QUERY_PER_KEY * chunk
    slots = owners * 2 * heads
    vmem = pl.BlockSpec(memory_space=pltpu.VMEM)
    kept = [(slots, 1, rows), (slots, HEAD_WIDTH + TILE, rows)]
    if plan["last"]:
        out_shape = [jax.ShapeDtypeStruct((2 * chunk, heads * GROUP), jnp.bfloat16)] * len(which)
    else:
        out_shape = [jax.ShapeDtypeStruct(shape, jnp.float32) for shape in kept]
    operands = 1 + len(marks) + len(packets) + (0 if state is None else 2)
    in_specs = [vmem] * operands
    scratch = [pltpu.VMEM(shape, jnp.float32) for shape in kept] if plan["last"] else []
    if fetch:
        in_specs.append(pl.BlockSpec(memory_space=pltpu.HBM))
        for _, columns in fetch:
            out_shape.append(jax.ShapeDtypeStruct((out_weight.shape[0], columns), out_weight.dtype))
        scratch.append(pltpu.SemaphoreType.DMA((PIECES * len(fetch),)))
    flops = 4 * owners * heads * rows * HEAD_WIDTH * count * chunk * 2
    return pl.pallas_call(
        functools.partial(attend_kernel, plan),
        out_shape=out_shape,
        in_specs=in_specs,
        out_specs=[vmem] * len(out_shape),
        scratch_shapes=scratch,
        cost_estimate=pl.CostEstimate(
            flops=flops, bytes_accessed=4 << 20, transcendentals=flops // 512
        ),
        compiler_params=pltpu.CompilerParams(vmem_limit_bytes=VMEM_LIMIT),
        name="attend",
    )(turned, *marks, *packets, *(state or ()), *([out_weight] if fetch else []))


def turn_kernel(heads, chunk, *refs):
    q_refs, turned_ref = refs[:-1], refs[-1]
    for i, q_ref in enumerate(q_refs):
        for half in range(2):
            for h in range(heads):
                columns = [slice(at, at + HEAD_WIDTH) for at in range(h * GROUP, (h + 1) * GROUP, HEAD_WIDTH)]
                q = jnp.concatenate(
                    [q_ref[half * chunk : (half + 1) * chunk, at] for at in columns], axis=0
                )
                turned_ref[(2 * i + half) * heads + h] = jnp.transpose(q)


def turn(heads, chunk, queries):
    vmem = pl.BlockSpec(memory_space=pltpu.VMEM)
    owners = len(queries)
    shape = (2 * owners * heads, HEAD_WIDTH, QUERY_PER_KEY * chunk)
    return pl.pallas_call(
        functools.partial(turn_kernel, heads, chunk),
        out_shape=jax.ShapeDtypeStruct(shape, jnp.bfloat16),
        in_specs=[vmem] * owners,
        out_specs=vmem,
        cost_estimate=pl.CostEstimate(flops=1 << 10, bytes_accessed=1 << 10, transcendentals=0),
        compiler_params=pltpu.CompilerParams(vmem_limit_bytes=VMEM_LIMIT),
        name="turn",
    )(*queries)


def leaving_first(ref):
    chunk = ref.shape[0] // 2
    mine = lax.axis_index("inner").astype(jnp.int32)
    halves = [ref[pl.ds(pl.multiple_of(half * chunk, chunk), chunk)] for half in (1 - mine, mine)]
    return jnp.concatenate(halves, axis=0)


def rows_of_core(held_ref, core):
    depth = held_ref.shape[0] // 2
    return held_ref[pl.ds(pl.multiple_of(core * depth, depth), depth)]


def begin_kernel(own_ref, held_ref, begun_ref):
    begun_ref[...] = product(leaving_first(own_ref), rows_of_core(held_ref, my_core()))


def begin(own, held):
    vmem = pl.BlockSpec(memory_space=pltpu.VMEM)
    return pl.pallas_call(
        begin_kernel,
        out_shape=jax.ShapeDtypeStruct((own.shape[0], held.shape[1]), jnp.float32),
        in_specs=[vmem, vmem],
        out_specs=vmem,
        cost_estimate=pl.CostEstimate(flops=1 << 10, bytes_accessed=1 << 10, transcendentals=0),
        compiler_params=pltpu.CompilerParams(vmem_limit_bytes=VMEM_LIMIT),
        name="begin",
    )(own, held)


def project_kernel(bring, begun, own_ref, other_ref, held_ref, *refs):
    refs, copies = list(refs), []
    if bring:
        w_ref, sems = refs.pop(0), refs.pop()
    if begun:
        begun_ref = refs.pop(0)
    sent_ref, kept_ref = refs.pop(0), refs.pop(0)
    for n, (first, _) in enumerate(bring):
        copies += fetch_columns(w_ref, first, refs.pop(0), sems, n * PIECES)
    chunk, core = sent_ref.shape[0], my_core()
    other = leaving_first(other_ref)
    if begun:
        total = begun_ref[...] + product(other, rows_of_core(held_ref, 1 - core))
    else:
        (rows_ref,) = refs
        own, part = leaving_first(own_ref), own_ref.shape[1]
        rows_ref[:, :part] = jnp.where(core == 0, own, other)
        rows_ref[:, part:] = jnp.where(core == 0, other, own)
        total = product(rows_ref[...], held_ref[...])
    both = total.astype(sent_ref.dtype)
    sent_ref[...] = both[:chunk]
    kept_ref[...] = both[chunk:]
    for copy in copies:
        copy.wait()


def project(own, other, held, out_weight, bring, begun=None):
    rows, (depth, width) = own.shape[0], held.shape
    vmem = pl.BlockSpec(memory_space=pltpu.VMEM)
    out_shape = [jax.ShapeDtypeStruct((rows // 2, width), jnp.bfloat16)] * 2
    out_shape += [jax.ShapeDtypeStruct((depth, columns), held.dtype) for _, columns in bring]
    in_specs, operands, scratch = [vmem] * 3, [own, other, held], []
    if begun is None:
        scratch.append(pltpu.VMEM((rows, depth), jnp.bfloat16))
    if bring:
        in_specs.append(pl.BlockSpec(memory_space=pltpu.HBM))
        operands.append(out_weight)
        scratch.append(pltpu.SemaphoreType.DMA((PIECES * len(bring),)))
    if begun is not None:
        in_specs.append(vmem)
        operands.append(begun)
    return pl.pallas_call(
        functools.partial(project_kernel, bring, begun is not None),
        out_shape=out_shape,
        in_specs=in_specs,
        out_specs=[vmem] * len(out_shape),
        scratch_shapes=scratch,
        cost_estimate=pl.CostEstimate(flops=1 << 10, bytes_accessed=1 << 10, transcendentals=0),
        compiler_params=pltpu.CompilerParams(vmem_limit_bytes=VMEM_LIMIT),
        name="project",
    )(*operands)


def prepare_kernel(
    chunk, q_ref, k_ref, v_ref, position_ref, sent_ref, kept_ref, mark_ref, *query_refs_and_scratch
):
    *query_refs, first_ref, sems = query_refs_and_scratch
    rows, width = k_ref.shape[0], k_ref.shape[1] // 2
    columns = query_refs[0].shape[1]
    copies = [pltpu.make_async_copy(position_ref, first_ref, sems.at[4])]
    for n, (ref, core) in enumerate(((sent_ref, 1 - my_core()), (kept_ref, my_core()))):
        at = pl.ds(pl.multiple_of(core * width, width), width)
        for m, source in enumerate((k_ref, v_ref)):
            to = ref.at[pl.ds(0, rows), pl.ds(m * width, width)]
            copies.append(pltpu.make_async_copy(source.at[:, at], to, sems.at[2 * n + m]))
    for n, (ref, core) in enumerate(zip(query_refs, (1 - my_core(), my_core()))):
        at = pl.ds(pl.multiple_of(core * columns, columns), columns)
        copies.append(pltpu.make_async_copy(q_ref.at[:, at], ref, sems.at[5 + n]))
    for copy in copies:
        copy.start()
    copies[0].wait()
    c = lax.div(first_ref[0], jnp.int32(chunk)).astype(jnp.float32)
    mark_ref[...] = jnp.full(mark_ref.shape, c, jnp.float32).astype(jnp.bfloat16)
    sent_ref[rows:] = jnp.full((TILE, 2 * width), c, jnp.float32).astype(jnp.bfloat16)
    for copy in copies[1:]:
        copy.wait()


def prepare(queries, keys, values, positions):
    vmem = pl.BlockSpec(memory_space=pltpu.VMEM)
    hbm = pl.BlockSpec(memory_space=pltpu.HBM)
    rows, width = keys.shape
    operands = [pltpu.with_memory_space_constraint(x, pltpu.HBM) for x in (queries, keys, values, positions)]
    return pl.pallas_call(
        functools.partial(prepare_kernel, rows // 2),
        out_shape=[
            jax.ShapeDtypeStruct((rows + TILE, width), jnp.bfloat16),
            jax.ShapeDtypeStruct((rows, width), jnp.bfloat16),
            jax.ShapeDtypeStruct((HEADER, width // 2), jnp.bfloat16),
        ]
        + [jax.ShapeDtypeStruct((rows, queries.shape[1] // 2), jnp.bfloat16)] * 2,
        in_specs=[hbm] * 4,
        out_specs=[vmem] * 5,
        scratch_shapes=[
            pltpu.SMEM(positions.shape, jnp.int32),
            pltpu.SemaphoreType.DMA((7,)),
        ],
        compiler_params=pltpu.CompilerParams(vmem_limit_bytes=VMEM_LIMIT),
        name="prepare",
    )(*operands)


def finish_kernel(first, pairs, *refs):
    out_ref, total_ref, sem = refs[-3:]
    at = 0
    for mine, theirs in zip(refs[:pairs], refs[pairs : 2 * pairs]):
        width = mine.shape[1]
        total = mine[...].astype(jnp.float32) + theirs[...].astype(jnp.float32)
        total_ref[:, at : at + width] = total.astype(total_ref.dtype)
        at += width
    copy = pltpu.make_async_copy(total_ref, out_ref.at[:, pl.ds(first, at)], sem)
    copy.start()
    copy.wait()


def finish(kept, received, first, columns, written=None):
    vmem, hbm = pl.BlockSpec(memory_space=pltpu.VMEM), pl.BlockSpec(memory_space=pltpu.HBM)
    rows, width = kept[0].shape[0], sum(part.shape[1] for part in kept)
    pairs = len(kept)
    return pl.pallas_call(
        functools.partial(finish_kernel, first, pairs),
        out_shape=jax.ShapeDtypeStruct((rows, columns), kept[0].dtype),
        in_specs=[vmem] * (2 * pairs) + ([] if written is None else [hbm]),
        out_specs=hbm,
        input_output_aliases={} if written is None else {2 * pairs: 0},
        scratch_shapes=[pltpu.VMEM((rows, width), kept[0].dtype), pltpu.SemaphoreType.DMA],
        cost_estimate=pl.CostEstimate(flops=1 << 10, bytes_accessed=1 << 10, transcendentals=0),
        compiler_params=pltpu.CompilerParams(vmem_limit_bytes=VMEM_LIMIT),
        name="finish",
    )(*kept, *received, *([] if written is None else [written]))


def after(value, *events):
    return lax.optimization_barrier((value, *events))[0]


def split_over_cores(count, queries, keys, values, positions, out_weight, fetch):
    chips, half = count // 2, count // 4
    rows, chunk = queries.shape[0], queries.shape[0] // 2
    heads = keys.shape[1] // HEAD_WIDTH // 2
    sibling = [(b, b ^ 1) for b in range(count)]
    clock, counter = ring_pairs(chips, 1), ring_pairs(chips, -1)
    width = heads * HEAD_WIDTH
    up = lambda x: lax.ppermute(x, "blk", clock)
    down = lambda x: lax.ppermute(x, "blk", counter)

    sent, x, mark, q_sent, q_own = prepare(queries, keys, values, positions)
    got = lax.ppermute(sent, "blk", sibling)
    header = jnp.concatenate([mark, got[rows : rows + HEADER, :width]], axis=1)
    y = got[:rows]
    x_first, y_first = (jnp.concatenate([part, header], axis=0) for part in (x, y))
    q_got = lax.ppermute(q_sent, "blk", sibling)
    turned = turn(heads, chunk, [q_own, q_got])

    def call(pairs, state, own=False, last=False, fetch=None, which=(0, 1)):
        each = range(len(pairs))
        plan = dict(
            heads=heads,
            chunk=chunk,
            owners=2,
            own=own,
            own_at=lambda i: i,
            last=last,
            members=[(2 * j + i, 0) for j in each for i in range(2)],
            headers=[(1 + 2 * j + pairs[j][2], rows, i * width) for j in each for i in range(2)],
            owner_headers=[(0, rows, 0), (0, rows, width)],
            fetch=fetch,
            which=which,
        )
        packets = [packet for pair in pairs for packet in pair[:2]]
        return attend(plan, turned, [y_first], packets, state, out_weight)

    up_first, up_second, down_first, down_second = x_first, y, y_first, x
    state = call([(x, y_first, 1)], None, own=True)
    held = []
    for r in range(1, half):
        if r > 1:
            up_first, down_first, *state = lax.optimization_barrier((up_first, down_first, *state))
        up_first, up_second = up(up_first), up(up_second)
        down_first, down_second = down(down_first), down(down_second)
        if r > 1:
            *state, more = call(arrived, state, fetch=fetch[len(held) : len(held) + 1])
            held.append(more)
        arrived = [(up_first, up_second, 0), (down_second, down_first, 1)]
    up_first, down_first, *state = lax.optimization_barrier((up_first, down_first, *state))
    far = (up(up_first), down(down_first), 1)
    *state, more = call(arrived, state, fetch=fetch[len(held) :])
    held.append(more)
    (theirs,) = call([far], state, last=True, which=(1,))
    other = lax.ppermute(theirs, "blk", sibling)
    (own,) = call([far], state, last=True, which=(0,))
    return own, other, held


def one_head_a_device(count, queries, keys, values, positions):
    rows, chunk = queries.shape[0], queries.shape[0] // 2
    heads = keys.shape[1] // HEAD_WIDTH
    c = (positions[:1] // chunk).astype(jnp.bfloat16).reshape(1, 1)
    header = jnp.broadcast_to(c, (TILE, 2 * keys.shape[1]))
    packet = jnp.concatenate([jnp.concatenate([keys, values], axis=1), header], axis=0)
    packets = lax.all_gather(packet, "blk", axis=0, tiled=True)
    size = rows + TILE
    here = lax.axis_index("blk")
    order = lax.rem(here + jnp.arange(count), count)
    packets = packets.reshape(count, size, -1)[order].reshape(count * size, -1)
    plan = dict(
        heads=heads,
        chunk=chunk,
        owners=1,
        own=True,
        own_at=lambda i: 0,
        last=True,
        members=[(0, j * size) for j in range(count)],
        headers=[(0, j * size + rows, 0) for j in range(count)],
        owner_headers=[(0, rows, 0)],
    )
    turned = turn(heads, chunk, [queries])
    return attend(plan, turned, [], [packets], None)[0]


def shards(count, inner, queries, keys, values, positions, out_weight):
    heads = keys.shape[1] // HEAD_WIDTH
    if heads % 2:
        attended = one_head_a_device(count, queries, keys, values, positions)
        partial = jnp.dot(attended, out_weight, preferred_element_type=jnp.float32)
        return lax.psum_scatter(
            partial.astype(jnp.bfloat16), "inner", scatter_dimension=0, tiled=True
        )
    out_weight = pltpu.with_memory_space_constraint(out_weight, pltpu.HBM)
    shares = (10, 9, 8, 7, 6)
    widths = [out_weight.shape[1] * share // sum(shares) for share in shares]
    cuts = [(sum(widths[:j]), columns) for j, columns in enumerate(widths)]
    own, other, held = split_over_cores(
        count, queries, keys, values, positions, out_weight, cuts[:3]
    )
    bring = [cuts[j + 2 : j + 3] if j > 0 else [] for j in range(len(cuts))]
    received, kept = [], []
    for j in range(len(cuts)):
        source = own if j == 0 else after(own, sent)
        begun = begin(own, held[0]) if j == 0 else None
        sent, keep, *rest = project(source, other, held[j], out_weight, bring[j], begun)
        held += rest
        received.append(lax.ppermute(sent, "inner", [(0, 1), (1, 0)]))
        kept.append(keep)
    columns = out_weight.shape[1]
    result = finish(kept[:-1], received[:-1], 0, columns)
    return finish(kept[-1:], received[-1:], cuts[-1][0], columns, result)


def solution(mesh):
    placed = (P("blk", "inner"), P("blk", "inner"), P("blk", "inner"), P("blk"), P("inner", None))
    return jax.shard_map(
        functools.partial(shards, mesh.shape["blk"], mesh.shape["inner"]),
        mesh=mesh,
        in_specs=placed,
        out_specs=P(("blk", "inner"), None),
        check_vma=False,
    )
```

```python
import functools
import math

import jax
import jax.numpy as jnp
from jax import lax
from jax.experimental import pallas as pl
from jax.experimental.pallas import tpu as pltpu
from jax.sharding import PartitionSpec as P

HEAD_WIDTH = 128
QUERY_PER_KEY = 5
GROUP = QUERY_PER_KEY * HEAD_WIDTH
EXP2_SCALE = math.log2(math.e) / math.sqrt(HEAD_WIDTH)
MASKED = -1e30
VMEM_LIMIT = 16 * 1024 * 1024
TILE = 16
HEADER = 8
PIECES = 5


def ring_of_chips(chips):
    half = chips // 2
    if chips == 8:
        return [2 * z for z in range(half)] + [2 * z + 1 for z in reversed(range(half))]
    return list(range(half)) + list(reversed(range(half, chips)))


def ring_pairs(chips, step):
    ring = ring_of_chips(chips)
    return [
        (2 * ring[i] + core, 2 * ring[(i + step) % chips] + core)
        for i in range(chips)
        for core in range(2)
    ]


def my_core():
    return lax.rem(lax.axis_index("blk"), 2).astype(jnp.int32)


def product(a, b):
    return jnp.dot(a, b, preferred_element_type=jnp.float32)


def weigh(scores, high):
    return jnp.exp2((scores - high) * EXP2_SCALE).astype(jnp.bfloat16)


def turned_values(blocks):
    v = jnp.concatenate(blocks, axis=0)
    return jnp.concatenate([jnp.transpose(v), jnp.ones((TILE, v.shape[0]), v.dtype)], axis=0)


def fetch_columns(w_ref, first, held_ref, sems, sem):
    depth, width = held_ref.shape[0] // PIECES, held_ref.shape[1]
    copies = []
    for p in range(PIECES):
        at = pl.ds(p * depth, depth)
        copies.append(
            pltpu.make_async_copy(
                w_ref.at[at, pl.ds(first, width)], held_ref.at[at], sems.at[sem + p]
            )
        )
        copies[-1].start()
    return copies


def attend_kernel(plan, *refs):
    heads, chunk, owners = plan["heads"], plan["chunk"], plan["owners"]
    refs = list(refs)
    q_ref = refs.pop(0)
    mark_refs = [refs.pop(0) for _ in range(plan["marks"])]
    packets = [refs.pop(0) for _ in range(plan["packets"])]
    if plan["carried"]:
        in_high, in_sums = refs.pop(0), refs.pop(0)
    fetch = plan["fetch"]
    if fetch:
        w_ref = refs.pop(0)
    if plan["last"]:
        out_refs = {i: refs.pop(0) for i in plan["which"]}
    copies = []
    if fetch:
        sems = refs.pop()
        for n, (first, _) in enumerate(fetch):
            held_ref = refs.pop(0 if plan["last"] else 2)
            copies += fetch_columns(w_ref, first, held_ref, sems, n * PIECES)
    high_ref, sums_ref = refs

    sources = mark_refs + packets
    numbers = [
        jnp.max(
            sources[packet][row : row + HEADER, column : column + HEAD_WIDTH].astype(jnp.float32)
        ).astype(jnp.int32)
        for packet, row, column in plan["owner_headers"] + plan["headers"]
    ]
    owner_c, member_c = numbers[:owners], numbers[owners:]

    def rows_of(j, half, column):
        packet, row = plan["members"][j]
        at = row + half * chunk
        at = at if isinstance(half, int) else pl.multiple_of(at, TILE)
        return packets[packet][pl.ds(at, chunk), pl.ds(column, HEAD_WIDTH)]

    def state_at(i, half, h):
        return (2 * i + half) * heads + h

    rows = QUERY_PER_KEY * chunk
    causal = lax.broadcasted_iota(jnp.int32, (chunk, rows), 0) <= lax.rem(
        lax.broadcasted_iota(jnp.int32, (chunk, rows), 1), chunk
    )
    count = len(plan["members"])

    def one_chain(group, h, i, shared):
        first, done = group[0], group[-1] == count - 1
        k_at = pl.multiple_of(h * HEAD_WIDTH, HEAD_WIDTH)
        v_at = pl.multiple_of((heads + h) * HEAD_WIDTH, HEAD_WIDTH)
        late_at, early_at = state_at(i, 1, h), state_at(i, 0, h)
        if "keys" not in shared:
            shared["keys"] = jnp.concatenate([rows_of(j, 0, k_at) for j in group], axis=0)
            shared["values"] = turned_values([rows_of(j, 0, v_at) for j in group])
        carried = None
        if first > 0:
            carried = [(ref[early_at], ref[late_at]) for ref in (high_ref, sums_ref)]
        elif plan["carried"]:
            carried = [(ref[early_at], ref[late_at]) for ref in (in_high, in_sums)]
        pairs = []
        for j in group:
            if plan["own"] and j == plan["own_at"](i):
                pairs += [(j, 0, causal), (j, 1, causal)]
            else:
                pairs.append((j, (member_c[j] > owner_c[i]).astype(jnp.int32), None))
        base = product(shared["keys"], q_ref[late_at])
        scores = []
        for j, half, mask in pairs:
            s = product(rows_of(j, half, k_at), q_ref[state_at(i, half, h)])
            scores.append(s if mask is None else jnp.where(mask, s, MASKED))
        values = turned_values([rows_of(j, half, v_at) for j, half, _ in pairs])
        tops = [jnp.max(s, axis=0, keepdims=True) for s in scores]
        highs = []
        for side in range(2):
            some = [jnp.where(half == side, top, MASKED) for (_, half, _), top in zip(pairs, tops)]
            if side == 1:
                some.append(jnp.max(base, axis=0, keepdims=True))
            if carried is not None:
                some.append(carried[0][side])
            highs.append(functools.reduce(jnp.maximum, some))
        yield
        base_weights = weigh(base, highs[1])
        weights = [
            weigh(s, jnp.where(half == 1, highs[1], highs[0])) for (_, half, _), s in zip(pairs, scores)
        ]
        zero = jnp.zeros_like(weights[0])
        chosen = [
            jnp.concatenate(
                [jnp.where(half == side, w, zero) for (_, half, _), w in zip(pairs, weights)], axis=0
            )
            for side in range(2)
        ]
        yield
        for side, at in ((0, early_at), (1, late_at)):
            sums = product(values, chosen[side])
            if side == 1:
                sums = sums + product(shared["values"], base_weights)
            if carried is not None:
                shrink = jnp.exp2((carried[0][side] - highs[side]) * EXP2_SCALE)
                sums = sums + carried[1][side] * shrink
            if plan["last"] and done:
                mixed = sums[:HEAD_WIDTH] * (1.0 / sums[HEAD_WIDTH : HEAD_WIDTH + 1])
                mixed = jnp.transpose(mixed.astype(out_refs[i].dtype))
                for g in range(QUERY_PER_KEY):
                    to = pl.multiple_of(h * GROUP + g * HEAD_WIDTH, HEAD_WIDTH)
                    out_refs[i][side * chunk : (side + 1) * chunk, pl.ds(to, HEAD_WIDTH)] = mixed[
                        g * chunk : (g + 1) * chunk
                    ]
            else:
                high_ref[at] = highs[side]
                sums_ref[at] = sums
        yield

    def staggered(chains):
        for t in range(len(chains) + 2):
            for stage in (2, 1, 0):
                if 0 <= t - stage < len(chains):
                    next(chains[t - stage])

    for first in range(0, count, 6):
        group = range(first, min(first + 6, count))

        def run(heads_at_once, group=group):
            chains = []
            for h in heads_at_once:
                shared = {}
                chains += [one_chain(group, h, i, shared) for i in plan["which"]]
            staggered(chains)

        if fetch:

            def one_head(h, carry):
                run([h])
                return carry

            lax.fori_loop(0, heads, one_head, 0)
        else:
            run(range(heads))
    for copy in copies:
        copy.wait()


def attend(plan, turned, marks, packets, state, out_weight=None):
    heads, chunk, owners = plan["heads"], plan["chunk"], plan["owners"]
    count = len(plan["members"])
    plan = dict(plan, marks=len(marks), packets=len(packets), carried=state is not None)
    fetch = plan.setdefault("fetch", None)
    which = plan.setdefault("which", range(owners))
    rows = QUERY_PER_KEY * chunk
    slots = owners * 2 * heads
    vmem = pl.BlockSpec(memory_space=pltpu.VMEM)
    kept = [(slots, 1, rows), (slots, HEAD_WIDTH + TILE, rows)]
    if plan["last"]:
        out_shape = [jax.ShapeDtypeStruct((2 * chunk, heads * GROUP), jnp.bfloat16)] * len(which)
    else:
        out_shape = [jax.ShapeDtypeStruct(shape, jnp.float32) for shape in kept]
    operands = 1 + len(marks) + len(packets) + (0 if state is None else 2)
    in_specs = [vmem] * operands
    scratch = [pltpu.VMEM(shape, jnp.float32) for shape in kept] if plan["last"] else []
    if fetch:
        in_specs.append(pl.BlockSpec(memory_space=pltpu.HBM))
        for _, columns in fetch:
            out_shape.append(jax.ShapeDtypeStruct((out_weight.shape[0], columns), out_weight.dtype))
        scratch.append(pltpu.SemaphoreType.DMA((PIECES * len(fetch),)))
    flops = 4 * owners * heads * rows * HEAD_WIDTH * count * chunk * 2
    return pl.pallas_call(
        functools.partial(attend_kernel, plan),
        out_shape=out_shape,
        in_specs=in_specs,
        out_specs=[vmem] * len(out_shape),
        scratch_shapes=scratch,
        cost_estimate=pl.CostEstimate(
            flops=flops, bytes_accessed=4 << 20, transcendentals=flops // 512
        ),
        compiler_params=pltpu.CompilerParams(vmem_limit_bytes=VMEM_LIMIT),
        name="attend",
    )(turned, *marks, *packets, *(state or ()), *([out_weight] if fetch else []))


def turn_kernel(heads, chunk, *refs):
    q_refs, turned_ref = refs[:-1], refs[-1]
    for i, q_ref in enumerate(q_refs):
        for half in range(2):
            for h in range(heads):
                columns = [slice(at, at + HEAD_WIDTH) for at in range(h * GROUP, (h + 1) * GROUP, HEAD_WIDTH)]
                q = jnp.concatenate(
                    [q_ref[half * chunk : (half + 1) * chunk, at] for at in columns], axis=0
                )
                turned_ref[(2 * i + half) * heads + h] = jnp.transpose(q)


def turn(heads, chunk, queries):
    vmem = pl.BlockSpec(memory_space=pltpu.VMEM)
    owners = len(queries)
    shape = (2 * owners * heads, HEAD_WIDTH, QUERY_PER_KEY * chunk)
    return pl.pallas_call(
        functools.partial(turn_kernel, heads, chunk),
        out_shape=jax.ShapeDtypeStruct(shape, jnp.bfloat16),
        in_specs=[vmem] * owners,
        out_specs=vmem,
        cost_estimate=pl.CostEstimate(flops=1 << 10, bytes_accessed=1 << 10, transcendentals=0),
        compiler_params=pltpu.CompilerParams(vmem_limit_bytes=VMEM_LIMIT),
        name="turn",
    )(*queries)


def leaving_first(ref):
    chunk = ref.shape[0] // 2
    mine = lax.axis_index("inner").astype(jnp.int32)
    halves = [ref[pl.ds(pl.multiple_of(half * chunk, chunk), chunk)] for half in (1 - mine, mine)]
    return jnp.concatenate(halves, axis=0)


def rows_of_core(held_ref, core):
    depth = held_ref.shape[0] // 2
    return held_ref[pl.ds(pl.multiple_of(core * depth, depth), depth)]


def begin_kernel(own_ref, held_ref, begun_ref):
    begun_ref[...] = product(leaving_first(own_ref), rows_of_core(held_ref, my_core()))


def begin(own, held):
    vmem = pl.BlockSpec(memory_space=pltpu.VMEM)
    return pl.pallas_call(
        begin_kernel,
        out_shape=jax.ShapeDtypeStruct((own.shape[0], held.shape[1]), jnp.float32),
        in_specs=[vmem, vmem],
        out_specs=vmem,
        cost_estimate=pl.CostEstimate(flops=1 << 10, bytes_accessed=1 << 10, transcendentals=0),
        compiler_params=pltpu.CompilerParams(vmem_limit_bytes=VMEM_LIMIT),
        name="begin",
    )(own, held)


def project_kernel(bring, begun, own_ref, other_ref, held_ref, *refs):
    refs, copies = list(refs), []
    if bring:
        w_ref, sems = refs.pop(0), refs.pop()
    if begun:
        begun_ref = refs.pop(0)
    sent_ref, kept_ref = refs.pop(0), refs.pop(0)
    for n, (first, _) in enumerate(bring):
        copies += fetch_columns(w_ref, first, refs.pop(0), sems, n * PIECES)
    chunk, core = sent_ref.shape[0], my_core()
    other = leaving_first(other_ref)
    if begun:
        total = begun_ref[...] + product(other, rows_of_core(held_ref, 1 - core))
    else:
        (rows_ref,) = refs
        own, part = leaving_first(own_ref), own_ref.shape[1]
        rows_ref[:, :part] = jnp.where(core == 0, own, other)
        rows_ref[:, part:] = jnp.where(core == 0, other, own)
        total = product(rows_ref[...], held_ref[...])
    both = total.astype(sent_ref.dtype)
    sent_ref[...] = both[:chunk]
    kept_ref[...] = both[chunk:]
    for copy in copies:
        copy.wait()


def project(own, other, held, out_weight, bring, begun=None):
    rows, (depth, width) = own.shape[0], held.shape
    vmem = pl.BlockSpec(memory_space=pltpu.VMEM)
    out_shape = [jax.ShapeDtypeStruct((rows // 2, width), jnp.bfloat16)] * 2
    out_shape += [jax.ShapeDtypeStruct((depth, columns), held.dtype) for _, columns in bring]
    in_specs, operands, scratch = [vmem] * 3, [own, other, held], []
    if begun is None:
        scratch.append(pltpu.VMEM((rows, depth), jnp.bfloat16))
    if bring:
        in_specs.append(pl.BlockSpec(memory_space=pltpu.HBM))
        operands.append(out_weight)
        scratch.append(pltpu.SemaphoreType.DMA((PIECES * len(bring),)))
    if begun is not None:
        in_specs.append(vmem)
        operands.append(begun)
    return pl.pallas_call(
        functools.partial(project_kernel, bring, begun is not None),
        out_shape=out_shape,
        in_specs=in_specs,
        out_specs=[vmem] * len(out_shape),
        scratch_shapes=scratch,
        cost_estimate=pl.CostEstimate(flops=1 << 10, bytes_accessed=1 << 10, transcendentals=0),
        compiler_params=pltpu.CompilerParams(vmem_limit_bytes=VMEM_LIMIT),
        name="project",
    )(*operands)


def prepare_kernel(
    chunk, q_ref, k_ref, v_ref, position_ref, sent_ref, kept_ref, mark_ref, *query_refs_and_scratch
):
    *query_refs, first_ref, sems = query_refs_and_scratch
    rows, width = k_ref.shape[0], k_ref.shape[1] // 2
    columns = query_refs[0].shape[1]
    copies = [pltpu.make_async_copy(position_ref, first_ref, sems.at[4])]
    for n, (ref, core) in enumerate(((sent_ref, 1 - my_core()), (kept_ref, my_core()))):
        at = pl.ds(pl.multiple_of(core * width, width), width)
        for m, source in enumerate((k_ref, v_ref)):
            to = ref.at[pl.ds(0, rows), pl.ds(m * width, width)]
            copies.append(pltpu.make_async_copy(source.at[:, at], to, sems.at[2 * n + m]))
    for n, (ref, core) in enumerate(zip(query_refs, (1 - my_core(), my_core()))):
        at = pl.ds(pl.multiple_of(core * columns, columns), columns)
        copies.append(pltpu.make_async_copy(q_ref.at[:, at], ref, sems.at[5 + n]))
    for copy in copies:
        copy.start()
    copies[0].wait()
    c = lax.div(first_ref[0], jnp.int32(chunk)).astype(jnp.float32)
    mark_ref[...] = jnp.full(mark_ref.shape, c, jnp.float32).astype(jnp.bfloat16)
    sent_ref[rows:] = jnp.full((TILE, 2 * width), c, jnp.float32).astype(jnp.bfloat16)
    for copy in copies[1:]:
        copy.wait()


def prepare(queries, keys, values, positions):
    vmem = pl.BlockSpec(memory_space=pltpu.VMEM)
    hbm = pl.BlockSpec(memory_space=pltpu.HBM)
    rows, width = keys.shape
    operands = [pltpu.with_memory_space_constraint(x, pltpu.HBM) for x in (queries, keys, values, positions)]
    return pl.pallas_call(
        functools.partial(prepare_kernel, rows // 2),
        out_shape=[
            jax.ShapeDtypeStruct((rows + TILE, width), jnp.bfloat16),
            jax.ShapeDtypeStruct((rows, width), jnp.bfloat16),
            jax.ShapeDtypeStruct((HEADER, width // 2), jnp.bfloat16),
        ]
        + [jax.ShapeDtypeStruct((rows, queries.shape[1] // 2), jnp.bfloat16)] * 2,
        in_specs=[hbm] * 4,
        out_specs=[vmem] * 5,
        scratch_shapes=[
            pltpu.SMEM(positions.shape, jnp.int32),
            pltpu.SemaphoreType.DMA((7,)),
        ],
        compiler_params=pltpu.CompilerParams(vmem_limit_bytes=VMEM_LIMIT),
        name="prepare",
    )(*operands)


def finish_kernel(first, pairs, *refs):
    out_ref, total_ref, sem = refs[-3:]
    at = 0
    for mine, theirs in zip(refs[:pairs], refs[pairs : 2 * pairs]):
        width = mine.shape[1]
        total = mine[...].astype(jnp.float32) + theirs[...].astype(jnp.float32)
        total_ref[:, at : at + width] = total.astype(total_ref.dtype)
        at += width
    copy = pltpu.make_async_copy(total_ref, out_ref.at[:, pl.ds(first, at)], sem)
    copy.start()
    copy.wait()


def finish(kept, received, first, columns, written=None):
    vmem, hbm = pl.BlockSpec(memory_space=pltpu.VMEM), pl.BlockSpec(memory_space=pltpu.HBM)
    rows, width = kept[0].shape[0], sum(part.shape[1] for part in kept)
    pairs = len(kept)
    return pl.pallas_call(
        functools.partial(finish_kernel, first, pairs),
        out_shape=jax.ShapeDtypeStruct((rows, columns), kept[0].dtype),
        in_specs=[vmem] * (2 * pairs) + ([] if written is None else [hbm]),
        out_specs=hbm,
        input_output_aliases={} if written is None else {2 * pairs: 0},
        scratch_shapes=[pltpu.VMEM((rows, width), kept[0].dtype), pltpu.SemaphoreType.DMA],
        cost_estimate=pl.CostEstimate(flops=1 << 10, bytes_accessed=1 << 10, transcendentals=0),
        compiler_params=pltpu.CompilerParams(vmem_limit_bytes=VMEM_LIMIT),
        name="finish",
    )(*kept, *received, *([] if written is None else [written]))


def after(value, *events):
    return lax.optimization_barrier((value, *events))[0]


def split_over_cores(count, queries, keys, values, positions, out_weight, fetch):
    chips, half = count // 2, count // 4
    rows, chunk = queries.shape[0], queries.shape[0] // 2
    heads = keys.shape[1] // HEAD_WIDTH // 2
    sibling = [(b, b ^ 1) for b in range(count)]
    clock, counter = ring_pairs(chips, 1), ring_pairs(chips, -1)
    width = heads * HEAD_WIDTH
    up = lambda x: lax.ppermute(x, "blk", clock)
    down = lambda x: lax.ppermute(x, "blk", counter)

    sent, x, mark, q_sent, q_own = prepare(queries, keys, values, positions)
    got = lax.ppermute(sent, "blk", sibling)
    header = jnp.concatenate([mark, got[rows : rows + HEADER, :width]], axis=1)
    y = got[:rows]
    x_first, y_first = (jnp.concatenate([part, header], axis=0) for part in (x, y))
    q_got = lax.ppermute(q_sent, "blk", sibling)
    turned = turn(heads, chunk, [q_own, q_got])

    def call(pairs, state, own=False, last=False, fetch=None, which=(0, 1)):
        each = range(len(pairs))
        plan = dict(
            heads=heads,
            chunk=chunk,
            owners=2,
            own=own,
            own_at=lambda i: i,
            last=last,
            members=[(2 * j + i, 0) for j in each for i in range(2)],
            headers=[(1 + 2 * j + pairs[j][2], rows, i * width) for j in each for i in range(2)],
            owner_headers=[(0, rows, 0), (0, rows, width)],
            fetch=fetch,
            which=which,
        )
        packets = [packet for pair in pairs for packet in pair[:2]]
        return attend(plan, turned, [y_first], packets, state, out_weight)

    up_first, up_second, down_first, down_second = x_first, y, y_first, x
    held = {}

    def bring_with(groups, *arguments, **settings):
        cuts = [fetch[j] for j in groups]
        results = call(*arguments, fetch=cuts, **settings)
        held.update(zip(groups, results[2:]))
        return results[:2]

    state = bring_with((2, 3), [(x, y_first, 1)], None, own=True)
    for r in range(1, half):
        if r > 1:
            up_first, down_first, *state = lax.optimization_barrier((up_first, down_first, *state))
        up_first, up_second = up(up_first), up(up_second)
        down_first, down_second = down(down_first), down(down_second)
        if r > 1:
            state = bring_with((r - 2,), arrived, state)
        arrived = [(up_first, up_second, 0), (down_second, down_first, 1)]
    up_first, down_first, *state = lax.optimization_barrier((up_first, down_first, *state))
    far = (up(up_first), down(down_first), 1)
    state = call(arrived, state)
    (theirs,) = call([far], state, last=True, which=(1,))
    other = lax.ppermute(theirs, "blk", sibling)
    (own,) = call([far], state, last=True, which=(0,))
    return own, other, held


def one_head_a_device(count, queries, keys, values, positions):
    rows, chunk = queries.shape[0], queries.shape[0] // 2
    heads = keys.shape[1] // HEAD_WIDTH
    c = (positions[:1] // chunk).astype(jnp.bfloat16).reshape(1, 1)
    header = jnp.broadcast_to(c, (TILE, 2 * keys.shape[1]))
    packet = jnp.concatenate([jnp.concatenate([keys, values], axis=1), header], axis=0)
    packets = lax.all_gather(packet, "blk", axis=0, tiled=True)
    size = rows + TILE
    here = lax.axis_index("blk")
    order = lax.rem(here + jnp.arange(count), count)
    packets = packets.reshape(count, size, -1)[order].reshape(count * size, -1)
    plan = dict(
        heads=heads,
        chunk=chunk,
        owners=1,
        own=True,
        own_at=lambda i: 0,
        last=True,
        members=[(0, j * size) for j in range(count)],
        headers=[(0, j * size + rows, 0) for j in range(count)],
        owner_headers=[(0, rows, 0)],
    )
    turned = turn(heads, chunk, [queries])
    return attend(plan, turned, [], [packets], None)[0]


def shards(count, inner, queries, keys, values, positions, out_weight):
    heads = keys.shape[1] // HEAD_WIDTH
    if heads % 2:
        attended = one_head_a_device(count, queries, keys, values, positions)
        partial = jnp.dot(attended, out_weight, preferred_element_type=jnp.float32)
        return lax.psum_scatter(
            partial.astype(jnp.bfloat16), "inner", scatter_dimension=0, tiled=True
        )
    out_weight = pltpu.with_memory_space_constraint(out_weight, pltpu.HBM)
    shares = (10, 9, 8, 7, 6)
    widths = [out_weight.shape[1] * share // sum(shares) for share in shares]
    cuts = [(sum(widths[:j]), columns) for j, columns in enumerate(widths)]
    own, other, held = split_over_cores(
        count, queries, keys, values, positions, out_weight, cuts[:4]
    )
    bring = [cuts[4:] if j == 2 else [] for j in range(len(cuts))]
    received, kept = [], []
    for j in range(len(cuts)):
        source = own if j == 0 else after(own, sent)
        begun = begin(own, held[0]) if j == 0 else None
        sent, keep, *rest = project(source, other, held[j], out_weight, bring[j], begun)
        if rest:
            held[len(held)] = rest[0]
        received.append(lax.ppermute(sent, "inner", [(0, 1), (1, 0)]))
        kept.append(keep)
    columns = out_weight.shape[1]
    result = finish(kept[:-1], received[:-1], 0, columns)
    return finish(kept[-1:], received[-1:], cuts[-1][0], columns, result)


def solution(mesh):
    placed = (P("blk", "inner"), P("blk", "inner"), P("blk", "inner"), P("blk"), P("inner", None))
    return jax.shard_map(
        functools.partial(shards, mesh.shape["blk"], mesh.shape["inner"]),
        mesh=mesh,
        in_specs=placed,
        out_specs=P(("blk", "inner"), None),
        check_vma=False,
    )
```

```python
import functools
import math

import jax
import jax.numpy as jnp
from jax import lax
from jax.experimental import pallas as pl
from jax.experimental.pallas import tpu as pltpu
from jax.sharding import PartitionSpec as P

HEAD_WIDTH = 128
QUERY_PER_KEY = 5
GROUP = QUERY_PER_KEY * HEAD_WIDTH
EXP2_SCALE = math.log2(math.e) / math.sqrt(HEAD_WIDTH)
MASKED = -1e30
VMEM_LIMIT = 16 * 1024 * 1024
TILE = 16
HEADER = 8
PIECES = 5


def ring_of_chips(chips):
    half = chips // 2
    if chips == 8:
        return [2 * z for z in range(half)] + [2 * z + 1 for z in reversed(range(half))]
    return list(range(half)) + list(reversed(range(half, chips)))


def ring_pairs(chips, step, cross=False):
    ring = ring_of_chips(chips)
    return [
        (2 * ring[i] + core, 2 * ring[(i + step) % chips] + (1 - core if cross else core))
        for i in range(chips)
        for core in range(2)
    ]


def my_core():
    return lax.rem(lax.axis_index("blk"), 2).astype(jnp.int32)


def product(a, b):
    return jnp.dot(a, b, preferred_element_type=jnp.float32)


def weigh(scores, high):
    return jnp.exp2((scores - high) * EXP2_SCALE).astype(jnp.bfloat16)


def turned_values(blocks):
    v = jnp.concatenate(blocks, axis=0)
    return jnp.concatenate([jnp.transpose(v), jnp.ones((TILE, v.shape[0]), v.dtype)], axis=0)


def fetch_columns(w_ref, first, held_ref, sems, sem):
    depth, width = held_ref.shape[0] // PIECES, held_ref.shape[1]
    copies = []
    for p in range(PIECES):
        at = pl.ds(p * depth, depth)
        copies.append(
            pltpu.make_async_copy(
                w_ref.at[at, pl.ds(first, width)], held_ref.at[at], sems.at[sem + p]
            )
        )
        copies[-1].start()
    return copies


def attend_kernel(plan, *refs):
    heads, chunk, owners = plan["heads"], plan["chunk"], plan["owners"]
    refs = list(refs)
    q_ref = refs.pop(0)
    mark_refs = [refs.pop(0) for _ in range(plan["marks"])]
    packets = [refs.pop(0) for _ in range(plan["packets"])]
    if plan["carried"]:
        in_high, in_sums = refs.pop(0), refs.pop(0)
    fetch = plan["fetch"]
    if fetch:
        w_ref = refs.pop(0)
    if plan["last"]:
        out_refs = {i: refs.pop(0) for i in plan["which"]}
    copies = []
    if fetch:
        sems = refs.pop()
        for n, (first, _) in enumerate(fetch):
            held_ref = refs.pop(0 if plan["last"] else 2)
            copies += fetch_columns(w_ref, first, held_ref, sems, n * PIECES)
    high_ref, sums_ref = refs

    sources = mark_refs + packets
    numbers = [
        jnp.max(
            sources[packet][row : row + HEADER, column : column + HEAD_WIDTH].astype(jnp.float32)
        ).astype(jnp.int32)
        for packet, row, column in plan["owner_headers"] + plan["headers"]
    ]
    owner_c, member_c = numbers[:owners], numbers[owners:]

    def rows_of(j, half, column):
        packet, row = plan["members"][j]
        at = row + half * chunk
        at = at if isinstance(half, int) else pl.multiple_of(at, TILE)
        return packets[packet][pl.ds(at, chunk), pl.ds(column, HEAD_WIDTH)]

    def state_at(i, half, h):
        return (2 * i + half) * heads + h

    rows = QUERY_PER_KEY * chunk
    causal = lax.broadcasted_iota(jnp.int32, (chunk, rows), 0) <= lax.rem(
        lax.broadcasted_iota(jnp.int32, (chunk, rows), 1), chunk
    )
    count = len(plan["members"])

    def one_chain(group, h, i, shared):
        first, done = group[0], group[-1] == count - 1
        k_at = pl.multiple_of(h * HEAD_WIDTH, HEAD_WIDTH)
        v_at = pl.multiple_of((heads + h) * HEAD_WIDTH, HEAD_WIDTH)
        late_at, early_at = state_at(i, 1, h), state_at(i, 0, h)
        if "keys" not in shared:
            shared["keys"] = jnp.concatenate([rows_of(j, 0, k_at) for j in group], axis=0)
            shared["values"] = turned_values([rows_of(j, 0, v_at) for j in group])
        carried = None
        if first > 0:
            carried = [(ref[early_at], ref[late_at]) for ref in (high_ref, sums_ref)]
        elif plan["carried"]:
            carried = [(ref[early_at], ref[late_at]) for ref in (in_high, in_sums)]
        pairs = []
        for j in group:
            if plan["own"] and j == plan["own_at"](i):
                pairs += [(j, 0, causal), (j, 1, causal)]
            else:
                pairs.append((j, (member_c[j] > owner_c[i]).astype(jnp.int32), None))
        base = product(shared["keys"], q_ref[late_at])
        scores = []
        for j, half, mask in pairs:
            s = product(rows_of(j, half, k_at), q_ref[state_at(i, half, h)])
            scores.append(s if mask is None else jnp.where(mask, s, MASKED))
        values = turned_values([rows_of(j, half, v_at) for j, half, _ in pairs])
        tops = [jnp.max(s, axis=0, keepdims=True) for s in scores]
        highs = []
        for side in range(2):
            some = [jnp.where(half == side, top, MASKED) for (_, half, _), top in zip(pairs, tops)]
            if side == 1:
                some.append(jnp.max(base, axis=0, keepdims=True))
            if carried is not None:
                some.append(carried[0][side])
            highs.append(functools.reduce(jnp.maximum, some))
        yield
        base_weights = weigh(base, highs[1])
        weights = [
            weigh(s, jnp.where(half == 1, highs[1], highs[0])) for (_, half, _), s in zip(pairs, scores)
        ]
        zero = jnp.zeros_like(weights[0])
        chosen = [
            jnp.concatenate(
                [jnp.where(half == side, w, zero) for (_, half, _), w in zip(pairs, weights)], axis=0
            )
            for side in range(2)
        ]
        yield
        for side, at in ((0, early_at), (1, late_at)):
            sums = product(values, chosen[side])
            if side == 1:
                sums = sums + product(shared["values"], base_weights)
            if carried is not None:
                shrink = jnp.exp2((carried[0][side] - highs[side]) * EXP2_SCALE)
                sums = sums + carried[1][side] * shrink
            if plan["last"] and done:
                mixed = sums[:HEAD_WIDTH] * (1.0 / sums[HEAD_WIDTH : HEAD_WIDTH + 1])
                mixed = jnp.transpose(mixed.astype(out_refs[i].dtype))
                for g in range(QUERY_PER_KEY):
                    to = pl.multiple_of(h * GROUP + g * HEAD_WIDTH, HEAD_WIDTH)
                    out_refs[i][side * chunk : (side + 1) * chunk, pl.ds(to, HEAD_WIDTH)] = mixed[
                        g * chunk : (g + 1) * chunk
                    ]
            else:
                high_ref[at] = highs[side]
                sums_ref[at] = sums
        yield

    def staggered(chains):
        for t in range(len(chains) + 2):
            for stage in (2, 1, 0):
                if 0 <= t - stage < len(chains):
                    next(chains[t - stage])

    for first in range(0, count, 6):
        group = range(first, min(first + 6, count))

        def run(heads_at_once, group=group):
            chains = []
            for h in heads_at_once:
                shared = {}
                chains += [one_chain(group, h, i, shared) for i in plan["which"]]
            staggered(chains)

        if fetch:

            def one_head(h, carry):
                run([h])
                return carry

            lax.fori_loop(0, heads, one_head, 0)
        else:
            run(range(heads))
    for copy in copies:
        copy.wait()


def attend(plan, turned, marks, packets, state, out_weight=None):
    heads, chunk, owners = plan["heads"], plan["chunk"], plan["owners"]
    count = len(plan["members"])
    plan = dict(plan, marks=len(marks), packets=len(packets), carried=state is not None)
    fetch = plan.setdefault("fetch", None)
    which = plan.setdefault("which", range(owners))
    rows = QUERY_PER_KEY * chunk
    slots = owners * 2 * heads
    vmem = pl.BlockSpec(memory_space=pltpu.VMEM)
    kept = [(slots, 1, rows), (slots, HEAD_WIDTH + TILE, rows)]
    if plan["last"]:
        out_shape = [jax.ShapeDtypeStruct((2 * chunk, heads * GROUP), jnp.bfloat16)] * len(which)
    else:
        out_shape = [jax.ShapeDtypeStruct(shape, jnp.float32) for shape in kept]
    operands = 1 + len(marks) + len(packets) + (0 if state is None else 2)
    in_specs = [vmem] * operands
    scratch = [pltpu.VMEM(shape, jnp.float32) for shape in kept] if plan["last"] else []
    if fetch:
        in_specs.append(pl.BlockSpec(memory_space=pltpu.HBM))
        for _, columns in fetch:
            out_shape.append(jax.ShapeDtypeStruct((out_weight.shape[0], columns), out_weight.dtype))
        scratch.append(pltpu.SemaphoreType.DMA((PIECES * len(fetch),)))
    flops = 4 * owners * heads * rows * HEAD_WIDTH * count * chunk * 2
    return pl.pallas_call(
        functools.partial(attend_kernel, plan),
        out_shape=out_shape,
        in_specs=in_specs,
        out_specs=[vmem] * len(out_shape),
        scratch_shapes=scratch,
        cost_estimate=pl.CostEstimate(
            flops=flops, bytes_accessed=4 << 20, transcendentals=flops // 512
        ),
        compiler_params=pltpu.CompilerParams(vmem_limit_bytes=VMEM_LIMIT),
        name="attend",
    )(turned, *marks, *packets, *(state or ()), *([out_weight] if fetch else []))


def turn_kernel(heads, chunk, *refs):
    q_refs, turned_ref = refs[:-1], refs[-1]
    for i, q_ref in enumerate(q_refs):
        for half in range(2):
            for h in range(heads):
                columns = [slice(at, at + HEAD_WIDTH) for at in range(h * GROUP, (h + 1) * GROUP, HEAD_WIDTH)]
                q = jnp.concatenate(
                    [q_ref[half * chunk : (half + 1) * chunk, at] for at in columns], axis=0
                )
                turned_ref[(2 * i + half) * heads + h] = jnp.transpose(q)


def turn(heads, chunk, queries):
    vmem = pl.BlockSpec(memory_space=pltpu.VMEM)
    owners = len(queries)
    shape = (2 * owners * heads, HEAD_WIDTH, QUERY_PER_KEY * chunk)
    return pl.pallas_call(
        functools.partial(turn_kernel, heads, chunk),
        out_shape=jax.ShapeDtypeStruct(shape, jnp.bfloat16),
        in_specs=[vmem] * owners,
        out_specs=vmem,
        cost_estimate=pl.CostEstimate(flops=1 << 10, bytes_accessed=1 << 10, transcendentals=0),
        compiler_params=pltpu.CompilerParams(vmem_limit_bytes=VMEM_LIMIT),
        name="turn",
    )(*queries)


def leaving_first(ref):
    chunk = ref.shape[0] // 2
    mine = lax.axis_index("inner").astype(jnp.int32)
    halves = [ref[pl.ds(pl.multiple_of(half * chunk, chunk), chunk)] for half in (1 - mine, mine)]
    return jnp.concatenate(halves, axis=0)


def rows_of_core(held_ref, core):
    depth = held_ref.shape[0] // 2
    return held_ref[pl.ds(pl.multiple_of(core * depth, depth), depth)]


def begin_kernel(own_ref, held_ref, begun_ref):
    begun_ref[...] = product(leaving_first(own_ref), rows_of_core(held_ref, my_core()))


def begin(own, held):
    vmem = pl.BlockSpec(memory_space=pltpu.VMEM)
    return pl.pallas_call(
        begin_kernel,
        out_shape=jax.ShapeDtypeStruct((own.shape[0], held.shape[1]), jnp.float32),
        in_specs=[vmem, vmem],
        out_specs=vmem,
        cost_estimate=pl.CostEstimate(flops=1 << 10, bytes_accessed=1 << 10, transcendentals=0),
        compiler_params=pltpu.CompilerParams(vmem_limit_bytes=VMEM_LIMIT),
        name="begin",
    )(own, held)


def project_kernel(bring, begun, own_ref, other_ref, held_ref, *refs):
    refs, copies = list(refs), []
    if bring:
        w_ref, sems = refs.pop(0), refs.pop()
    if begun:
        begun_ref = refs.pop(0)
    sent_ref, kept_ref = refs.pop(0), refs.pop(0)
    for n, (first, _) in enumerate(bring):
        copies += fetch_columns(w_ref, first, refs.pop(0), sems, n * PIECES)
    chunk, core = sent_ref.shape[0], my_core()
    other = leaving_first(other_ref)
    if begun:
        total = begun_ref[...] + product(other, rows_of_core(held_ref, 1 - core))
    else:
        (rows_ref,) = refs
        own, part = leaving_first(own_ref), own_ref.shape[1]
        rows_ref[:, :part] = jnp.where(core == 0, own, other)
        rows_ref[:, part:] = jnp.where(core == 0, other, own)
        total = product(rows_ref[...], held_ref[...])
    both = total.astype(sent_ref.dtype)
    sent_ref[...] = both[:chunk]
    kept_ref[...] = both[chunk:]
    for copy in copies:
        copy.wait()


def project(own, other, held, out_weight, bring, begun=None):
    rows, (depth, width) = own.shape[0], held.shape
    vmem = pl.BlockSpec(memory_space=pltpu.VMEM)
    out_shape = [jax.ShapeDtypeStruct((rows // 2, width), jnp.bfloat16)] * 2
    out_shape += [jax.ShapeDtypeStruct((depth, columns), held.dtype) for _, columns in bring]
    in_specs, operands, scratch = [vmem] * 3, [own, other, held], []
    if begun is None:
        scratch.append(pltpu.VMEM((rows, depth), jnp.bfloat16))
    if bring:
        in_specs.append(pl.BlockSpec(memory_space=pltpu.HBM))
        operands.append(out_weight)
        scratch.append(pltpu.SemaphoreType.DMA((PIECES * len(bring),)))
    if begun is not None:
        in_specs.append(vmem)
        operands.append(begun)
    return pl.pallas_call(
        functools.partial(project_kernel, bring, begun is not None),
        out_shape=out_shape,
        in_specs=in_specs,
        out_specs=[vmem] * len(out_shape),
        scratch_shapes=scratch,
        cost_estimate=pl.CostEstimate(flops=1 << 10, bytes_accessed=1 << 10, transcendentals=0),
        compiler_params=pltpu.CompilerParams(vmem_limit_bytes=VMEM_LIMIT),
        name="project",
    )(*operands)


def prepare_kernel(
    chunk, q_ref, k_ref, v_ref, position_ref, sent_ref, kept_ref, *query_refs_and_scratch
):
    *query_refs, first_ref, sems = query_refs_and_scratch
    rows, width = k_ref.shape[0], k_ref.shape[1] // 2
    columns = query_refs[0].shape[1]
    copies = [pltpu.make_async_copy(position_ref, first_ref, sems.at[4])]
    for n, (ref, core) in enumerate(((sent_ref, 1 - my_core()), (kept_ref, my_core()))):
        at = pl.ds(pl.multiple_of(core * width, width), width)
        for m, source in enumerate((k_ref, v_ref)):
            to = ref.at[pl.ds(0, rows), pl.ds(m * width, width)]
            copies.append(pltpu.make_async_copy(source.at[:, at], to, sems.at[2 * n + m]))
    for n, (ref, core) in enumerate(zip(query_refs, (1 - my_core(), my_core()))):
        at = pl.ds(pl.multiple_of(core * columns, columns), columns)
        copies.append(pltpu.make_async_copy(q_ref.at[:, at], ref, sems.at[5 + n]))
    for copy in copies:
        copy.start()
    copies[0].wait()
    c = lax.div(first_ref[0], jnp.int32(chunk)).astype(jnp.float32)
    header = jnp.full((HEADER, 2 * width), c, jnp.float32).astype(jnp.bfloat16)
    sent_ref[rows:] = header
    kept_ref[rows:] = header
    for copy in copies[1:]:
        copy.wait()


def prepare(queries, keys, values, positions):
    vmem = pl.BlockSpec(memory_space=pltpu.VMEM)
    hbm = pl.BlockSpec(memory_space=pltpu.HBM)
    rows, width = keys.shape
    operands = [pltpu.with_memory_space_constraint(x, pltpu.HBM) for x in (queries, keys, values, positions)]
    return pl.pallas_call(
        functools.partial(prepare_kernel, rows // 2),
        out_shape=[jax.ShapeDtypeStruct((rows + HEADER, width), jnp.bfloat16)] * 2
        + [jax.ShapeDtypeStruct((rows, queries.shape[1] // 2), jnp.bfloat16)] * 2,
        in_specs=[hbm] * 4,
        out_specs=[vmem] * 4,
        scratch_shapes=[
            pltpu.SMEM(positions.shape, jnp.int32),
            pltpu.SemaphoreType.DMA((7,)),
        ],
        compiler_params=pltpu.CompilerParams(vmem_limit_bytes=VMEM_LIMIT),
        name="prepare",
    )(*operands)


def finish_kernel(first, pairs, *refs):
    out_ref, total_ref, sem = refs[-3:]
    at = 0
    for mine, theirs in zip(refs[:pairs], refs[pairs : 2 * pairs]):
        width = mine.shape[1]
        total = mine[...].astype(jnp.float32) + theirs[...].astype(jnp.float32)
        total_ref[:, at : at + width] = total.astype(total_ref.dtype)
        at += width
    copy = pltpu.make_async_copy(total_ref, out_ref.at[:, pl.ds(first, at)], sem)
    copy.start()
    copy.wait()


def finish(kept, received, first, columns, written=None):
    vmem, hbm = pl.BlockSpec(memory_space=pltpu.VMEM), pl.BlockSpec(memory_space=pltpu.HBM)
    rows, width = kept[0].shape[0], sum(part.shape[1] for part in kept)
    pairs = len(kept)
    return pl.pallas_call(
        functools.partial(finish_kernel, first, pairs),
        out_shape=jax.ShapeDtypeStruct((rows, columns), kept[0].dtype),
        in_specs=[vmem] * (2 * pairs) + ([] if written is None else [hbm]),
        out_specs=hbm,
        input_output_aliases={} if written is None else {2 * pairs: 0},
        scratch_shapes=[pltpu.VMEM((rows, width), kept[0].dtype), pltpu.SemaphoreType.DMA],
        cost_estimate=pl.CostEstimate(flops=1 << 10, bytes_accessed=1 << 10, transcendentals=0),
        compiler_params=pltpu.CompilerParams(vmem_limit_bytes=VMEM_LIMIT),
        name="finish",
    )(*kept, *received, *([] if written is None else [written]))


def after(value, *events):
    return lax.optimization_barrier((value, *events))[0]


def split_over_cores(count, queries, keys, values, positions, out_weight, fetch):
    chips, half = count // 2, count // 4
    rows, chunk = queries.shape[0], queries.shape[0] // 2
    heads = keys.shape[1] // HEAD_WIDTH // 2
    sibling = [(b, b ^ 1) for b in range(count)]
    clock, counter = ring_pairs(chips, 1), ring_pairs(chips, -1)
    up = lambda x: lax.ppermute(x, "blk", clock)
    down = lambda x: lax.ppermute(x, "blk", counter)
    cross_up, cross_down = ring_pairs(chips, 1, True), ring_pairs(chips, -1, True)

    sent, x, q_sent, q_own = prepare(queries, keys, values, positions)
    y = lax.ppermute(sent, "blk", sibling)
    q_got = lax.ppermute(q_sent, "blk", sibling)
    turned = turn(heads, chunk, [q_own, q_got])

    def call(pairs, state, own=False, last=False, fetch=None, which=(0, 1)):
        each = range(len(pairs))
        plan = dict(
            heads=heads,
            chunk=chunk,
            owners=2,
            own=own,
            own_at=lambda i: i,
            last=last,
            members=[(2 * j + i, 0) for j in each for i in range(2)],
            headers=[(2 + 2 * j + i, rows, 0) for j in each for i in range(2)],
            owner_headers=[(0, rows, 0), (1, rows, 0)],
            fetch=fetch,
            which=which,
        )
        packets = [packet for pair in pairs for packet in pair]
        return attend(plan, turned, [x, y], packets, state, out_weight)

    held = {}

    def bring_with(groups, *arguments, **settings):
        cuts = [fetch[j] for j in groups]
        results = call(*arguments, fetch=cuts, **settings)
        held.update(zip(groups, results[2:]))
        return results[:2]

    state = bring_with((2, 3), [(x, y)], None, own=True)
    for r in range(1, half):
        if r == 1:
            up_first, up_second = up(x), lax.ppermute(sent, "blk", cross_up)
            down_first, down_second = lax.ppermute(sent, "blk", cross_down), down(x)
        else:
            up_first, down_first, *state = lax.optimization_barrier((up_first, down_first, *state))
            up_first, up_second = up(up_first), up(up_second)
            down_first, down_second = down(down_first), down(down_second)
            state = bring_with((r - 2,), arrived, state)
        arrived = [(up_first, up_second), (down_second, down_first)]
    up_first, down_first, *state = lax.optimization_barrier((up_first, down_first, *state))
    far = (up(up_first), down(down_first))
    state = call(arrived, state)
    (theirs,) = call([far], state, last=True, which=(1,))
    other = lax.ppermute(theirs, "blk", sibling)
    (own,) = call([far], state, last=True, which=(0,))
    return own, other, held


def one_head_a_device(count, queries, keys, values, positions):
    rows, chunk = queries.shape[0], queries.shape[0] // 2
    heads = keys.shape[1] // HEAD_WIDTH
    c = (positions[:1] // chunk).astype(jnp.bfloat16).reshape(1, 1)
    header = jnp.broadcast_to(c, (TILE, 2 * keys.shape[1]))
    packet = jnp.concatenate([jnp.concatenate([keys, values], axis=1), header], axis=0)
    packets = lax.all_gather(packet, "blk", axis=0, tiled=True)
    size = rows + TILE
    here = lax.axis_index("blk")
    order = lax.rem(here + jnp.arange(count), count)
    packets = packets.reshape(count, size, -1)[order].reshape(count * size, -1)
    plan = dict(
        heads=heads,
        chunk=chunk,
        owners=1,
        own=True,
        own_at=lambda i: 0,
        last=True,
        members=[(0, j * size) for j in range(count)],
        headers=[(0, j * size + rows, 0) for j in range(count)],
        owner_headers=[(0, rows, 0)],
    )
    turned = turn(heads, chunk, [queries])
    return attend(plan, turned, [], [packets], None)[0]


def shards(count, inner, queries, keys, values, positions, out_weight):
    heads = keys.shape[1] // HEAD_WIDTH
    if heads % 2:
        attended = one_head_a_device(count, queries, keys, values, positions)
        partial = jnp.dot(attended, out_weight, preferred_element_type=jnp.float32)
        return lax.psum_scatter(
            partial.astype(jnp.bfloat16), "inner", scatter_dimension=0, tiled=True
        )
    out_weight = pltpu.with_memory_space_constraint(out_weight, pltpu.HBM)
    shares = (10, 9, 8, 7, 6)
    widths = [out_weight.shape[1] * share // sum(shares) for share in shares]
    cuts = [(sum(widths[:j]), columns) for j, columns in enumerate(widths)]
    own, other, held = split_over_cores(
        count, queries, keys, values, positions, out_weight, cuts[:4]
    )
    bring = [cuts[4:] if j == 2 else [] for j in range(len(cuts))]
    received, kept = [], []
    for j in range(len(cuts)):
        source = own if j == 0 else after(own, sent)
        begun = begin(own, held[0]) if j == 0 else None
        sent, keep, *rest = project(source, other, held[j], out_weight, bring[j], begun)
        if rest:
            held[len(held)] = rest[0]
        received.append(lax.ppermute(sent, "inner", [(0, 1), (1, 0)]))
        kept.append(keep)
    columns = out_weight.shape[1]
    result = finish(kept[:-1], received[:-1], 0, columns)
    return finish(kept[-1:], received[-1:], cuts[-1][0], columns, result)


def solution(mesh):
    placed = (P("blk", "inner"), P("blk", "inner"), P("blk", "inner"), P("blk"), P("inner", None))
    return jax.shard_map(
        functools.partial(shards, mesh.shape["blk"], mesh.shape["inner"]),
        mesh=mesh,
        in_specs=placed,
        out_specs=P(("blk", "inner"), None),
        check_vma=False,
    )
```

```python
import functools
import math

import jax
import jax.numpy as jnp
from jax import lax
from jax.experimental import pallas as pl
from jax.experimental.pallas import tpu as pltpu
from jax.sharding import PartitionSpec as P

HEAD_WIDTH = 128
QUERY_PER_KEY = 5
GROUP = QUERY_PER_KEY * HEAD_WIDTH
EXP2_SCALE = math.log2(math.e) / math.sqrt(HEAD_WIDTH)
MASKED = -1e30
VMEM_LIMIT = 16 * 1024 * 1024
TILE = 16
HEADER = 8
PIECES = 5


def ring_of_chips(chips):
    half = chips // 2
    if chips == 8:
        return [2 * z for z in range(half)] + [2 * z + 1 for z in reversed(range(half))]
    return list(range(half)) + list(reversed(range(half, chips)))


def ring_pairs(chips, step, cross=False):
    ring = ring_of_chips(chips)
    return [
        (2 * ring[i] + core, 2 * ring[(i + step) % chips] + (1 - core if cross else core))
        for i in range(chips)
        for core in range(2)
    ]


def my_core():
    return lax.rem(lax.axis_index("blk"), 2).astype(jnp.int32)


def product(a, b):
    return jnp.dot(a, b, preferred_element_type=jnp.float32)


def weigh(scores, high):
    return jnp.exp2((scores - high) * EXP2_SCALE).astype(jnp.bfloat16)


def turned_values(blocks):
    v = jnp.concatenate(blocks, axis=0)
    return jnp.concatenate([jnp.transpose(v), jnp.ones((TILE, v.shape[0]), v.dtype)], axis=0)


def fetch_columns(w_ref, first, held_ref, sems, sem):
    depth, width = held_ref.shape[0] // PIECES, held_ref.shape[1]
    copies = []
    for p in range(PIECES):
        at = pl.ds(p * depth, depth)
        copies.append(
            pltpu.make_async_copy(
                w_ref.at[at, pl.ds(first, width)], held_ref.at[at], sems.at[sem + p]
            )
        )
        copies[-1].start()
    return copies


def attend_kernel(plan, *refs):
    heads, chunk, owners = plan["heads"], plan["chunk"], plan["owners"]
    refs = list(refs)
    q_ref = refs.pop(0)
    mark_refs = [refs.pop(0) for _ in range(plan["marks"])]
    packets = [refs.pop(0) for _ in range(plan["packets"])]
    if plan["carried"]:
        in_high, in_sums = refs.pop(0), refs.pop(0)
    fetch = plan["fetch"]
    if fetch:
        w_ref = refs.pop(0)
    if plan["last"]:
        out_refs = {i: refs.pop(0) for i in plan["which"]}
    copies = []
    if fetch:
        sems = refs.pop()
        for n, (first, _) in enumerate(fetch):
            held_ref = refs.pop(0 if plan["last"] else 2)
            copies += fetch_columns(w_ref, first, held_ref, sems, n * PIECES)
    high_ref, sums_ref = refs

    sources = mark_refs + packets
    numbers = [
        jnp.max(
            sources[packet][row : row + HEADER, column : column + HEAD_WIDTH].astype(jnp.float32)
        ).astype(jnp.int32)
        for packet, row, column in plan["owner_headers"] + plan["headers"]
    ]
    owner_c, member_c = numbers[:owners], numbers[owners:]

    def rows_of(j, half, column):
        packet, row = plan["members"][j]
        at = row + half * chunk
        at = at if isinstance(half, int) else pl.multiple_of(at, TILE)
        return packets[packet][pl.ds(at, chunk), pl.ds(column, HEAD_WIDTH)]

    def state_at(i, half, h):
        return (2 * i + half) * heads + h

    rows = QUERY_PER_KEY * chunk
    causal = lax.broadcasted_iota(jnp.int32, (chunk, rows), 0) <= lax.rem(
        lax.broadcasted_iota(jnp.int32, (chunk, rows), 1), chunk
    )
    count = len(plan["members"])

    def one_chain(group, h, i, shared):
        first, done = group[0], group[-1] == count - 1
        k_at = pl.multiple_of(h * HEAD_WIDTH, HEAD_WIDTH)
        v_at = pl.multiple_of((heads + h) * HEAD_WIDTH, HEAD_WIDTH)
        late_at, early_at = state_at(i, 1, h), state_at(i, 0, h)
        if "keys" not in shared:
            shared["keys"] = jnp.concatenate([rows_of(j, 0, k_at) for j in group], axis=0)
            shared["values"] = turned_values([rows_of(j, 0, v_at) for j in group])
        carried = None
        if first > 0:
            carried = [(ref[early_at], ref[late_at]) for ref in (high_ref, sums_ref)]
        elif plan["carried"]:
            carried = [(ref[early_at], ref[late_at]) for ref in (in_high, in_sums)]
        pairs = []
        for j in group:
            if plan["own"] and j == plan["own_at"](i):
                pairs += [(j, 0, causal), (j, 1, causal)]
            else:
                pairs.append((j, (member_c[j] > owner_c[i]).astype(jnp.int32), None))
        base = product(shared["keys"], q_ref[late_at])
        scores = []
        for j, half, mask in pairs:
            s = product(rows_of(j, half, k_at), q_ref[state_at(i, half, h)])
            scores.append(s if mask is None else jnp.where(mask, s, MASKED))
        values = turned_values([rows_of(j, half, v_at) for j, half, _ in pairs])
        tops = [jnp.max(s, axis=0, keepdims=True) for s in scores]
        highs = []
        for side in range(2):
            some = [jnp.where(half == side, top, MASKED) for (_, half, _), top in zip(pairs, tops)]
            if side == 1:
                some.append(jnp.max(base, axis=0, keepdims=True))
            if carried is not None:
                some.append(carried[0][side])
            highs.append(functools.reduce(jnp.maximum, some))
        yield
        base_weights = weigh(base, highs[1])
        weights = [
            weigh(s, jnp.where(half == 1, highs[1], highs[0])) for (_, half, _), s in zip(pairs, scores)
        ]
        zero = jnp.zeros_like(weights[0])
        chosen = [
            jnp.concatenate(
                [jnp.where(half == side, w, zero) for (_, half, _), w in zip(pairs, weights)], axis=0
            )
            for side in range(2)
        ]
        yield
        for side, at in ((0, early_at), (1, late_at)):
            sums = product(values, chosen[side])
            if side == 1:
                sums = sums + product(shared["values"], base_weights)
            if carried is not None:
                shrink = jnp.exp2((carried[0][side] - highs[side]) * EXP2_SCALE)
                sums = sums + carried[1][side] * shrink
            if plan["last"] and done:
                mixed = sums[:HEAD_WIDTH] * (1.0 / sums[HEAD_WIDTH : HEAD_WIDTH + 1])
                mixed = jnp.transpose(mixed.astype(out_refs[i].dtype))
                for g in range(QUERY_PER_KEY):
                    to = pl.multiple_of(h * GROUP + g * HEAD_WIDTH, HEAD_WIDTH)
                    out_refs[i][side * chunk : (side + 1) * chunk, pl.ds(to, HEAD_WIDTH)] = mixed[
                        g * chunk : (g + 1) * chunk
                    ]
            else:
                high_ref[at] = highs[side]
                sums_ref[at] = sums
        yield

    def staggered(chains):
        for t in range(len(chains) + 2):
            for stage in (2, 1, 0):
                if 0 <= t - stage < len(chains):
                    next(chains[t - stage])

    for first in range(0, count, 6):
        group = range(first, min(first + 6, count))

        def run(heads_at_once, group=group):
            chains = []
            for h in heads_at_once:
                shared = {}
                chains += [one_chain(group, h, i, shared) for i in plan["which"]]
            staggered(chains)

        if fetch:

            def one_head(h, carry):
                run([h])
                return carry

            lax.fori_loop(0, heads, one_head, 0)
        else:
            run(range(heads))
    for copy in copies:
        copy.wait()


def attend(plan, turned, marks, packets, state, out_weight=None):
    heads, chunk, owners = plan["heads"], plan["chunk"], plan["owners"]
    count = len(plan["members"])
    plan = dict(plan, marks=len(marks), packets=len(packets), carried=state is not None)
    fetch = plan.setdefault("fetch", None)
    which = plan.setdefault("which", range(owners))
    rows = QUERY_PER_KEY * chunk
    slots = owners * 2 * heads
    vmem = pl.BlockSpec(memory_space=pltpu.VMEM)
    kept = [(slots, 1, rows), (slots, HEAD_WIDTH + TILE, rows)]
    if plan["last"]:
        out_shape = [jax.ShapeDtypeStruct((2 * chunk, heads * GROUP), jnp.bfloat16)] * len(which)
    else:
        out_shape = [jax.ShapeDtypeStruct(shape, jnp.float32) for shape in kept]
    operands = 1 + len(marks) + len(packets) + (0 if state is None else 2)
    in_specs = [vmem] * operands
    scratch = [pltpu.VMEM(shape, jnp.float32) for shape in kept] if plan["last"] else []
    if fetch:
        in_specs.append(pl.BlockSpec(memory_space=pltpu.HBM))
        for _, columns in fetch:
            out_shape.append(jax.ShapeDtypeStruct((out_weight.shape[0], columns), out_weight.dtype))
        scratch.append(pltpu.SemaphoreType.DMA((PIECES * len(fetch),)))
    flops = 4 * owners * heads * rows * HEAD_WIDTH * count * chunk * 2
    return pl.pallas_call(
        functools.partial(attend_kernel, plan),
        out_shape=out_shape,
        in_specs=in_specs,
        out_specs=[vmem] * len(out_shape),
        scratch_shapes=scratch,
        cost_estimate=pl.CostEstimate(
            flops=flops, bytes_accessed=4 << 20, transcendentals=flops // 512
        ),
        compiler_params=pltpu.CompilerParams(vmem_limit_bytes=VMEM_LIMIT),
        name="attend",
    )(turned, *marks, *packets, *(state or ()), *([out_weight] if fetch else []))


def turn_kernel(heads, chunk, *refs):
    q_refs, turned_ref = refs[:-1], refs[-1]
    for i, q_ref in enumerate(q_refs):
        for half in range(2):
            for h in range(heads):
                columns = [slice(at, at + HEAD_WIDTH) for at in range(h * GROUP, (h + 1) * GROUP, HEAD_WIDTH)]
                q = jnp.concatenate(
                    [q_ref[half * chunk : (half + 1) * chunk, at] for at in columns], axis=0
                )
                turned_ref[(2 * i + half) * heads + h] = jnp.transpose(q)


def turn(heads, chunk, queries):
    vmem = pl.BlockSpec(memory_space=pltpu.VMEM)
    owners = len(queries)
    shape = (2 * owners * heads, HEAD_WIDTH, QUERY_PER_KEY * chunk)
    return pl.pallas_call(
        functools.partial(turn_kernel, heads, chunk),
        out_shape=jax.ShapeDtypeStruct(shape, jnp.bfloat16),
        in_specs=[vmem] * owners,
        out_specs=vmem,
        cost_estimate=pl.CostEstimate(flops=1 << 10, bytes_accessed=1 << 10, transcendentals=0),
        compiler_params=pltpu.CompilerParams(vmem_limit_bytes=VMEM_LIMIT),
        name="turn",
    )(*queries)


def leaving_first(ref):
    chunk = ref.shape[0] // 2
    mine = lax.axis_index("inner").astype(jnp.int32)
    halves = [ref[pl.ds(pl.multiple_of(half * chunk, chunk), chunk)] for half in (1 - mine, mine)]
    return jnp.concatenate(halves, axis=0)


def rows_of_core(held_ref, core):
    depth = held_ref.shape[0] // 2
    return held_ref[pl.ds(pl.multiple_of(core * depth, depth), depth)]


def begin_kernel(own_ref, held_ref, begun_ref):
    begun_ref[...] = product(leaving_first(own_ref), rows_of_core(held_ref, my_core()))


def begin(own, held):
    vmem = pl.BlockSpec(memory_space=pltpu.VMEM)
    return pl.pallas_call(
        begin_kernel,
        out_shape=jax.ShapeDtypeStruct((own.shape[0], held.shape[1]), jnp.float32),
        in_specs=[vmem, vmem],
        out_specs=vmem,
        cost_estimate=pl.CostEstimate(flops=1 << 10, bytes_accessed=1 << 10, transcendentals=0),
        compiler_params=pltpu.CompilerParams(vmem_limit_bytes=VMEM_LIMIT),
        name="begin",
    )(own, held)


def project_kernel(bring, begun, own_ref, other_ref, held_ref, *refs):
    refs, copies = list(refs), []
    if bring:
        w_ref, sems = refs.pop(0), refs.pop()
    if begun:
        begun_ref = refs.pop(0)
    sent_ref, kept_ref = refs.pop(0), refs.pop(0)
    for n, (first, _) in enumerate(bring):
        copies += fetch_columns(w_ref, first, refs.pop(0), sems, n * PIECES)
    chunk, core = sent_ref.shape[0], my_core()
    other = leaving_first(other_ref)
    if begun:
        total = begun_ref[...] + product(other, rows_of_core(held_ref, 1 - core))
    else:
        (rows_ref,) = refs
        own, part = leaving_first(own_ref), own_ref.shape[1]
        rows_ref[:, :part] = jnp.where(core == 0, own, other)
        rows_ref[:, part:] = jnp.where(core == 0, other, own)
        total = product(rows_ref[...], held_ref[...])
    both = total.astype(sent_ref.dtype)
    sent_ref[...] = both[:chunk]
    kept_ref[...] = both[chunk:]
    for copy in copies:
        copy.wait()


def project(own, other, held, out_weight, bring, begun=None):
    rows, (depth, width) = own.shape[0], held.shape
    vmem = pl.BlockSpec(memory_space=pltpu.VMEM)
    out_shape = [jax.ShapeDtypeStruct((rows // 2, width), jnp.bfloat16)] * 2
    out_shape += [jax.ShapeDtypeStruct((depth, columns), held.dtype) for _, columns in bring]
    in_specs, operands, scratch = [vmem] * 3, [own, other, held], []
    if begun is None:
        scratch.append(pltpu.VMEM((rows, depth), jnp.bfloat16))
    if bring:
        in_specs.append(pl.BlockSpec(memory_space=pltpu.HBM))
        operands.append(out_weight)
        scratch.append(pltpu.SemaphoreType.DMA((PIECES * len(bring),)))
    if begun is not None:
        in_specs.append(vmem)
        operands.append(begun)
    return pl.pallas_call(
        functools.partial(project_kernel, bring, begun is not None),
        out_shape=out_shape,
        in_specs=in_specs,
        out_specs=[vmem] * len(out_shape),
        scratch_shapes=scratch,
        cost_estimate=pl.CostEstimate(flops=1 << 10, bytes_accessed=1 << 10, transcendentals=0),
        compiler_params=pltpu.CompilerParams(vmem_limit_bytes=VMEM_LIMIT),
        name="project",
    )(*operands)


def prepare_kernel(
    chunk, q_ref, k_ref, v_ref, position_ref, sent_ref, kept_ref, *query_refs_and_scratch
):
    *query_refs, first_ref, sems = query_refs_and_scratch
    rows, width = k_ref.shape[0], k_ref.shape[1] // 2
    columns = query_refs[0].shape[1]
    copies = [pltpu.make_async_copy(position_ref, first_ref, sems.at[4])]
    for n, (ref, core) in enumerate(((sent_ref, 1 - my_core()), (kept_ref, my_core()))):
        at = pl.ds(pl.multiple_of(core * width, width), width)
        for m, source in enumerate((k_ref, v_ref)):
            to = ref.at[pl.ds(0, rows), pl.ds(m * width, width)]
            copies.append(pltpu.make_async_copy(source.at[:, at], to, sems.at[2 * n + m]))
    for n, (ref, core) in enumerate(zip(query_refs, (1 - my_core(), my_core()))):
        at = pl.ds(pl.multiple_of(core * columns, columns), columns)
        copies.append(pltpu.make_async_copy(q_ref.at[:, at], ref, sems.at[5 + n]))
    for copy in copies:
        copy.start()
    copies[0].wait()
    c = lax.div(first_ref[0], jnp.int32(chunk)).astype(jnp.float32)
    header = jnp.full((HEADER, 2 * width), c, jnp.float32).astype(jnp.bfloat16)
    sent_ref[rows:] = header
    kept_ref[rows:] = header
    for copy in copies[1:]:
        copy.wait()


def prepare(queries, keys, values, positions):
    vmem = pl.BlockSpec(memory_space=pltpu.VMEM)
    hbm = pl.BlockSpec(memory_space=pltpu.HBM)
    rows, width = keys.shape
    operands = [pltpu.with_memory_space_constraint(x, pltpu.HBM) for x in (queries, keys, values, positions)]
    return pl.pallas_call(
        functools.partial(prepare_kernel, rows // 2),
        out_shape=[jax.ShapeDtypeStruct((rows + HEADER, width), jnp.bfloat16)] * 2
        + [jax.ShapeDtypeStruct((rows, queries.shape[1] // 2), jnp.bfloat16)] * 2,
        in_specs=[hbm] * 4,
        out_specs=[vmem] * 4,
        scratch_shapes=[
            pltpu.SMEM(positions.shape, jnp.int32),
            pltpu.SemaphoreType.DMA((7,)),
        ],
        compiler_params=pltpu.CompilerParams(vmem_limit_bytes=VMEM_LIMIT),
        name="prepare",
    )(*operands)


def finish_kernel(first, pairs, *refs):
    out_ref, total_ref, sem = refs[-3:]
    at = 0
    for mine, theirs in zip(refs[:pairs], refs[pairs : 2 * pairs]):
        width = mine.shape[1]
        total = mine[...].astype(jnp.float32) + theirs[...].astype(jnp.float32)
        total_ref[:, at : at + width] = total.astype(total_ref.dtype)
        at += width
    copy = pltpu.make_async_copy(total_ref, out_ref.at[:, pl.ds(first, at)], sem)
    copy.start()
    copy.wait()


def finish(kept, received, first, columns, written=None):
    vmem, hbm = pl.BlockSpec(memory_space=pltpu.VMEM), pl.BlockSpec(memory_space=pltpu.HBM)
    rows, width = kept[0].shape[0], sum(part.shape[1] for part in kept)
    pairs = len(kept)
    return pl.pallas_call(
        functools.partial(finish_kernel, first, pairs),
        out_shape=jax.ShapeDtypeStruct((rows, columns), kept[0].dtype),
        in_specs=[vmem] * (2 * pairs) + ([] if written is None else [hbm]),
        out_specs=hbm,
        input_output_aliases={} if written is None else {2 * pairs: 0},
        scratch_shapes=[pltpu.VMEM((rows, width), kept[0].dtype), pltpu.SemaphoreType.DMA],
        cost_estimate=pl.CostEstimate(flops=1 << 10, bytes_accessed=1 << 10, transcendentals=0),
        compiler_params=pltpu.CompilerParams(vmem_limit_bytes=VMEM_LIMIT),
        name="finish",
    )(*kept, *received, *([] if written is None else [written]))


def after(value, *events):
    return lax.optimization_barrier((value, *events))[0]


def split_over_cores(count, queries, keys, values, positions, out_weight, fetch):
    chips, half = count // 2, count // 4
    rows, chunk = queries.shape[0], queries.shape[0] // 2
    heads = keys.shape[1] // HEAD_WIDTH // 2
    sibling = [(b, b ^ 1) for b in range(count)]
    clock, counter = ring_pairs(chips, 1), ring_pairs(chips, -1)
    up = lambda x: lax.ppermute(x, "blk", clock)
    down = lambda x: lax.ppermute(x, "blk", counter)
    cross_up, cross_down = ring_pairs(chips, 1, True), ring_pairs(chips, -1, True)

    sent, x, q_sent, q_own = prepare(queries, keys, values, positions)
    y = lax.ppermute(sent, "blk", sibling)
    q_got = lax.ppermute(q_sent, "blk", sibling)
    turned = turn(heads, chunk, [q_own, q_got])

    def call(pairs, state, own=False, last=False, fetch=None, which=(0, 1)):
        each = range(len(pairs))
        plan = dict(
            heads=heads,
            chunk=chunk,
            owners=2,
            own=own,
            own_at=lambda i: i,
            last=last,
            members=[(2 * j + i, 0) for j in each for i in range(2)],
            headers=[(2 + 2 * j + i, rows, 0) for j in each for i in range(2)],
            owner_headers=[(0, rows, 0), (1, rows, 0)],
            fetch=fetch,
            which=which,
        )
        packets = [packet for pair in pairs for packet in pair]
        return attend(plan, turned, [x, y], packets, state, out_weight)

    held = {}

    def bring_with(groups, *arguments, **settings):
        cuts = [fetch[j] for j in groups]
        results = call(*arguments, fetch=cuts, **settings)
        held.update(zip(groups, results[2:]))
        return results[:2]

    state = bring_with((2,), [(x, y)], None, own=True)
    for r in range(1, half):
        if r == 1:
            up_first, up_second = up(x), lax.ppermute(sent, "blk", cross_up)
            down_first, down_second = lax.ppermute(sent, "blk", cross_down), down(x)
        else:
            up_first, down_first, *state = lax.optimization_barrier((up_first, down_first, *state))
            up_first, up_second = up(up_first), up(up_second)
            down_first, down_second = down(down_first), down(down_second)
            state = bring_with((0,) if r == half - 1 else (), arrived, state)
        arrived = [(up_first, up_second), (down_second, down_first)]
    up_first, down_first, *state = lax.optimization_barrier((up_first, down_first, *state))
    far = (up(up_first), down(down_first))
    state = bring_with((1,), arrived, state)
    (theirs,) = call([far], state, last=True, which=(1,))
    other = lax.ppermute(theirs, "blk", sibling)
    (own,) = call([far], state, last=True, which=(0,))
    return own, other, held


def one_head_a_device(count, queries, keys, values, positions):
    rows, chunk = queries.shape[0], queries.shape[0] // 2
    heads = keys.shape[1] // HEAD_WIDTH
    c = (positions[:1] // chunk).astype(jnp.bfloat16).reshape(1, 1)
    header = jnp.broadcast_to(c, (TILE, 2 * keys.shape[1]))
    packet = jnp.concatenate([jnp.concatenate([keys, values], axis=1), header], axis=0)
    packets = lax.all_gather(packet, "blk", axis=0, tiled=True)
    size = rows + TILE
    here = lax.axis_index("blk")
    order = lax.rem(here + jnp.arange(count), count)
    packets = packets.reshape(count, size, -1)[order].reshape(count * size, -1)
    plan = dict(
        heads=heads,
        chunk=chunk,
        owners=1,
        own=True,
        own_at=lambda i: 0,
        last=True,
        members=[(0, j * size) for j in range(count)],
        headers=[(0, j * size + rows, 0) for j in range(count)],
        owner_headers=[(0, rows, 0)],
    )
    turned = turn(heads, chunk, [queries])
    return attend(plan, turned, [], [packets], None)[0]


def shards(count, inner, queries, keys, values, positions, out_weight):
    heads = keys.shape[1] // HEAD_WIDTH
    if heads % 2:
        attended = one_head_a_device(count, queries, keys, values, positions)
        partial = jnp.dot(attended, out_weight, preferred_element_type=jnp.float32)
        return lax.psum_scatter(
            partial.astype(jnp.bfloat16), "inner", scatter_dimension=0, tiled=True
        )
    out_weight = pltpu.with_memory_space_constraint(out_weight, pltpu.HBM)
    shares = (10, 9, 8, 7, 6)
    widths = [out_weight.shape[1] * share // sum(shares) for share in shares]
    cuts = [(sum(widths[:j]), columns) for j, columns in enumerate(widths)]
    own, other, held = split_over_cores(
        count, queries, keys, values, positions, out_weight, cuts[:3]
    )
    bring = [cuts[j + 2 : j + 3] if j > 0 else [] for j in range(len(cuts))]
    received, kept = [], []
    for j in range(len(cuts)):
        source = own if j == 0 else after(own, sent)
        begun = begin(own, held[0]) if j == 0 else None
        sent, keep, *rest = project(source, other, held[j], out_weight, bring[j], begun)
        if rest:
            held[len(held)] = rest[0]
        received.append(lax.ppermute(sent, "inner", [(0, 1), (1, 0)]))
        kept.append(keep)
    columns = out_weight.shape[1]
    result = finish(kept[:-1], received[:-1], 0, columns)
    return finish(kept[-1:], received[-1:], cuts[-1][0], columns, result)


def solution(mesh):
    placed = (P("blk", "inner"), P("blk", "inner"), P("blk", "inner"), P("blk"), P("inner", None))
    return jax.shard_map(
        functools.partial(shards, mesh.shape["blk"], mesh.shape["inner"]),
        mesh=mesh,
        in_specs=placed,
        out_specs=P(("blk", "inner"), None),
        check_vma=False,
    )
```

```python
import functools
import math

import jax
import jax.numpy as jnp
from jax import lax
from jax.experimental import pallas as pl
from jax.experimental.pallas import tpu as pltpu
from jax.sharding import PartitionSpec as P

HEAD_WIDTH = 128
QUERY_PER_KEY = 5
GROUP = QUERY_PER_KEY * HEAD_WIDTH
EXP2_SCALE = math.log2(math.e) / math.sqrt(HEAD_WIDTH)
MASKED = -1e30
VMEM_LIMIT = 16 * 1024 * 1024
TILE = 16
HEADER = 8
PIECES = 5


def ring_of_chips(chips):
    half = chips // 2
    if chips == 8:
        return [2 * z for z in range(half)] + [2 * z + 1 for z in reversed(range(half))]
    return list(range(half)) + list(reversed(range(half, chips)))


def ring_pairs(chips, step, cross=False):
    ring = ring_of_chips(chips)
    return [
        (2 * ring[i] + core, 2 * ring[(i + step) % chips] + (1 - core if cross else core))
        for i in range(chips)
        for core in range(2)
    ]


def my_core():
    return lax.rem(lax.axis_index("blk"), 2).astype(jnp.int32)


def product(a, b):
    return jnp.dot(a, b, preferred_element_type=jnp.float32)


def weigh(scores, high):
    return jnp.exp2((scores - high) * EXP2_SCALE).astype(jnp.bfloat16)


def turned_values(blocks):
    v = jnp.concatenate(blocks, axis=0)
    return jnp.concatenate([jnp.transpose(v), jnp.ones((TILE, v.shape[0]), v.dtype)], axis=0)


def fetch_columns(w_ref, first, held_ref, sems, sem):
    depth, width = held_ref.shape[0] // PIECES, held_ref.shape[1]
    copies = []
    for p in range(PIECES):
        at = pl.ds(p * depth, depth)
        copies.append(
            pltpu.make_async_copy(
                w_ref.at[at, pl.ds(first, width)], held_ref.at[at], sems.at[sem + p]
            )
        )
        copies[-1].start()
    return copies


def attend_kernel(plan, *refs):
    heads, chunk, owners = plan["heads"], plan["chunk"], plan["owners"]
    refs = list(refs)
    q_ref = refs.pop(0)
    mark_refs = [refs.pop(0) for _ in range(plan["marks"])]
    packets = [refs.pop(0) for _ in range(plan["packets"])]
    if plan["carried"]:
        in_high, in_sums = refs.pop(0), refs.pop(0)
    fetch = plan["fetch"]
    if fetch:
        w_ref = refs.pop(0)
    if plan["last"]:
        out_refs = {i: refs.pop(0) for i in plan["which"]}
    copies = []
    if fetch:
        sems = refs.pop()
        for n, (first, _) in enumerate(fetch):
            held_ref = refs.pop(0 if plan["last"] else 2)
            copies += fetch_columns(w_ref, first, held_ref, sems, n * PIECES)
    high_ref, sums_ref = refs

    sources = mark_refs + packets
    numbers = [
        jnp.max(
            sources[packet][row : row + HEADER].astype(jnp.float32)
        ).astype(jnp.int32)
        for packet, row in plan["owner_headers"] + plan["headers"]
    ]
    owner_c, member_c = numbers[:owners], numbers[owners:]

    def rows_of(j, half, block):
        packet, row = plan["members"][j]
        at = row + (2 * block + half) * chunk
        return packets[packet][pl.ds(at if isinstance(at, int) else pl.multiple_of(at, TILE), chunk)]

    def state_at(i, half, h):
        return (2 * i + half) * heads + h

    rows = QUERY_PER_KEY * chunk
    causal = lax.broadcasted_iota(jnp.int32, (chunk, rows), 0) <= lax.rem(
        lax.broadcasted_iota(jnp.int32, (chunk, rows), 1), chunk
    )
    count = len(plan["members"])

    def one_chain(group, h, i, shared):
        first, done = group[0], group[-1] == count - 1
        k_at, v_at = h, heads + h
        late_at, early_at = state_at(i, 1, h), state_at(i, 0, h)
        if "keys" not in shared:
            shared["keys"] = jnp.concatenate([rows_of(j, 0, k_at) for j in group], axis=0)
            shared["values"] = turned_values([rows_of(j, 0, v_at) for j in group])
        carried = None
        if first > 0:
            carried = [(ref[early_at], ref[late_at]) for ref in (high_ref, sums_ref)]
        elif plan["carried"]:
            carried = [(ref[early_at], ref[late_at]) for ref in (in_high, in_sums)]
        pairs = []
        for j in group:
            if plan["own"] and j == plan["own_at"](i):
                pairs += [(j, 0, causal), (j, 1, causal)]
            else:
                pairs.append((j, (member_c[j] > owner_c[i]).astype(jnp.int32), None))
        base = product(shared["keys"], q_ref[late_at])
        scores = []
        for j, half, mask in pairs:
            s = product(rows_of(j, half, k_at), q_ref[state_at(i, half, h)])
            scores.append(s if mask is None else jnp.where(mask, s, MASKED))
        values = turned_values([rows_of(j, half, v_at) for j, half, _ in pairs])
        tops = [jnp.max(s, axis=0, keepdims=True) for s in scores]
        highs = []
        for side in range(2):
            some = [jnp.where(half == side, top, MASKED) for (_, half, _), top in zip(pairs, tops)]
            if side == 1:
                some.append(jnp.max(base, axis=0, keepdims=True))
            if carried is not None:
                some.append(carried[0][side])
            highs.append(functools.reduce(jnp.maximum, some))
        yield
        base_weights = weigh(base, highs[1])
        weights = [
            weigh(s, jnp.where(half == 1, highs[1], highs[0])) for (_, half, _), s in zip(pairs, scores)
        ]
        zero = jnp.zeros_like(weights[0])
        chosen = [
            jnp.concatenate(
                [jnp.where(half == side, w, zero) for (_, half, _), w in zip(pairs, weights)], axis=0
            )
            for side in range(2)
        ]
        yield
        for side, at in ((0, early_at), (1, late_at)):
            sums = product(values, chosen[side])
            if side == 1:
                sums = sums + product(shared["values"], base_weights)
            if carried is not None:
                shrink = jnp.exp2((carried[0][side] - highs[side]) * EXP2_SCALE)
                sums = sums + carried[1][side] * shrink
            if plan["last"] and done:
                mixed = sums[:HEAD_WIDTH] * (1.0 / sums[HEAD_WIDTH : HEAD_WIDTH + 1])
                mixed = jnp.transpose(mixed.astype(out_refs[i].dtype))
                for g in range(QUERY_PER_KEY):
                    to = pl.multiple_of(h * GROUP + g * HEAD_WIDTH, HEAD_WIDTH)
                    out_refs[i][side * chunk : (side + 1) * chunk, pl.ds(to, HEAD_WIDTH)] = mixed[
                        g * chunk : (g + 1) * chunk
                    ]
            else:
                high_ref[at] = highs[side]
                sums_ref[at] = sums
        yield

    def staggered(chains):
        for t in range(len(chains) + 2):
            for stage in (2, 1, 0):
                if 0 <= t - stage < len(chains):
                    next(chains[t - stage])

    for first in range(0, count, 6):
        group = range(first, min(first + 6, count))

        def run(heads_at_once, group=group):
            chains = []
            for h in heads_at_once:
                shared = {}
                chains += [one_chain(group, h, i, shared) for i in plan["which"]]
            staggered(chains)

        if fetch:

            def one_head(h, carry):
                run([h])
                return carry

            lax.fori_loop(0, heads, one_head, 0)
        else:
            run(range(heads))
    for copy in copies:
        copy.wait()


def attend(plan, turned, marks, packets, state, out_weight=None):
    heads, chunk, owners = plan["heads"], plan["chunk"], plan["owners"]
    count = len(plan["members"])
    plan = dict(plan, marks=len(marks), packets=len(packets), carried=state is not None)
    fetch = plan.setdefault("fetch", None)
    which = plan.setdefault("which", range(owners))
    rows = QUERY_PER_KEY * chunk
    slots = owners * 2 * heads
    vmem = pl.BlockSpec(memory_space=pltpu.VMEM)
    kept = [(slots, 1, rows), (slots, HEAD_WIDTH + TILE, rows)]
    if plan["last"]:
        out_shape = [jax.ShapeDtypeStruct((2 * chunk, heads * GROUP), jnp.bfloat16)] * len(which)
    else:
        out_shape = [jax.ShapeDtypeStruct(shape, jnp.float32) for shape in kept]
    operands = 1 + len(marks) + len(packets) + (0 if state is None else 2)
    in_specs = [vmem] * operands
    scratch = [pltpu.VMEM(shape, jnp.float32) for shape in kept] if plan["last"] else []
    if fetch:
        in_specs.append(pl.BlockSpec(memory_space=pltpu.HBM))
        for _, columns in fetch:
            out_shape.append(jax.ShapeDtypeStruct((out_weight.shape[0], columns), out_weight.dtype))
        scratch.append(pltpu.SemaphoreType.DMA((PIECES * len(fetch),)))
    flops = 4 * owners * heads * rows * HEAD_WIDTH * count * chunk * 2
    return pl.pallas_call(
        functools.partial(attend_kernel, plan),
        out_shape=out_shape,
        in_specs=in_specs,
        out_specs=[vmem] * len(out_shape),
        scratch_shapes=scratch,
        cost_estimate=pl.CostEstimate(
            flops=flops, bytes_accessed=4 << 20, transcendentals=flops // 512
        ),
        compiler_params=pltpu.CompilerParams(vmem_limit_bytes=VMEM_LIMIT),
        name="attend",
    )(turned, *marks, *packets, *(state or ()), *([out_weight] if fetch else []))


def turn_kernel(heads, chunk, *refs):
    q_refs, turned_ref = refs[:-1], refs[-1]
    for i, q_ref in enumerate(q_refs):
        for half in range(2):
            for h in range(heads):
                columns = [slice(at, at + HEAD_WIDTH) for at in range(h * GROUP, (h + 1) * GROUP, HEAD_WIDTH)]
                q = jnp.concatenate(
                    [q_ref[half * chunk : (half + 1) * chunk, at] for at in columns], axis=0
                )
                turned_ref[(2 * i + half) * heads + h] = jnp.transpose(q)


def turn(heads, chunk, queries):
    vmem = pl.BlockSpec(memory_space=pltpu.VMEM)
    owners = len(queries)
    shape = (2 * owners * heads, HEAD_WIDTH, QUERY_PER_KEY * chunk)
    return pl.pallas_call(
        functools.partial(turn_kernel, heads, chunk),
        out_shape=jax.ShapeDtypeStruct(shape, jnp.bfloat16),
        in_specs=[vmem] * owners,
        out_specs=vmem,
        cost_estimate=pl.CostEstimate(flops=1 << 10, bytes_accessed=1 << 10, transcendentals=0),
        compiler_params=pltpu.CompilerParams(vmem_limit_bytes=VMEM_LIMIT),
        name="turn",
    )(*queries)


def leaving_first(ref):
    chunk = ref.shape[0] // 2
    mine = lax.axis_index("inner").astype(jnp.int32)
    halves = [ref[pl.ds(pl.multiple_of(half * chunk, chunk), chunk)] for half in (1 - mine, mine)]
    return jnp.concatenate(halves, axis=0)


def rows_of_core(held_ref, core):
    depth = held_ref.shape[0] // 2
    return held_ref[pl.ds(pl.multiple_of(core * depth, depth), depth)]


def begin_kernel(own_ref, held_ref, begun_ref):
    begun_ref[...] = product(leaving_first(own_ref), rows_of_core(held_ref, my_core()))


def begin(own, held):
    vmem = pl.BlockSpec(memory_space=pltpu.VMEM)
    return pl.pallas_call(
        begin_kernel,
        out_shape=jax.ShapeDtypeStruct((own.shape[0], held.shape[1]), jnp.float32),
        in_specs=[vmem, vmem],
        out_specs=vmem,
        cost_estimate=pl.CostEstimate(flops=1 << 10, bytes_accessed=1 << 10, transcendentals=0),
        compiler_params=pltpu.CompilerParams(vmem_limit_bytes=VMEM_LIMIT),
        name="begin",
    )(own, held)


def project_kernel(bring, begun, own_ref, other_ref, held_ref, *refs):
    refs, copies = list(refs), []
    if bring:
        w_ref, sems = refs.pop(0), refs.pop()
    if begun:
        begun_ref = refs.pop(0)
    sent_ref, kept_ref = refs.pop(0), refs.pop(0)
    for n, (first, _) in enumerate(bring):
        copies += fetch_columns(w_ref, first, refs.pop(0), sems, n * PIECES)
    chunk, core = sent_ref.shape[0], my_core()
    other = leaving_first(other_ref)
    if begun:
        total = begun_ref[...] + product(other, rows_of_core(held_ref, 1 - core))
    else:
        (rows_ref,) = refs
        own, part = leaving_first(own_ref), own_ref.shape[1]
        rows_ref[:, :part] = jnp.where(core == 0, own, other)
        rows_ref[:, part:] = jnp.where(core == 0, other, own)
        total = product(rows_ref[...], held_ref[...])
    both = total.astype(sent_ref.dtype)
    sent_ref[...] = both[:chunk]
    kept_ref[...] = both[chunk:]
    for copy in copies:
        copy.wait()


def project(own, other, held, out_weight, bring, begun=None):
    rows, (depth, width) = own.shape[0], held.shape
    vmem = pl.BlockSpec(memory_space=pltpu.VMEM)
    out_shape = [jax.ShapeDtypeStruct((rows // 2, width), jnp.bfloat16)] * 2
    out_shape += [jax.ShapeDtypeStruct((depth, columns), held.dtype) for _, columns in bring]
    in_specs, operands, scratch = [vmem] * 3, [own, other, held], []
    if begun is None:
        scratch.append(pltpu.VMEM((rows, depth), jnp.bfloat16))
    if bring:
        in_specs.append(pl.BlockSpec(memory_space=pltpu.HBM))
        operands.append(out_weight)
        scratch.append(pltpu.SemaphoreType.DMA((PIECES * len(bring),)))
    if begun is not None:
        in_specs.append(vmem)
        operands.append(begun)
    return pl.pallas_call(
        functools.partial(project_kernel, bring, begun is not None),
        out_shape=out_shape,
        in_specs=in_specs,
        out_specs=[vmem] * len(out_shape),
        scratch_shapes=scratch,
        cost_estimate=pl.CostEstimate(flops=1 << 10, bytes_accessed=1 << 10, transcendentals=0),
        compiler_params=pltpu.CompilerParams(vmem_limit_bytes=VMEM_LIMIT),
        name="project",
    )(*operands)


def prepare_kernel(
    chunk, q_ref, k_ref, v_ref, position_ref, sent_ref, kept_ref, *query_refs_and_scratch
):
    *query_refs, first_ref, sems = query_refs_and_scratch
    rows, heads = k_ref.shape[0], k_ref.shape[1] // HEAD_WIDTH // 2
    columns = query_refs[0].shape[1]
    copies = [pltpu.make_async_copy(position_ref, first_ref, sems.at[0])]
    for ref, core in ((sent_ref, 1 - my_core()), (kept_ref, my_core())):
        for m, source in enumerate((k_ref, v_ref)):
            for h in range(heads):
                at = pl.ds(pl.multiple_of((core * heads + h) * HEAD_WIDTH, HEAD_WIDTH), HEAD_WIDTH)
                to = ref.at[pl.ds((m * heads + h) * rows, rows)]
                copies.append(pltpu.make_async_copy(source.at[:, at], to, sems.at[len(copies)]))
    for ref, core in zip(query_refs, (1 - my_core(), my_core())):
        at = pl.ds(pl.multiple_of(core * columns, columns), columns)
        copies.append(pltpu.make_async_copy(q_ref.at[:, at], ref, sems.at[len(copies)]))
    for copy in copies:
        copy.start()
    copies[0].wait()
    c = lax.div(first_ref[0], jnp.int32(chunk)).astype(jnp.float32)
    header = jnp.full((HEADER, HEAD_WIDTH), c, jnp.float32).astype(jnp.bfloat16)
    sent_ref[2 * heads * rows :] = header
    kept_ref[2 * heads * rows :] = header
    for copy in copies[1:]:
        copy.wait()


def prepare(queries, keys, values, positions):
    vmem = pl.BlockSpec(memory_space=pltpu.VMEM)
    hbm = pl.BlockSpec(memory_space=pltpu.HBM)
    rows, blocks = keys.shape[0], keys.shape[1] // HEAD_WIDTH
    operands = [pltpu.with_memory_space_constraint(x, pltpu.HBM) for x in (queries, keys, values, positions)]
    return pl.pallas_call(
        functools.partial(prepare_kernel, rows // 2),
        out_shape=[jax.ShapeDtypeStruct((blocks * rows + HEADER, HEAD_WIDTH), jnp.bfloat16)] * 2
        + [jax.ShapeDtypeStruct((rows, queries.shape[1] // 2), jnp.bfloat16)] * 2,
        in_specs=[hbm] * 4,
        out_specs=[vmem] * 4,
        scratch_shapes=[
            pltpu.SMEM(positions.shape, jnp.int32),
            pltpu.SemaphoreType.DMA((3 + 2 * blocks,)),
        ],
        compiler_params=pltpu.CompilerParams(vmem_limit_bytes=VMEM_LIMIT),
        name="prepare",
    )(*operands)


def finish_kernel(first, pairs, *refs):
    out_ref, total_ref, sem = refs[-3:]
    at = 0
    for mine, theirs in zip(refs[:pairs], refs[pairs : 2 * pairs]):
        width = mine.shape[1]
        total = mine[...].astype(jnp.float32) + theirs[...].astype(jnp.float32)
        total_ref[:, at : at + width] = total.astype(total_ref.dtype)
        at += width
    copy = pltpu.make_async_copy(total_ref, out_ref.at[:, pl.ds(first, at)], sem)
    copy.start()
    copy.wait()


def finish(kept, received, first, columns, written=None):
    vmem, hbm = pl.BlockSpec(memory_space=pltpu.VMEM), pl.BlockSpec(memory_space=pltpu.HBM)
    rows, width = kept[0].shape[0], sum(part.shape[1] for part in kept)
    pairs = len(kept)
    return pl.pallas_call(
        functools.partial(finish_kernel, first, pairs),
        out_shape=jax.ShapeDtypeStruct((rows, columns), kept[0].dtype),
        in_specs=[vmem] * (2 * pairs) + ([] if written is None else [hbm]),
        out_specs=hbm,
        input_output_aliases={} if written is None else {2 * pairs: 0},
        scratch_shapes=[pltpu.VMEM((rows, width), kept[0].dtype), pltpu.SemaphoreType.DMA],
        cost_estimate=pl.CostEstimate(flops=1 << 10, bytes_accessed=1 << 10, transcendentals=0),
        compiler_params=pltpu.CompilerParams(vmem_limit_bytes=VMEM_LIMIT),
        name="finish",
    )(*kept, *received, *([] if written is None else [written]))


def after(value, *events):
    return lax.optimization_barrier((value, *events))[0]


def split_over_cores(count, queries, keys, values, positions, out_weight, fetch):
    chips, half = count // 2, count // 4
    rows, chunk = queries.shape[0], queries.shape[0] // 2
    heads = keys.shape[1] // HEAD_WIDTH // 2
    sibling = [(b, b ^ 1) for b in range(count)]
    clock, counter = ring_pairs(chips, 1), ring_pairs(chips, -1)
    up = lambda x: lax.ppermute(x, "blk", clock)
    down = lambda x: lax.ppermute(x, "blk", counter)
    cross_up, cross_down = ring_pairs(chips, 1, True), ring_pairs(chips, -1, True)

    sent, x, q_sent, q_own = prepare(queries, keys, values, positions)
    y = lax.ppermute(sent, "blk", sibling)
    q_got = lax.ppermute(q_sent, "blk", sibling)
    turned = turn(heads, chunk, [q_own, q_got])

    def call(pairs, state, own=False, last=False, fetch=None, which=(0, 1)):
        each = range(len(pairs))
        plan = dict(
            heads=heads,
            chunk=chunk,
            owners=2,
            own=own,
            own_at=lambda i: i,
            last=last,
            members=[(2 * j + i, 0) for j in each for i in range(2)],
            headers=[(2 + 2 * j + i, 2 * heads * rows) for j in each for i in range(2)],
            owner_headers=[(0, 2 * heads * rows), (1, 2 * heads * rows)],
            fetch=fetch,
            which=which,
        )
        packets = [packet for pair in pairs for packet in pair]
        return attend(plan, turned, [x, y], packets, state, out_weight)

    held = {}

    def bring_with(groups, *arguments, **settings):
        cuts = [fetch[j] for j in groups]
        results = call(*arguments, fetch=cuts, **settings)
        held.update(zip(groups, results[2:]))
        return results[:2]

    state = bring_with((2,), [(x, y)], None, own=True)
    for r in range(1, half):
        if r == 1:
            up_first, up_second = up(x), lax.ppermute(sent, "blk", cross_up)
            down_first, down_second = lax.ppermute(sent, "blk", cross_down), down(x)
        else:
            up_first, down_first, *state = lax.optimization_barrier((up_first, down_first, *state))
            up_first, up_second = up(up_first), up(up_second)
            down_first, down_second = down(down_first), down(down_second)
            state = bring_with((0,) if r == half - 1 else (), arrived, state)
        arrived = [(up_first, up_second), (down_second, down_first)]
    up_first, down_first, *state = lax.optimization_barrier((up_first, down_first, *state))
    far = (up(up_first), down(down_first))
    state = bring_with((1,), arrived, state)
    (theirs,) = call([far], state, last=True, which=(1,))
    other = lax.ppermute(theirs, "blk", sibling)
    (own,) = call([far], state, last=True, which=(0,))
    return own, other, held


def one_head_a_device(count, queries, keys, values, positions):
    rows, chunk = queries.shape[0], queries.shape[0] // 2
    heads = keys.shape[1] // HEAD_WIDTH
    c = (positions[:1] // chunk).astype(jnp.bfloat16).reshape(1, 1)
    blocks = [x[:, h * HEAD_WIDTH : (h + 1) * HEAD_WIDTH] for x in (keys, values) for h in range(heads)]
    packet = jnp.concatenate(blocks + [jnp.broadcast_to(c, (TILE, HEAD_WIDTH))], axis=0)
    packets = lax.all_gather(packet, "blk", axis=0, tiled=True)
    size = packet.shape[0]
    here = lax.axis_index("blk")
    order = lax.rem(here + jnp.arange(count), count)
    packets = packets.reshape(count, size, -1)[order].reshape(count * size, -1)
    plan = dict(
        heads=heads,
        chunk=chunk,
        owners=1,
        own=True,
        own_at=lambda i: 0,
        last=True,
        members=[(0, j * size) for j in range(count)],
        headers=[(0, (j + 1) * size - TILE) for j in range(count)],
        owner_headers=[(0, size - TILE)],
    )
    turned = turn(heads, chunk, [queries])
    return attend(plan, turned, [], [packets], None)[0]


def shards(count, inner, queries, keys, values, positions, out_weight):
    heads = keys.shape[1] // HEAD_WIDTH
    if heads % 2:
        attended = one_head_a_device(count, queries, keys, values, positions)
        partial = jnp.dot(attended, out_weight, preferred_element_type=jnp.float32)
        return lax.psum_scatter(
            partial.astype(jnp.bfloat16), "inner", scatter_dimension=0, tiled=True
        )
    out_weight = pltpu.with_memory_space_constraint(out_weight, pltpu.HBM)
    shares = (10, 9, 8, 7, 6)
    widths = [out_weight.shape[1] * share // sum(shares) for share in shares]
    cuts = [(sum(widths[:j]), columns) for j, columns in enumerate(widths)]
    own, other, held = split_over_cores(
        count, queries, keys, values, positions, out_weight, cuts[:3]
    )
    bring = [cuts[j + 2 : j + 3] if j > 0 else [] for j in range(len(cuts))]
    received, kept = [], []
    for j in range(len(cuts)):
        source = own if j == 0 else after(own, sent)
        begun = begin(own, held[0]) if j == 0 else None
        sent, keep, *rest = project(source, other, held[j], out_weight, bring[j], begun)
        if rest:
            held[len(held)] = rest[0]
        received.append(lax.ppermute(sent, "inner", [(0, 1), (1, 0)]))
        kept.append(keep)
    columns = out_weight.shape[1]
    result = finish(kept[:-1], received[:-1], 0, columns)
    return finish(kept[-1:], received[-1:], cuts[-1][0], columns, result)


def solution(mesh):
    placed = (P("blk", "inner"), P("blk", "inner"), P("blk", "inner"), P("blk"), P("inner", None))
    return jax.shard_map(
        functools.partial(shards, mesh.shape["blk"], mesh.shape["inner"]),
        mesh=mesh,
        in_specs=placed,
        out_specs=P(("blk", "inner"), None),
        check_vma=False,
    )
```

```python
import functools
import math

import jax
import jax.numpy as jnp
from jax import lax
from jax.experimental import pallas as pl
from jax.experimental.pallas import tpu as pltpu
from jax.sharding import PartitionSpec as P

HEAD_WIDTH = 128
QUERY_PER_KEY = 5
GROUP = QUERY_PER_KEY * HEAD_WIDTH
EXP2_SCALE = math.log2(math.e) / math.sqrt(HEAD_WIDTH)
MASKED = -1e30
VMEM_LIMIT = 16 * 1024 * 1024
TILE = 16
HEADER = 8
PIECES = 5


def ring_of_chips(chips):
    half = chips // 2
    if chips == 8:
        return [2 * z for z in range(half)] + [2 * z + 1 for z in reversed(range(half))]
    return list(range(half)) + list(reversed(range(half, chips)))


def ring_pairs(chips, step, cross=False):
    ring = ring_of_chips(chips)
    return [
        (2 * ring[i] + core, 2 * ring[(i + step) % chips] + (1 - core if cross else core))
        for i in range(chips)
        for core in range(2)
    ]


def my_core():
    return lax.rem(lax.axis_index("blk"), 2).astype(jnp.int32)


def product(a, b):
    return jnp.dot(a, b, preferred_element_type=jnp.float32)


def weigh(scores, high):
    return jnp.exp2((scores - high) * EXP2_SCALE).astype(jnp.bfloat16)


def turned_values(blocks):
    v = jnp.concatenate(blocks, axis=0)
    return jnp.concatenate([jnp.transpose(v), jnp.ones((TILE, v.shape[0]), v.dtype)], axis=0)


def fetch_columns(w_ref, first, held_ref, sems, sem):
    depth, width = held_ref.shape[0] // PIECES, held_ref.shape[1]
    copies = []
    for p in range(PIECES):
        at = pl.ds(p * depth, depth)
        copies.append(
            pltpu.make_async_copy(
                w_ref.at[at, pl.ds(first, width)], held_ref.at[at], sems.at[sem + p]
            )
        )
        copies[-1].start()
    return copies


def attend_kernel(plan, *refs):
    heads, chunk, owners = plan["heads"], plan["chunk"], plan["owners"]
    refs = list(refs)
    q_ref = refs.pop(0)
    mark_refs = [refs.pop(0) for _ in range(plan["marks"])]
    packets = [refs.pop(0) for _ in range(plan["packets"])]
    if plan["carried"]:
        in_high, in_sums = refs.pop(0), refs.pop(0)
    fetch = plan["fetch"]
    if fetch:
        w_ref = refs.pop(0)
    if plan["last"]:
        out_refs = {i: refs.pop(0) for i in plan["which"]}
    copies = []
    if fetch:
        sems = refs.pop()
        for n, (first, _) in enumerate(fetch):
            held_ref = refs.pop(0 if plan["last"] else 2)
            copies += fetch_columns(w_ref, first, held_ref, sems, n * PIECES)
    high_ref, sums_ref = refs

    sources = mark_refs + packets
    numbers = [
        jnp.max(
            sources[packet][row : row + HEADER].astype(jnp.float32)
        ).astype(jnp.int32)
        for packet, row in plan["owner_headers"] + plan["headers"]
    ]
    owner_c, member_c = numbers[:owners], numbers[owners:]

    def rows_of(j, half, block):
        packet, row = plan["members"][j]
        at = row + (2 * block + half) * chunk
        return packets[packet][pl.ds(at if isinstance(at, int) else pl.multiple_of(at, TILE), chunk)]

    def state_at(i, half, h):
        return (2 * i + half) * heads + h

    rows = QUERY_PER_KEY * chunk
    causal = lax.broadcasted_iota(jnp.int32, (chunk, rows), 0) <= lax.rem(
        lax.broadcasted_iota(jnp.int32, (chunk, rows), 1), chunk
    )
    count = len(plan["members"])

    def one_chain(group, h, i, shared):
        first, done = group[0], group[-1] == count - 1
        k_at, v_at = h, heads + h
        late_at, early_at = state_at(i, 1, h), state_at(i, 0, h)
        if "keys" not in shared:
            shared["keys"] = jnp.concatenate([rows_of(j, 0, k_at) for j in group], axis=0)
            shared["values"] = turned_values([rows_of(j, 0, v_at) for j in group])
        carried = None
        if first > 0:
            carried = [(ref[early_at], ref[late_at]) for ref in (high_ref, sums_ref)]
        elif plan["carried"]:
            carried = [(ref[early_at], ref[late_at]) for ref in (in_high, in_sums)]
        pairs = []
        for j in group:
            if plan["own"] and j == plan["own_at"](i):
                pairs += [(j, 0, causal), (j, 1, causal)]
            else:
                pairs.append((j, (member_c[j] > owner_c[i]).astype(jnp.int32), None))
        base = product(shared["keys"], q_ref[late_at])
        scores = []
        for j, half, mask in pairs:
            s = product(rows_of(j, half, k_at), q_ref[state_at(i, half, h)])
            scores.append(s if mask is None else jnp.where(mask, s, MASKED))
        values = turned_values([rows_of(j, half, v_at) for j, half, _ in pairs])
        tops = [jnp.max(s, axis=0, keepdims=True) for s in scores]
        highs = []
        for side in range(2):
            some = [jnp.where(half == side, top, MASKED) for (_, half, _), top in zip(pairs, tops)]
            if side == 1:
                some.append(jnp.max(base, axis=0, keepdims=True))
            if carried is not None:
                some.append(carried[0][side])
            highs.append(functools.reduce(jnp.maximum, some))
        yield
        base_weights = weigh(base, highs[1])
        weights = [
            weigh(s, jnp.where(half == 1, highs[1], highs[0])) for (_, half, _), s in zip(pairs, scores)
        ]
        zero = jnp.zeros_like(weights[0])
        chosen = [
            jnp.concatenate(
                [jnp.where(half == side, w, zero) for (_, half, _), w in zip(pairs, weights)], axis=0
            )
            for side in range(2)
        ]
        yield
        for side, at in ((0, early_at), (1, late_at)):
            sums = product(values, chosen[side])
            if side == 1:
                sums = sums + product(shared["values"], base_weights)
            if carried is not None:
                shrink = jnp.exp2((carried[0][side] - highs[side]) * EXP2_SCALE)
                sums = sums + carried[1][side] * shrink
            if plan["last"] and done:
                mixed = sums[:HEAD_WIDTH] * (1.0 / sums[HEAD_WIDTH : HEAD_WIDTH + 1])
                mixed = jnp.transpose(mixed.astype(out_refs[i].dtype))
                for g in range(QUERY_PER_KEY):
                    to = pl.multiple_of(h * GROUP + g * HEAD_WIDTH, HEAD_WIDTH)
                    out_refs[i][side * chunk : (side + 1) * chunk, pl.ds(to, HEAD_WIDTH)] = mixed[
                        g * chunk : (g + 1) * chunk
                    ]
            else:
                high_ref[at] = highs[side]
                sums_ref[at] = sums
        yield

    def staggered(chains):
        for t in range(len(chains) + 2):
            for stage in (2, 1, 0):
                if 0 <= t - stage < len(chains):
                    next(chains[t - stage])

    for first in range(0, count, 6):
        group = range(first, min(first + 6, count))

        def run(heads_at_once, group=group):
            chains = []
            for h in heads_at_once:
                shared = {}
                chains += [one_chain(group, h, i, shared) for i in plan["which"]]
            staggered(chains)

        if fetch:

            def one_head(h, carry):
                run([h])
                return carry

            lax.fori_loop(0, heads, one_head, 0)
        else:
            run(range(heads))
    for copy in copies:
        copy.wait()


def attend(plan, turned, marks, packets, state, out_weight=None):
    heads, chunk, owners = plan["heads"], plan["chunk"], plan["owners"]
    count = len(plan["members"])
    plan = dict(plan, marks=len(marks), packets=len(packets), carried=state is not None)
    fetch = plan.setdefault("fetch", None)
    which = plan.setdefault("which", range(owners))
    rows = QUERY_PER_KEY * chunk
    slots = owners * 2 * heads
    vmem = pl.BlockSpec(memory_space=pltpu.VMEM)
    kept = [(slots, 1, rows), (slots, HEAD_WIDTH + TILE, rows)]
    if plan["last"]:
        out_shape = [jax.ShapeDtypeStruct((2 * chunk, heads * GROUP), jnp.bfloat16)] * len(which)
    else:
        out_shape = [jax.ShapeDtypeStruct(shape, jnp.float32) for shape in kept]
    operands = 1 + len(marks) + len(packets) + (0 if state is None else 2)
    in_specs = [vmem] * operands
    scratch = [pltpu.VMEM(shape, jnp.float32) for shape in kept] if plan["last"] else []
    if fetch:
        in_specs.append(pl.BlockSpec(memory_space=pltpu.HBM))
        for _, columns in fetch:
            out_shape.append(jax.ShapeDtypeStruct((out_weight.shape[0], columns), out_weight.dtype))
        scratch.append(pltpu.SemaphoreType.DMA((PIECES * len(fetch),)))
    flops = 4 * owners * heads * rows * HEAD_WIDTH * count * chunk * 2
    return pl.pallas_call(
        functools.partial(attend_kernel, plan),
        out_shape=out_shape,
        in_specs=in_specs,
        out_specs=[vmem] * len(out_shape),
        scratch_shapes=scratch,
        cost_estimate=pl.CostEstimate(
            flops=flops, bytes_accessed=4 << 20, transcendentals=flops // 512
        ),
        compiler_params=pltpu.CompilerParams(vmem_limit_bytes=VMEM_LIMIT),
        name="attend",
    )(turned, *marks, *packets, *(state or ()), *([out_weight] if fetch else []))


def turn_kernel(heads, chunk, *refs):
    q_refs, turned_ref = refs[:-1], refs[-1]
    for i, q_ref in enumerate(q_refs):
        for half in range(2):
            for h in range(heads):
                columns = [slice(at, at + HEAD_WIDTH) for at in range(h * GROUP, (h + 1) * GROUP, HEAD_WIDTH)]
                q = jnp.concatenate(
                    [q_ref[half * chunk : (half + 1) * chunk, at] for at in columns], axis=0
                )
                turned_ref[(2 * i + half) * heads + h] = jnp.transpose(q)


def turn(heads, chunk, queries):
    vmem = pl.BlockSpec(memory_space=pltpu.VMEM)
    owners = len(queries)
    shape = (2 * owners * heads, HEAD_WIDTH, QUERY_PER_KEY * chunk)
    return pl.pallas_call(
        functools.partial(turn_kernel, heads, chunk),
        out_shape=jax.ShapeDtypeStruct(shape, jnp.bfloat16),
        in_specs=[vmem] * owners,
        out_specs=vmem,
        cost_estimate=pl.CostEstimate(flops=1 << 10, bytes_accessed=1 << 10, transcendentals=0),
        compiler_params=pltpu.CompilerParams(vmem_limit_bytes=VMEM_LIMIT),
        name="turn",
    )(*queries)


def half_of(ref, keep):
    chunk = ref.shape[0] // 2
    mine = lax.axis_index("inner").astype(jnp.int32)
    return ref[pl.ds(pl.multiple_of((mine if keep else 1 - mine) * chunk, chunk), chunk)]


def leaving_first(ref):
    return jnp.concatenate([half_of(ref, False), half_of(ref, True)], axis=0)


def rows_of_core(held_ref, core):
    depth = held_ref.shape[0] // 2
    return held_ref[pl.ds(pl.multiple_of(core * depth, depth), depth)]


def begin_kernel(own_ref, held_ref, begun_ref):
    begun_ref[...] = product(half_of(own_ref, False), rows_of_core(held_ref, my_core()))


def first_kernel(own_ref, other_ref, held_ref, begun_ref, sent_ref):
    total = begun_ref[...] + product(half_of(other_ref, False), rows_of_core(held_ref, 1 - my_core()))
    sent_ref[...] = total.astype(sent_ref.dtype)


def kept_kernel(own_ref, other_ref, held_ref, kept_ref):
    core = my_core()
    total = product(half_of(own_ref, True), rows_of_core(held_ref, core))
    total = total + product(half_of(other_ref, True), rows_of_core(held_ref, 1 - core))
    kept_ref[...] = total.astype(kept_ref.dtype)


def part_of_first(kernel, kind, *operands):
    vmem = pl.BlockSpec(memory_space=pltpu.VMEM)
    own, held = operands[0], operands[1 if kernel is begin_kernel else 2]
    return pl.pallas_call(
        kernel,
        out_shape=jax.ShapeDtypeStruct((own.shape[0] // 2, held.shape[1]), kind),
        in_specs=[vmem] * len(operands),
        out_specs=vmem,
        cost_estimate=pl.CostEstimate(flops=1 << 10, bytes_accessed=1 << 10, transcendentals=0),
        compiler_params=pltpu.CompilerParams(vmem_limit_bytes=VMEM_LIMIT),
        name="project_first",
    )(*operands)


def project_kernel(bring, own_ref, other_ref, held_ref, *refs):
    refs, copies = list(refs), []
    if bring:
        w_ref, sems = refs.pop(0), refs.pop()
    sent_ref, kept_ref = refs.pop(0), refs.pop(0)
    for n, (first, _) in enumerate(bring):
        copies += fetch_columns(w_ref, first, refs.pop(0), sems, n * PIECES)
    (rows_ref,) = refs
    own, other = leaving_first(own_ref), leaving_first(other_ref)
    chunk, part, left = sent_ref.shape[0], own_ref.shape[1], my_core() == 0
    rows_ref[:, :part] = jnp.where(left, own, other)
    rows_ref[:, part:] = jnp.where(left, other, own)
    both = product(rows_ref[...], held_ref[...]).astype(sent_ref.dtype)
    sent_ref[...] = both[:chunk]
    kept_ref[...] = both[chunk:]
    for copy in copies:
        copy.wait()


def project(own, other, held, out_weight, bring):
    rows, (depth, width) = own.shape[0], held.shape
    vmem = pl.BlockSpec(memory_space=pltpu.VMEM)
    out_shape = [jax.ShapeDtypeStruct((rows // 2, width), jnp.bfloat16)] * 2
    out_shape += [jax.ShapeDtypeStruct((depth, columns), held.dtype) for _, columns in bring]
    in_specs, operands = [vmem] * 3, [own, other, held]
    scratch = [pltpu.VMEM((rows, depth), jnp.bfloat16)]
    if bring:
        in_specs.append(pl.BlockSpec(memory_space=pltpu.HBM))
        operands.append(out_weight)
        scratch.append(pltpu.SemaphoreType.DMA((PIECES * len(bring),)))
    return pl.pallas_call(
        functools.partial(project_kernel, bring),
        out_shape=out_shape,
        in_specs=in_specs,
        out_specs=[vmem] * len(out_shape),
        scratch_shapes=scratch,
        cost_estimate=pl.CostEstimate(flops=1 << 10, bytes_accessed=1 << 10, transcendentals=0),
        compiler_params=pltpu.CompilerParams(vmem_limit_bytes=VMEM_LIMIT),
        name="project",
    )(*operands)


def prepare_kernel(
    chunk, q_ref, k_ref, v_ref, position_ref, sent_ref, kept_ref, *query_refs_and_scratch
):
    *query_refs, first_ref, sems = query_refs_and_scratch
    rows, heads = k_ref.shape[0], k_ref.shape[1] // HEAD_WIDTH // 2
    columns = query_refs[0].shape[1]
    copies = [pltpu.make_async_copy(position_ref, first_ref, sems.at[0])]
    for ref, core in ((sent_ref, 1 - my_core()), (kept_ref, my_core())):
        for m, source in enumerate((k_ref, v_ref)):
            for h in range(heads):
                at = pl.ds(pl.multiple_of((core * heads + h) * HEAD_WIDTH, HEAD_WIDTH), HEAD_WIDTH)
                to = ref.at[pl.ds((m * heads + h) * rows, rows)]
                copies.append(pltpu.make_async_copy(source.at[:, at], to, sems.at[len(copies)]))
    for ref, core in zip(query_refs, (1 - my_core(), my_core())):
        at = pl.ds(pl.multiple_of(core * columns, columns), columns)
        copies.append(pltpu.make_async_copy(q_ref.at[:, at], ref, sems.at[len(copies)]))
    for copy in copies:
        copy.start()
    copies[0].wait()
    c = lax.div(first_ref[0], jnp.int32(chunk)).astype(jnp.float32)
    header = jnp.full((HEADER, HEAD_WIDTH), c, jnp.float32).astype(jnp.bfloat16)
    sent_ref[2 * heads * rows :] = header
    kept_ref[2 * heads * rows :] = header
    for copy in copies[1:]:
        copy.wait()


def prepare(queries, keys, values, positions):
    vmem = pl.BlockSpec(memory_space=pltpu.VMEM)
    hbm = pl.BlockSpec(memory_space=pltpu.HBM)
    rows, blocks = keys.shape[0], keys.shape[1] // HEAD_WIDTH
    operands = [pltpu.with_memory_space_constraint(x, pltpu.HBM) for x in (queries, keys, values, positions)]
    return pl.pallas_call(
        functools.partial(prepare_kernel, rows // 2),
        out_shape=[jax.ShapeDtypeStruct((blocks * rows + HEADER, HEAD_WIDTH), jnp.bfloat16)] * 2
        + [jax.ShapeDtypeStruct((rows, queries.shape[1] // 2), jnp.bfloat16)] * 2,
        in_specs=[hbm] * 4,
        out_specs=[vmem] * 4,
        scratch_shapes=[
            pltpu.SMEM(positions.shape, jnp.int32),
            pltpu.SemaphoreType.DMA((3 + 2 * blocks,)),
        ],
        compiler_params=pltpu.CompilerParams(vmem_limit_bytes=VMEM_LIMIT),
        name="prepare",
    )(*operands)


def finish_kernel(first, pairs, *refs):
    out_ref, total_ref, sem = refs[-3:]
    at = 0
    for mine, theirs in zip(refs[:pairs], refs[pairs : 2 * pairs]):
        width = mine.shape[1]
        total = mine[...].astype(jnp.float32) + theirs[...].astype(jnp.float32)
        total_ref[:, at : at + width] = total.astype(total_ref.dtype)
        at += width
    copy = pltpu.make_async_copy(total_ref, out_ref.at[:, pl.ds(first, at)], sem)
    copy.start()
    copy.wait()


def finish(kept, received, first, columns, written=None):
    vmem, hbm = pl.BlockSpec(memory_space=pltpu.VMEM), pl.BlockSpec(memory_space=pltpu.HBM)
    rows, width = kept[0].shape[0], sum(part.shape[1] for part in kept)
    pairs = len(kept)
    return pl.pallas_call(
        functools.partial(finish_kernel, first, pairs),
        out_shape=jax.ShapeDtypeStruct((rows, columns), kept[0].dtype),
        in_specs=[vmem] * (2 * pairs) + ([] if written is None else [hbm]),
        out_specs=hbm,
        input_output_aliases={} if written is None else {2 * pairs: 0},
        scratch_shapes=[pltpu.VMEM((rows, width), kept[0].dtype), pltpu.SemaphoreType.DMA],
        cost_estimate=pl.CostEstimate(flops=1 << 10, bytes_accessed=1 << 10, transcendentals=0),
        compiler_params=pltpu.CompilerParams(vmem_limit_bytes=VMEM_LIMIT),
        name="finish",
    )(*kept, *received, *([] if written is None else [written]))


def after(value, *events):
    return lax.optimization_barrier((value, *events))[0]


def split_over_cores(count, queries, keys, values, positions, out_weight, fetch):
    chips, half = count // 2, count // 4
    rows, chunk = queries.shape[0], queries.shape[0] // 2
    heads = keys.shape[1] // HEAD_WIDTH // 2
    sibling = [(b, b ^ 1) for b in range(count)]
    clock, counter = ring_pairs(chips, 1), ring_pairs(chips, -1)
    up = lambda x: lax.ppermute(x, "blk", clock)
    down = lambda x: lax.ppermute(x, "blk", counter)
    cross_up, cross_down = ring_pairs(chips, 1, True), ring_pairs(chips, -1, True)

    sent, x, q_sent, q_own = prepare(queries, keys, values, positions)
    y = lax.ppermute(sent, "blk", sibling)
    q_got = lax.ppermute(q_sent, "blk", sibling)
    turned = turn(heads, chunk, [q_own, q_got])

    def call(pairs, state, own=False, last=False, fetch=None, which=(0, 1)):
        each = range(len(pairs))
        plan = dict(
            heads=heads,
            chunk=chunk,
            owners=2,
            own=own,
            own_at=lambda i: i,
            last=last,
            members=[(2 * j + i, 0) for j in each for i in range(2)],
            headers=[(2 + 2 * j + i, 2 * heads * rows) for j in each for i in range(2)],
            owner_headers=[(0, 2 * heads * rows), (1, 2 * heads * rows)],
            fetch=fetch,
            which=which,
        )
        packets = [packet for pair in pairs for packet in pair]
        return attend(plan, turned, [x, y], packets, state, out_weight)

    held = {}

    def bring_with(groups, *arguments, **settings):
        cuts = [fetch[j] for j in groups]
        results = call(*arguments, fetch=cuts, **settings)
        held.update(zip(groups, results[2:]))
        return results[:2]

    state = bring_with((2,), [(x, y)], None, own=True)
    for r in range(1, half):
        if r == 1:
            up_first, up_second = up(x), lax.ppermute(sent, "blk", cross_up)
            down_first, down_second = lax.ppermute(sent, "blk", cross_down), down(x)
        else:
            up_first, down_first, *state = lax.optimization_barrier((up_first, down_first, *state))
            up_first, up_second = up(up_first), up(up_second)
            down_first, down_second = down(down_first), down(down_second)
            state = bring_with((0,) if r == half - 1 else (), arrived, state)
        arrived = [(up_first, up_second), (down_second, down_first)]
    up_first, down_first, *state = lax.optimization_barrier((up_first, down_first, *state))
    far = (up(up_first), down(down_first))
    state = bring_with((1,), arrived, state)
    (theirs,) = call([far], state, last=True, which=(1,))
    other = lax.ppermute(theirs, "blk", sibling)
    (own,) = call([far], state, last=True, which=(0,))
    return own, other, held


def one_head_a_device(count, queries, keys, values, positions):
    rows, chunk = queries.shape[0], queries.shape[0] // 2
    heads = keys.shape[1] // HEAD_WIDTH
    c = (positions[:1] // chunk).astype(jnp.bfloat16).reshape(1, 1)
    blocks = [x[:, h * HEAD_WIDTH : (h + 1) * HEAD_WIDTH] for x in (keys, values) for h in range(heads)]
    packet = jnp.concatenate(blocks + [jnp.broadcast_to(c, (TILE, HEAD_WIDTH))], axis=0)
    packets = lax.all_gather(packet, "blk", axis=0, tiled=True)
    size = packet.shape[0]
    here = lax.axis_index("blk")
    order = lax.rem(here + jnp.arange(count), count)
    packets = packets.reshape(count, size, -1)[order].reshape(count * size, -1)
    plan = dict(
        heads=heads,
        chunk=chunk,
        owners=1,
        own=True,
        own_at=lambda i: 0,
        last=True,
        members=[(0, j * size) for j in range(count)],
        headers=[(0, (j + 1) * size - TILE) for j in range(count)],
        owner_headers=[(0, size - TILE)],
    )
    turned = turn(heads, chunk, [queries])
    return attend(plan, turned, [], [packets], None)[0]


def shards(count, inner, queries, keys, values, positions, out_weight):
    heads = keys.shape[1] // HEAD_WIDTH
    if heads % 2:
        attended = one_head_a_device(count, queries, keys, values, positions)
        partial = jnp.dot(attended, out_weight, preferred_element_type=jnp.float32)
        return lax.psum_scatter(
            partial.astype(jnp.bfloat16), "inner", scatter_dimension=0, tiled=True
        )
    out_weight = pltpu.with_memory_space_constraint(out_weight, pltpu.HBM)
    shares = (10, 9, 8, 7, 6)
    widths = [out_weight.shape[1] * share // sum(shares) for share in shares]
    cuts = [(sum(widths[:j]), columns) for j, columns in enumerate(widths)]
    own, other, held = split_over_cores(
        count, queries, keys, values, positions, out_weight, cuts[:3]
    )
    bring = [cuts[j + 2 : j + 3] if j > 0 else [] for j in range(len(cuts))]
    begun = part_of_first(begin_kernel, jnp.float32, own, held[0])
    sent = part_of_first(first_kernel, jnp.bfloat16, own, other, held[0], begun)
    received, kept = [], [None]
    for j in range(len(cuts)):
        if j > 0:
            source = after(own, sent)
            sent, keep, *rest = project(source, other, held[j], out_weight, bring[j])
            kept.append(keep)
            if rest:
                held[len(held)] = rest[0]
        received.append(lax.ppermute(sent, "inner", [(0, 1), (1, 0)]))
    kept[0] = part_of_first(kept_kernel, jnp.bfloat16, after(own, sent), other, held[0])
    columns = out_weight.shape[1]
    result = finish(kept[:-1], received[:-1], 0, columns)
    return finish(kept[-1:], received[-1:], cuts[-1][0], columns, result)


def solution(mesh):
    placed = (P("blk", "inner"), P("blk", "inner"), P("blk", "inner"), P("blk"), P("inner", None))
    return jax.shard_map(
        functools.partial(shards, mesh.shape["blk"], mesh.shape["inner"]),
        mesh=mesh,
        in_specs=placed,
        out_specs=P(("blk", "inner"), None),
        check_vma=False,
    )
```

```python
import functools
import math

import jax
import jax.numpy as jnp
from jax import lax
from jax.experimental import pallas as pl
from jax.experimental.pallas import tpu as pltpu
from jax.sharding import PartitionSpec as P

HEAD_WIDTH = 128
QUERY_PER_KEY = 5
GROUP = QUERY_PER_KEY * HEAD_WIDTH
EXP2_SCALE = math.log2(math.e) / math.sqrt(HEAD_WIDTH)
MASKED = -1e30
VMEM_LIMIT = 16 * 1024 * 1024
TILE = 16
HEADER = 8
PIECES = 5


def ring_of_chips(chips):
    half = chips // 2
    if chips == 8:
        return [2 * z for z in range(half)] + [2 * z + 1 for z in reversed(range(half))]
    return list(range(half)) + list(reversed(range(half, chips)))


def ring_pairs(chips, step, cross=False):
    ring = ring_of_chips(chips)
    return [
        (2 * ring[i] + core, 2 * ring[(i + step) % chips] + (1 - core if cross else core))
        for i in range(chips)
        for core in range(2)
    ]


def my_core():
    return lax.rem(lax.axis_index("blk"), 2).astype(jnp.int32)


def product(a, b):
    return jnp.dot(a, b, preferred_element_type=jnp.float32)


def weigh(scores, high):
    return jnp.exp2((scores - high) * EXP2_SCALE).astype(jnp.bfloat16)


def turned_values(blocks):
    v = jnp.concatenate(blocks, axis=0)
    return jnp.concatenate([jnp.transpose(v), jnp.ones((TILE, v.shape[0]), v.dtype)], axis=0)


def fetch_columns(w_ref, first, held_ref, sems, sem):
    depth, width = held_ref.shape[0] // PIECES, held_ref.shape[1]
    copies = []
    for p in range(PIECES):
        at = pl.ds(p * depth, depth)
        copies.append(
            pltpu.make_async_copy(
                w_ref.at[at, pl.ds(first, width)], held_ref.at[at], sems.at[sem + p]
            )
        )
        copies[-1].start()
    return copies


def attend_kernel(plan, *refs):
    heads, chunk, owners = plan["heads"], plan["chunk"], plan["owners"]
    refs = list(refs)
    q_ref = refs.pop(0)
    mark_refs = [refs.pop(0) for _ in range(plan["marks"])]
    packets = [refs.pop(0) for _ in range(plan["packets"])]
    if plan["carried"]:
        in_high, in_sums = refs.pop(0), refs.pop(0)
    fetch = plan["fetch"]
    if fetch:
        w_ref = refs.pop(0)
    if plan["last"]:
        out_refs = {i: refs.pop(0) for i in plan["which"]}
    copies = []
    if fetch:
        sems = refs.pop()
        for n, (first, _) in enumerate(fetch):
            held_ref = refs.pop(0 if plan["last"] else 2)
            copies += fetch_columns(w_ref, first, held_ref, sems, n * PIECES)
    if plan["part"] is None:
        high_ref, sums_ref = refs

    sources = mark_refs + packets
    numbers = [
        jnp.max(
            sources[packet][row : row + HEADER].astype(jnp.float32)
        ).astype(jnp.int32)
        for packet, row in plan["owner_headers"] + plan["headers"]
    ]
    owner_c, member_c = numbers[:owners], numbers[owners:]

    def rows_of(j, half, block):
        packet, row = plan["members"][j]
        at = row + (2 * block + half) * chunk
        return packets[packet][pl.ds(at if isinstance(at, int) else pl.multiple_of(at, TILE), chunk)]

    def state_at(i, half, h):
        return (2 * i + half) * heads + h

    rows = QUERY_PER_KEY * chunk
    causal = lax.broadcasted_iota(jnp.int32, (chunk, rows), 0) <= lax.rem(
        lax.broadcasted_iota(jnp.int32, (chunk, rows), 1), chunk
    )
    count = len(plan["members"])

    def one_chain(group, h, i, shared):
        first, done = group[0], group[-1] == count - 1
        k_at, v_at = h, heads + h
        late_at, early_at = state_at(i, 1, h), state_at(i, 0, h)
        if "keys" not in shared:
            shared["keys"] = jnp.concatenate([rows_of(j, 0, k_at) for j in group], axis=0)
            shared["values"] = turned_values([rows_of(j, 0, v_at) for j in group])
        carried = None
        if first > 0:
            carried = [(ref[early_at], ref[late_at]) for ref in (high_ref, sums_ref)]
        elif plan["carried"]:
            carried = [(ref[early_at], ref[late_at]) for ref in (in_high, in_sums)]
        pairs = []
        for j in group:
            if plan["own"] and j == plan["own_at"](i):
                pairs += [(j, 0, causal), (j, 1, causal)]
            else:
                pairs.append((j, (member_c[j] > owner_c[i]).astype(jnp.int32), None))
        base = product(shared["keys"], q_ref[late_at])
        scores = []
        for j, half, mask in pairs:
            s = product(rows_of(j, half, k_at), q_ref[state_at(i, half, h)])
            scores.append(s if mask is None else jnp.where(mask, s, MASKED))
        values = turned_values([rows_of(j, half, v_at) for j, half, _ in pairs])
        tops = [jnp.max(s, axis=0, keepdims=True) for s in scores]
        highs = []
        for side in range(2):
            some = [jnp.where(half == side, top, MASKED) for (_, half, _), top in zip(pairs, tops)]
            if side == 1:
                some.append(jnp.max(base, axis=0, keepdims=True))
            if carried is not None:
                some.append(carried[0][side])
            highs.append(functools.reduce(jnp.maximum, some))
        yield
        base_weights = weigh(base, highs[1])
        weights = [
            weigh(s, jnp.where(half == 1, highs[1], highs[0])) for (_, half, _), s in zip(pairs, scores)
        ]
        zero = jnp.zeros_like(weights[0])
        chosen = [
            jnp.concatenate(
                [jnp.where(half == side, w, zero) for (_, half, _), w in zip(pairs, weights)], axis=0
            )
            for side in range(2)
        ]
        yield
        for side, at in ((0, early_at), (1, late_at)):
            sums = product(values, chosen[side])
            if side == 1:
                sums = sums + product(shared["values"], base_weights)
            if carried is not None:
                shrink = jnp.exp2((carried[0][side] - highs[side]) * EXP2_SCALE)
                sums = sums + carried[1][side] * shrink
            if plan["last"] and done:
                mixed = sums[:HEAD_WIDTH] * (1.0 / sums[HEAD_WIDTH : HEAD_WIDTH + 1])
                mixed = jnp.transpose(mixed.astype(out_refs[i].dtype))
                place = side
                if plan["sent_first"]:
                    place = (lax.axis_index("inner") == side).astype(jnp.int32)
                rows_at = pl.ds(pl.multiple_of(place * chunk, TILE), chunk)
                for g in range(QUERY_PER_KEY):
                    to = pl.multiple_of(h * GROUP + g * HEAD_WIDTH, HEAD_WIDTH)
                    out_refs[i][rows_at, pl.ds(to, HEAD_WIDTH)] = mixed[g * chunk : (g + 1) * chunk]
            else:
                high_ref[at] = highs[side]
                sums_ref[at] = sums
        yield

    def one_side(h, i, side):
        at = state_at(i, side, h)
        visible = [member_c[j] > owner_c[i] if side else member_c[j] < owner_c[i] for j in range(count)]
        halves = ([(j, 0) for j in range(count)] if side else []) + [(j, side) for j in range(count)]
        k = jnp.concatenate([rows_of(j, half, h) for j, half in halves], axis=0)
        values = turned_values([rows_of(j, half, heads + h) for j, half in halves])
        s = product(k, q_ref[at])
        whole = (len(halves) - count) * chunk
        blocks = [s[whole + j * chunk : whole + (j + 1) * chunk] for j in range(count)]
        tops = [in_high[at]]
        if side:
            tops.append(jnp.max(s[:whole], axis=0, keepdims=True))
        for block, seen in zip(blocks, visible):
            tops.append(jnp.where(seen, jnp.max(block, axis=0, keepdims=True), MASKED))
        high = functools.reduce(jnp.maximum, tops)
        yield
        weights = [weigh(s[:whole], high)] if side else []
        for block, seen in zip(blocks, visible):
            w = weigh(block, high)
            weights.append(jnp.where(seen, w, jnp.zeros_like(w)))
        weights = jnp.concatenate(weights, axis=0)
        yield
        shrink = jnp.exp2((in_high[at] - high) * EXP2_SCALE)
        sums = product(values, weights) + in_sums[at] * shrink
        mixed = sums[:HEAD_WIDTH] * (1.0 / sums[HEAD_WIDTH : HEAD_WIDTH + 1])
        mixed = jnp.transpose(mixed.astype(out_refs[i].dtype))
        for g in range(QUERY_PER_KEY):
            to = h * GROUP + g * HEAD_WIDTH
            out_refs[i][:, to : to + HEAD_WIDTH] = mixed[g * chunk : (g + 1) * chunk]
        yield

    def staggered(chains):
        for t in range(len(chains) + 2):
            for stage in (2, 1, 0):
                if 0 <= t - stage < len(chains):
                    next(chains[t - stage])

    if plan["part"] is not None:
        mine = lax.axis_index("inner").astype(jnp.int32)
        for side in range(2):

            @pl.when((mine == side) == (plan["part"] == "kept"))
            def _(side=side):
                staggered([one_side(h, i, side) for h in range(heads) for i in plan["which"]])

        return

    for first in range(0, count, 6):
        group = range(first, min(first + 6, count))

        def run(heads_at_once, group=group):
            chains = []
            for h in heads_at_once:
                shared = {}
                chains += [one_chain(group, h, i, shared) for i in plan["which"]]
            staggered(chains)

        if fetch:

            def one_head(h, carry):
                run([h])
                return carry

            lax.fori_loop(0, heads, one_head, 0)
        else:
            run(range(heads))
    for copy in copies:
        copy.wait()


def attend(plan, turned, marks, packets, state, out_weight=None):
    heads, chunk, owners = plan["heads"], plan["chunk"], plan["owners"]
    count = len(plan["members"])
    plan = dict(plan, marks=len(marks), packets=len(packets), carried=state is not None)
    fetch = plan.setdefault("fetch", None)
    which = plan.setdefault("which", range(owners))
    part = plan.setdefault("part", None)
    plan.setdefault("sent_first", False)
    rows = QUERY_PER_KEY * chunk
    slots = owners * 2 * heads
    vmem = pl.BlockSpec(memory_space=pltpu.VMEM)
    kept = [(slots, 1, rows), (slots, HEAD_WIDTH + TILE, rows)]
    if plan["last"]:
        shape = ((2 if part is None else 1) * chunk, heads * GROUP)
        out_shape = [jax.ShapeDtypeStruct(shape, jnp.bfloat16)] * len(which)
    else:
        out_shape = [jax.ShapeDtypeStruct(shape, jnp.float32) for shape in kept]
    operands = 1 + len(marks) + len(packets) + (0 if state is None else 2)
    in_specs = [vmem] * operands
    scratch = []
    if plan["last"] and part is None:
        scratch = [pltpu.VMEM(shape, jnp.float32) for shape in kept]
    if fetch:
        in_specs.append(pl.BlockSpec(memory_space=pltpu.HBM))
        for _, columns in fetch:
            out_shape.append(jax.ShapeDtypeStruct((out_weight.shape[0], columns), out_weight.dtype))
        scratch.append(pltpu.SemaphoreType.DMA((PIECES * len(fetch),)))
    flops = 4 * owners * heads * rows * HEAD_WIDTH * count * chunk * 2
    return pl.pallas_call(
        functools.partial(attend_kernel, plan),
        out_shape=out_shape,
        in_specs=in_specs,
        out_specs=[vmem] * len(out_shape),
        scratch_shapes=scratch,
        cost_estimate=pl.CostEstimate(
            flops=flops, bytes_accessed=4 << 20, transcendentals=flops // 512
        ),
        compiler_params=pltpu.CompilerParams(vmem_limit_bytes=VMEM_LIMIT),
        name="attend",
    )(turned, *marks, *packets, *(state or ()), *([out_weight] if fetch else []))


def turn_kernel(heads, chunk, *refs):
    q_refs, turned_ref = refs[:-1], refs[-1]
    for i, q_ref in enumerate(q_refs):
        for half in range(2):
            for h in range(heads):
                columns = [slice(at, at + HEAD_WIDTH) for at in range(h * GROUP, (h + 1) * GROUP, HEAD_WIDTH)]
                q = jnp.concatenate(
                    [q_ref[half * chunk : (half + 1) * chunk, at] for at in columns], axis=0
                )
                turned_ref[(2 * i + half) * heads + h] = jnp.transpose(q)


def turn(heads, chunk, queries):
    vmem = pl.BlockSpec(memory_space=pltpu.VMEM)
    owners = len(queries)
    shape = (2 * owners * heads, HEAD_WIDTH, QUERY_PER_KEY * chunk)
    return pl.pallas_call(
        functools.partial(turn_kernel, heads, chunk),
        out_shape=jax.ShapeDtypeStruct(shape, jnp.bfloat16),
        in_specs=[vmem] * owners,
        out_specs=vmem,
        cost_estimate=pl.CostEstimate(flops=1 << 10, bytes_accessed=1 << 10, transcendentals=0),
        compiler_params=pltpu.CompilerParams(vmem_limit_bytes=VMEM_LIMIT),
        name="turn",
    )(*queries)


def rows_of_core(held_ref, core):
    depth = held_ref.shape[0] // 2
    return held_ref[pl.ds(pl.multiple_of(core * depth, depth), depth)]


def join_heads(own_ref, other_ref, rows_ref):
    part, left = own_ref.shape[1], my_core() == 0
    rows_ref[:, :part] = jnp.where(left, own_ref[...], other_ref[...])
    rows_ref[:, part:] = jnp.where(left, other_ref[...], own_ref[...])


def begin_kernel(own_ref, held_ref, begun_ref):
    begun_ref[...] = product(own_ref[...], rows_of_core(held_ref, my_core()))


def first_kernel(other_ref, held_ref, begun_ref, sent_ref):
    total = begun_ref[...] + product(other_ref[...], rows_of_core(held_ref, 1 - my_core()))
    sent_ref[...] = total.astype(sent_ref.dtype)


def project_kernel(bring, *refs):
    refs, copies = list(refs), []
    sent_rows, kept_rows, held_ref = refs[:2], refs[2:4], refs[4]
    refs = refs[5:]
    if bring:
        w_ref, sems = refs.pop(0), refs.pop()
    sent_ref, kept_ref = refs.pop(0), refs.pop(0)
    for n, (first, _) in enumerate(bring):
        copies += fetch_columns(w_ref, first, refs.pop(0), sems, n * PIECES)
    (rows_ref,) = refs
    chunk = sent_ref.shape[0]
    join_heads(*sent_rows, rows_ref.at[:chunk])
    join_heads(*kept_rows, rows_ref.at[chunk:])
    both = product(rows_ref[...], held_ref[...]).astype(sent_ref.dtype)
    sent_ref[...] = both[:chunk]
    kept_ref[...] = both[chunk:]
    for copy in copies:
        copy.wait()


def keep_kernel(own_ref, other_ref, held_ref, kept_ref, rows_ref):
    join_heads(own_ref, other_ref, rows_ref)
    kept_ref[...] = product(rows_ref[...], held_ref[...]).astype(kept_ref.dtype)


def multiply(kernel, operands, outputs, scratch=(), weight=None):
    vmem = pl.BlockSpec(memory_space=pltpu.VMEM)
    more = [] if weight is None else [weight]
    return pl.pallas_call(
        kernel,
        out_shape=[jax.ShapeDtypeStruct(shape, kind) for shape, kind in outputs],
        in_specs=[vmem] * len(operands) + [pl.BlockSpec(memory_space=pltpu.HBM)] * len(more),
        out_specs=[vmem] * len(outputs),
        scratch_shapes=list(scratch),
        cost_estimate=pl.CostEstimate(flops=1 << 10, bytes_accessed=1 << 10, transcendentals=0),
        compiler_params=pltpu.CompilerParams(vmem_limit_bytes=VMEM_LIMIT),
        name="multiply",
    )(*operands, *more)


def prepare_kernel(
    chunk, q_ref, k_ref, v_ref, position_ref, sent_ref, kept_ref, *query_refs_and_scratch
):
    *query_refs, first_ref, sems = query_refs_and_scratch
    rows, heads = k_ref.shape[0], k_ref.shape[1] // HEAD_WIDTH // 2
    columns = query_refs[0].shape[1]
    copies = [pltpu.make_async_copy(position_ref, first_ref, sems.at[0])]
    for ref, core in ((sent_ref, 1 - my_core()), (kept_ref, my_core())):
        for m, source in enumerate((k_ref, v_ref)):
            for h in range(heads):
                at = pl.ds(pl.multiple_of((core * heads + h) * HEAD_WIDTH, HEAD_WIDTH), HEAD_WIDTH)
                to = ref.at[pl.ds((m * heads + h) * rows, rows)]
                copies.append(pltpu.make_async_copy(source.at[:, at], to, sems.at[len(copies)]))
    for ref, core in zip(query_refs, (1 - my_core(), my_core())):
        at = pl.ds(pl.multiple_of(core * columns, columns), columns)
        copies.append(pltpu.make_async_copy(q_ref.at[:, at], ref, sems.at[len(copies)]))
    for copy in copies:
        copy.start()
    copies[0].wait()
    c = lax.div(first_ref[0], jnp.int32(chunk)).astype(jnp.float32)
    header = jnp.full((HEADER, HEAD_WIDTH), c, jnp.float32).astype(jnp.bfloat16)
    sent_ref[2 * heads * rows :] = header
    kept_ref[2 * heads * rows :] = header
    for copy in copies[1:]:
        copy.wait()


def prepare(queries, keys, values, positions):
    vmem = pl.BlockSpec(memory_space=pltpu.VMEM)
    hbm = pl.BlockSpec(memory_space=pltpu.HBM)
    rows, blocks = keys.shape[0], keys.shape[1] // HEAD_WIDTH
    operands = [pltpu.with_memory_space_constraint(x, pltpu.HBM) for x in (queries, keys, values, positions)]
    return pl.pallas_call(
        functools.partial(prepare_kernel, rows // 2),
        out_shape=[jax.ShapeDtypeStruct((blocks * rows + HEADER, HEAD_WIDTH), jnp.bfloat16)] * 2
        + [jax.ShapeDtypeStruct((rows, queries.shape[1] // 2), jnp.bfloat16)] * 2,
        in_specs=[hbm] * 4,
        out_specs=[vmem] * 4,
        scratch_shapes=[
            pltpu.SMEM(positions.shape, jnp.int32),
            pltpu.SemaphoreType.DMA((3 + 2 * blocks,)),
        ],
        compiler_params=pltpu.CompilerParams(vmem_limit_bytes=VMEM_LIMIT),
        name="prepare",
    )(*operands)


def finish_kernel(first, pairs, *refs):
    out_ref, total_ref, sem = refs[-3:]
    at = 0
    for mine, theirs in zip(refs[:pairs], refs[pairs : 2 * pairs]):
        width = mine.shape[1]
        total = mine[...].astype(jnp.float32) + theirs[...].astype(jnp.float32)
        total_ref[:, at : at + width] = total.astype(total_ref.dtype)
        at += width
    copy = pltpu.make_async_copy(total_ref, out_ref.at[:, pl.ds(first, at)], sem)
    copy.start()
    copy.wait()


def finish(kept, received, first, columns, written=None):
    vmem, hbm = pl.BlockSpec(memory_space=pltpu.VMEM), pl.BlockSpec(memory_space=pltpu.HBM)
    rows, width = kept[0].shape[0], sum(part.shape[1] for part in kept)
    pairs = len(kept)
    return pl.pallas_call(
        functools.partial(finish_kernel, first, pairs),
        out_shape=jax.ShapeDtypeStruct((rows, columns), kept[0].dtype),
        in_specs=[vmem] * (2 * pairs) + ([] if written is None else [hbm]),
        out_specs=hbm,
        input_output_aliases={} if written is None else {2 * pairs: 0},
        scratch_shapes=[pltpu.VMEM((rows, width), kept[0].dtype), pltpu.SemaphoreType.DMA],
        cost_estimate=pl.CostEstimate(flops=1 << 10, bytes_accessed=1 << 10, transcendentals=0),
        compiler_params=pltpu.CompilerParams(vmem_limit_bytes=VMEM_LIMIT),
        name="finish",
    )(*kept, *received, *([] if written is None else [written]))


def after(value, *events):
    return lax.optimization_barrier((value, events))[0]


def split_over_cores(count, queries, keys, values, positions, out_weight, fetch):
    chips, half = count // 2, count // 4
    rows, chunk = queries.shape[0], queries.shape[0] // 2
    heads = keys.shape[1] // HEAD_WIDTH // 2
    sibling = [(b, b ^ 1) for b in range(count)]
    clock, counter = ring_pairs(chips, 1), ring_pairs(chips, -1)
    up = lambda x: lax.ppermute(x, "blk", clock)
    down = lambda x: lax.ppermute(x, "blk", counter)
    cross_up, cross_down = ring_pairs(chips, 1, True), ring_pairs(chips, -1, True)

    sent, x, q_sent, q_own = prepare(queries, keys, values, positions)
    y = lax.ppermute(sent, "blk", sibling)
    q_got = lax.ppermute(q_sent, "blk", sibling)
    turned = turn(heads, chunk, [q_own, q_got])

    def call(pairs, state, own=False, last=False, fetch=None, which=(0, 1), part=None):
        each = range(len(pairs))
        plan = dict(
            heads=heads,
            chunk=chunk,
            owners=2,
            own=own,
            own_at=lambda i: i,
            last=last,
            members=[(2 * j + i, 0) for j in each for i in range(2)],
            headers=[(2 + 2 * j + i, 2 * heads * rows) for j in each for i in range(2)],
            owner_headers=[(0, 2 * heads * rows), (1, 2 * heads * rows)],
            fetch=fetch,
            which=which,
            part=part,
            sent_first=True,
        )
        packets = [packet for pair in pairs for packet in pair]
        return attend(plan, turned, [x, y], packets, state, out_weight)

    held = {}

    def bring_with(groups, *arguments, **settings):
        cuts = [fetch[j] for j in groups]
        results = call(*arguments, fetch=cuts, **settings)
        held.update(zip(groups, results[2:]))
        return results[:2]

    state = bring_with((2,), [(x, y)], None, own=True)
    for r in range(1, half):
        if r == 1:
            up_first, up_second = up(x), lax.ppermute(sent, "blk", cross_up)
            down_first, down_second = lax.ppermute(sent, "blk", cross_down), down(x)
        else:
            up_first, down_first, *state = lax.optimization_barrier((up_first, down_first, *state))
            up_first, up_second = up(up_first), up(up_second)
            down_first, down_second = down(down_first), down(down_second)
            state = bring_with((0,) if r == half - 1 else (), arrived, state)
        arrived = [(up_first, up_second), (down_second, down_first)]
    up_first, down_first, *state = lax.optimization_barrier((up_first, down_first, *state))
    far = (up(up_first), down(down_first))
    state = bring_with((1,), arrived, state)
    (theirs,) = call([far], state, last=True, which=(1,))
    other = [lax.ppermute(rows, "blk", sibling) for rows in (theirs[:chunk], theirs[chunk:])]
    (own,) = call([far], state, last=True, which=(0,), part="sent")

    def own_to_keep(event):
        return call([far], after(state, event), last=True, which=(0,), part="kept")[0]

    return own, other, held, own_to_keep


def one_head_a_device(count, queries, keys, values, positions):
    rows, chunk = queries.shape[0], queries.shape[0] // 2
    heads = keys.shape[1] // HEAD_WIDTH
    c = (positions[:1] // chunk).astype(jnp.bfloat16).reshape(1, 1)
    blocks = [x[:, h * HEAD_WIDTH : (h + 1) * HEAD_WIDTH] for x in (keys, values) for h in range(heads)]
    packet = jnp.concatenate(blocks + [jnp.broadcast_to(c, (TILE, HEAD_WIDTH))], axis=0)
    packets = lax.all_gather(packet, "blk", axis=0, tiled=True)
    size = packet.shape[0]
    here = lax.axis_index("blk")
    order = lax.rem(here + jnp.arange(count), count)
    packets = packets.reshape(count, size, -1)[order].reshape(count * size, -1)
    plan = dict(
        heads=heads,
        chunk=chunk,
        owners=1,
        own=True,
        own_at=lambda i: 0,
        last=True,
        members=[(0, j * size) for j in range(count)],
        headers=[(0, (j + 1) * size - TILE) for j in range(count)],
        owner_headers=[(0, size - TILE)],
    )
    turned = turn(heads, chunk, [queries])
    return attend(plan, turned, [], [packets], None)[0]


def shards(count, inner, queries, keys, values, positions, out_weight):
    heads = keys.shape[1] // HEAD_WIDTH
    if heads % 2:
        attended = one_head_a_device(count, queries, keys, values, positions)
        partial = jnp.dot(attended, out_weight, preferred_element_type=jnp.float32)
        return lax.psum_scatter(
            partial.astype(jnp.bfloat16), "inner", scatter_dimension=0, tiled=True
        )
    out_weight = pltpu.with_memory_space_constraint(out_weight, pltpu.HBM)
    shares = (10, 9, 8, 7, 6)
    widths = [out_weight.shape[1] * share // sum(shares) for share in shares]
    cuts = [(sum(widths[:j]), columns) for j, columns in enumerate(widths)]
    own, (other, other_kept), held, own_to_keep = split_over_cores(
        count, queries, keys, values, positions, out_weight, cuts[:3]
    )
    chunk, depth, kind = own.shape[0], out_weight.shape[0], own.dtype
    (begun,) = multiply(begin_kernel, [own, held[0]], [((chunk, widths[0]), jnp.float32)])
    (sent,) = multiply(first_kernel, [other, held[0], begun], [((chunk, widths[0]), kind)])
    own_kept = own_to_keep(sent)
    received, kept = [], [None]
    for j in range(len(cuts)):
        if j > 0:
            bring = cuts[j + 2 : j + 3]
            results = multiply(
                functools.partial(project_kernel, bring),
                [after(own, sent), other, own_kept, other_kept, held[j]],
                [((chunk, widths[j]), kind)] * 2 + [((depth, columns), kind) for _, columns in bring],
                [pltpu.VMEM((2 * chunk, depth), kind)] + [pltpu.SemaphoreType.DMA((PIECES,))] * len(bring),
                out_weight if bring else None,
            )
            sent, keep = results[:2]
            kept.append(keep)
            if bring:
                held[j + 2] = results[2]
        received.append(lax.ppermute(sent, "inner", [(0, 1), (1, 0)]))
    (kept[0],) = multiply(
        keep_kernel,
        [after(own_kept, sent), other_kept, held[0]],
        [((chunk, widths[0]), kind)],
        [pltpu.VMEM((chunk, depth), kind)],
    )
    columns = out_weight.shape[1]
    result = finish(kept[:-1], received[:-1], 0, columns)
    return finish(kept[-1:], received[-1:], cuts[-1][0], columns, result)


def solution(mesh):
    placed = (P("blk", "inner"), P("blk", "inner"), P("blk", "inner"), P("blk"), P("inner", None))
    return jax.shard_map(
        functools.partial(shards, mesh.shape["blk"], mesh.shape["inner"]),
        mesh=mesh,
        in_specs=placed,
        out_specs=P(("blk", "inner"), None),
        check_vma=False,
    )
```

```python
import functools
import math

import jax
import jax.numpy as jnp
from jax import lax
from jax.experimental import pallas as pl
from jax.experimental.pallas import tpu as pltpu
from jax.sharding import PartitionSpec as P

HEAD_WIDTH = 128
QUERY_PER_KEY = 5
GROUP = QUERY_PER_KEY * HEAD_WIDTH
EXP2_SCALE = math.log2(math.e) / math.sqrt(HEAD_WIDTH)
MASKED = -1e30
VMEM_LIMIT = 16 * 1024 * 1024
TILE = 16
HEADER = 8
PIECES = 5


def ring_of_chips(chips):
    half = chips // 2
    if chips == 8:
        return [2 * z for z in range(half)] + [2 * z + 1 for z in reversed(range(half))]
    return list(range(half)) + list(reversed(range(half, chips)))


def ring_pairs(chips, step, cross=False):
    ring = ring_of_chips(chips)
    return [
        (2 * ring[i] + core, 2 * ring[(i + step) % chips] + (1 - core if cross else core))
        for i in range(chips)
        for core in range(2)
    ]


def my_core():
    return lax.rem(lax.axis_index("blk"), 2).astype(jnp.int32)


def product(a, b):
    return jnp.dot(a, b, preferred_element_type=jnp.float32)


def weigh(scores, high):
    return jnp.exp2((scores - high) * EXP2_SCALE).astype(jnp.bfloat16)


def turned_values(blocks):
    v = jnp.concatenate(blocks, axis=0)
    return jnp.concatenate([jnp.transpose(v), jnp.ones((TILE, v.shape[0]), v.dtype)], axis=0)


def fetch_columns(w_ref, first, held_ref, sems, sem):
    depth, width = held_ref.shape[0] // PIECES, held_ref.shape[1]
    copies = []
    for p in range(PIECES):
        at = pl.ds(p * depth, depth)
        copies.append(
            pltpu.make_async_copy(
                w_ref.at[at, pl.ds(first, width)], held_ref.at[at], sems.at[sem + p]
            )
        )
        copies[-1].start()
    return copies


def attend_kernel(plan, *refs):
    heads, chunk, owners = plan["heads"], plan["chunk"], plan["owners"]
    refs = list(refs)
    q_ref = refs.pop(0)
    mark_refs = [refs.pop(0) for _ in range(plan["marks"])]
    packets = [refs.pop(0) for _ in range(plan["packets"])]
    if plan["carried"]:
        in_high, in_sums = refs.pop(0), refs.pop(0)
    fetch = plan["fetch"]
    if fetch:
        w_ref = refs.pop(0)
    if plan["last"]:
        out_refs = {i: refs.pop(0) for i in plan["which"]}
    copies = []
    if fetch:
        sems = refs.pop()
        for n, (first, _) in enumerate(fetch):
            held_ref = refs.pop(0 if plan["last"] else 2)
            copies += fetch_columns(w_ref, first, held_ref, sems, n * PIECES)
    if plan["part"] is None:
        high_ref, sums_ref = refs

    sources = mark_refs + packets
    numbers = [
        jnp.max(
            sources[packet][row : row + HEADER].astype(jnp.float32)
        ).astype(jnp.int32)
        for packet, row in plan["owner_headers"] + plan["headers"]
    ]
    owner_c, member_c = numbers[:owners], numbers[owners:]

    def rows_of(j, half, block):
        packet, row = plan["members"][j]
        at = row + (2 * block + half) * chunk
        return packets[packet][pl.ds(at if isinstance(at, int) else pl.multiple_of(at, TILE), chunk)]

    def state_at(i, half, h):
        return (2 * i + half) * heads + h

    rows = QUERY_PER_KEY * chunk
    causal = lax.broadcasted_iota(jnp.int32, (chunk, rows), 0) <= lax.rem(
        lax.broadcasted_iota(jnp.int32, (chunk, rows), 1), chunk
    )
    count = len(plan["members"])

    def one_chain(group, h, i, shared):
        first, done = group[0], group[-1] == count - 1
        k_at, v_at = h, heads + h
        late_at, early_at = state_at(i, 1, h), state_at(i, 0, h)
        if "keys" not in shared:
            shared["keys"] = jnp.concatenate([rows_of(j, 0, k_at) for j in group], axis=0)
            shared["values"] = turned_values([rows_of(j, 0, v_at) for j in group])
        carried = None
        if first > 0:
            carried = [(ref[early_at], ref[late_at]) for ref in (high_ref, sums_ref)]
        elif plan["carried"]:
            carried = [(ref[early_at], ref[late_at]) for ref in (in_high, in_sums)]
        pairs = []
        for j in group:
            if plan["own"] and j == plan["own_at"](i):
                pairs += [(j, 0, causal), (j, 1, causal)]
            else:
                pairs.append((j, (member_c[j] > owner_c[i]).astype(jnp.int32), None))
        base = product(shared["keys"], q_ref[late_at])
        scores = []
        for j, half, mask in pairs:
            s = product(rows_of(j, half, k_at), q_ref[state_at(i, half, h)])
            scores.append(s if mask is None else jnp.where(mask, s, MASKED))
        values = turned_values([rows_of(j, half, v_at) for j, half, _ in pairs])
        tops = [jnp.max(s, axis=0, keepdims=True) for s in scores]
        highs = []
        for side in range(2):
            some = [jnp.where(half == side, top, MASKED) for (_, half, _), top in zip(pairs, tops)]
            if side == 1:
                some.append(jnp.max(base, axis=0, keepdims=True))
            if carried is not None:
                some.append(carried[0][side])
            highs.append(functools.reduce(jnp.maximum, some))
        yield
        base_weights = weigh(base, highs[1])
        weights = [
            weigh(s, jnp.where(half == 1, highs[1], highs[0])) for (_, half, _), s in zip(pairs, scores)
        ]
        zero = jnp.zeros_like(weights[0])
        chosen = [
            jnp.concatenate(
                [jnp.where(half == side, w, zero) for (_, half, _), w in zip(pairs, weights)], axis=0
            )
            for side in range(2)
        ]
        yield
        for side, at in ((0, early_at), (1, late_at)):
            sums = product(values, chosen[side])
            if side == 1:
                sums = sums + product(shared["values"], base_weights)
            if carried is not None:
                shrink = jnp.exp2((carried[0][side] - highs[side]) * EXP2_SCALE)
                sums = sums + carried[1][side] * shrink
            if plan["last"] and done:
                mixed = sums[:HEAD_WIDTH] * (1.0 / sums[HEAD_WIDTH : HEAD_WIDTH + 1])
                mixed = jnp.transpose(mixed.astype(out_refs[i].dtype))
                place = side
                if plan["sent_first"]:
                    place = (lax.axis_index("inner") == side).astype(jnp.int32)
                rows_at = pl.ds(pl.multiple_of(place * chunk, TILE), chunk)
                for g in range(QUERY_PER_KEY):
                    to = pl.multiple_of(h * GROUP + g * HEAD_WIDTH, HEAD_WIDTH)
                    out_refs[i][rows_at, pl.ds(to, HEAD_WIDTH)] = mixed[g * chunk : (g + 1) * chunk]
            else:
                high_ref[at] = highs[side]
                sums_ref[at] = sums
        yield

    def one_side(h, i, side):
        at = state_at(i, side, h)
        visible = [member_c[j] > owner_c[i] if side else member_c[j] < owner_c[i] for j in range(count)]
        halves = ([(j, 0) for j in range(count)] if side else []) + [(j, side) for j in range(count)]
        k = jnp.concatenate([rows_of(j, half, h) for j, half in halves], axis=0)
        values = turned_values([rows_of(j, half, heads + h) for j, half in halves])
        s = product(k, q_ref[at])
        whole = (len(halves) - count) * chunk
        blocks = [s[whole + j * chunk : whole + (j + 1) * chunk] for j in range(count)]
        tops = [in_high[at]]
        if side:
            tops.append(jnp.max(s[:whole], axis=0, keepdims=True))
        for block, seen in zip(blocks, visible):
            tops.append(jnp.where(seen, jnp.max(block, axis=0, keepdims=True), MASKED))
        high = functools.reduce(jnp.maximum, tops)
        yield
        weights = [weigh(s[:whole], high)] if side else []
        for block, seen in zip(blocks, visible):
            w = weigh(block, high)
            weights.append(jnp.where(seen, w, jnp.zeros_like(w)))
        weights = jnp.concatenate(weights, axis=0)
        yield
        shrink = jnp.exp2((in_high[at] - high) * EXP2_SCALE)
        sums = product(values, weights) + in_sums[at] * shrink
        mixed = sums[:HEAD_WIDTH] * (1.0 / sums[HEAD_WIDTH : HEAD_WIDTH + 1])
        mixed = jnp.transpose(mixed.astype(out_refs[i].dtype))
        for g in range(QUERY_PER_KEY):
            to = h * GROUP + g * HEAD_WIDTH
            out_refs[i][:, to : to + HEAD_WIDTH] = mixed[g * chunk : (g + 1) * chunk]
        yield

    def staggered(chains):
        for t in range(len(chains) + 2):
            for stage in (2, 1, 0):
                if 0 <= t - stage < len(chains):
                    next(chains[t - stage])

    if plan["part"] is not None:
        mine = lax.axis_index("inner").astype(jnp.int32)
        for side in range(2):

            @pl.when((mine == side) == (plan["part"] == "kept"))
            def _(side=side):
                staggered([one_side(h, i, side) for h in range(heads) for i in plan["which"]])

        return

    for first in range(0, count, 6):
        group = range(first, min(first + 6, count))

        def run(heads_at_once, group=group):
            chains = []
            for h in heads_at_once:
                shared = {}
                chains += [one_chain(group, h, i, shared) for i in plan["which"]]
            staggered(chains)

        if fetch:

            def one_head(h, carry):
                run([h])
                return carry

            lax.fori_loop(0, heads, one_head, 0)
        else:
            run(range(heads))
    for copy in copies:
        copy.wait()


def attend(plan, turned, marks, packets, state, out_weight=None):
    heads, chunk, owners = plan["heads"], plan["chunk"], plan["owners"]
    count = len(plan["members"])
    plan = dict(plan, marks=len(marks), packets=len(packets), carried=state is not None)
    fetch = plan.setdefault("fetch", None)
    which = plan.setdefault("which", range(owners))
    part = plan.setdefault("part", None)
    plan.setdefault("sent_first", False)
    rows = QUERY_PER_KEY * chunk
    slots = owners * 2 * heads
    vmem = pl.BlockSpec(memory_space=pltpu.VMEM)
    kept = [(slots, 1, rows), (slots, HEAD_WIDTH + TILE, rows)]
    if plan["last"]:
        shape = ((2 if part is None else 1) * chunk, heads * GROUP)
        out_shape = [jax.ShapeDtypeStruct(shape, jnp.bfloat16)] * len(which)
    else:
        out_shape = [jax.ShapeDtypeStruct(shape, jnp.float32) for shape in kept]
    operands = 1 + len(marks) + len(packets) + (0 if state is None else 2)
    in_specs = [vmem] * operands
    scratch = []
    if plan["last"] and part is None:
        scratch = [pltpu.VMEM(shape, jnp.float32) for shape in kept]
    if fetch:
        in_specs.append(pl.BlockSpec(memory_space=pltpu.HBM))
        for _, columns in fetch:
            out_shape.append(jax.ShapeDtypeStruct((out_weight.shape[0], columns), out_weight.dtype))
        scratch.append(pltpu.SemaphoreType.DMA((PIECES * len(fetch),)))
    flops = 4 * owners * heads * rows * HEAD_WIDTH * count * chunk * 2
    return pl.pallas_call(
        functools.partial(attend_kernel, plan),
        out_shape=out_shape,
        in_specs=in_specs,
        out_specs=[vmem] * len(out_shape),
        scratch_shapes=scratch,
        cost_estimate=pl.CostEstimate(
            flops=flops, bytes_accessed=4 << 20, transcendentals=flops // 512
        ),
        compiler_params=pltpu.CompilerParams(vmem_limit_bytes=VMEM_LIMIT),
        name="attend",
    )(turned, *marks, *packets, *(state or ()), *([out_weight] if fetch else []))


def turn_kernel(heads, chunk, *refs):
    q_refs, turned_ref = refs[:-1], refs[-1]
    for i, q_ref in enumerate(q_refs):
        for half in range(2):
            for h in range(heads):
                columns = [slice(at, at + HEAD_WIDTH) for at in range(h * GROUP, (h + 1) * GROUP, HEAD_WIDTH)]
                q = jnp.concatenate(
                    [q_ref[half * chunk : (half + 1) * chunk, at] for at in columns], axis=0
                )
                turned_ref[(2 * i + half) * heads + h] = jnp.transpose(q)


def turn(heads, chunk, queries):
    vmem = pl.BlockSpec(memory_space=pltpu.VMEM)
    owners = len(queries)
    shape = (2 * owners * heads, HEAD_WIDTH, QUERY_PER_KEY * chunk)
    return pl.pallas_call(
        functools.partial(turn_kernel, heads, chunk),
        out_shape=jax.ShapeDtypeStruct(shape, jnp.bfloat16),
        in_specs=[vmem] * owners,
        out_specs=vmem,
        cost_estimate=pl.CostEstimate(flops=1 << 10, bytes_accessed=1 << 10, transcendentals=0),
        compiler_params=pltpu.CompilerParams(vmem_limit_bytes=VMEM_LIMIT),
        name="turn",
    )(*queries)


def rows_of_core(held_ref, core):
    depth = held_ref.shape[0] // 2
    return held_ref[pl.ds(pl.multiple_of(core * depth, depth), depth)]


def join_heads(own_ref, other_ref, rows_ref):
    part, left = own_ref.shape[1], my_core() == 0
    rows_ref[:, :part] = jnp.where(left, own_ref[...], other_ref[...])
    rows_ref[:, part:] = jnp.where(left, other_ref[...], own_ref[...])


def begin_kernel(own_ref, held_ref, begun_ref):
    begun_ref[...] = product(own_ref[...], rows_of_core(held_ref, my_core()))


def first_kernel(other_ref, held_ref, begun_ref, sent_ref):
    total = begun_ref[...] + product(other_ref[...], rows_of_core(held_ref, 1 - my_core()))
    sent_ref[...] = total.astype(sent_ref.dtype)


def project_kernel(bring, *refs):
    refs, copies = list(refs), []
    sent_rows, kept_rows, held_ref = refs[:2], refs[2:4], refs[4]
    refs = refs[5:]
    if bring:
        w_ref, sems = refs.pop(0), refs.pop()
    sent_ref, kept_ref = refs.pop(0), refs.pop(0)
    for n, (first, _) in enumerate(bring):
        copies += fetch_columns(w_ref, first, refs.pop(0), sems, n * PIECES)
    (rows_ref,) = refs
    chunk = sent_ref.shape[0]
    join_heads(*sent_rows, rows_ref.at[:chunk])
    join_heads(*kept_rows, rows_ref.at[chunk:])
    both = product(rows_ref[...], held_ref[...]).astype(sent_ref.dtype)
    sent_ref[...] = both[:chunk]
    kept_ref[...] = both[chunk:]
    for copy in copies:
        copy.wait()


def keep_kernel(own_ref, other_ref, held_ref, kept_ref, rows_ref):
    join_heads(own_ref, other_ref, rows_ref)
    kept_ref[...] = product(rows_ref[...], held_ref[...]).astype(kept_ref.dtype)


def multiply(kernel, operands, outputs, scratch=(), weight=None):
    vmem = pl.BlockSpec(memory_space=pltpu.VMEM)
    more = [] if weight is None else [weight]
    return pl.pallas_call(
        kernel,
        out_shape=[jax.ShapeDtypeStruct(shape, kind) for shape, kind in outputs],
        in_specs=[vmem] * len(operands) + [pl.BlockSpec(memory_space=pltpu.HBM)] * len(more),
        out_specs=[vmem] * len(outputs),
        scratch_shapes=list(scratch),
        cost_estimate=pl.CostEstimate(flops=1 << 10, bytes_accessed=1 << 10, transcendentals=0),
        compiler_params=pltpu.CompilerParams(vmem_limit_bytes=VMEM_LIMIT),
        name="multiply",
    )(*operands, *more)


def prepare_kernel(
    chunk, q_ref, k_ref, v_ref, position_ref, sent_ref, kept_ref, *query_refs_and_scratch
):
    *query_refs, first_ref, sems = query_refs_and_scratch
    rows, heads = k_ref.shape[0], k_ref.shape[1] // HEAD_WIDTH // 2
    columns = query_refs[0].shape[1]
    copies = [pltpu.make_async_copy(position_ref, first_ref, sems.at[0])]
    for ref, core in ((sent_ref, 1 - my_core()), (kept_ref, my_core())):
        for m, source in enumerate((k_ref, v_ref)):
            for h in range(heads):
                at = pl.ds(pl.multiple_of((core * heads + h) * HEAD_WIDTH, HEAD_WIDTH), HEAD_WIDTH)
                to = ref.at[pl.ds((m * heads + h) * rows, rows)]
                copies.append(pltpu.make_async_copy(source.at[:, at], to, sems.at[len(copies)]))
    for ref, core in zip(query_refs, (1 - my_core(), my_core())):
        at = pl.ds(pl.multiple_of(core * columns, columns), columns)
        copies.append(pltpu.make_async_copy(q_ref.at[:, at], ref, sems.at[len(copies)]))
    for copy in copies:
        copy.start()
    copies[0].wait()
    c = lax.div(first_ref[0], jnp.int32(chunk)).astype(jnp.float32)
    header = jnp.full((HEADER, HEAD_WIDTH), c, jnp.float32).astype(jnp.bfloat16)
    sent_ref[2 * heads * rows :] = header
    kept_ref[2 * heads * rows :] = header
    for copy in copies[1:]:
        copy.wait()


def prepare(queries, keys, values, positions):
    vmem = pl.BlockSpec(memory_space=pltpu.VMEM)
    hbm = pl.BlockSpec(memory_space=pltpu.HBM)
    rows, blocks = keys.shape[0], keys.shape[1] // HEAD_WIDTH
    operands = [pltpu.with_memory_space_constraint(x, pltpu.HBM) for x in (queries, keys, values, positions)]
    return pl.pallas_call(
        functools.partial(prepare_kernel, rows // 2),
        out_shape=[jax.ShapeDtypeStruct((blocks * rows + HEADER, HEAD_WIDTH), jnp.bfloat16)] * 2
        + [jax.ShapeDtypeStruct((rows, queries.shape[1] // 2), jnp.bfloat16)] * 2,
        in_specs=[hbm] * 4,
        out_specs=[vmem] * 4,
        scratch_shapes=[
            pltpu.SMEM(positions.shape, jnp.int32),
            pltpu.SemaphoreType.DMA((3 + 2 * blocks,)),
        ],
        compiler_params=pltpu.CompilerParams(vmem_limit_bytes=VMEM_LIMIT),
        name="prepare",
    )(*operands)


def finish_kernel(first, pairs, *refs):
    out_ref, total_ref, sem = refs[-3:]
    at = 0
    for mine, theirs in zip(refs[:pairs], refs[pairs : 2 * pairs]):
        width = mine.shape[1]
        total = mine[...].astype(jnp.float32) + theirs[...].astype(jnp.float32)
        total_ref[:, at : at + width] = total.astype(total_ref.dtype)
        at += width
    copy = pltpu.make_async_copy(total_ref, out_ref.at[:, pl.ds(first, at)], sem)
    copy.start()
    copy.wait()


def finish(kept, received, first, columns, written=None):
    vmem, hbm = pl.BlockSpec(memory_space=pltpu.VMEM), pl.BlockSpec(memory_space=pltpu.HBM)
    rows, width = kept[0].shape[0], sum(part.shape[1] for part in kept)
    pairs = len(kept)
    return pl.pallas_call(
        functools.partial(finish_kernel, first, pairs),
        out_shape=jax.ShapeDtypeStruct((rows, columns), kept[0].dtype),
        in_specs=[vmem] * (2 * pairs) + ([] if written is None else [hbm]),
        out_specs=hbm,
        input_output_aliases={} if written is None else {2 * pairs: 0},
        scratch_shapes=[pltpu.VMEM((rows, width), kept[0].dtype), pltpu.SemaphoreType.DMA],
        cost_estimate=pl.CostEstimate(flops=1 << 10, bytes_accessed=1 << 10, transcendentals=0),
        compiler_params=pltpu.CompilerParams(vmem_limit_bytes=VMEM_LIMIT),
        name="finish",
    )(*kept, *received, *([] if written is None else [written]))


def after(value, *events):
    return lax.optimization_barrier((value, events))[0]


def split_over_cores(count, queries, keys, values, positions, out_weight, fetch):
    chips, half = count // 2, count // 4
    rows, chunk = queries.shape[0], queries.shape[0] // 2
    heads = keys.shape[1] // HEAD_WIDTH // 2
    sibling = [(b, b ^ 1) for b in range(count)]
    clock, counter = ring_pairs(chips, 1), ring_pairs(chips, -1)
    up = lambda x: lax.ppermute(x, "blk", clock)
    down = lambda x: lax.ppermute(x, "blk", counter)
    cross_up, cross_down = ring_pairs(chips, 1, True), ring_pairs(chips, -1, True)

    sent, x, q_sent, q_own = prepare(queries, keys, values, positions)
    y = lax.ppermute(sent, "blk", sibling)
    q_got = lax.ppermute(q_sent, "blk", sibling)
    turned = turn(heads, chunk, [q_own, q_got])

    def call(pairs, state, own=False, last=False, fetch=None, which=(0, 1), part=None):
        each = range(len(pairs))
        plan = dict(
            heads=heads,
            chunk=chunk,
            owners=2,
            own=own,
            own_at=lambda i: i,
            last=last,
            members=[(2 * j + i, 0) for j in each for i in range(2)],
            headers=[(2 + 2 * j + i, 2 * heads * rows) for j in each for i in range(2)],
            owner_headers=[(0, 2 * heads * rows), (1, 2 * heads * rows)],
            fetch=fetch,
            which=which,
            part=part,
            sent_first=True,
        )
        packets = [packet for pair in pairs for packet in pair]
        return attend(plan, turned, [x, y], packets, state, out_weight)

    held = {}

    def bring_with(groups, *arguments, **settings):
        cuts = [fetch[j] for j in groups]
        results = call(*arguments, fetch=cuts, **settings)
        held.update(zip(groups, results[2:]))
        return results[:2]

    state = bring_with((2,), [(x, y)], None, own=True)
    for r in range(1, half):
        if r == 1:
            up_first, up_second = up(x), lax.ppermute(sent, "blk", cross_up)
            down_first, down_second = lax.ppermute(sent, "blk", cross_down), down(x)
        else:
            up_first, down_first, *state = lax.optimization_barrier((up_first, down_first, *state))
            up_first, up_second = up(up_first), up(up_second)
            down_first, down_second = down(down_first), down(down_second)
            state = bring_with((0,) if r == half - 1 else (), arrived, state)
        arrived = [(up_first, up_second), (down_second, down_first)]
    up_first, down_first, *state = lax.optimization_barrier((up_first, down_first, *state))
    far = (up(up_first), down(down_first))
    state = bring_with((1,), arrived, state)
    (theirs,) = call([far], state, last=True, which=(1,))
    other = lax.ppermute(theirs[:chunk], "blk", sibling)
    (own,) = call([far], state, last=True, which=(0,), part="sent")

    def rows_to_keep(event):
        other = lax.ppermute(after(theirs[chunk:], event), "blk", sibling)
        return call([far], after(state, event), last=True, which=(0,), part="kept")[0], other

    return own, other, held, rows_to_keep


def one_head_a_device(count, queries, keys, values, positions):
    rows, chunk = queries.shape[0], queries.shape[0] // 2
    heads = keys.shape[1] // HEAD_WIDTH
    c = (positions[:1] // chunk).astype(jnp.bfloat16).reshape(1, 1)
    blocks = [x[:, h * HEAD_WIDTH : (h + 1) * HEAD_WIDTH] for x in (keys, values) for h in range(heads)]
    packet = jnp.concatenate(blocks + [jnp.broadcast_to(c, (TILE, HEAD_WIDTH))], axis=0)
    packets = lax.all_gather(packet, "blk", axis=0, tiled=True)
    size = packet.shape[0]
    here = lax.axis_index("blk")
    order = lax.rem(here + jnp.arange(count), count)
    packets = packets.reshape(count, size, -1)[order].reshape(count * size, -1)
    plan = dict(
        heads=heads,
        chunk=chunk,
        owners=1,
        own=True,
        own_at=lambda i: 0,
        last=True,
        members=[(0, j * size) for j in range(count)],
        headers=[(0, (j + 1) * size - TILE) for j in range(count)],
        owner_headers=[(0, size - TILE)],
    )
    turned = turn(heads, chunk, [queries])
    return attend(plan, turned, [], [packets], None)[0]


def shards(count, inner, queries, keys, values, positions, out_weight):
    heads = keys.shape[1] // HEAD_WIDTH
    if heads % 2:
        attended = one_head_a_device(count, queries, keys, values, positions)
        partial = jnp.dot(attended, out_weight, preferred_element_type=jnp.float32)
        return lax.psum_scatter(
            partial.astype(jnp.bfloat16), "inner", scatter_dimension=0, tiled=True
        )
    out_weight = pltpu.with_memory_space_constraint(out_weight, pltpu.HBM)
    shares = (10, 9, 8, 7, 6)
    widths = [out_weight.shape[1] * share // sum(shares) for share in shares]
    cuts = [(sum(widths[:j]), columns) for j, columns in enumerate(widths)]
    own, other, held, rows_to_keep = split_over_cores(
        count, queries, keys, values, positions, out_weight, cuts[:3]
    )
    chunk, depth, kind = own.shape[0], out_weight.shape[0], own.dtype
    (begun,) = multiply(begin_kernel, [own, held[0]], [((chunk, widths[0]), jnp.float32)])
    (sent,) = multiply(first_kernel, [other, held[0], begun], [((chunk, widths[0]), kind)])
    own_kept, other_kept = rows_to_keep(sent)
    received, kept = [], [None]
    for j in range(len(cuts)):
        if j > 0:
            bring = cuts[j + 2 : j + 3]
            results = multiply(
                functools.partial(project_kernel, bring),
                [after(own, sent), other, own_kept, other_kept, held[j]],
                [((chunk, widths[j]), kind)] * 2 + [((depth, columns), kind) for _, columns in bring],
                [pltpu.VMEM((2 * chunk, depth), kind)] + [pltpu.SemaphoreType.DMA((PIECES,))] * len(bring),
                out_weight if bring else None,
            )
            sent, keep = results[:2]
            kept.append(keep)
            if bring:
                held[j + 2] = results[2]
        received.append(lax.ppermute(sent, "inner", [(0, 1), (1, 0)]))
    (kept[0],) = multiply(
        keep_kernel,
        [after(own_kept, sent), other_kept, held[0]],
        [((chunk, widths[0]), kind)],
        [pltpu.VMEM((chunk, depth), kind)],
    )
    columns = out_weight.shape[1]
    result = finish(kept[:-1], received[:-1], 0, columns)
    return finish(kept[-1:], received[-1:], cuts[-1][0], columns, result)


def solution(mesh):
    placed = (P("blk", "inner"), P("blk", "inner"), P("blk", "inner"), P("blk"), P("inner", None))
    return jax.shard_map(
        functools.partial(shards, mesh.shape["blk"], mesh.shape["inner"]),
        mesh=mesh,
        in_specs=placed,
        out_specs=P(("blk", "inner"), None),
        check_vma=False,
    )
```

```python
import functools
import math

import jax
import jax.numpy as jnp
from jax import lax
from jax.experimental import pallas as pl
from jax.experimental.pallas import tpu as pltpu
from jax.sharding import PartitionSpec as P

HEAD_WIDTH = 128
QUERY_PER_KEY = 5
GROUP = QUERY_PER_KEY * HEAD_WIDTH
EXP2_SCALE = math.log2(math.e) / math.sqrt(HEAD_WIDTH)
MASKED = -1e30
VMEM_LIMIT = 16 * 1024 * 1024
TILE = 16
HEADER = 8
PIECES = 5


def ring_of_chips(chips):
    half = chips // 2
    if chips == 8:
        return [2 * z for z in range(half)] + [2 * z + 1 for z in reversed(range(half))]
    return list(range(half)) + list(reversed(range(half, chips)))


def ring_pairs(chips, step, cross=False):
    ring = ring_of_chips(chips)
    return [
        (2 * ring[i] + core, 2 * ring[(i + step) % chips] + (1 - core if cross else core))
        for i in range(chips)
        for core in range(2)
    ]


def my_core():
    return lax.rem(lax.axis_index("blk"), 2).astype(jnp.int32)


def product(a, b):
    return jnp.dot(a, b, preferred_element_type=jnp.float32)


def weigh(scores, high):
    return jnp.exp2((scores - high) * EXP2_SCALE).astype(jnp.bfloat16)


def turned_values(blocks):
    v = jnp.concatenate(blocks, axis=0)
    return jnp.concatenate([jnp.transpose(v), jnp.ones((TILE, v.shape[0]), v.dtype)], axis=0)


def fetch_columns(w_ref, first, held_ref, sems, sem):
    depth, width = held_ref.shape[0] // PIECES, held_ref.shape[1]
    copies = []
    for p in range(PIECES):
        at = pl.ds(p * depth, depth)
        copies.append(
            pltpu.make_async_copy(
                w_ref.at[at, pl.ds(first, width)], held_ref.at[at], sems.at[sem + p]
            )
        )
        copies[-1].start()
    return copies


def attend_kernel(plan, *refs):
    heads, chunk, owners = plan["heads"], plan["chunk"], plan["owners"]
    refs = list(refs)
    q_ref = refs.pop(0)
    mark_refs = [refs.pop(0) for _ in range(plan["marks"])]
    packets = [refs.pop(0) for _ in range(plan["packets"])]
    if plan["carried"]:
        in_high, in_sums = refs.pop(0), refs.pop(0)
    fetch = plan["fetch"]
    if fetch:
        w_ref = refs.pop(0)
    if plan["last"]:
        out_refs = {i: refs.pop(0) for i in plan["which"]}
    copies = []
    if fetch:
        sems = refs.pop()
        for n, (first, _) in enumerate(fetch):
            held_ref = refs.pop(0 if plan["last"] else 2)
            copies += fetch_columns(w_ref, first, held_ref, sems, n * PIECES)
    if plan["part"] is None:
        high_ref, sums_ref = refs

    sources = mark_refs + packets
    numbers = [
        jnp.max(
            sources[packet][row : row + HEADER].astype(jnp.float32)
        ).astype(jnp.int32)
        for packet, row in plan["owner_headers"] + plan["headers"]
    ]
    owner_c, member_c = numbers[:owners], numbers[owners:]

    def rows_of(j, half, block):
        packet, row = plan["members"][j]
        at = row + (2 * block + half) * chunk
        return packets[packet][pl.ds(at if isinstance(at, int) else pl.multiple_of(at, TILE), chunk)]

    def state_at(i, half, h):
        return (2 * i + half) * heads + h

    rows = QUERY_PER_KEY * chunk
    causal = lax.broadcasted_iota(jnp.int32, (chunk, rows), 0) <= lax.rem(
        lax.broadcasted_iota(jnp.int32, (chunk, rows), 1), chunk
    )
    count = len(plan["members"])

    def one_chain(group, h, i, shared):
        first, done = group[0], group[-1] == count - 1
        k_at, v_at = h, heads + h
        late_at, early_at = state_at(i, 1, h), state_at(i, 0, h)
        if "keys" not in shared:
            shared["keys"] = jnp.concatenate([rows_of(j, 0, k_at) for j in group], axis=0)
            shared["values"] = turned_values([rows_of(j, 0, v_at) for j in group])
        carried = None
        if first > 0:
            carried = [(ref[early_at], ref[late_at]) for ref in (high_ref, sums_ref)]
        elif plan["carried"]:
            carried = [(ref[early_at], ref[late_at]) for ref in (in_high, in_sums)]
        pairs = []
        for j in group:
            if plan["own"] and j == plan["own_at"](i):
                pairs += [(j, 0, causal), (j, 1, causal)]
            else:
                pairs.append((j, (member_c[j] > owner_c[i]).astype(jnp.int32), None))
        base = product(shared["keys"], q_ref[late_at])
        scores = []
        for j, half, mask in pairs:
            s = product(rows_of(j, half, k_at), q_ref[state_at(i, half, h)])
            scores.append(s if mask is None else jnp.where(mask, s, MASKED))
        values = turned_values([rows_of(j, half, v_at) for j, half, _ in pairs])
        tops = [jnp.max(s, axis=0, keepdims=True) for s in scores]
        highs = []
        for side in range(2):
            some = [jnp.where(half == side, top, MASKED) for (_, half, _), top in zip(pairs, tops)]
            if side == 1:
                some.append(jnp.max(base, axis=0, keepdims=True))
            if carried is not None:
                some.append(carried[0][side])
            highs.append(functools.reduce(jnp.maximum, some))
        yield
        base_weights = weigh(base, highs[1])
        weights = [
            weigh(s, jnp.where(half == 1, highs[1], highs[0])) for (_, half, _), s in zip(pairs, scores)
        ]
        zero = jnp.zeros_like(weights[0])
        chosen = [
            jnp.concatenate(
                [jnp.where(half == side, w, zero) for (_, half, _), w in zip(pairs, weights)], axis=0
            )
            for side in range(2)
        ]
        yield
        for side, at in ((0, early_at), (1, late_at)):
            sums = product(values, chosen[side])
            if side == 1:
                sums = sums + product(shared["values"], base_weights)
            if carried is not None:
                shrink = jnp.exp2((carried[0][side] - highs[side]) * EXP2_SCALE)
                sums = sums + carried[1][side] * shrink
            if plan["last"] and done:
                mixed = sums[:HEAD_WIDTH] * (1.0 / sums[HEAD_WIDTH : HEAD_WIDTH + 1])
                mixed = jnp.transpose(mixed.astype(out_refs[i].dtype))
                place = side
                if plan["sent_first"]:
                    place = (lax.axis_index("inner") == side).astype(jnp.int32)
                rows_at = pl.ds(pl.multiple_of(place * chunk, TILE), chunk)
                for g in range(QUERY_PER_KEY):
                    to = pl.multiple_of(h * GROUP + g * HEAD_WIDTH, HEAD_WIDTH)
                    out_refs[i][rows_at, pl.ds(to, HEAD_WIDTH)] = mixed[g * chunk : (g + 1) * chunk]
            else:
                high_ref[at] = highs[side]
                sums_ref[at] = sums
        yield

    def one_side(h, i, side):
        at = state_at(i, side, h)
        visible = [member_c[j] > owner_c[i] if side else member_c[j] < owner_c[i] for j in range(count)]
        halves = ([(j, 0) for j in range(count)] if side else []) + [(j, side) for j in range(count)]
        k = jnp.concatenate([rows_of(j, half, h) for j, half in halves], axis=0)
        values = turned_values([rows_of(j, half, heads + h) for j, half in halves])
        s = product(k, q_ref[at])
        whole = (len(halves) - count) * chunk
        blocks = [s[whole + j * chunk : whole + (j + 1) * chunk] for j in range(count)]
        tops = [in_high[at]]
        if side:
            tops.append(jnp.max(s[:whole], axis=0, keepdims=True))
        for block, seen in zip(blocks, visible):
            tops.append(jnp.where(seen, jnp.max(block, axis=0, keepdims=True), MASKED))
        high = functools.reduce(jnp.maximum, tops)
        yield
        weights = [weigh(s[:whole], high)] if side else []
        for block, seen in zip(blocks, visible):
            w = weigh(block, high)
            weights.append(jnp.where(seen, w, jnp.zeros_like(w)))
        weights = jnp.concatenate(weights, axis=0)
        yield
        shrink = jnp.exp2((in_high[at] - high) * EXP2_SCALE)
        sums = product(values, weights) + in_sums[at] * shrink
        mixed = sums[:HEAD_WIDTH] * (1.0 / sums[HEAD_WIDTH : HEAD_WIDTH + 1])
        mixed = jnp.transpose(mixed.astype(out_refs[i].dtype))
        for g in range(QUERY_PER_KEY):
            to = h * GROUP + g * HEAD_WIDTH
            out_refs[i][:, to : to + HEAD_WIDTH] = mixed[g * chunk : (g + 1) * chunk]
        yield

    def staggered(chains):
        for t in range(len(chains) + 2):
            for stage in (2, 1, 0):
                if 0 <= t - stage < len(chains):
                    next(chains[t - stage])

    if plan["part"] is not None:
        mine = lax.axis_index("inner").astype(jnp.int32)
        for side in range(2):

            @pl.when((mine == side) == (plan["part"] == "kept"))
            def _(side=side):
                staggered([one_side(h, i, side) for h in range(heads) for i in plan["which"]])

        return

    for first in range(0, count, 6):
        group = range(first, min(first + 6, count))

        def run(heads_at_once, group=group):
            chains = []
            for h in heads_at_once:
                shared = {}
                chains += [one_chain(group, h, i, shared) for i in plan["which"]]
            staggered(chains)

        if fetch:

            def one_head(h, carry):
                run([h])
                return carry

            lax.fori_loop(0, heads, one_head, 0)
        else:
            run(range(heads))
    for copy in copies:
        copy.wait()


def attend(plan, turned, marks, packets, state, out_weight=None):
    heads, chunk, owners = plan["heads"], plan["chunk"], plan["owners"]
    count = len(plan["members"])
    plan = dict(plan, marks=len(marks), packets=len(packets), carried=state is not None)
    fetch = plan.setdefault("fetch", None)
    which = plan.setdefault("which", range(owners))
    part = plan.setdefault("part", None)
    plan.setdefault("sent_first", False)
    rows = QUERY_PER_KEY * chunk
    slots = owners * 2 * heads
    vmem = pl.BlockSpec(memory_space=pltpu.VMEM)
    kept = [(slots, 1, rows), (slots, HEAD_WIDTH + TILE, rows)]
    if plan["last"]:
        shape = ((2 if part is None else 1) * chunk, heads * GROUP)
        out_shape = [jax.ShapeDtypeStruct(shape, jnp.bfloat16)] * len(which)
    else:
        out_shape = [jax.ShapeDtypeStruct(shape, jnp.float32) for shape in kept]
    operands = 1 + len(marks) + len(packets) + (0 if state is None else 2)
    in_specs = [vmem] * operands
    scratch = []
    if plan["last"] and part is None:
        scratch = [pltpu.VMEM(shape, jnp.float32) for shape in kept]
    if fetch:
        in_specs.append(pl.BlockSpec(memory_space=pltpu.HBM))
        for _, columns in fetch:
            out_shape.append(jax.ShapeDtypeStruct((out_weight.shape[0], columns), out_weight.dtype))
        scratch.append(pltpu.SemaphoreType.DMA((PIECES * len(fetch),)))
    flops = 4 * owners * heads * rows * HEAD_WIDTH * count * chunk * 2
    return pl.pallas_call(
        functools.partial(attend_kernel, plan),
        out_shape=out_shape,
        in_specs=in_specs,
        out_specs=[vmem] * len(out_shape),
        scratch_shapes=scratch,
        cost_estimate=pl.CostEstimate(
            flops=flops, bytes_accessed=4 << 20, transcendentals=flops // 512
        ),
        compiler_params=pltpu.CompilerParams(vmem_limit_bytes=VMEM_LIMIT),
        name="attend",
    )(turned, *marks, *packets, *(state or ()), *([out_weight] if fetch else []))


def turn_kernel(heads, chunk, *refs):
    q_refs, turned_ref = refs[:-1], refs[-1]
    for i, q_ref in enumerate(q_refs):
        for half in range(2):
            for h in range(heads):
                columns = [slice(at, at + HEAD_WIDTH) for at in range(h * GROUP, (h + 1) * GROUP, HEAD_WIDTH)]
                q = jnp.concatenate(
                    [q_ref[half * chunk : (half + 1) * chunk, at] for at in columns], axis=0
                )
                turned_ref[(2 * i + half) * heads + h] = jnp.transpose(q)


def turn(heads, chunk, queries):
    vmem = pl.BlockSpec(memory_space=pltpu.VMEM)
    owners = len(queries)
    shape = (2 * owners * heads, HEAD_WIDTH, QUERY_PER_KEY * chunk)
    return pl.pallas_call(
        functools.partial(turn_kernel, heads, chunk),
        out_shape=jax.ShapeDtypeStruct(shape, jnp.bfloat16),
        in_specs=[vmem] * owners,
        out_specs=vmem,
        cost_estimate=pl.CostEstimate(flops=1 << 10, bytes_accessed=1 << 10, transcendentals=0),
        compiler_params=pltpu.CompilerParams(vmem_limit_bytes=VMEM_LIMIT),
        name="turn",
    )(*queries)


def rows_of_core(held_ref, core):
    depth = held_ref.shape[0] // 2
    return held_ref[pl.ds(pl.multiple_of(core * depth, depth), depth)]


def join_heads(own_ref, other_ref, rows_ref):
    part, left = own_ref.shape[1], my_core() == 0
    rows_ref[:, :part] = jnp.where(left, own_ref[...], other_ref[...])
    rows_ref[:, part:] = jnp.where(left, other_ref[...], own_ref[...])


def begin_kernel(own_ref, held_ref, begun_ref):
    begun_ref[...] = product(own_ref[...], rows_of_core(held_ref, my_core()))


def first_kernel(other_ref, held_ref, begun_ref, sent_ref):
    total = begun_ref[...] + product(other_ref[...], rows_of_core(held_ref, 1 - my_core()))
    sent_ref[...] = total.astype(sent_ref.dtype)


def project_kernel(bring, *refs):
    refs, copies = list(refs), []
    sent_rows, kept_rows, held_ref = refs[:2], refs[2:4], refs[4]
    refs = refs[5:]
    if bring:
        w_ref, sems = refs.pop(0), refs.pop()
    sent_ref, kept_ref = refs.pop(0), refs.pop(0)
    for n, (first, _) in enumerate(bring):
        copies += fetch_columns(w_ref, first, refs.pop(0), sems, n * PIECES)
    (rows_ref,) = refs
    chunk = sent_ref.shape[0]
    join_heads(*sent_rows, rows_ref.at[:chunk])
    join_heads(*kept_rows, rows_ref.at[chunk:])
    both = product(rows_ref[...], held_ref[...]).astype(sent_ref.dtype)
    sent_ref[...] = both[:chunk]
    kept_ref[...] = both[chunk:]
    for copy in copies:
        copy.wait()


def keep_kernel(own_ref, other_ref, held_ref, kept_ref, rows_ref):
    join_heads(own_ref, other_ref, rows_ref)
    kept_ref[...] = product(rows_ref[...], held_ref[...]).astype(kept_ref.dtype)


def multiply(kernel, operands, outputs, scratch=(), weight=None):
    vmem = pl.BlockSpec(memory_space=pltpu.VMEM)
    more = [] if weight is None else [weight]
    return pl.pallas_call(
        kernel,
        out_shape=[jax.ShapeDtypeStruct(shape, kind) for shape, kind in outputs],
        in_specs=[vmem] * len(operands) + [pl.BlockSpec(memory_space=pltpu.HBM)] * len(more),
        out_specs=[vmem] * len(outputs),
        scratch_shapes=list(scratch),
        cost_estimate=pl.CostEstimate(flops=1 << 10, bytes_accessed=1 << 10, transcendentals=0),
        compiler_params=pltpu.CompilerParams(vmem_limit_bytes=VMEM_LIMIT),
        name="multiply",
    )(*operands, *more)


def prepare_kernel(
    chunk, q_ref, k_ref, v_ref, position_ref, sent_ref, kept_ref, *query_refs_and_scratch
):
    *query_refs, first_ref, sems = query_refs_and_scratch
    rows, heads = k_ref.shape[0], k_ref.shape[1] // HEAD_WIDTH // 2
    columns = query_refs[0].shape[1]
    copies = [pltpu.make_async_copy(position_ref, first_ref, sems.at[0])]
    for ref, core in ((sent_ref, 1 - my_core()), (kept_ref, my_core())):
        for m, source in enumerate((k_ref, v_ref)):
            for h in range(heads):
                at = pl.ds(pl.multiple_of((core * heads + h) * HEAD_WIDTH, HEAD_WIDTH), HEAD_WIDTH)
                to = ref.at[pl.ds((m * heads + h) * rows, rows)]
                copies.append(pltpu.make_async_copy(source.at[:, at], to, sems.at[len(copies)]))
    for ref, core in zip(query_refs, (1 - my_core(), my_core())):
        at = pl.ds(pl.multiple_of(core * columns, columns), columns)
        copies.append(pltpu.make_async_copy(q_ref.at[:, at], ref, sems.at[len(copies)]))
    for copy in copies:
        copy.start()
    copies[0].wait()
    c = lax.div(first_ref[0], jnp.int32(chunk)).astype(jnp.float32)
    header = jnp.full((HEADER, HEAD_WIDTH), c, jnp.float32).astype(jnp.bfloat16)
    sent_ref[2 * heads * rows :] = header
    kept_ref[2 * heads * rows :] = header
    for copy in copies[1:]:
        copy.wait()


def prepare(queries, keys, values, positions):
    vmem = pl.BlockSpec(memory_space=pltpu.VMEM)
    hbm = pl.BlockSpec(memory_space=pltpu.HBM)
    rows, blocks = keys.shape[0], keys.shape[1] // HEAD_WIDTH
    operands = [pltpu.with_memory_space_constraint(x, pltpu.HBM) for x in (queries, keys, values, positions)]
    return pl.pallas_call(
        functools.partial(prepare_kernel, rows // 2),
        out_shape=[jax.ShapeDtypeStruct((blocks * rows + HEADER, HEAD_WIDTH), jnp.bfloat16)] * 2
        + [jax.ShapeDtypeStruct((rows, queries.shape[1] // 2), jnp.bfloat16)] * 2,
        in_specs=[hbm] * 4,
        out_specs=[vmem] * 4,
        scratch_shapes=[
            pltpu.SMEM(positions.shape, jnp.int32),
            pltpu.SemaphoreType.DMA((3 + 2 * blocks,)),
        ],
        compiler_params=pltpu.CompilerParams(vmem_limit_bytes=VMEM_LIMIT),
        name="prepare",
    )(*operands)


def finish_kernel(first, pairs, *refs):
    out_ref, total_ref, sem = refs[-3:]
    at = 0
    for mine, theirs in zip(refs[:pairs], refs[pairs : 2 * pairs]):
        width = mine.shape[1]
        total = mine[...].astype(jnp.float32) + theirs[...].astype(jnp.float32)
        total_ref[:, at : at + width] = total.astype(total_ref.dtype)
        at += width
    copy = pltpu.make_async_copy(total_ref, out_ref.at[:, pl.ds(first, at)], sem)
    copy.start()
    copy.wait()


def finish(kept, received, first, columns, written=None):
    vmem, hbm = pl.BlockSpec(memory_space=pltpu.VMEM), pl.BlockSpec(memory_space=pltpu.HBM)
    rows, width = kept[0].shape[0], sum(part.shape[1] for part in kept)
    pairs = len(kept)
    return pl.pallas_call(
        functools.partial(finish_kernel, first, pairs),
        out_shape=jax.ShapeDtypeStruct((rows, columns), kept[0].dtype),
        in_specs=[vmem] * (2 * pairs) + ([] if written is None else [hbm]),
        out_specs=hbm,
        input_output_aliases={} if written is None else {2 * pairs: 0},
        scratch_shapes=[pltpu.VMEM((rows, width), kept[0].dtype), pltpu.SemaphoreType.DMA],
        cost_estimate=pl.CostEstimate(flops=1 << 10, bytes_accessed=1 << 10, transcendentals=0),
        compiler_params=pltpu.CompilerParams(vmem_limit_bytes=VMEM_LIMIT),
        name="finish",
    )(*kept, *received, *([] if written is None else [written]))


def after(value, *events):
    return lax.optimization_barrier((value, events))[0]


def split_over_cores(count, queries, keys, values, positions, out_weight, fetch):
    chips, half = count // 2, count // 4
    rows, chunk = queries.shape[0], queries.shape[0] // 2
    heads = keys.shape[1] // HEAD_WIDTH // 2
    sibling = [(b, b ^ 1) for b in range(count)]
    clock, counter = ring_pairs(chips, 1), ring_pairs(chips, -1)
    up = lambda x: lax.ppermute(x, "blk", clock)
    down = lambda x: lax.ppermute(x, "blk", counter)
    cross_up, cross_down = ring_pairs(chips, 1, True), ring_pairs(chips, -1, True)

    sent, x, q_sent, q_own = prepare(queries, keys, values, positions)
    y = lax.ppermute(sent, "blk", sibling)
    q_got = lax.ppermute(q_sent, "blk", sibling)
    turned = turn(heads, chunk, [q_own, q_got])

    def call(pairs, state, own=False, last=False, fetch=None, which=(0, 1), part=None):
        each = range(len(pairs))
        plan = dict(
            heads=heads,
            chunk=chunk,
            owners=2,
            own=own,
            own_at=lambda i: i,
            last=last,
            members=[(2 * j + i, 0) for j in each for i in range(2)],
            headers=[(2 + 2 * j + i, 2 * heads * rows) for j in each for i in range(2)],
            owner_headers=[(0, 2 * heads * rows), (1, 2 * heads * rows)],
            fetch=fetch,
            which=which,
            part=part,
            sent_first=True,
        )
        packets = [packet for pair in pairs for packet in pair]
        return attend(plan, turned, [x, y], packets, state, out_weight)

    held = {}

    def bring_with(groups, *arguments, **settings):
        cuts = [fetch[j] for j in groups]
        results = call(*arguments, fetch=cuts, **settings)
        held.update(zip(groups, results[2:]))
        return results[:2]

    state = bring_with((2,), [(x, y)], None, own=True)
    for r in range(1, half):
        if r == 1:
            up_first, up_second = up(x), lax.ppermute(sent, "blk", cross_up)
            down_first, down_second = lax.ppermute(sent, "blk", cross_down), down(x)
        else:
            up_first, down_first, *state = lax.optimization_barrier((up_first, down_first, *state))
            up_first, up_second = up(up_first), up(up_second)
            down_first, down_second = down(down_first), down(down_second)
            state = bring_with((0,) if r == half - 1 else (), arrived, state)
        arrived = [(up_first, up_second), (down_second, down_first)]
    up_first, down_first, *state = lax.optimization_barrier((up_first, down_first, *state))
    far = (up(up_first), down(down_first))
    state = bring_with((1,), arrived, state)
    (theirs,) = call([far], state, last=True, which=(1,))
    other = [lax.ppermute(rows, "blk", sibling) for rows in (theirs[:chunk], theirs[chunk:])]
    (own,) = call([far], state, last=True, which=(0,), part="sent")

    def own_to_keep(event):
        return call([far], after(state, event), last=True, which=(0,), part="kept")[0]

    return own, other, held, own_to_keep


def one_head_a_device(count, queries, keys, values, positions):
    rows, chunk = queries.shape[0], queries.shape[0] // 2
    heads = keys.shape[1] // HEAD_WIDTH
    c = (positions[:1] // chunk).astype(jnp.bfloat16).reshape(1, 1)
    blocks = [x[:, h * HEAD_WIDTH : (h + 1) * HEAD_WIDTH] for x in (keys, values) for h in range(heads)]
    packet = jnp.concatenate(blocks + [jnp.broadcast_to(c, (TILE, HEAD_WIDTH))], axis=0)
    packets = lax.all_gather(packet, "blk", axis=0, tiled=True)
    size = packet.shape[0]
    here = lax.axis_index("blk")
    order = lax.rem(here + jnp.arange(count), count)
    packets = packets.reshape(count, size, -1)[order].reshape(count * size, -1)
    plan = dict(
        heads=heads,
        chunk=chunk,
        owners=1,
        own=True,
        own_at=lambda i: 0,
        last=True,
        members=[(0, j * size) for j in range(count)],
        headers=[(0, (j + 1) * size - TILE) for j in range(count)],
        owner_headers=[(0, size - TILE)],
    )
    turned = turn(heads, chunk, [queries])
    return attend(plan, turned, [], [packets], None)[0]


def shards(count, inner, queries, keys, values, positions, out_weight):
    heads = keys.shape[1] // HEAD_WIDTH
    if heads % 2:
        attended = one_head_a_device(count, queries, keys, values, positions)
        partial = jnp.dot(attended, out_weight, preferred_element_type=jnp.float32)
        return lax.psum_scatter(
            partial.astype(jnp.bfloat16), "inner", scatter_dimension=0, tiled=True
        )
    out_weight = pltpu.with_memory_space_constraint(out_weight, pltpu.HBM)
    shares = (11, 10, 8, 6, 5)
    widths = [out_weight.shape[1] * share // sum(shares) for share in shares]
    cuts = [(sum(widths[:j]), columns) for j, columns in enumerate(widths)]
    own, (other, other_kept), held, own_to_keep = split_over_cores(
        count, queries, keys, values, positions, out_weight, cuts[:3]
    )
    chunk, depth, kind = own.shape[0], out_weight.shape[0], own.dtype
    (begun,) = multiply(begin_kernel, [own, held[0]], [((chunk, widths[0]), jnp.float32)])
    (sent,) = multiply(first_kernel, [other, held[0], begun], [((chunk, widths[0]), kind)])
    own_kept = own_to_keep(sent)
    received, kept = [], [None]
    for j in range(len(cuts)):
        if j > 0:
            bring = cuts[j + 2 : j + 3]
            results = multiply(
                functools.partial(project_kernel, bring),
                [after(own, sent), other, own_kept, other_kept, held[j]],
                [((chunk, widths[j]), kind)] * 2 + [((depth, columns), kind) for _, columns in bring],
                [pltpu.VMEM((2 * chunk, depth), kind)] + [pltpu.SemaphoreType.DMA((PIECES,))] * len(bring),
                out_weight if bring else None,
            )
            sent, keep = results[:2]
            kept.append(keep)
            if bring:
                held[j + 2] = results[2]
        received.append(lax.ppermute(sent, "inner", [(0, 1), (1, 0)]))
    (kept[0],) = multiply(
        keep_kernel,
        [after(own_kept, sent), other_kept, held[0]],
        [((chunk, widths[0]), kind)],
        [pltpu.VMEM((chunk, depth), kind)],
    )
    columns = out_weight.shape[1]
    result = finish(kept[:-1], received[:-1], 0, columns)
    return finish(kept[-1:], received[-1:], cuts[-1][0], columns, result)


def solution(mesh):
    placed = (P("blk", "inner"), P("blk", "inner"), P("blk", "inner"), P("blk"), P("inner", None))
    return jax.shard_map(
        functools.partial(shards, mesh.shape["blk"], mesh.shape["inner"]),
        mesh=mesh,
        in_specs=placed,
        out_specs=P(("blk", "inner"), None),
        check_vma=False,
    )
```
